32 devices in a mesh: grp: 4 (over x, core), blk: 8 (over z, y).
Axes of the slice: x: 2, y: 2, z: 4, core: 2. Of those that a mesh axis runs over, the one named last changes fastest.
Arguments:
- block_input: bfloat16 [4, 1024, 2048], P('grp', 'blk'), may hold values from -6 to 6
- doc_lens: int32 [4, 8], P('grp'), may hold values from 1 to 1024, as said below
- norm_attn: bfloat16 [2048], P('blk'), may hold values from 0.5 to 1.5
- w_qkv: bfloat16 [2048, 6144], P('blk'), may hold values from -0.125 to 0.125
- w_out: bfloat16 [2048, 2048], P('blk'), may hold values from -2 to 2
- norm_mlp: bfloat16 [2048], P('blk'), may hold values from 0.5 to 1.5
- w_gate: bfloat16 [2048, 5632], P('blk'), may hold values from -0.125 to 0.125
- w_up: bfloat16 [2048, 5632], P('blk'), may hold values from -0.125 to 0.125
- w_down: bfloat16 [5632, 2048], P('blk'), may hold values from -0.078125 to 0.078125
- cot: bfloat16 [4, 1024, 2048], P('grp', 'blk'), may hold values from -6 to 6
Outputs:
- block_out: bfloat16 [4, 1024, 2048], P('grp', 'blk')
- x_grad: bfloat16 [4, 1024, 2048], P('grp', 'blk')
- grad_norm_attn: float32 [2048], P('blk')
- grad_qkv: float32 [2048, 6144], P('blk')
- grad_out: float32 [2048, 2048], P('blk')
- grad_norm_mlp: float32 [2048], P('blk')
- grad_gate: float32 [2048, 5632], P('blk')
- grad_up: float32 [2048, 5632], P('blk')
- grad_down: float32 [5632, 2048], P('blk')
The draws below stay inside these ranges and needn't reach their ends.
Inputs may be any that keep to these rules, and one draw needn't show every extreme that they name: `doc_lens`: each row lists the lengths of 8 documents packed in order over its stream; they sum to 1024, and one of them begins within the first 128 positions and ends within the last 128.
All inputs are finite; a program needn't handle non-finite values.
Results may differ from the reference program's by a relative error of at most 0.023.
Values may be sent and summed in bfloat16 or wider, within the bound.
A program may use at most 640 MiB of HBM per device.

```python
import math
import jax
import jax.numpy as jnp
from jax import lax

D = 2048
HEADS = 16
HEAD = 128
FF = 5632
TOK_DEV = 128
DOCS = 8
SEQ = 1024
STREAMS = 4


def draw_doc_lens(key, part):
    key = jax.random.fold_in(key, 7)
    key_short, key_where = jax.random.split(key)
    short_most = (TOK_DEV - 1) // (DOCS - 1)
    short_lens = jax.random.randint(key_short, (STREAMS, DOCS), 1, short_most + 1)
    long_at = jax.random.randint(key_where, (STREAMS, 1), 0, DOCS)
    column = jnp.arange(DOCS)[None, :]
    short_lens = jnp.where(column == long_at, 0, short_lens)
    longest = SEQ - jnp.sum(short_lens, axis=1, keepdims=True)
    return jnp.where(column == long_at, longest, short_lens).astype(jnp.int32)


def block_scale(stream_key, extent, cuts, low, high):
    level, own = 1.0, jax.random.fold_in(stream_key, 6)
    for axis_at, parts in cuts:
        draws = jnp.exp(jax.random.uniform(jax.random.fold_in(own, axis_at), (parts,), jnp.float32, low / len(cuts), high / len(cuts)))
        level = level * jnp.repeat(draws, extent[axis_at] // parts).reshape([-1 if axis == axis_at else 1 for axis in range(len(extent))])
    return level


def noise(key, extent, scale, most, pieces=(), kind=jnp.bfloat16):
    values = scale * jax.random.normal(key, extent, jnp.float32)
    if pieces:
        values = values * block_scale(key, extent, pieces, -0.22, 0.18)
    return jnp.clip(values, -most, most).astype(kind)


def setup_inputs(seed: int = 0) -> dict:
    splits = jax.random.split(jax.random.key(seed), 11)
    return {
        "block_input": noise(splits[0], (STREAMS, SEQ, D), 1.0, 6.0, ((0, 4), (1, 8))),
        "doc_lens": draw_doc_lens(jax.random.fold_in(splits[10], 71), 0),
        "norm_attn": jnp.clip(1.0 + 0.1 * jax.random.normal(splits[2], (D,), jnp.float32), 0.5, 1.5).astype(jnp.bfloat16),
        "w_qkv": noise(splits[3], (D, 3 * D), D ** -0.5, 0.125, ((0, 8),)),
        "w_out": noise(splits[4], (D, D), (max(D // 256, 1)) ** -0.5, 2.0, ((0, 8),)),
        "norm_mlp": jnp.clip(1.0 + 0.1 * jax.random.normal(splits[5], (D,), jnp.float32), 0.5, 1.5).astype(jnp.bfloat16),
        "w_gate": noise(splits[6], (D, FF), D ** -0.5, 0.125, ((0, 8),)),
        "w_up": noise(splits[7], (D, FF), D ** -0.5, 0.125, ((0, 8),)),
        "w_down": noise(splits[8], (FF, D), FF ** -0.5, 0.078125, ((0, 8),)),
        "cot": noise(splits[9], (STREAMS, SEQ, D), 1.0, 6.0, ((0, 4), (1, 8))),
    }


EPS = 1e-05
NEGATIVE = -1e+30

@jax.custom_vjp
def low(v):
    return lax.optimization_barrier(v.astype(jnp.bfloat16)).astype(jnp.float32)

@jax.custom_vjp
def low_back(v):
    return v

def low_keep(v):
    return (low(v), None)

def low_pass(kept, grad):
    return (grad,)

def back_keep(v):
    return (v, None)

def back_low(kept, grad):
    return (low(grad),)
low.defvjp(low_keep, low_pass)
low_back.defvjp(back_keep, back_low)

def rms_scale(values):
    return lax.rsqrt(lax.optimization_barrier(jnp.mean(values * values, axis=-1, keepdims=True)) + EPS)

def rotate(tensor, places):
    half_size = HEAD // 2
    freqs = jnp.exp(jnp.arange(half_size, dtype=jnp.float32) * (-2.0 * math.log(10000.0) / HEAD))
    angles = places.astype(jnp.float32)[..., None] * freqs
    cosine = jnp.cos(angles)[..., None, :]
    sine_part = jnp.sin(angles)[..., None, :]
    first_half = tensor[..., :half_size]
    second_half = tensor[..., half_size:]
    return jnp.concatenate([first_half * cosine - second_half * sine_part, second_half * cosine + first_half * sine_part], axis=-1)

def doc_info(lengths):
    starts = (jnp.cumsum(lengths) - lengths).astype(jnp.int32)
    places = jnp.arange(SEQ, dtype=jnp.int32)
    inside = starts[None, :] <= places[:, None]
    segment = (lax.optimization_barrier(jnp.sum(inside.astype(jnp.int32), axis=1)) - 1).astype(jnp.int32)
    begins = lax.optimization_barrier(jnp.max(jnp.where(inside, starts[None, :], 0), axis=1)).astype(jnp.int32)
    return (segment, (places - begins).astype(jnp.int32))

def attend_stream(operands):
    queries, keys_all, values_all, segment = operands
    block_rows = math.gcd(SEQ, 512)
    score_scale = HEAD ** (-0.5)
    key_places = jnp.arange(SEQ, dtype=jnp.int32)

    def one_block(block_index):
        offset = (block_index * block_rows).astype(jnp.int32)
        query_block = lax.dynamic_slice_in_dim(queries, offset, block_rows, 0)
        query_seg = lax.dynamic_slice_in_dim(segment, offset, block_rows, 0)
        query_places = offset + jnp.arange(block_rows, dtype=jnp.int32)
        scores = low_back(jnp.einsum('qhd,khd->hqk', query_block, keys_all, precision=lax.Precision.HIGHEST) * score_scale)
        allowed = (query_seg[:, None] == segment[None, :]) & (key_places[None, :] <= query_places[:, None])
        masked = jnp.where(allowed[None], scores, NEGATIVE)
        row_peak = lax.optimization_barrier(jnp.max(masked, axis=-1, keepdims=True))
        raw_weight = jnp.where(allowed[None], jnp.exp(masked - row_peak), 0.0)
        prob_rows = low(raw_weight / lax.optimization_barrier(jnp.sum(raw_weight, axis=-1, keepdims=True)))
        return jnp.einsum('hqk,khd->qhd', prob_rows, values_all, precision=lax.Precision.HIGHEST)
    blocks = lax.map(jax.checkpoint(one_block), jnp.arange(SEQ // block_rows, dtype=jnp.int32))
    return blocks.reshape(SEQ, HEADS, HEAD)

def forward(x_float, gain_one, w_qkv, w_out, gain_two, w_gate, w_up, w_down, segments, places):
    flat_rows = x_float.reshape(-1, D)
    normed_one = low(flat_rows * rms_scale(flat_rows) * gain_one)
    projected = low_back(jnp.dot(normed_one, w_qkv, precision=lax.Precision.HIGHEST))
    heads_all = projected.reshape(STREAMS, SEQ, 3, HEADS, HEAD)
    queries = low(rotate(heads_all[:, :, 0], places))
    keys_all = low(rotate(heads_all[:, :, 1], places))
    values_all = low(heads_all[:, :, 2])
    attended = lax.map(attend_stream, (queries, keys_all, values_all, segments))
    attended = low(low_back(attended.reshape(-1, D)))
    resid = flat_rows + low_back(jnp.dot(attended, w_out, precision=lax.Precision.HIGHEST))
    normed_two = low(resid * rms_scale(resid) * gain_two)
    gate_proj = low_back(jnp.dot(normed_two, w_gate, precision=lax.Precision.HIGHEST))
    up_proj = low_back(jnp.dot(normed_two, w_up, precision=lax.Precision.HIGHEST))
    hidden = low(jax.nn.silu(gate_proj) * up_proj)
    result = resid + jnp.dot(hidden, w_down, precision=lax.Precision.HIGHEST)
    return result.reshape(x_float.shape)

def reference(block_input, doc_lens, norm_attn, w_qkv, w_out, norm_mlp, w_gate, w_up, w_down, cot):
    segments, places = jax.vmap(doc_info)(doc_lens)
    inputs = tuple((entry_arr.astype(jnp.float32) for entry_arr in (block_input, norm_attn, w_qkv, w_out, norm_mlp, w_gate, w_up, w_down)))

    def wrapped(*floats):
        return forward(*floats, segments, places)
    block_out, pull_back = jax.vjp(wrapped, *inputs)
    gradients = pull_back(cot.astype(jnp.float32))
    return (block_out.astype(jnp.bfloat16), gradients[0].astype(jnp.bfloat16), gradients[1], gradients[2], gradients[3], gradients[4], gradients[5], gradients[6], gradients[7])
```

```python
import math

import jax
import jax.numpy as jnp
from jax import lax
from jax.sharding import PartitionSpec as P

HEADS = 16
HEAD = 128


EPS = 1e-05
NEGATIVE = -1e30


def angle_tables(places):
    half_size = HEAD // 2
    freqs = jnp.exp(jnp.arange(half_size, dtype=jnp.float32) * (-2.0 * math.log(10000.0) / HEAD))
    angles = places.astype(jnp.float32)[:, None] * freqs
    return (jnp.cos(angles)[:, None, :], jnp.sin(angles)[:, None, :])


def rotate(tensor, cosine, sine_part):
    half_size = HEAD // 2
    first_half = tensor[..., :half_size]
    second_half = tensor[..., half_size:]
    return jnp.concatenate(
        [
            first_half * cosine - second_half * sine_part,
            second_half * cosine + first_half * sine_part,
        ],
        axis=-1,
    )


def unrotate(tensor, cosine, sine_part):
    half_size = HEAD // 2
    first_half = tensor[..., :half_size]
    second_half = tensor[..., half_size:]
    return jnp.concatenate(
        [
            first_half * cosine + second_half * sine_part,
            second_half * cosine - first_half * sine_part,
        ],
        axis=-1,
    )


def segment_of(places, starts):
    return jnp.sum((starts[None, :] <= places[:, None]).astype(jnp.int32), axis=1) - 1


def start_of(places, starts):
    return jnp.max(jnp.where(starts[None, :] <= places[:, None], starts[None, :], 0), axis=1)


def contract_rows(left, right):
    return lax.dot_general(
        left, right, (((1,), (1,)), ((), ())), preferred_element_type=jnp.float32
    )


def weight_term(left, right):

    def term(start, count):
        return lax.dot_general(
            left, right, (((0,), (0,)), ((), ())), preferred_element_type=jnp.float32
        )

    return term


def shard_grad(term_fn, shard_rows):
    shared = lax.psum_scatter(
        term_fn(jnp.int32(0), shard_rows * lax.axis_size("blk")).astype(jnp.bfloat16),
        "blk",
        scatter_dimension=0,
        tiled=True,
    )
    return lax.psum(shared, "grp").astype(jnp.float32)


def per_device_gather(block_input, doc_lens, norm_attn, w_qkv, w_out, norm_mlp, w_gate, w_up, w_down, cot):
    tok_rows = block_input.shape[1]
    width = block_input.shape[2]
    score_scale = HEAD ** (-0.5)
    shards = (norm_attn, w_qkv, w_out, norm_mlp, w_gate, w_up, w_down)
    gathered = (
        lax.all_gather(shards[0], "blk", axis=0, tiled=True),
        lax.all_gather(shards[1], "blk", axis=0, tiled=True),
        lax.all_gather(shards[2], "blk", axis=0, tiled=True),
        lax.all_gather(shards[3], "blk", axis=0, tiled=True),
        lax.all_gather(shards[4], "blk", axis=0, tiled=True),
        lax.all_gather(shards[5], "blk", axis=0, tiled=True),
        lax.all_gather(shards[6], "blk", axis=0, tiled=True),
    )
    gain_one, weight_qkv, weight_out, gain_two, weight_gate, weight_up, weight_down = gathered
    place_rows = lax.axis_index("blk") * tok_rows + jnp.arange(tok_rows, dtype=jnp.int32)
    lengths = doc_lens[0]
    starts = jnp.cumsum(lengths) - lengths
    query_seg = segment_of(place_rows, starts)
    cosine, sine_part = angle_tables(place_rows - start_of(place_rows, starts))
    x_float = block_input[0].astype(jnp.float32)
    inv_one = lax.rsqrt(jnp.mean(x_float * x_float, axis=-1, keepdims=True) + EPS)
    normed_one = (x_float * inv_one * gain_one.astype(jnp.float32)).astype(jnp.bfloat16)
    projected = jnp.dot(normed_one, weight_qkv, preferred_element_type=jnp.float32)
    heads_all = projected.reshape(tok_rows, 3, HEADS, HEAD)
    queries = rotate(heads_all[:, 0], cosine, sine_part).astype(jnp.bfloat16)
    keys_own = rotate(heads_all[:, 1], cosine, sine_part).astype(jnp.bfloat16)
    values_own = heads_all[:, 2].astype(jnp.bfloat16)

    def pair_mask(count):
        key_places = jnp.arange(count, dtype=jnp.int32)
        key_seg = segment_of(key_places, starts)
        return (query_seg[:, None] == key_seg[None, :]) & (
            key_places[None, :] <= place_rows[:, None]
        )

    piece = (
        lax.all_gather(keys_own, "blk", axis=0, tiled=True),
        lax.all_gather(values_own, "blk", axis=0, tiled=True),
    )
    count = piece[0].shape[0]
    row_peak = jnp.full((HEADS, tok_rows), NEGATIVE, jnp.float32)
    key_piece, value_piece = piece
    count = key_piece.shape[0]
    allowed = pair_mask(count)[None]
    scores = (
        jnp.einsum("qhd,khd->hqk", queries, key_piece, preferred_element_type=jnp.float32)
        * score_scale
    )
    scores = jnp.where(allowed, scores, NEGATIVE)
    new_peak = jnp.maximum(row_peak, jnp.max(scores, axis=-1))
    weights_now = jnp.where(allowed, jnp.exp(scores - new_peak[..., None]), 0.0)
    row_total = jnp.sum(weights_now, axis=-1)
    accum = jnp.einsum(
        "hqk,khd->hqd",
        weights_now.astype(jnp.bfloat16),
        value_piece,
        preferred_element_type=jnp.float32,
    )
    row_peak, row_total, accum = (new_peak, row_total, accum)
    log_total = row_peak + jnp.log(row_total)
    attended = (accum / row_total[..., None]).transpose(1, 0, 2)
    attended_b = attended.reshape(tok_rows, width).astype(jnp.bfloat16)
    resid = x_float + jnp.dot(attended_b, weight_out, preferred_element_type=jnp.float32)
    inv_two = lax.rsqrt(jnp.mean(resid * resid, axis=-1, keepdims=True) + EPS)
    normed_two = (resid * inv_two * gain_two.astype(jnp.float32)).astype(jnp.bfloat16)
    gate_proj = jnp.dot(normed_two, weight_gate, preferred_element_type=jnp.float32)
    up_proj = jnp.dot(normed_two, weight_up, preferred_element_type=jnp.float32)
    sigmoid_gate = jax.nn.sigmoid(gate_proj)
    swish = gate_proj * sigmoid_gate
    hidden = (swish * up_proj).astype(jnp.bfloat16)
    block_out = (resid + jnp.dot(hidden, weight_down, preferred_element_type=jnp.float32)).astype(
        jnp.bfloat16
    )
    again = (
        lax.all_gather(shards[0], "blk", axis=0, tiled=True),
        lax.all_gather(shards[1], "blk", axis=0, tiled=True),
        lax.all_gather(shards[2], "blk", axis=0, tiled=True),
        lax.all_gather(shards[3], "blk", axis=0, tiled=True),
        lax.all_gather(shards[4], "blk", axis=0, tiled=True),
        lax.all_gather(shards[5], "blk", axis=0, tiled=True),
        lax.all_gather(shards[6], "blk", axis=0, tiled=True),
    )
    back_gain_one, back_qkv, back_out, back_gain_two, back_gate, back_up, back_down = again
    seed = cot[0]
    seed_float = seed.astype(jnp.float32)
    dhidden = contract_rows(seed, back_down)
    dgate = (dhidden * up_proj * sigmoid_gate * (1.0 + gate_proj * (1.0 - sigmoid_gate))).astype(
        jnp.bfloat16
    )
    dup = (dhidden * swish).astype(jnp.bfloat16)
    dnormed_two = contract_rows(dgate, back_gate) + contract_rows(dup, back_up)
    a_two = dnormed_two * back_gain_two.astype(jnp.float32)
    dresid = (
        seed_float
        + inv_two * a_two
        - resid * inv_two**3 * jnp.mean(a_two * resid, axis=-1, keepdims=True)
    )
    dresid_b = dresid.astype(jnp.bfloat16)
    dattended = (
        contract_rows(dresid_b, back_out).astype(jnp.bfloat16).reshape(tok_rows, HEADS, HEAD)
    )
    delta = jnp.sum(dattended.astype(jnp.float32) * attended, axis=-1).T
    piece = (
        lax.all_gather(keys_own, "blk", axis=0, tiled=True),
        lax.all_gather(values_own, "blk", axis=0, tiled=True),
    )
    count = piece[0].shape[0]
    key_piece, value_piece = piece
    count = key_piece.shape[0]
    score_count = key_piece.shape[0]
    allowed = pair_mask(score_count)[None]
    scores = (
        jnp.einsum("qhd,khd->hqk", queries, key_piece, preferred_element_type=jnp.float32)
        * score_scale
    )
    probs = jnp.where(allowed, jnp.exp(scores - log_total[..., None]), 0.0)
    dprobs = jnp.einsum("qhd,khd->hqk", dattended, value_piece, preferred_element_type=jnp.float32)
    dscores = (probs * (dprobs - delta[..., None])).astype(jnp.bfloat16)
    probs, dscores = (probs, dscores)
    dquery_acc = score_scale * jnp.einsum(
        "hqk,khd->hqd", dscores, key_piece, preferred_element_type=jnp.float32
    )
    dkeys = score_scale * jnp.einsum(
        "hqk,qhd->khd", dscores, queries, preferred_element_type=jnp.float32
    )
    dvalues = jnp.einsum(
        "hqk,qhd->khd", probs.astype(jnp.bfloat16), dattended, preferred_element_type=jnp.float32
    )
    stacked = jnp.concatenate([dkeys.reshape(count, width), dvalues.reshape(count, width)], axis=1)
    grads_buffer = stacked
    dquery_acc, grads_buffer = (dquery_acc, grads_buffer)
    own_grads = lax.psum_scatter(
        grads_buffer.astype(jnp.bfloat16), "blk", scatter_dimension=0, tiled=True
    ).astype(jnp.float32)
    dkey = unrotate(own_grads[:, :width].reshape(tok_rows, HEADS, HEAD), cosine, sine_part)
    dvalue = own_grads[:, width:].reshape(tok_rows, HEADS, HEAD)
    dquery = unrotate(dquery_acc.transpose(1, 0, 2), cosine, sine_part)
    dqkv = (
        jnp.stack([dquery, dkey, dvalue], axis=1).reshape(tok_rows, 3 * width).astype(jnp.bfloat16)
    )
    dnormed_one = contract_rows(dqkv, back_qkv)
    a_one = dnormed_one * back_gain_one.astype(jnp.float32)
    x_grad = (
        dresid
        + inv_one * a_one
        - x_float * inv_one**3 * jnp.mean(a_one * x_float, axis=-1, keepdims=True)
    ).astype(jnp.bfloat16)
    width_rows = norm_attn.shape[0]
    gain_terms = jnp.stack(
        [
            jnp.sum(dnormed_one * x_float * inv_one, axis=0),
            jnp.sum(dnormed_two * resid * inv_two, axis=0),
        ],
        axis=1,
    )

    def gain_slice(start, count):
        return gain_terms

    grad_down = shard_grad(weight_term(hidden, seed), w_down.shape[0])
    grad_gate = shard_grad(weight_term(normed_two, dgate), width_rows)
    grad_up = shard_grad(weight_term(normed_two, dup), width_rows)
    grad_out = shard_grad(weight_term(attended_b, dresid_b), width_rows)
    grad_qkv = shard_grad(weight_term(normed_one, dqkv), width_rows)
    gain_grads = shard_grad(gain_slice, width_rows)
    return (
        block_out[None],
        x_grad[None],
        gain_grads[:, 0],
        grad_qkv,
        grad_out,
        gain_grads[:, 1],
        grad_gate,
        grad_up,
        grad_down,
    )


def split_columns(shard, parts):
    rows, columns = shard.shape
    n = lax.axis_size("blk")
    cut = shard.reshape(rows, parts, n, columns // (parts * n)).transpose(2, 0, 1, 3)
    mixed = lax.all_to_all(cut, "blk", split_axis=0, concat_axis=0, tiled=True)
    return mixed.reshape(n * rows, columns // n)


def merge_columns(grad, parts):
    rows, columns = grad.shape
    n = lax.axis_size("blk")
    cut = grad.reshape(n, rows // n, columns)
    mixed = lax.all_to_all(cut, "blk", split_axis=0, concat_axis=0, tiled=True)
    mixed = mixed.reshape(n, rows // n, parts, columns // parts).transpose(1, 2, 0, 3)
    return mixed.reshape(rows // n, columns * n)


def gather_rows(block):
    return lax.all_gather(block, "blk", axis=0, tiled=True)


def scatter_rows(partial):
    return lax.psum_scatter(
        partial.astype(jnp.bfloat16), "blk", scatter_dimension=0, tiled=True
    ).astype(jnp.float32)


def dot_f32(left, right):
    return jnp.dot(left, right, preferred_element_type=jnp.float32)


def dot_t(left, right):
    return lax.dot_general(
        left, right, (((0,), (0,)), ((), ())), preferred_element_type=jnp.float32
    )


def per_device(block_input, doc_lens, norm_attn, w_qkv, w_out, norm_mlp, w_gate, w_up, w_down, cot):
    n = lax.axis_size("blk")
    tok_rows, width = block_input.shape[1:]
    seq = tok_rows * n
    heads = HEADS // n
    score_scale = HEAD ** (-0.5)
    gain_one = gather_rows(norm_attn).astype(jnp.float32)
    gain_two = gather_rows(norm_mlp).astype(jnp.float32)
    qkv_columns = split_columns(w_qkv, 3)
    places = jnp.arange(seq, dtype=jnp.int32)
    lengths = doc_lens[0]
    starts = jnp.cumsum(lengths) - lengths
    segment = segment_of(places, starts)
    cosine, sine_part = angle_tables(places - start_of(places, starts))
    allowed = (segment[:, None] == segment[None, :]) & (places[None, :] <= places[:, None])

    def normed(values, gain):
        inv = lax.rsqrt(jnp.mean(values * values, axis=-1, keepdims=True) + EPS)
        return inv, (values * inv * gain).astype(jnp.bfloat16)

    x_float = block_input[0].astype(jnp.float32)
    inv_one, normed_own = normed(x_float, gain_one)
    normed_one = gather_rows(normed_own)
    gate_columns = split_columns(w_gate, 1)
    up_columns = split_columns(w_up, 1)
    seed = gather_rows(cot[0])
    projected = dot_f32(normed_one, qkv_columns).reshape(seq, 3, heads, HEAD)
    queries = rotate(projected[:, 0], cosine, sine_part).astype(jnp.bfloat16)
    keys = rotate(projected[:, 1], cosine, sine_part).astype(jnp.bfloat16)
    values = projected[:, 2].astype(jnp.bfloat16)
    scores = (
        jnp.einsum("qhd,khd->hqk", queries, keys, preferred_element_type=jnp.float32) * score_scale
    )
    scores = jnp.where(allowed[None], scores, NEGATIVE)
    peak = jnp.max(scores, axis=-1)
    raw = jnp.exp(scores - peak[..., None])
    total = jnp.sum(raw, axis=-1)
    attended = jnp.einsum(
        "hqk,khd->hqd", raw.astype(jnp.bfloat16), values, preferred_element_type=jnp.float32
    )
    log_total = peak + jnp.log(total)
    attended = (attended / total[..., None]).transpose(1, 0, 2)
    attended_b = attended.reshape(seq, heads * HEAD).astype(jnp.bfloat16)
    resid = x_float + scatter_rows(dot_f32(attended_b, w_out))
    inv_two, normed_own = normed(resid, gain_two)
    normed_two = gather_rows(normed_own)
    gate_proj = dot_f32(normed_two, gate_columns)
    up_proj = dot_f32(normed_two, up_columns)
    sigmoid_gate = jax.nn.sigmoid(gate_proj)
    swish = gate_proj * sigmoid_gate
    hidden = (swish * up_proj).astype(jnp.bfloat16)
    dhidden = contract_rows(seed, w_down)
    dgate = (dhidden * up_proj * sigmoid_gate * (1.0 + gate_proj * (1.0 - sigmoid_gate))).astype(
        jnp.bfloat16
    )
    dup = (dhidden * swish).astype(jnp.bfloat16)
    dnormed_two = scatter_rows(contract_rows(dgate, gate_columns) + contract_rows(dup, up_columns))
    a_two = dnormed_two * gain_two
    dresid = (
        cot[0].astype(jnp.float32)
        + inv_two * a_two
        - resid * inv_two**3 * jnp.mean(a_two * resid, axis=-1, keepdims=True)
    )
    dresid_b = gather_rows(dresid.astype(jnp.bfloat16))
    block_out = (resid + scatter_rows(dot_f32(hidden, w_down))).astype(jnp.bfloat16)
    grad_down = lax.psum(dot_t(hidden, seed).astype(jnp.bfloat16), "grp").astype(jnp.float32)
    grad_gate = lax.psum(
        merge_columns(dot_t(normed_two, dgate).astype(jnp.bfloat16), 1), "grp"
    ).astype(jnp.float32)
    grad_up = lax.psum(
        merge_columns(dot_t(normed_two, dup).astype(jnp.bfloat16), 1), "grp"
    ).astype(jnp.float32)
    dattended = contract_rows(dresid_b, w_out).astype(jnp.bfloat16).reshape(seq, heads, HEAD)
    grad_out = lax.psum(dot_t(attended_b, dresid_b).astype(jnp.bfloat16), "grp").astype(
        jnp.float32
    )
    delta = jnp.sum(dattended.astype(jnp.float32) * attended, axis=-1).T
    probs = jnp.exp(scores - log_total[..., None])
    dprobs = jnp.einsum("qhd,khd->hqk", dattended, values, preferred_element_type=jnp.float32)
    dscores = (probs * (dprobs - delta[..., None])).astype(jnp.bfloat16)
    dquery = score_scale * jnp.einsum(
        "hqk,khd->qhd", dscores, keys, preferred_element_type=jnp.float32
    )
    dkey = score_scale * jnp.einsum(
        "hqk,qhd->khd", dscores, queries, preferred_element_type=jnp.float32
    )
    dvalue = jnp.einsum(
        "hqk,qhd->khd", probs.astype(jnp.bfloat16), dattended, preferred_element_type=jnp.float32
    )
    dqkv = (
        jnp.stack(
            [unrotate(dquery, cosine, sine_part), unrotate(dkey, cosine, sine_part), dvalue], axis=1
        )
        .reshape(seq, 3 * heads * HEAD)
        .astype(jnp.bfloat16)
    )
    dnormed_one = scatter_rows(contract_rows(dqkv, qkv_columns))
    grad_qkv = lax.psum(
        merge_columns(dot_t(normed_one, dqkv).astype(jnp.bfloat16), 3), "grp"
    ).astype(jnp.float32)
    a_one = dnormed_one * gain_one
    x_grad = (
        dresid
        + inv_one * a_one
        - x_float * inv_one**3 * jnp.mean(a_one * x_float, axis=-1, keepdims=True)
    ).astype(jnp.bfloat16)
    gain_terms = jnp.stack(
        [
            jnp.sum(dnormed_one * x_float * inv_one, axis=0),
            jnp.sum(dnormed_two * resid * inv_two, axis=0),
        ]
    )
    gain_grads = lax.psum(
        lax.psum_scatter(gain_terms, "blk", scatter_dimension=1, tiled=True), "grp"
    )
    return (
        block_out[None],
        x_grad[None],
        gain_grads[0],
        grad_qkv,
        grad_out,
        gain_grads[1],
        grad_gate,
        grad_up,
        grad_down,
    )


def body_for(mesh):
    return per_device if HEADS % mesh.shape["blk"] == 0 else per_device_gather


def solution(mesh):
    return jax.shard_map(
        body_for(mesh),
        mesh=mesh,
        in_specs=(
            P("grp", "blk", None),
            P("grp", None),
            P("blk"),
            P("blk", None),
            P("blk", None),
            P("blk"),
            P("blk", None),
            P("blk", None),
            P("blk", None),
            P("grp", "blk", None),
        ),
        out_specs=(
            P("grp", "blk", None),
            P("grp", "blk", None),
            P("blk"),
            P("blk", None),
            P("blk", None),
            P("blk"),
            P("blk", None),
            P("blk", None),
            P("blk", None),
        ),
        check_vma=False,
    )
```

```python
import functools
import math

import jax
import jax.numpy as jnp
from jax import lax
from jax.experimental import pallas as pl
from jax.experimental.pallas import tpu as pltpu
from jax.sharding import PartitionSpec as P

HEADS = 16
HEAD = 128


EPS = 1e-05
NEGATIVE = -1e30


def angle_tables(places):
    half_size = HEAD // 2
    freqs = jnp.exp(jnp.arange(half_size, dtype=jnp.float32) * (-2.0 * math.log(10000.0) / HEAD))
    angles = places.astype(jnp.float32)[:, None] * freqs
    return (jnp.cos(angles)[:, None, :], jnp.sin(angles)[:, None, :])


def rotate(tensor, cosine, sine_part):
    half_size = HEAD // 2
    first_half = tensor[..., :half_size]
    second_half = tensor[..., half_size:]
    return jnp.concatenate(
        [
            first_half * cosine - second_half * sine_part,
            second_half * cosine + first_half * sine_part,
        ],
        axis=-1,
    )


def unrotate(tensor, cosine, sine_part):
    half_size = HEAD // 2
    first_half = tensor[..., :half_size]
    second_half = tensor[..., half_size:]
    return jnp.concatenate(
        [
            first_half * cosine + second_half * sine_part,
            second_half * cosine - first_half * sine_part,
        ],
        axis=-1,
    )


def segment_of(places, starts):
    return jnp.sum((starts[None, :] <= places[:, None]).astype(jnp.int32), axis=1) - 1


def start_of(places, starts):
    return jnp.max(jnp.where(starts[None, :] <= places[:, None], starts[None, :], 0), axis=1)


def contract_rows(left, right):
    return lax.dot_general(
        left, right, (((1,), (1,)), ((), ())), preferred_element_type=jnp.float32
    )


def weight_term(left, right):

    def term(start, count):
        return lax.dot_general(
            left, right, (((0,), (0,)), ((), ())), preferred_element_type=jnp.float32
        )

    return term


def shard_grad(term_fn, shard_rows):
    shared = lax.psum_scatter(
        term_fn(jnp.int32(0), shard_rows * lax.axis_size("blk")).astype(jnp.bfloat16),
        "blk",
        scatter_dimension=0,
        tiled=True,
    )
    return lax.psum(shared, "grp").astype(jnp.float32)


def per_device_gather(block_input, doc_lens, norm_attn, w_qkv, w_out, norm_mlp, w_gate, w_up, w_down, cot):
    tok_rows = block_input.shape[1]
    width = block_input.shape[2]
    score_scale = HEAD ** (-0.5)
    shards = (norm_attn, w_qkv, w_out, norm_mlp, w_gate, w_up, w_down)
    gathered = (
        lax.all_gather(shards[0], "blk", axis=0, tiled=True),
        lax.all_gather(shards[1], "blk", axis=0, tiled=True),
        lax.all_gather(shards[2], "blk", axis=0, tiled=True),
        lax.all_gather(shards[3], "blk", axis=0, tiled=True),
        lax.all_gather(shards[4], "blk", axis=0, tiled=True),
        lax.all_gather(shards[5], "blk", axis=0, tiled=True),
        lax.all_gather(shards[6], "blk", axis=0, tiled=True),
    )
    gain_one, weight_qkv, weight_out, gain_two, weight_gate, weight_up, weight_down = gathered
    place_rows = lax.axis_index("blk") * tok_rows + jnp.arange(tok_rows, dtype=jnp.int32)
    lengths = doc_lens[0]
    starts = jnp.cumsum(lengths) - lengths
    query_seg = segment_of(place_rows, starts)
    cosine, sine_part = angle_tables(place_rows - start_of(place_rows, starts))
    x_float = block_input[0].astype(jnp.float32)
    inv_one = lax.rsqrt(jnp.mean(x_float * x_float, axis=-1, keepdims=True) + EPS)
    normed_one = (x_float * inv_one * gain_one.astype(jnp.float32)).astype(jnp.bfloat16)
    projected = jnp.dot(normed_one, weight_qkv, preferred_element_type=jnp.float32)
    heads_all = projected.reshape(tok_rows, 3, HEADS, HEAD)
    queries = rotate(heads_all[:, 0], cosine, sine_part).astype(jnp.bfloat16)
    keys_own = rotate(heads_all[:, 1], cosine, sine_part).astype(jnp.bfloat16)
    values_own = heads_all[:, 2].astype(jnp.bfloat16)

    def pair_mask(count):
        key_places = jnp.arange(count, dtype=jnp.int32)
        key_seg = segment_of(key_places, starts)
        return (query_seg[:, None] == key_seg[None, :]) & (
            key_places[None, :] <= place_rows[:, None]
        )

    piece = (
        lax.all_gather(keys_own, "blk", axis=0, tiled=True),
        lax.all_gather(values_own, "blk", axis=0, tiled=True),
    )
    count = piece[0].shape[0]
    row_peak = jnp.full((HEADS, tok_rows), NEGATIVE, jnp.float32)
    key_piece, value_piece = piece
    count = key_piece.shape[0]
    allowed = pair_mask(count)[None]
    scores = (
        jnp.einsum("qhd,khd->hqk", queries, key_piece, preferred_element_type=jnp.float32)
        * score_scale
    )
    scores = jnp.where(allowed, scores, NEGATIVE)
    new_peak = jnp.maximum(row_peak, jnp.max(scores, axis=-1))
    weights_now = jnp.where(allowed, jnp.exp(scores - new_peak[..., None]), 0.0)
    row_total = jnp.sum(weights_now, axis=-1)
    accum = jnp.einsum(
        "hqk,khd->hqd",
        weights_now.astype(jnp.bfloat16),
        value_piece,
        preferred_element_type=jnp.float32,
    )
    row_peak, row_total, accum = (new_peak, row_total, accum)
    log_total = row_peak + jnp.log(row_total)
    attended = (accum / row_total[..., None]).transpose(1, 0, 2)
    attended_b = attended.reshape(tok_rows, width).astype(jnp.bfloat16)
    resid = x_float + jnp.dot(attended_b, weight_out, preferred_element_type=jnp.float32)
    inv_two = lax.rsqrt(jnp.mean(resid * resid, axis=-1, keepdims=True) + EPS)
    normed_two = (resid * inv_two * gain_two.astype(jnp.float32)).astype(jnp.bfloat16)
    gate_proj = jnp.dot(normed_two, weight_gate, preferred_element_type=jnp.float32)
    up_proj = jnp.dot(normed_two, weight_up, preferred_element_type=jnp.float32)
    sigmoid_gate = jax.nn.sigmoid(gate_proj)
    swish = gate_proj * sigmoid_gate
    hidden = (swish * up_proj).astype(jnp.bfloat16)
    block_out = (resid + jnp.dot(hidden, weight_down, preferred_element_type=jnp.float32)).astype(
        jnp.bfloat16
    )
    again = (
        lax.all_gather(shards[0], "blk", axis=0, tiled=True),
        lax.all_gather(shards[1], "blk", axis=0, tiled=True),
        lax.all_gather(shards[2], "blk", axis=0, tiled=True),
        lax.all_gather(shards[3], "blk", axis=0, tiled=True),
        lax.all_gather(shards[4], "blk", axis=0, tiled=True),
        lax.all_gather(shards[5], "blk", axis=0, tiled=True),
        lax.all_gather(shards[6], "blk", axis=0, tiled=True),
    )
    back_gain_one, back_qkv, back_out, back_gain_two, back_gate, back_up, back_down = again
    seed = cot[0]
    seed_float = seed.astype(jnp.float32)
    dhidden = contract_rows(seed, back_down)
    dgate = (dhidden * up_proj * sigmoid_gate * (1.0 + gate_proj * (1.0 - sigmoid_gate))).astype(
        jnp.bfloat16
    )
    dup = (dhidden * swish).astype(jnp.bfloat16)
    dnormed_two = contract_rows(dgate, back_gate) + contract_rows(dup, back_up)
    a_two = dnormed_two * back_gain_two.astype(jnp.float32)
    dresid = (
        seed_float
        + inv_two * a_two
        - resid * inv_two**3 * jnp.mean(a_two * resid, axis=-1, keepdims=True)
    )
    dresid_b = dresid.astype(jnp.bfloat16)
    dattended = (
        contract_rows(dresid_b, back_out).astype(jnp.bfloat16).reshape(tok_rows, HEADS, HEAD)
    )
    delta = jnp.sum(dattended.astype(jnp.float32) * attended, axis=-1).T
    piece = (
        lax.all_gather(keys_own, "blk", axis=0, tiled=True),
        lax.all_gather(values_own, "blk", axis=0, tiled=True),
    )
    count = piece[0].shape[0]
    key_piece, value_piece = piece
    count = key_piece.shape[0]
    score_count = key_piece.shape[0]
    allowed = pair_mask(score_count)[None]
    scores = (
        jnp.einsum("qhd,khd->hqk", queries, key_piece, preferred_element_type=jnp.float32)
        * score_scale
    )
    probs = jnp.where(allowed, jnp.exp(scores - log_total[..., None]), 0.0)
    dprobs = jnp.einsum("qhd,khd->hqk", dattended, value_piece, preferred_element_type=jnp.float32)
    dscores = (probs * (dprobs - delta[..., None])).astype(jnp.bfloat16)
    probs, dscores = (probs, dscores)
    dquery_acc = score_scale * jnp.einsum(
        "hqk,khd->hqd", dscores, key_piece, preferred_element_type=jnp.float32
    )
    dkeys = score_scale * jnp.einsum(
        "hqk,qhd->khd", dscores, queries, preferred_element_type=jnp.float32
    )
    dvalues = jnp.einsum(
        "hqk,qhd->khd", probs.astype(jnp.bfloat16), dattended, preferred_element_type=jnp.float32
    )
    stacked = jnp.concatenate([dkeys.reshape(count, width), dvalues.reshape(count, width)], axis=1)
    grads_buffer = stacked
    dquery_acc, grads_buffer = (dquery_acc, grads_buffer)
    own_grads = lax.psum_scatter(
        grads_buffer.astype(jnp.bfloat16), "blk", scatter_dimension=0, tiled=True
    ).astype(jnp.float32)
    dkey = unrotate(own_grads[:, :width].reshape(tok_rows, HEADS, HEAD), cosine, sine_part)
    dvalue = own_grads[:, width:].reshape(tok_rows, HEADS, HEAD)
    dquery = unrotate(dquery_acc.transpose(1, 0, 2), cosine, sine_part)
    dqkv = (
        jnp.stack([dquery, dkey, dvalue], axis=1).reshape(tok_rows, 3 * width).astype(jnp.bfloat16)
    )
    dnormed_one = contract_rows(dqkv, back_qkv)
    a_one = dnormed_one * back_gain_one.astype(jnp.float32)
    x_grad = (
        dresid
        + inv_one * a_one
        - x_float * inv_one**3 * jnp.mean(a_one * x_float, axis=-1, keepdims=True)
    ).astype(jnp.bfloat16)
    width_rows = norm_attn.shape[0]
    gain_terms = jnp.stack(
        [
            jnp.sum(dnormed_one * x_float * inv_one, axis=0),
            jnp.sum(dnormed_two * resid * inv_two, axis=0),
        ],
        axis=1,
    )

    def gain_slice(start, count):
        return gain_terms

    grad_down = shard_grad(weight_term(hidden, seed), w_down.shape[0])
    grad_gate = shard_grad(weight_term(normed_two, dgate), width_rows)
    grad_up = shard_grad(weight_term(normed_two, dup), width_rows)
    grad_out = shard_grad(weight_term(attended_b, dresid_b), width_rows)
    grad_qkv = shard_grad(weight_term(normed_one, dqkv), width_rows)
    gain_grads = shard_grad(gain_slice, width_rows)
    return (
        block_out[None],
        x_grad[None],
        gain_grads[:, 0],
        grad_qkv,
        grad_out,
        gain_grads[:, 1],
        grad_gate,
        grad_up,
        grad_down,
    )


MESH = pl.DeviceIdType.MESH
VMEM_BYTES = 56 * 2**20


def ring_place(block, n):
    up, row = block // 2, block % 2
    return (1 - row) * up + row * (n - 1 - up)


def ring_block(place, n):
    back = place // (n // 2)
    return (1 - back) * 2 * place + back * (2 * (n - 1 - place) + 1)


def at_offset(place, offset, n):
    return ring_block((place + offset + n) % n, n)


def greet(devices):
    barrier = pltpu.get_barrier_semaphore()
    for device in devices:
        pl.semaphore_signal(barrier, inc=1, device_id=device, device_id_type=MESH)
    pl.semaphore_wait(barrier, len(devices))


def push(src, dst, send_sem, recv_sem, device):
    return pltpu.make_async_remote_copy(
        src_ref=src,
        dst_ref=dst,
        send_sem=send_sem,
        recv_sem=recv_sem,
        device_id=device,
        device_id_type=MESH,
    )


def kernel_params(collective_id):
    return pltpu.CompilerParams(
        collective_id=collective_id, has_side_effects=True, vmem_limit_bytes=VMEM_BYTES
    )


def gather_kernel(n, x_ref, o_ref, local_sem, send, recv):
    grp, me = lax.axis_index("grp"), lax.axis_index("blk")
    place = ring_place(me, n)
    ends = ((grp, at_offset(place, 1, n)), (grp, at_offset(place, -1, n)))
    greet(ends)
    rows = x_ref.shape[0]
    half = rows // 2
    own = pltpu.make_async_copy(x_ref, o_ref.at[me], local_sem)
    own.start()
    copies = {}
    for step in range(n // 2):
        for chunk in range(2):
            for way in range(2):
                if step == n // 2 - 1 and chunk != way:
                    continue
                block = at_offset(place, step if way else -step, n)
                part = pl.ds(chunk * half, half)
                if step:
                    copies[step - 1, chunk, way].wait_recv()
                copy = push(
                    x_ref.at[part] if step == 0 else o_ref.at[block, part],
                    o_ref.at[block, part],
                    send.at[step, chunk, way],
                    recv.at[step, chunk, way],
                    ends[way],
                )
                copy.start()
                copies[step, chunk, way] = copy
    for (step, chunk, way), copy in copies.items():
        if (step + 1, chunk, way) not in copies:
            copy.wait_recv()
    for copy in copies.values():
        copy.wait_send()
    own.wait()


def ring_gather(block):
    n = lax.axis_size("blk")
    rows, columns = block.shape
    return pl.pallas_call(
        functools.partial(gather_kernel, n),
        out_shape=jax.ShapeDtypeStruct((n, rows, columns), block.dtype),
        in_specs=[pl.BlockSpec(memory_space=pl.ANY)],
        out_specs=pl.BlockSpec(memory_space=pl.ANY),
        scratch_shapes=[pltpu.SemaphoreType.DMA]
        + [pltpu.SemaphoreType.DMA((n // 2, 2, 2))] * 2,
        compiler_params=kernel_params(0),
        name="ring_gather",
    )(block).reshape(n * rows, columns)


def scatter_kernel(n, p_ref, o_ref, held, send, recv):
    grp, me = lax.axis_index("grp"), lax.axis_index("blk")
    place = ring_place(me, n)
    ends = ((grp, at_offset(place, 1, n)), (grp, at_offset(place, -1, n)))
    greet(ends)
    rows, columns = o_ref.shape
    half, wide = rows // 2, columns // 2
    copies = {}
    for step in range(n):
        for chunk in range(2):
            for way in range(2):
                part = pl.ds(chunk * half, half)
                lanes = pl.ds(way * wide, wide)
                offset = (step + 1) if way else -(step + 1)
                block = at_offset(place, offset, n)
                if step:
                    copies[step - 1, chunk, way].wait_recv()
                    total = held[way, step - 1, part].astype(jnp.float32) + p_ref[
                        block, part, lanes
                    ].astype(jnp.float32)
                    if step == n - 1:
                        o_ref[part, lanes] = total
                        continue
                    held[way, step - 1, part] = total.astype(jnp.bfloat16)
                copy = push(
                    held.at[way, step - 1, part] if step else p_ref.at[block, part, lanes],
                    held.at[way, step, part],
                    send.at[step, chunk, way],
                    recv.at[step, chunk, way],
                    ends[way],
                )
                copy.start()
                copies[step, chunk, way] = copy
    for copy in copies.values():
        copy.wait_send()


def ring_scatter(partial):
    n = lax.axis_size("blk")
    rows, columns = partial.shape
    rows //= n
    return pl.pallas_call(
        functools.partial(scatter_kernel, n),
        out_shape=jax.ShapeDtypeStruct((rows, columns), jnp.float32),
        in_specs=[pl.BlockSpec(memory_space=pltpu.VMEM)],
        out_specs=pl.BlockSpec(memory_space=pltpu.VMEM),
        scratch_shapes=[pltpu.VMEM((2, n - 1, rows, columns // 2), jnp.bfloat16)]
        + [pltpu.SemaphoreType.DMA((n - 1, 2, 2))] * 2,
        compiler_params=kernel_params(1),
        name="ring_scatter",
    )(partial.astype(jnp.bfloat16).reshape(n, rows, columns))


def team(grp):
    over, core = grp // 2, grp % 2
    return over, core, (1 - over) * 2 + core, over * 2 + 1 - core


def spread_pieces(n, slab_of, out, near, sems):
    s_blk, r_blk, s_x, r_x, s_c, r_c = sems
    grp, me = lax.axis_index("grp"), lax.axis_index("blk")
    over, core, grp_x, grp_c = team(grp)
    sent = []
    arriving = {}
    for k in range(1, n):
        to = (me + k) % n
        copy = push(slab_of(to), out.at[core, over, me], s_blk.at[k], r_blk.at[k], (grp, to))
        copy.start()
        sent.append(copy)
        arriving[k] = copy
    near.wait()
    from_x, from_c, far = {}, {}, {}
    for k in range(n):
        source = (me - k + n) % n
        if k:
            arriving[k].wait_recv()
        piece = out.at[core, over, source]
        from_x[k] = push(piece, piece, s_x.at[k], r_x.at[k], (grp_x, me))
        from_c[k] = push(piece, piece, s_c.at[0, k], r_c.at[0, k], (grp_c, me))
        from_x[k].start()
        from_c[k].start()
    for k in range(n):
        source = (me - k + n) % n
        from_x[k].wait_recv()
        piece = out.at[core, 1 - over, source]
        far[k] = push(piece, piece, s_c.at[1, k], r_c.at[1, k], (grp_c, me))
        far[k].start()
    for k in range(n):
        from_c[k].wait_recv()
        far[k].wait_recv()
    for copy in sent + list(from_x.values()) + list(from_c.values()) + list(far.values()):
        copy.wait_send()


def spread_sems(n):
    dma = pltpu.SemaphoreType.DMA
    return [dma((n,)), dma((n,)), dma((n,)), dma((n,)), dma((2, n)), dma((2, n))]


def team_and_ring(n):
    grp, me = lax.axis_index("grp"), lax.axis_index("blk")
    _, _, grp_x, grp_c = team(grp)
    return [(grp, (me + k) % n) for k in range(1, n)] + [(grp_x, me), (grp_c, me)]


def weights_kernel(n, slab, gains, out, gains_out, local_sem, gain_sem, s_gain, r_gain, *sems):
    grp, me = lax.axis_index("grp"), lax.axis_index("blk")
    over, core, _, _ = team(grp)
    greet(team_and_ring(n))
    near = pltpu.make_async_copy(slab.at[me], out.at[core, over, me], local_sem)
    near.start()
    own_gain = pltpu.make_async_copy(gains, gains_out.at[me], gain_sem)
    own_gain.start()
    gain_copies = []
    for k in range(1, n):
        copy = push(gains, gains_out.at[me], s_gain.at[k], r_gain.at[k], (grp, (me + k) % n))
        copy.start()
        gain_copies.append(copy)
    spread_pieces(n, lambda to: slab.at[to], out, near, sems)
    own_gain.wait()
    for copy in gain_copies:
        copy.wait()


def spread_weights(slab, gains):
    n = lax.axis_size("blk")
    dma = pltpu.SemaphoreType.DMA
    return pl.pallas_call(
        functools.partial(weights_kernel, n),
        out_shape=(
            jax.ShapeDtypeStruct((2, 2) + slab.shape, slab.dtype),
            jax.ShapeDtypeStruct((n,) + gains.shape, gains.dtype),
        ),
        in_specs=[pl.BlockSpec(memory_space=pl.ANY)] * 2,
        out_specs=[pl.BlockSpec(memory_space=pl.ANY)] * 2,
        scratch_shapes=[dma, dma, dma((n,)), dma((n,))] + spread_sems(n),
        compiler_params=kernel_params(2),
        name="spread_weights",
    )(slab, gains)


def grads_kernel(n, wide, tall, out, out_tall, near_c, near_x, mine, tall_c, tall_x, *all_sems):
    s_rc, r_rc, s_rx, r_rx, s_tc, r_tc, s_tx, r_tx, s_t, r_t, local_sem, tall_sem = all_sems[:12]
    sems = all_sems[12:]
    grp, me = lax.axis_index("grp"), lax.axis_index("blk")
    over, core, grp_x, grp_c = team(grp)
    greet(team_and_ring(n))
    first, second = [], []
    for k in range(n):
        to = (me + k) % n
        copy = push(wide.at[to, 1 - core], near_c.at[to], s_rc.at[k], r_rc.at[k], (grp_c, me))
        copy.start()
        first.append(copy)
    tall_first = push(tall.at[1 - core], tall_c, s_tc, r_tc, (grp_c, me))
    tall_first.start()
    f32 = jnp.float32
    for k in range(n):
        to = (me + k) % n
        first[k].wait_recv()
        near_c[to, 1 - over] = (
            wide[to, core, 1 - over].astype(f32) + near_c[to, 1 - over].astype(f32)
        ).astype(jnp.bfloat16)
        copy = push(near_c.at[to, 1 - over], near_x.at[to], s_rx.at[k], r_rx.at[k], (grp_x, me))
        copy.start()
        second.append(copy)
    tall_first.wait_recv()
    tall_c[1 - over] = (tall[core, 1 - over].astype(f32) + tall_c[1 - over].astype(f32)).astype(
        jnp.bfloat16
    )
    tall_second = push(tall_c.at[1 - over], tall_x, s_tx, r_tx, (grp_x, me))
    tall_second.start()
    for k in range(n):
        to = (me + k) % n
        second[k].wait_recv()
        mine[to] = (
            wide[to, core, over].astype(f32)
            + near_c[to, over].astype(f32)
            + near_x[to].astype(f32)
        ).astype(jnp.bfloat16)
    near = pltpu.make_async_copy(mine.at[me], out.at[core, over, me], local_sem)
    near.start()
    tall_second.wait_recv()
    tall_x[...] = (
        tall[core, over].astype(f32) + tall_c[over].astype(f32) + tall_x[...].astype(f32)
    ).astype(jnp.bfloat16)
    tall_own = pltpu.make_async_copy(tall_x, out_tall.at[core, over], tall_sem)
    tall_own.start()
    tall_to_x = push(tall_x, out_tall.at[core, over], s_t.at[0], r_t.at[0], (grp_x, me))
    tall_to_c = push(tall_x, out_tall.at[core, over], s_t.at[1], r_t.at[1], (grp_c, me))
    tall_to_x.start()
    tall_to_c.start()
    spread_pieces(n, lambda to: mine.at[to], out, near, sems)
    tall_to_x.wait_recv()
    piece = out_tall.at[core, 1 - over]
    tall_far = push(piece, piece, s_t.at[2], r_t.at[2], (grp_c, me))
    tall_far.start()
    tall_to_c.wait_recv()
    tall_far.wait_recv()
    tall_own.wait()
    for copy in first + second + [tall_first, tall_second, tall_to_x, tall_to_c, tall_far]:
        copy.wait_send()


def sum_grads(wide, tall):
    n = lax.axis_size("blk")
    dma = pltpu.SemaphoreType.DMA
    rows, columns = wide.shape
    rows //= 4 * n
    tall_rows, tall_columns = tall.shape
    tall_rows //= 4
    bf16 = jnp.bfloat16
    return pl.pallas_call(
        functools.partial(grads_kernel, n),
        out_shape=(
            jax.ShapeDtypeStruct((2, 2, n, rows, columns), bf16),
            jax.ShapeDtypeStruct((2, 2, tall_rows, tall_columns), bf16),
        ),
        in_specs=[pl.BlockSpec(memory_space=pltpu.VMEM)] * 2,
        out_specs=[pl.BlockSpec(memory_space=pl.ANY)] * 2,
        scratch_shapes=[
            pltpu.VMEM((n, 2, rows, columns), bf16),
            pltpu.VMEM((n, rows, columns), bf16),
            pltpu.VMEM((n, rows, columns), bf16),
            pltpu.VMEM((2, tall_rows, tall_columns), bf16),
            pltpu.VMEM((tall_rows, tall_columns), bf16),
        ]
        + [dma((n,))] * 4
        + [dma] * 4
        + [dma((3,))] * 2
        + [dma] * 2
        + spread_sems(n),
        compiler_params=kernel_params(3),
        name="sum_grads",
    )(wide.reshape(n, 2, 2, rows, columns), tall.reshape(2, 2, tall_rows, tall_columns))


def gains_kernel(n, teams, terms, out, heard, send, recv):
    grp, me = lax.axis_index("grp"), lax.axis_index("blk")
    others = [(i, k) for i in range(teams) for k in range(n) if i or k]
    greet([((grp + i) % teams, (me + k) % n) for i, k in others])
    copies = []
    for i, k in others:
        to = (me + k) % n
        copy = push(
            terms.at[to], heard.at[i, k], send.at[i, k], recv.at[i, k], ((grp + i) % teams, to)
        )
        copy.start()
        copies.append(copy)
    heard[0, 0] = terms[me]
    for copy in copies:
        copy.wait()
    out[...] = jnp.sum(heard[...].reshape((teams * n,) + out.shape), axis=0)


def sum_gains(terms):
    n, teams = lax.axis_size("blk"), lax.axis_size("grp")
    dma = pltpu.SemaphoreType.DMA
    return pl.pallas_call(
        functools.partial(gains_kernel, n, teams),
        out_shape=jax.ShapeDtypeStruct(terms.shape[1:], jnp.float32),
        in_specs=[pl.BlockSpec(memory_space=pltpu.VMEM)],
        out_specs=pl.BlockSpec(memory_space=pltpu.VMEM),
        scratch_shapes=[pltpu.VMEM((teams,) + terms.shape, jnp.float32)]
        + [dma((teams, n))] * 2,
        compiler_params=kernel_params(4),
        name="sum_gains",
    )(terms)


def dot_f32(left, right):
    return jnp.dot(left, right, preferred_element_type=jnp.float32)


def dot_t(left, right):
    return lax.dot_general(
        left, right, (((0,), (0,)), ((), ())), preferred_element_type=jnp.float32
    )


def pad_to(array, axis, size):
    widths = [(0, 0)] * array.ndim
    widths[axis] = (0, size - array.shape[axis])
    return jnp.pad(array, widths)


def per_device(block_input, doc_lens, norm_attn, w_qkv, w_out, norm_mlp, w_gate, w_up, w_down, cot):
    n = lax.axis_size("blk")
    tok_rows, width = block_input.shape[1:]
    seq = tok_rows * n
    heads = HEADS // n
    head_lanes = heads * HEAD
    score_scale = HEAD ** (-0.5)
    units = w_down.shape[0]
    lanes = -(-units // 128) * 128
    bf16 = jnp.bfloat16

    over, core, _, _ = team(lax.axis_index("grp"))
    quarter = w_qkv.shape[0] // 4
    first_row = (2 * core + over) * quarter

    def quarter_of(weight):
        return lax.dynamic_slice_in_dim(weight, first_row, quarter, 0)

    slab = jnp.concatenate(
        [
            quarter_of(w_qkv)
            .reshape(quarter, 3, n, head_lanes)
            .transpose(2, 0, 1, 3)
            .reshape(n, quarter, 3 * head_lanes)
        ]
        + [
            pad_to(quarter_of(w).reshape(quarter, n, units).transpose(1, 0, 2), 2, lanes)
            for w in (w_gate, w_up)
        ],
        axis=2,
    )
    gains = pad_to(jnp.stack([norm_attn, norm_mlp]).astype(jnp.float32), 0, 8)
    columns_all, gains_all = spread_weights(slab, gains)
    columns_all = columns_all.transpose(2, 0, 1, 3, 4).reshape(width, slab.shape[2])
    qkv_columns = columns_all[:, : 3 * head_lanes]
    gate_columns = columns_all[:, 3 * head_lanes : 3 * head_lanes + lanes]
    up_columns = columns_all[:, 3 * head_lanes + lanes :]
    gain_one = gains_all[:, 0].reshape(width)
    gain_two = gains_all[:, 1].reshape(width)
    down_rows = pad_to(w_down, 0, lanes)

    places = jnp.arange(seq, dtype=jnp.int32)
    lengths = doc_lens[0]
    starts = jnp.cumsum(lengths) - lengths
    segment = segment_of(places, starts)
    cosine, sine_part = angle_tables(places - start_of(places, starts))
    allowed = (segment[:, None] == segment[None, :]) & (places[None, :] <= places[:, None])

    def normed(values, gain):
        inv = lax.rsqrt(jnp.mean(values * values, axis=-1, keepdims=True) + EPS)
        return inv, (values * inv * gain).astype(bf16)

    x_float = block_input[0].astype(jnp.float32)
    inv_one, normed_own = normed(x_float, gain_one)
    normed_one = ring_gather(normed_own)
    seed = ring_gather(cot[0])
    projected = dot_f32(normed_one, qkv_columns).reshape(seq, 3, heads, HEAD)
    queries = rotate(projected[:, 0], cosine, sine_part).astype(bf16)
    keys = rotate(projected[:, 1], cosine, sine_part).astype(bf16)
    values = projected[:, 2].astype(bf16)
    scores = (
        jnp.einsum("qhd,khd->hqk", queries, keys, preferred_element_type=jnp.float32) * score_scale
    )
    scores = jnp.where(allowed[None], scores, NEGATIVE)
    peak = jnp.max(scores, axis=-1)
    raw = jnp.exp(scores - peak[..., None])
    total = jnp.sum(raw, axis=-1)
    attended = jnp.einsum(
        "hqk,khd->hqd", raw.astype(bf16), values, preferred_element_type=jnp.float32
    )
    log_total = peak + jnp.log(total)
    attended = (attended / total[..., None]).transpose(1, 0, 2)
    attended_b = attended.reshape(seq, head_lanes).astype(bf16)
    resid = x_float + ring_scatter(dot_f32(attended_b, w_out))
    inv_two, normed_own = normed(resid, gain_two)
    normed_two = ring_gather(normed_own)
    gate_proj = dot_f32(normed_two, gate_columns)
    up_proj = dot_f32(normed_two, up_columns)
    sigmoid_gate = jax.nn.sigmoid(gate_proj)
    swish = gate_proj * sigmoid_gate
    hidden = (swish * up_proj).astype(bf16)
    dhidden = contract_rows(seed, down_rows)
    dgate = (dhidden * up_proj * sigmoid_gate * (1.0 + gate_proj * (1.0 - sigmoid_gate))).astype(
        bf16
    )
    dup = (dhidden * swish).astype(bf16)
    dnormed_two = ring_scatter(contract_rows(dgate, gate_columns) + contract_rows(dup, up_columns))
    a_two = dnormed_two * gain_two
    dresid = (
        cot[0].astype(jnp.float32)
        + inv_two * a_two
        - resid * inv_two**3 * jnp.mean(a_two * resid, axis=-1, keepdims=True)
    )
    dresid_b = ring_gather(dresid.astype(bf16))
    block_out = (resid + ring_scatter(dot_f32(hidden, down_rows))).astype(bf16)
    dattended = contract_rows(dresid_b, w_out).astype(bf16).reshape(seq, heads, HEAD)
    delta = jnp.sum(dattended.astype(jnp.float32) * attended, axis=-1).T
    probs = jnp.exp(scores - log_total[..., None])
    dprobs = jnp.einsum("qhd,khd->hqk", dattended, values, preferred_element_type=jnp.float32)
    dscores = (probs * (dprobs - delta[..., None])).astype(bf16)
    dquery = score_scale * jnp.einsum(
        "hqk,khd->qhd", dscores, keys, preferred_element_type=jnp.float32
    )
    dkey = score_scale * jnp.einsum(
        "hqk,qhd->khd", dscores, queries, preferred_element_type=jnp.float32
    )
    dvalue = jnp.einsum(
        "hqk,qhd->khd", probs.astype(bf16), dattended, preferred_element_type=jnp.float32
    )
    dqkv = (
        jnp.stack(
            [unrotate(dquery, cosine, sine_part), unrotate(dkey, cosine, sine_part), dvalue], axis=1
        )
        .reshape(seq, 3 * head_lanes)
        .astype(bf16)
    )
    dnormed_one = ring_scatter(contract_rows(dqkv, qkv_columns))
    a_one = dnormed_one * gain_one
    x_grad = (
        dresid
        + inv_one * a_one
        - x_float * inv_one**3 * jnp.mean(a_one * x_float, axis=-1, keepdims=True)
    ).astype(bf16)
    wide = jnp.concatenate(
        [
            dot_t(normed_one, dqkv).astype(bf16),
            dot_t(normed_two, dgate).astype(bf16),
            dot_t(normed_two, dup).astype(bf16),
        ],
        axis=1,
    )
    tall = jnp.concatenate(
        [dot_t(attended_b, dresid_b).astype(bf16), dot_t(hidden, seed).astype(bf16)], axis=0
    )
    wide_sum, tall_sum = sum_grads(wide, tall)
    wide_sum = wide_sum.astype(jnp.float32)
    tall_sum = tall_sum.reshape(tall.shape).astype(jnp.float32)
    shard_rows = 4 * quarter

    def merged(part):
        return part.transpose(0, 1, 3, 2, 4).reshape(shard_rows, n * part.shape[-1])

    grad_qkv = (
        wide_sum[..., : 3 * head_lanes]
        .reshape(2, 2, n, quarter, 3, head_lanes)
        .transpose(0, 1, 3, 4, 2, 5)
        .reshape(shard_rows, 3 * width)
    )
    grad_gate = merged(wide_sum[..., 3 * head_lanes : 3 * head_lanes + units])
    grad_up = merged(wide_sum[..., 3 * head_lanes + lanes : 3 * head_lanes + lanes + units])
    grad_out = tall_sum[:head_lanes]
    grad_down = tall_sum[head_lanes : head_lanes + units]
    gain_terms = jnp.stack(
        [
            jnp.sum(dnormed_one * x_float * inv_one, axis=0),
            jnp.sum(dnormed_two * resid * inv_two, axis=0),
        ]
    )
    gain_grads = sum_gains(pad_to(gain_terms, 0, 8).reshape(8, n, -1).transpose(1, 0, 2))
    return (
        block_out[None],
        x_grad[None],
        gain_grads[0],
        grad_qkv,
        grad_out,
        gain_grads[1],
        grad_gate,
        grad_up,
        grad_down,
    )


def body_for(mesh):
    return per_device if HEADS % mesh.shape["blk"] == 0 else per_device_gather


def solution(mesh):
    return jax.shard_map(
        body_for(mesh),
        mesh=mesh,
        in_specs=(
            P("grp", "blk", None),
            P("grp", None),
            P("blk"),
            P("blk", None),
            P("blk", None),
            P("blk"),
            P("blk", None),
            P("blk", None),
            P("blk", None),
            P("grp", "blk", None),
        ),
        out_specs=(
            P("grp", "blk", None),
            P("grp", "blk", None),
            P("blk"),
            P("blk", None),
            P("blk", None),
            P("blk"),
            P("blk", None),
            P("blk", None),
            P("blk", None),
        ),
        check_vma=False,
    )
```

```python
import functools
import math

import jax
import jax.numpy as jnp
from jax import lax
from jax.experimental import pallas as pl
from jax.experimental.pallas import tpu as pltpu
from jax.sharding import PartitionSpec as P

HEADS = 16
HEAD = 128


EPS = 1e-05
NEGATIVE = -1e30


def angle_tables(places):
    half_size = HEAD // 2
    freqs = jnp.exp(jnp.arange(half_size, dtype=jnp.float32) * (-2.0 * math.log(10000.0) / HEAD))
    angles = places.astype(jnp.float32)[:, None] * freqs
    return (jnp.cos(angles)[:, None, :], jnp.sin(angles)[:, None, :])


def rotate(tensor, cosine, sine_part):
    half_size = HEAD // 2
    first_half = tensor[..., :half_size]
    second_half = tensor[..., half_size:]
    return jnp.concatenate(
        [
            first_half * cosine - second_half * sine_part,
            second_half * cosine + first_half * sine_part,
        ],
        axis=-1,
    )


def unrotate(tensor, cosine, sine_part):
    half_size = HEAD // 2
    first_half = tensor[..., :half_size]
    second_half = tensor[..., half_size:]
    return jnp.concatenate(
        [
            first_half * cosine + second_half * sine_part,
            second_half * cosine - first_half * sine_part,
        ],
        axis=-1,
    )


def segment_of(places, starts):
    return jnp.sum((starts[None, :] <= places[:, None]).astype(jnp.int32), axis=1) - 1


def start_of(places, starts):
    return jnp.max(jnp.where(starts[None, :] <= places[:, None], starts[None, :], 0), axis=1)


def contract_rows(left, right):
    return lax.dot_general(
        left, right, (((1,), (1,)), ((), ())), preferred_element_type=jnp.float32
    )


def weight_term(left, right):

    def term(start, count):
        return lax.dot_general(
            left, right, (((0,), (0,)), ((), ())), preferred_element_type=jnp.float32
        )

    return term


def shard_grad(term_fn, shard_rows):
    shared = lax.psum_scatter(
        term_fn(jnp.int32(0), shard_rows * lax.axis_size("blk")).astype(jnp.bfloat16),
        "blk",
        scatter_dimension=0,
        tiled=True,
    )
    return lax.psum(shared, "grp").astype(jnp.float32)


def per_device_gather(block_input, doc_lens, norm_attn, w_qkv, w_out, norm_mlp, w_gate, w_up, w_down, cot):
    tok_rows = block_input.shape[1]
    width = block_input.shape[2]
    score_scale = HEAD ** (-0.5)
    shards = (norm_attn, w_qkv, w_out, norm_mlp, w_gate, w_up, w_down)
    gathered = (
        lax.all_gather(shards[0], "blk", axis=0, tiled=True),
        lax.all_gather(shards[1], "blk", axis=0, tiled=True),
        lax.all_gather(shards[2], "blk", axis=0, tiled=True),
        lax.all_gather(shards[3], "blk", axis=0, tiled=True),
        lax.all_gather(shards[4], "blk", axis=0, tiled=True),
        lax.all_gather(shards[5], "blk", axis=0, tiled=True),
        lax.all_gather(shards[6], "blk", axis=0, tiled=True),
    )
    gain_one, weight_qkv, weight_out, gain_two, weight_gate, weight_up, weight_down = gathered
    place_rows = lax.axis_index("blk") * tok_rows + jnp.arange(tok_rows, dtype=jnp.int32)
    lengths = doc_lens[0]
    starts = jnp.cumsum(lengths) - lengths
    query_seg = segment_of(place_rows, starts)
    cosine, sine_part = angle_tables(place_rows - start_of(place_rows, starts))
    x_float = block_input[0].astype(jnp.float32)
    inv_one = lax.rsqrt(jnp.mean(x_float * x_float, axis=-1, keepdims=True) + EPS)
    normed_one = (x_float * inv_one * gain_one.astype(jnp.float32)).astype(jnp.bfloat16)
    projected = jnp.dot(normed_one, weight_qkv, preferred_element_type=jnp.float32)
    heads_all = projected.reshape(tok_rows, 3, HEADS, HEAD)
    queries = rotate(heads_all[:, 0], cosine, sine_part).astype(jnp.bfloat16)
    keys_own = rotate(heads_all[:, 1], cosine, sine_part).astype(jnp.bfloat16)
    values_own = heads_all[:, 2].astype(jnp.bfloat16)

    def pair_mask(count):
        key_places = jnp.arange(count, dtype=jnp.int32)
        key_seg = segment_of(key_places, starts)
        return (query_seg[:, None] == key_seg[None, :]) & (
            key_places[None, :] <= place_rows[:, None]
        )

    piece = (
        lax.all_gather(keys_own, "blk", axis=0, tiled=True),
        lax.all_gather(values_own, "blk", axis=0, tiled=True),
    )
    count = piece[0].shape[0]
    row_peak = jnp.full((HEADS, tok_rows), NEGATIVE, jnp.float32)
    key_piece, value_piece = piece
    count = key_piece.shape[0]
    allowed = pair_mask(count)[None]
    scores = (
        jnp.einsum("qhd,khd->hqk", queries, key_piece, preferred_element_type=jnp.float32)
        * score_scale
    )
    scores = jnp.where(allowed, scores, NEGATIVE)
    new_peak = jnp.maximum(row_peak, jnp.max(scores, axis=-1))
    weights_now = jnp.where(allowed, jnp.exp(scores - new_peak[..., None]), 0.0)
    row_total = jnp.sum(weights_now, axis=-1)
    accum = jnp.einsum(
        "hqk,khd->hqd",
        weights_now.astype(jnp.bfloat16),
        value_piece,
        preferred_element_type=jnp.float32,
    )
    row_peak, row_total, accum = (new_peak, row_total, accum)
    log_total = row_peak + jnp.log(row_total)
    attended = (accum / row_total[..., None]).transpose(1, 0, 2)
    attended_b = attended.reshape(tok_rows, width).astype(jnp.bfloat16)
    resid = x_float + jnp.dot(attended_b, weight_out, preferred_element_type=jnp.float32)
    inv_two = lax.rsqrt(jnp.mean(resid * resid, axis=-1, keepdims=True) + EPS)
    normed_two = (resid * inv_two * gain_two.astype(jnp.float32)).astype(jnp.bfloat16)
    gate_proj = jnp.dot(normed_two, weight_gate, preferred_element_type=jnp.float32)
    up_proj = jnp.dot(normed_two, weight_up, preferred_element_type=jnp.float32)
    sigmoid_gate = jax.nn.sigmoid(gate_proj)
    swish = gate_proj * sigmoid_gate
    hidden = (swish * up_proj).astype(jnp.bfloat16)
    block_out = (resid + jnp.dot(hidden, weight_down, preferred_element_type=jnp.float32)).astype(
        jnp.bfloat16
    )
    again = (
        lax.all_gather(shards[0], "blk", axis=0, tiled=True),
        lax.all_gather(shards[1], "blk", axis=0, tiled=True),
        lax.all_gather(shards[2], "blk", axis=0, tiled=True),
        lax.all_gather(shards[3], "blk", axis=0, tiled=True),
        lax.all_gather(shards[4], "blk", axis=0, tiled=True),
        lax.all_gather(shards[5], "blk", axis=0, tiled=True),
        lax.all_gather(shards[6], "blk", axis=0, tiled=True),
    )
    back_gain_one, back_qkv, back_out, back_gain_two, back_gate, back_up, back_down = again
    seed = cot[0]
    seed_float = seed.astype(jnp.float32)
    dhidden = contract_rows(seed, back_down)
    dgate = (dhidden * up_proj * sigmoid_gate * (1.0 + gate_proj * (1.0 - sigmoid_gate))).astype(
        jnp.bfloat16
    )
    dup = (dhidden * swish).astype(jnp.bfloat16)
    dnormed_two = contract_rows(dgate, back_gate) + contract_rows(dup, back_up)
    a_two = dnormed_two * back_gain_two.astype(jnp.float32)
    dresid = (
        seed_float
        + inv_two * a_two
        - resid * inv_two**3 * jnp.mean(a_two * resid, axis=-1, keepdims=True)
    )
    dresid_b = dresid.astype(jnp.bfloat16)
    dattended = (
        contract_rows(dresid_b, back_out).astype(jnp.bfloat16).reshape(tok_rows, HEADS, HEAD)
    )
    delta = jnp.sum(dattended.astype(jnp.float32) * attended, axis=-1).T
    piece = (
        lax.all_gather(keys_own, "blk", axis=0, tiled=True),
        lax.all_gather(values_own, "blk", axis=0, tiled=True),
    )
    count = piece[0].shape[0]
    key_piece, value_piece = piece
    count = key_piece.shape[0]
    score_count = key_piece.shape[0]
    allowed = pair_mask(score_count)[None]
    scores = (
        jnp.einsum("qhd,khd->hqk", queries, key_piece, preferred_element_type=jnp.float32)
        * score_scale
    )
    probs = jnp.where(allowed, jnp.exp(scores - log_total[..., None]), 0.0)
    dprobs = jnp.einsum("qhd,khd->hqk", dattended, value_piece, preferred_element_type=jnp.float32)
    dscores = (probs * (dprobs - delta[..., None])).astype(jnp.bfloat16)
    probs, dscores = (probs, dscores)
    dquery_acc = score_scale * jnp.einsum(
        "hqk,khd->hqd", dscores, key_piece, preferred_element_type=jnp.float32
    )
    dkeys = score_scale * jnp.einsum(
        "hqk,qhd->khd", dscores, queries, preferred_element_type=jnp.float32
    )
    dvalues = jnp.einsum(
        "hqk,qhd->khd", probs.astype(jnp.bfloat16), dattended, preferred_element_type=jnp.float32
    )
    stacked = jnp.concatenate([dkeys.reshape(count, width), dvalues.reshape(count, width)], axis=1)
    grads_buffer = stacked
    dquery_acc, grads_buffer = (dquery_acc, grads_buffer)
    own_grads = lax.psum_scatter(
        grads_buffer.astype(jnp.bfloat16), "blk", scatter_dimension=0, tiled=True
    ).astype(jnp.float32)
    dkey = unrotate(own_grads[:, :width].reshape(tok_rows, HEADS, HEAD), cosine, sine_part)
    dvalue = own_grads[:, width:].reshape(tok_rows, HEADS, HEAD)
    dquery = unrotate(dquery_acc.transpose(1, 0, 2), cosine, sine_part)
    dqkv = (
        jnp.stack([dquery, dkey, dvalue], axis=1).reshape(tok_rows, 3 * width).astype(jnp.bfloat16)
    )
    dnormed_one = contract_rows(dqkv, back_qkv)
    a_one = dnormed_one * back_gain_one.astype(jnp.float32)
    x_grad = (
        dresid
        + inv_one * a_one
        - x_float * inv_one**3 * jnp.mean(a_one * x_float, axis=-1, keepdims=True)
    ).astype(jnp.bfloat16)
    width_rows = norm_attn.shape[0]
    gain_terms = jnp.stack(
        [
            jnp.sum(dnormed_one * x_float * inv_one, axis=0),
            jnp.sum(dnormed_two * resid * inv_two, axis=0),
        ],
        axis=1,
    )

    def gain_slice(start, count):
        return gain_terms

    grad_down = shard_grad(weight_term(hidden, seed), w_down.shape[0])
    grad_gate = shard_grad(weight_term(normed_two, dgate), width_rows)
    grad_up = shard_grad(weight_term(normed_two, dup), width_rows)
    grad_out = shard_grad(weight_term(attended_b, dresid_b), width_rows)
    grad_qkv = shard_grad(weight_term(normed_one, dqkv), width_rows)
    gain_grads = shard_grad(gain_slice, width_rows)
    return (
        block_out[None],
        x_grad[None],
        gain_grads[:, 0],
        grad_qkv,
        grad_out,
        gain_grads[:, 1],
        grad_gate,
        grad_up,
        grad_down,
    )


MESH = pl.DeviceIdType.MESH
VMEM_BYTES = 62 * 2**20


def ring_place(block, n):
    up, row = block // 2, block % 2
    return (1 - row) * up + row * (n - 1 - up)


def ring_block(place, n):
    back = place // (n // 2)
    return (1 - back) * 2 * place + back * (2 * (n - 1 - place) + 1)


def at_offset(place, offset, n):
    return ring_block((place + offset + n) % n, n)


def greet(devices):
    barrier = pltpu.get_barrier_semaphore()
    for device in devices:
        pl.semaphore_signal(barrier, inc=1, device_id=device, device_id_type=MESH)
    pl.semaphore_wait(barrier, len(devices))


def push(src, dst, send_sem, recv_sem, device):
    return pltpu.make_async_remote_copy(
        src_ref=src,
        dst_ref=dst,
        send_sem=send_sem,
        recv_sem=recv_sem,
        device_id=device,
        device_id_type=MESH,
    )


def kernel_params(collective_id):
    return pltpu.CompilerParams(
        collective_id=collective_id, has_side_effects=True, vmem_limit_bytes=VMEM_BYTES
    )


def dot_f32(left, right):
    return jnp.dot(left, right, preferred_element_type=jnp.float32)


def dot_t(left, right):
    return lax.dot_general(
        left, right, (((0,), (0,)), ((), ())), preferred_element_type=jnp.float32
    )


def nt_dot(left, right):
    return lax.dot_general(
        left, right, (((1,), (1,)), ((), ())), preferred_element_type=jnp.float32
    )


def ring_ends(n):
    grp, me = lax.axis_index("grp"), lax.axis_index("blk")
    place = ring_place(me, n)
    return place, ((grp, at_offset(place, 1, n)), (grp, at_offset(place, -1, n)))


class Gather:
    def __init__(self, n, buf, send, recv, ends, own=None):
        self.n, self.buf, self.send, self.recv, self.ends = n, buf, send, recv, ends
        self.own = buf.at[0] if own is None else own
        self.half = buf.shape[1] // 2

    def copy(self, step, chunk, way):
        part = pl.ds(chunk * self.half, self.half)
        if isinstance(step, int):
            target = min(2 * step + 1 + way, self.n - 1)
        else:
            target = jnp.minimum(2 * step + 1 + way, self.n - 1)
        first = isinstance(step, int) and step == 0
        return push(
            self.own.at[part] if first else self.buf.at[2 * step - 1 + way, part],
            self.buf.at[target, part],
            self.send.at[step, chunk, way],
            self.recv.at[step, chunk, way],
            self.ends[way],
        )

    def landed(self, step, chunk, way):
        target = jnp.minimum(2 * step + 1 + way, self.n - 1)
        place = self.buf.at[target, pl.ds(chunk * self.half, self.half)]
        sems = (self.send.at[step, chunk, way], self.recv.at[step, chunk, way])
        return push(place, place, *sems, self.ends[way])

    def used(self, step, chunk, way):
        return step < self.n // 2 - 1 or chunk == way

    def start(self):
        for chunk in range(2):
            for way in range(2):
                self.copy(0, chunk, way).start()

    def advance(self, step):
        for chunk in range(2):
            for way in range(2):
                if isinstance(step, int):
                    if self.used(step, chunk, way):
                        self.copy(step, chunk, way).wait_recv()
                        if step + 1 < self.n // 2 and self.used(step + 1, chunk, way):
                            self.copy(step + 1, chunk, way).start()
                elif chunk == way:
                    self.landed(step, chunk, way).wait_recv()
                    pl.when(step + 1 < self.n // 2)(self.copy(step + 1, chunk, way).start)
                else:
                    pl.when(step < self.n // 2 - 1)(self.landed(step, chunk, way).wait_recv)
                    pl.when(step + 1 < self.n // 2 - 1)(self.copy(step + 1, chunk, way).start)

    def finish(self):
        for step in range(self.n // 2):
            for chunk in range(2):
                for way in range(2):
                    if self.used(step, chunk, way):
                        self.copy(step, chunk, way).wait_send()


class Scatter:
    def __init__(self, n, held, terms, send, recv, ends, term):
        self.n, self.held, self.terms, self.send, self.recv = n, held, terms, send, recv
        self.ends, self.term = ends, term
        self.half = held.shape[2] // 2

    def copy(self, step, chunk, way):
        part = pl.ds(chunk * self.half, self.half)
        return push(
            self.held.at[way, step, part],
            self.held.at[way, step + 1, part],
            self.send.at[step, chunk, way],
            self.recv.at[step, chunk, way],
            self.ends[way],
        )

    def step(self, step):
        for way in range(2):
            self.terms[way] = self.term(step, way)
        for chunk in range(2):
            for way in range(2):
                part = pl.ds(chunk * self.half, self.half)

                def first(way=way, part=part):
                    self.held[way, step, part] = self.terms[way, part].astype(jnp.bfloat16)

                def later(chunk=chunk, way=way, part=part):
                    self.copy(step - 1, chunk, way).wait_recv()
                    self.held[way, step, part] = (
                        self.terms[way, part] + self.held[way, step, part].astype(jnp.float32)
                    ).astype(jnp.bfloat16)

                if isinstance(step, int):
                    (later if step else first)()
                else:
                    pl.when(step == 0)(first)
                    pl.when(step > 0)(later)
                self.copy(step, chunk, way).start()

    def result(self, way):
        for chunk in range(2):
            self.copy(self.n - 2, chunk, way).wait_recv()
        return self.term(self.n - 1, way) + self.held[way, self.n - 1].astype(jnp.float32)

    def finish(self):
        def body(step, _):
            for chunk in range(2):
                for way in range(2):
                    self.copy(step, chunk, way).wait_send()
            return 0

        lax.fori_loop(0, self.n - 1, body, 0)


def behind(step, way, n):
    near = 2 * step + 1 + way
    far = 2 * (n - 1 - step) - way
    if isinstance(step, int):
        return 0 if step == n - 1 else min(near, far, n - 1)
    return jnp.where(step == n - 1, 0, jnp.minimum(jnp.minimum(near, far), n - 1))


def team(grp):
    over, core = grp // 2, grp % 2
    return over, core, (1 - over) * 2 + core, over * 2 + 1 - core


def mlp_kernel(
    n,
    lanes,
    ob,
    w_out,
    x_ref,
    gain,
    weights,
    w_down,
    seed_hbm,
    seed_own,
    block_out,
    dresid_out,
    dattended,
    gain_terms,
    wide_sum,
    down_sum,
    dresid,
    normed,
    seed,
    gate_up,
    down,
    hidden,
    dgate_up,
    held_one,
    held_two,
    terms,
    resid,
    wide,
    wide_c,
    tall,
    tall_c,
    load_sem,
    s_one,
    r_one,
    s_two,
    r_two,
    s_three,
    r_three,
    s_norm,
    r_norm,
    s_dres,
    r_dres,
    s_wc,
    r_wc,
    s_wx,
    r_wx,
    s_tall,
    r_tall,
):
    f32, bf16 = jnp.float32, jnp.bfloat16
    grp, me = lax.axis_index("grp"), lax.axis_index("blk")
    over, core, grp_x, grp_c = team(grp)
    _, ends = ring_ends(n)
    units = w_down.shape[0]
    loads = [
        pltpu.make_async_copy(weights, gate_up, load_sem.at[0]),
        pltpu.make_async_copy(w_down, down.at[pl.ds(0, units)], load_sem.at[1]),
        pltpu.make_async_copy(
            seed_hbm.at[pl.ds(1, n - 1)], seed.at[pl.ds(1, n - 1)], load_sem.at[2]
        ),
        pltpu.make_async_copy(seed_own, seed.at[0], load_sem.at[3]),
    ]
    for load in loads:
        load.start()
    if units < lanes:
        down[pl.ds(units, lanes - units)] = jnp.zeros((lanes - units, down.shape[1]), bf16)
    greet(list(ends) + [(grp_x, me), (grp_c, me)])
    columns = x_ref.shape[1]
    half = columns // 2

    def out_term(step, way):
        return dot_f32(ob[behind(step, way, n)], w_out[:, way * half : (way + 1) * half])

    one = Scatter(n, held_one, terms, s_one, r_one, ends, out_term)
    one.step(0)
    lax.fori_loop(1, n - 1, lambda step, _: (one.step(step), 0)[1], 0)
    for way in range(2):
        part = slice(way * half, (way + 1) * half)
        resid[:, part] = x_ref[:, part].astype(f32) + one.result(way)
    value = resid[...]
    inv = lax.rsqrt(jnp.mean(value * value, axis=-1, keepdims=True) + EPS)
    normed[0] = (value * inv * gain[...]).astype(bf16)
    gather = Gather(n, normed, s_norm, r_norm, ends)
    gather.start()
    one.finish()
    for load in loads:
        load.wait()

    def mlp(slot, _):
        both = dot_f32(normed[slot], gate_up[...])
        grad = nt_dot(seed[slot], down[...])
        gate, up = both[:, :lanes], both[:, lanes:]
        sig = jax.nn.sigmoid(gate)
        swish = gate * sig
        hidden[slot] = (swish * up).astype(bf16)
        dgate_up[slot, :, :lanes] = (grad * up * sig * (1.0 + gate * (1.0 - sig))).astype(bf16)
        dgate_up[slot, :, lanes:] = (grad * swish).astype(bf16)
        return 0

    def norm_term(step, way):
        return nt_dot(dgate_up[behind(step, way, n)], gate_up[way * half : (way + 1) * half, :])

    two = Scatter(n, held_two, terms, s_two, r_two, ends, norm_term)

    def turn(t, _):
        pl.when(t > 0)(lambda: gather.advance(t - 1))
        low = jnp.maximum(2 * t - 1, 0)
        lax.fori_loop(low, jnp.minimum(2 * t + 1, n), mlp, 0)
        pl.when(t > 0)(lambda: two.step(t - 1))
        return 0

    lax.fori_loop(0, n // 2 + 1, turn, 0)

    tall_rows = lanes // 4

    def tall_at(first, count):
        return pl.ds(pl.multiple_of(first * tall_rows, tall_rows), count * tall_rows)

    tall_tile = 256 if lanes % 256 == 0 else 128
    tiles = lanes // tall_tile

    def tall_grad(tile):
        at = pl.multiple_of(tile * tall_tile, tall_tile)
        left = hidden[:, :, pl.ds(at, tall_tile)].reshape(-1, tall_tile)
        grad_rows = dot_t(left, seed[...].reshape(-1, columns)).astype(bf16)
        tall[pl.ds(at, tall_tile)] = grad_rows

    def rest(step, _):
        two.step(step)
        pl.when(step - n // 2 < tiles)(lambda: tall_grad(step - n // 2))
        return 0

    lax.fori_loop(n // 2, n - 1, rest, 0)
    for tile in range(n // 2 - 1, tiles):
        tall_grad(tile)
    tall_one = push(tall.at[tall_at(2 - 2 * core, 2)], tall_c, s_tall.at[0], r_tall.at[0], (grp_c, me))
    tall_one.start()

    value = resid[...]
    inv = lax.rsqrt(jnp.mean(value * value, axis=-1, keepdims=True) + EPS)
    for way in range(2):
        part = slice(way * half, (way + 1) * half)
        dresid_out[:, part] = two.result(way)
    dnormed = dresid_out[...]
    gain_terms[...] = jnp.sum(dnormed * value * inv, axis=0, keepdims=True)
    a_two = dnormed * gain[...]
    total = (
        seed[0].astype(f32)
        + inv * a_two
        - value * inv**3 * jnp.mean(a_two * value, axis=-1, keepdims=True)
    )
    dresid_out[...] = total
    dresid[0] = total.astype(bf16)
    back = Gather(n, dresid, s_dres, r_dres, ends)
    back.start()
    two.finish()

    def down_term(step, way):
        return dot_f32(hidden[behind(step, way, n)], down[:, way * half : (way + 1) * half])

    three = Scatter(n, held_one, terms, s_three, r_three, ends, down_term)

    def dob(slot, _):
        dattended[slot] = nt_dot(dresid[slot], w_out[...]).astype(bf16)
        return 0

    def wide_copy_c(tile):
        return push(
            wide.at[tile, 1 - core], wide_c.at[tile], s_wc.at[tile], r_wc.at[tile], (grp_c, me)
        )

    def wide_copy_x(tile):
        return push(
            wide_c.at[tile, 1 - over], wide_sum.at[tile], s_wx.at[tile], r_wx.at[tile], (grp_x, me)
        )

    quarter = wide.shape[3]

    def wide_grad(tile):
        at = pl.multiple_of(tile * 4 * quarter, 4 * quarter)
        left = normed[:, :, pl.ds(at, 4 * quarter)].reshape(-1, 4 * quarter)
        grad = dot_t(left, dgate_up[...].reshape(-1, 2 * lanes)).astype(bf16)
        wide[tile] = grad.reshape(2, 2, quarter, 2 * lanes)
        wide_copy_c(tile).start()

    def wide_pass(tile):
        wide_copy_c(tile).wait_recv()
        wide_c[tile, 1 - over] = (
            wide[tile, core, 1 - over].astype(f32) + wide_c[tile, 1 - over].astype(f32)
        ).astype(bf16)
        wide_copy_x(tile).start()

    tall_two = push(tall_c.at[tall_at(1 - over, 1)], down_sum, s_tall.at[1], r_tall.at[1], (grp_x, me))

    def again(t, _):
        pl.when(t > 0)(lambda: back.advance(t - 1))
        low = jnp.maximum(2 * t - 1, 0)
        lax.fori_loop(low, jnp.minimum(2 * t + 1, n), dob, 0)

        def inner(step, _):
            pl.when(step < n - 1)(lambda: three.step(step))
            pl.when(step > 0)(lambda: wide_pass(step - 1))
            wide_grad(step)
            return 0

        lax.fori_loop(2 * t, jnp.minimum(2 * t + 2, n), inner, 0)
        return 0

    lax.fori_loop(0, n // 2 + 1, again, 0)
    wide_pass(n - 1)
    tall_one.wait_recv()
    tall_c[tall_at(1 - over, 1)] = (
        tall[tall_at(2 * core + 1 - over, 1)].astype(f32)
        + tall_c[tall_at(1 - over, 1)].astype(f32)
    ).astype(bf16)
    tall_two.start()
    for way in range(2):
        part = slice(way * half, (way + 1) * half)
        block_out[:, part] = (resid[:, part] + three.result(way)).astype(bf16)

    def wide_take(tile, _):
        wide_copy_x(tile).wait_recv()
        wide_sum[tile] = (
            wide[tile, core, over].astype(f32)
            + wide_c[tile, over].astype(f32)
            + wide_sum[tile].astype(f32)
        ).astype(bf16)
        return 0

    lax.fori_loop(0, n, wide_take, 0)
    tall_two.wait_recv()
    down_sum[...] = (
        tall[tall_at(2 * core + over, 1)].astype(f32)
        + tall_c[tall_at(over, 1)].astype(f32)
        + down_sum[...].astype(f32)
    ).astype(bf16)
    gather.finish()
    back.finish()
    three.finish()
    tall_one.wait_send()
    tall_two.wait_send()

    def sent(tile, _):
        wide_copy_c(tile).wait_send()
        wide_copy_x(tile).wait_send()
        return 0

    lax.fori_loop(0, n, sent, 0)


def mlp_and_back(ob, w_out, x_own, gain, weights, lanes, w_down, seed, seed_own):
    n = lax.axis_size("blk")
    _, rows, columns = seed.shape
    head_lanes = ob.shape[2]
    quarter = columns // (4 * n)
    f32, bf16 = jnp.float32, jnp.bfloat16
    vmem, dma = pltpu.VMEM, pltpu.SemaphoreType.DMA
    in_vmem, anywhere = pl.BlockSpec(memory_space=vmem), pl.BlockSpec(memory_space=pl.ANY)
    ring = [dma((n - 1, 2, 2))] * 6 + [dma((n // 2, 2, 2))] * 4
    return pl.pallas_call(
        functools.partial(mlp_kernel, n, lanes),
        out_shape=(
            jax.ShapeDtypeStruct((rows, columns), bf16),
            jax.ShapeDtypeStruct((rows, columns), f32),
            jax.ShapeDtypeStruct((n, rows, head_lanes), bf16),
            jax.ShapeDtypeStruct((1, columns), f32),
            jax.ShapeDtypeStruct((n, quarter, 2 * lanes), bf16),
            jax.ShapeDtypeStruct((lanes // 4, columns), bf16),
            jax.ShapeDtypeStruct((n, rows, columns), bf16),
        ),
        in_specs=[in_vmem] * 4 + [anywhere] * 4,
        out_specs=[in_vmem] * 7,
        scratch_shapes=[
            vmem((n, rows, columns), bf16),
            vmem((n, rows, columns), bf16),
            vmem((columns, 2 * lanes), bf16),
            vmem((lanes, columns), bf16),
            vmem((n, rows, lanes), bf16),
            vmem((n, rows, 2 * lanes), bf16),
            vmem((2, n, rows, columns // 2), bf16),
            vmem((2, n, rows, columns // 2), bf16),
            vmem((2, rows, columns // 2), f32),
            vmem((rows, columns), f32),
            vmem((n, 2, 2, quarter, 2 * lanes), bf16),
            vmem((n, 2, quarter, 2 * lanes), bf16),
            vmem((lanes, columns), bf16),
            vmem((lanes // 2, columns), bf16),
            dma((4,)),
        ]
        + ring
        + [dma((n,))] * 4
        + [dma((2,))] * 2,
        compiler_params=kernel_params(5),
        name="mlp_and_back",
    )(ob, w_out, x_own, gain, weights, w_down, seed, seed_own)


class Spread:
    def __init__(self, n, pieces, out, sems):
        self.n, self.pieces, self.out = n, pieces, out
        self.s_blk, self.r_blk, self.s_x, self.r_x, self.s_c, self.r_c = sems
        self.grp, self.me = lax.axis_index("grp"), lax.axis_index("blk")
        self.over, self.core, self.grp_x, self.grp_c = team(self.grp)

    def first(self, k):
        to = (self.me + k) % self.n
        place = self.out.at[self.me, 2 * self.core + self.over]
        return push(
            self.pieces.at[to], place, self.s_blk.at[k], self.r_blk.at[k], (self.grp, to)
        )

    def own(self, sem):
        place = self.out.at[self.me, 2 * self.core + self.over]
        return pltpu.make_async_copy(self.pieces.at[self.me], place, sem)

    def to_x(self, k):
        piece = self.out.at[(self.me - k + self.n) % self.n, 2 * self.core + self.over]
        return push(piece, piece, self.s_x.at[k], self.r_x.at[k], (self.grp_x, self.me))

    def to_core(self, k, far):
        over = 1 - self.over if far else self.over
        piece = self.out.at[(self.me - k + self.n) % self.n, 2 * self.core + over]
        sems = (self.s_c.at[int(far), k], self.r_c.at[int(far), k])
        return push(piece, piece, *sems, (self.grp_c, self.me))

    def pass_on(self, k):
        pl.when(k > 0)(self.first(k).wait_recv)
        self.to_x(k).start()
        self.to_core(k, False).start()

    def pass_far(self, k):
        self.to_x(k).wait_recv()
        self.to_core(k, True).start()

    def arrived(self, k):
        for far in (False, True):
            self.to_core(k, far).wait_recv()

    def finish(self):
        def body(k, _):
            pl.when(k > 0)(self.first(k).wait_send)
            self.to_x(k).wait_send()
            for far in (False, True):
                self.to_core(k, far).wait_send()
            return 0

        lax.fori_loop(0, self.n, body, 0)


def each(count, body, low=0):
    lax.fori_loop(low, count, lambda k, _: (body(k), 0)[1], 0)


def spread_sems(n):
    dma = pltpu.SemaphoreType.DMA
    return [dma((n,)), dma((n,)), dma((n,)), dma((n,)), dma((2, n)), dma((2, n))]


def team_and_ring(n):
    grp, me = lax.axis_index("grp"), lax.axis_index("blk")
    _, _, grp_x, grp_c = team(grp)
    return [(grp, (me + k) % n) for k in range(1, n)] + [(grp_x, me), (grp_c, me)]


def fill_row(row, gains_all, which, share):
    for block in range(gains_all.shape[0]):
        row[:, block * share : (block + 1) * share] = gains_all[block, which : which + 1, :]


def turned(value, cosine, sine_part):
    half_size = HEAD // 2
    swapped = jnp.concatenate([value[:, half_size:], value[:, :half_size]], axis=1)
    return value * cosine + swapped * sine_part


def attend_kernel(
    n,
    heads,
    x_own,
    cosine,
    sine_part,
    first_key,
    query_place,
    key_place,
    slab_qkv,
    slab_gate_up,
    gains,
    seed_own,
    gains_all,
    columns_qkv,
    normed,
    qkv,
    attended,
    attended_b,
    log_total,
    gate_up,
    seed,
    x_all,
    gain_row,
    local,
    s_gain,
    r_gain,
    s_x,
    r_x,
    s_seed,
    r_seed,
    *spread_all,
):
    f32, bf16 = jnp.float32, jnp.bfloat16
    grp, me = lax.axis_index("grp"), lax.axis_index("blk")
    _, ends = ring_ends(n)
    rows, columns = x_own.shape
    spread_qkv = Spread(n, slab_qkv, columns_qkv, spread_all[:6])
    spread_gu = Spread(n, slab_gate_up, gate_up, spread_all[6:])
    near_gain = pltpu.make_async_copy(gains, gains_all.at[me], local.at[0])
    near_gain.start()
    near_qkv = spread_qkv.own(local.at[1])
    near_qkv.start()
    x_all[0] = x_own[...]
    greet(team_and_ring(n))

    def gain(k):
        return push(gains, gains_all.at[me], s_gain.at[k], r_gain.at[k], (grp, (me + k) % n))

    each(n, lambda k: gain(k).start(), 1)
    x_ring = Gather(n, x_all, s_x, r_x, ends)
    x_ring.start()
    each(n, lambda k: spread_qkv.first(k).start(), 1)
    near_gu = spread_gu.own(local.at[2])
    near_gu.start()

    def norm(slot):
        value = x_all[slot].astype(f32)
        inv = lax.rsqrt(jnp.mean(value * value, axis=-1, keepdims=True) + EPS)
        normed[slot] = (value * inv * gain_row[...]).astype(bf16)

    near_gain.wait()
    each(n, lambda k: gain(k).wait_recv(), 1)
    fill_row(gain_row, gains_all, 0, columns // n)

    def arrive(t):
        pl.when(t > 0)(lambda: x_ring.advance(t - 1))
        low = jnp.maximum(2 * t - 1, 0)
        each(jnp.minimum(2 * t + 1, n), norm, low)
        pl.when(t == 1)(near_qkv.wait)
        pl.when(t == 2)(lambda: each(n, spread_qkv.pass_on))
        pl.when(t == 3)(lambda: each(n, spread_qkv.pass_far))

    each(n // 2 + 1, arrive)
    seed_ring = Gather(n, seed, s_seed, r_seed, ends, seed_own)
    seed_ring.start()
    each(n, lambda k: spread_gu.first(k).start(), 1)
    each(n, spread_qkv.arrived)

    head_lanes = heads * HEAD
    pair = 2 * rows

    def project(i):
        both = normed[pl.ds(2 * i, 2)].reshape(pair, columns)
        result = dot_f32(both, columns_qkv[...].reshape(columns, 3 * head_lanes))
        at = pl.ds(pl.multiple_of(i * pair, pair), pair)
        table_c, table_s = cosine[at, :], sine_part[at, :]
        for piece in range(3 * heads):
            lane = slice(piece * HEAD, (piece + 1) * HEAD)
            value = result[:, lane]
            if piece < 2 * heads:
                value = turned(value, table_c, table_s)
            qkv[at, lane] = value.astype(bf16)

    each(n // 2, project)
    near_gu.wait()

    def tile(i):
        for head in range(heads):
            lane = slice(head * HEAD, (head + 1) * HEAD)
            at = pl.ds(pl.multiple_of(i * pair, pair), pair)
            keys = qkv[:, head_lanes + head * HEAD : head_lanes + (head + 1) * HEAD]
            values = qkv[:, 2 * head_lanes + head * HEAD : 2 * head_lanes + (head + 1) * HEAD]
            scores = nt_dot(qkv[at, lane], keys) * HEAD ** (-0.5)
            allowed = (key_place[...] >= first_key[at, :]) & (key_place[...] <= query_place[at, :])
            scores = jnp.where(allowed, scores, NEGATIVE)
            peak = jnp.max(scores, axis=-1, keepdims=True)
            raw = jnp.exp(scores - peak)
            total = jnp.sum(raw, axis=-1, keepdims=True)
            out = dot_f32(raw.astype(bf16), values) / total
            attended[at, lane] = out
            attended_b[at, lane] = out.astype(bf16)
            log_total[head, at, :] = peak + jnp.log(total)
        seed_ring.advance(i)
        each(2 * i + 2, spread_gu.pass_on, 2 * i)

    each(n // 2, tile)
    each(n, spread_gu.pass_far)
    each(n, spread_gu.arrived)
    near_qkv_sent = [spread_qkv, spread_gu]
    for spread in near_qkv_sent:
        spread.finish()
    each(n, lambda k: gain(k).wait_send(), 1)
    x_ring.finish()
    seed_ring.finish()


def attend(slab_qkv, slab_gate_up, gains, x_own, seed_own, cosine, sine_part, first_key, places):
    n = lax.axis_size("blk")
    rows, columns = x_own.shape
    seq = n * rows
    lanes = slab_qkv.shape[2]
    head_lanes = lanes // 3
    heads = head_lanes // HEAD
    f32, bf16 = jnp.float32, jnp.bfloat16
    vmem, dma = pltpu.VMEM, pltpu.SemaphoreType.DMA
    in_vmem, anywhere = pl.BlockSpec(memory_space=vmem), pl.BlockSpec(memory_space=pl.ANY)
    return pl.pallas_call(
        functools.partial(attend_kernel, n, heads),
        out_shape=(
            jax.ShapeDtypeStruct((n,) + gains.shape, f32),
            jax.ShapeDtypeStruct((n, 4) + slab_qkv.shape[1:], bf16),
            jax.ShapeDtypeStruct((n, rows, columns), bf16),
            jax.ShapeDtypeStruct((seq, lanes), bf16),
            jax.ShapeDtypeStruct((seq, head_lanes), f32),
            jax.ShapeDtypeStruct((seq, head_lanes), bf16),
            jax.ShapeDtypeStruct((heads, seq, 1), f32),
            jax.ShapeDtypeStruct((n, 4) + slab_gate_up.shape[1:], bf16),
            jax.ShapeDtypeStruct((n, rows, columns), bf16),
        ),
        in_specs=[in_vmem] * 6 + [anywhere] * 4,
        out_specs=[in_vmem] * 7 + [anywhere] * 2,
        scratch_shapes=[
            vmem((n, rows, columns), bf16),
            vmem((1, columns), f32),
            dma((3,)),
            dma((n,)),
            dma((n,)),
        ]
        + [dma((n // 2, 2, 2))] * 4
        + spread_sems(n) * 2,
        compiler_params=kernel_params(0),
        name="attend",
    )(
        x_own,
        cosine,
        sine_part,
        first_key,
        places.reshape(seq, 1),
        places.reshape(1, seq),
        slab_qkv,
        slab_gate_up,
        gains,
        seed_own,
    )


def finish_kernel(
    n,
    dqkv,
    x_own,
    gain,
    dresid,
    terms_two,
    out_grad,
    weights,
    normed_hbm,
    gate_up_sum,
    down_sum,
    x_grad,
    gain_grads,
    wide_gate_up,
    wide_qkv,
    tall_down,
    tall_out,
    normed,
    columns_qkv,
    held,
    terms,
    wide,
    wide_c,
    wide_x,
    out_c,
    out_x,
    gain_slabs,
    gain_heard,
    gain_team,
    load_sem,
    s_ring,
    r_ring,
    s_wc,
    r_wc,
    s_wx,
    r_wx,
    s_tall,
    r_tall,
    s_gain,
    r_gain,
    *spread_all,
):
    f32, bf16 = jnp.float32, jnp.bfloat16
    grp, me = lax.axis_index("grp"), lax.axis_index("blk")
    over, core, grp_x, grp_c = team(grp)
    _, ends = ring_ends(n)
    columns = x_own.shape[1]
    half = columns // 2
    lanes = wide.shape[4]
    quarter = wide.shape[3]
    load_normed = pltpu.make_async_copy(normed_hbm, normed, load_sem.at[0])
    load_qkv = pltpu.make_async_copy(weights, columns_qkv, load_sem.at[1])
    load_normed.start()
    load_qkv.start()
    spread_gu = Spread(n, gate_up_sum, wide_gate_up, spread_all[:6])
    spread_qkv = Spread(n, wide_x, wide_qkv, spread_all[6:])
    near_gu = spread_gu.own(load_sem.at[2])
    near_gu.start()
    greet(team_and_ring(n))

    down_own = pltpu.make_async_copy(down_sum, tall_down.at[2 * core + over], load_sem.at[3])
    down_own.start()
    down_place = tall_down.at[2 * core + over]
    down_x = push(down_sum, down_place, s_tall.at[0], r_tall.at[0], (grp_x, me))
    down_c = push(down_sum, down_place, s_tall.at[1], r_tall.at[1], (grp_c, me))
    far_place = tall_down.at[2 * core + 1 - over]
    down_far = push(far_place, far_place, s_tall.at[2], r_tall.at[2], (grp_c, me))
    out_one = push(out_grad.at[1 - core], out_c, s_tall.at[3], r_tall.at[3], (grp_c, me))
    out_two = push(out_c.at[1 - over], out_x, s_tall.at[4], r_tall.at[4], (grp_x, me))
    out_place = tall_out.at[2 * core + over]
    out_own = pltpu.make_async_copy(out_x, out_place, load_sem.at[4])
    out_to_x = push(out_x, out_place, s_tall.at[5], r_tall.at[5], (grp_x, me))
    out_to_c = push(out_x, out_place, s_tall.at[6], r_tall.at[6], (grp_c, me))
    out_far_place = tall_out.at[2 * core + 1 - over]
    out_far = push(out_far_place, out_far_place, s_tall.at[7], r_tall.at[7], (grp_c, me))
    out_one.start()

    load_qkv.wait()

    def term(step, way):
        return nt_dot(dqkv[behind(step, way, n)], columns_qkv[way * half : (way + 1) * half, :])

    ring = Scatter(n, held, terms, s_ring, r_ring, ends, term)

    def copy_c(k):
        tile = (me + k) % n
        return push(wide.at[tile, 1 - core], wide_c.at[tile], s_wc.at[k], r_wc.at[k], (grp_c, me))

    def copy_x(k):
        tile = (me + k) % n
        return push(
            wide_c.at[tile, 1 - over], wide_x.at[tile], s_wx.at[k], r_wx.at[k], (grp_x, me)
        )

    def grad(k):
        tile = (me + k) % n
        at = pl.multiple_of(tile * 4 * quarter, 4 * quarter)
        left = normed[:, :, pl.ds(at, 4 * quarter)].reshape(-1, 4 * quarter)
        rows = dot_t(left, dqkv[...].reshape(-1, lanes)).astype(bf16)
        wide[tile] = rows.reshape(2, 2, quarter, lanes)
        copy_c(k).start()

    def pass_x(k):
        tile = (me + k) % n
        copy_c(k).wait_recv()
        wide_c[tile, 1 - over] = (
            wide[tile, core, 1 - over].astype(f32) + wide_c[tile, 1 - over].astype(f32)
        ).astype(bf16)
        copy_x(k).start()

    ring.step(0)
    each(n, lambda k: spread_gu.first(k).start(), 1)
    out_one.wait_recv()
    out_c[1 - over] = (
        out_grad[core, 1 - over].astype(f32) + out_c[1 - over].astype(f32)
    ).astype(bf16)
    out_two.start()
    down_x.start()
    down_c.start()
    load_normed.wait()
    near_gu.wait()

    def turn(k):
        grad(k)
        pl.when(k > 0)(lambda: pass_x(k - 1))
        pl.when(k < n - 2)(lambda: ring.step(k + 1))

    each(n, turn)
    pass_x(n - 1)

    x_float = x_own[...].astype(f32)
    inv = lax.rsqrt(jnp.mean(x_float * x_float, axis=-1, keepdims=True) + EPS)
    for way in range(2):
        terms[way] = ring.result(way)
    dnormed = jnp.concatenate([terms[0], terms[1]], axis=1)
    terms_one = jnp.sum(dnormed * x_float * inv, axis=0, keepdims=True)
    share = columns // n
    for block in range(n):
        gain_slabs[block] = jnp.zeros_like(gain_slabs[block])
        lane = slice(block * share, (block + 1) * share)
        gain_slabs[block, 0:1, :] = terms_one[:, lane]
        gain_slabs[block, 1:2, :] = terms_two[:, lane]

    def gain_blk(k):
        to = (me + k) % n
        return push(gain_slabs.at[to], gain_heard.at[k], s_gain.at[k], r_gain.at[k], (grp, to))

    each(n, lambda k: gain_blk(k).start(), 1)
    a_one = dnormed * gain[...]
    x_grad[...] = (
        dresid[...]
        + inv * a_one
        - x_float * inv**3 * jnp.mean(a_one * x_float, axis=-1, keepdims=True)
    ).astype(bf16)
    each(n, spread_gu.pass_on)

    def take(k):
        tile = (me + k) % n
        copy_x(k).wait_recv()
        wide_x[tile] = (
            wide[tile, core, over].astype(f32)
            + wide_c[tile, over].astype(f32)
            + wide_x[tile].astype(f32)
        ).astype(bf16)

    def take_and_push(k):
        take(k)
        spread_qkv.first(k).start()

    each(n, take_and_push, 1)
    take(0)
    near_qkv = spread_qkv.own(load_sem.at[5])
    near_qkv.start()
    gain_heard[0] = gain_slabs[me]
    each(n, lambda k: gain_blk(k).wait_recv(), 1)
    gain_team[0] = jnp.sum(gain_heard[...], axis=0)
    gain_c = push(gain_team.at[0], gain_team.at[1], s_gain.at[n], r_gain.at[n], (grp_c, me))
    gain_c.start()
    out_two.wait_recv()
    out_x[...] = (
        out_grad[core, over].astype(f32) + out_c[over].astype(f32) + out_x[...].astype(f32)
    ).astype(bf16)
    out_own.start()
    out_to_x.start()
    out_to_c.start()
    each(n, spread_gu.pass_far)
    down_x.wait_recv()
    down_far.start()
    gain_c.wait_recv()
    gain_team[2] = gain_team[0] + gain_team[1]
    gain_x = push(
        gain_team.at[2], gain_team.at[3], s_gain.at[n + 1], r_gain.at[n + 1], (grp_x, me)
    )
    gain_x.start()
    near_qkv.wait()
    each(n, spread_qkv.pass_on)
    out_to_x.wait_recv()
    out_far.start()
    each(n, spread_qkv.pass_far)
    gain_x.wait_recv()
    gain_grads[...] = gain_team[2] + gain_team[3]
    each(n, spread_gu.arrived)
    each(n, spread_qkv.arrived)
    spread_gu.finish()
    spread_qkv.finish()
    ring.finish()
    down_own.wait()
    out_own.wait()
    for copy in (down_c, down_far, out_to_c, out_far):
        copy.wait()
    for copy in (down_x, out_one, out_two, out_to_x, gain_c, gain_x):
        copy.wait_send()

    def sent(k):
        copy_c(k).wait_send()
        copy_x(k).wait_send()
        pl.when(k > 0)(gain_blk(k).wait_send)

    each(n, sent)


def finish(
    dqkv, x_own, gain, dresid, terms_two, out_grad, weights, normed, gate_up_sum, down_sum
):
    n, rows, columns = normed.shape
    lanes = dqkv.shape[2]
    quarter = columns // (4 * n)
    share = columns // n
    f32, bf16 = jnp.float32, jnp.bfloat16
    vmem, dma = pltpu.VMEM, pltpu.SemaphoreType.DMA
    in_vmem, anywhere = pl.BlockSpec(memory_space=vmem), pl.BlockSpec(memory_space=pl.ANY)
    out_rows = out_grad.shape[0] // 4
    return pl.pallas_call(
        functools.partial(finish_kernel, n),
        out_shape=(
            jax.ShapeDtypeStruct((rows, columns), bf16),
            jax.ShapeDtypeStruct((8, share), f32),
            jax.ShapeDtypeStruct((n, 4) + gate_up_sum.shape[1:], bf16),
            jax.ShapeDtypeStruct((n, 4, quarter, lanes), bf16),
            jax.ShapeDtypeStruct((4,) + down_sum.shape, bf16),
            jax.ShapeDtypeStruct((4, out_rows, columns), bf16),
        ),
        in_specs=[in_vmem] * 6 + [anywhere] * 4,
        out_specs=[in_vmem] * 2 + [anywhere] * 4,
        scratch_shapes=[
            vmem((n, rows, columns), bf16),
            vmem((columns, lanes), bf16),
            vmem((2, n, rows, columns // 2), bf16),
            vmem((2, rows, columns // 2), f32),
            vmem((n, 2, 2, quarter, lanes), bf16),
            vmem((n, 2, quarter, lanes), bf16),
            vmem((n, quarter, lanes), bf16),
            vmem((2, out_rows, columns), bf16),
            vmem((out_rows, columns), bf16),
            vmem((n, 8, share), f32),
            vmem((n, 8, share), f32),
            vmem((4, 8, share), f32),
            dma((6,)),
        ]
        + [dma((n - 1, 2, 2))] * 2
        + [dma((n,))] * 4
        + [dma((8,))] * 2
        + [dma((n + 2,))] * 2
        + spread_sems(n) * 2,
        compiler_params=kernel_params(6),
        name="finish",
    )(
        dqkv,
        x_own,
        gain,
        dresid,
        terms_two,
        out_grad.reshape(2, 2, out_rows, columns),
        weights,
        normed,
        gate_up_sum,
        down_sum,
    )


def assemble_kernel(n, units, lanes, head_lanes, qkv, gate_up, down, out, *grads):
    grad_qkv, grad_out, grad_gate, grad_up, grad_down = grads
    f32 = jnp.float32
    for source in range(n):
        for part in range(3):
            first = (part * n + source) * head_lanes
            grad_qkv[:, first : first + head_lanes] = qkv[
                source, :, part * head_lanes : (part + 1) * head_lanes
            ].astype(f32)
        first = source * units
        grad_gate[:, first : first + units] = gate_up[source, :, :units].astype(f32)
        grad_up[:, first : first + units] = gate_up[source, :, lanes : lanes + units].astype(f32)
    grad_out[...] = out[...].astype(f32)
    grad_down[...] = down[...].astype(f32)


def assemble(qkv, gate_up, down, out, units, steps=4):
    n, rows, qkv_lanes = qkv.shape
    columns = down.shape[1]
    lanes = gate_up.shape[2] // 2
    head_lanes = qkv_lanes // 3
    step = rows // steps
    down_step = units // steps
    f32 = jnp.float32

    def wide(width):
        return pl.BlockSpec((n, step, width), lambda i: (0, i, 0))

    def flat(height, width):
        return pl.BlockSpec((height, width), lambda i: (i, 0))

    return pl.pallas_call(
        functools.partial(assemble_kernel, n, units, lanes, head_lanes),
        grid=(steps,),
        out_shape=(
            jax.ShapeDtypeStruct((rows, n * qkv_lanes), f32),
            jax.ShapeDtypeStruct((rows, columns), f32),
            jax.ShapeDtypeStruct((rows, n * units), f32),
            jax.ShapeDtypeStruct((rows, n * units), f32),
            jax.ShapeDtypeStruct((units, columns), f32),
        ),
        in_specs=[
            wide(qkv_lanes),
            wide(2 * lanes),
            flat(down_step, columns),
            flat(out.shape[0] // steps, columns),
        ],
        out_specs=[
            flat(step, n * qkv_lanes),
            flat(step, columns),
            flat(step, n * units),
            flat(step, n * units),
            flat(down_step, columns),
        ],
        compiler_params=pltpu.CompilerParams(vmem_limit_bytes=VMEM_BYTES),
        name="assemble",
    )(qkv, gate_up, down, out)


def pad_to(array, axis, size):
    widths = [(0, 0)] * array.ndim
    widths[axis] = (0, size - array.shape[axis])
    return jnp.pad(array, widths)


def per_device(block_input, doc_lens, norm_attn, w_qkv, w_out, norm_mlp, w_gate, w_up, w_down, cot):
    n = lax.axis_size("blk")
    tok_rows, width = block_input.shape[1:]
    seq = tok_rows * n
    heads = HEADS // n
    head_lanes = heads * HEAD
    qkv_lanes = 3 * head_lanes
    score_scale = HEAD ** (-0.5)
    units = w_down.shape[0]
    lanes = -(-units // 128) * 128
    bf16 = jnp.bfloat16

    over, core, _, _ = team(lax.axis_index("grp"))
    quarter = w_qkv.shape[0] // 4
    first_row = (2 * core + over) * quarter

    def quarter_of(weight):
        return lax.dynamic_slice_in_dim(weight, first_row, quarter, 0)

    slab_qkv = (
        quarter_of(w_qkv)
        .reshape(quarter, 3, n, head_lanes)
        .transpose(2, 0, 1, 3)
        .reshape(n, quarter, qkv_lanes)
    )
    slab_gate_up = jnp.concatenate(
        [
            pad_to(quarter_of(w).reshape(quarter, n, units).transpose(1, 0, 2), 2, lanes)
            for w in (w_gate, w_up)
        ],
        axis=2,
    )
    gains = pad_to(jnp.stack([norm_attn, norm_mlp]).astype(jnp.float32), 0, 8)
    place = ring_place(lax.axis_index("blk"), n)
    offsets = [0] + [k * sign for k in range(1, n // 2) for sign in (-1, 1)] + [n // 2]
    blocks = jnp.stack([at_offset(place, offset, n) for offset in offsets])
    places = (blocks[:, None] * tok_rows + jnp.arange(tok_rows, dtype=jnp.int32)).reshape(seq)
    lengths = doc_lens[0]
    starts = jnp.cumsum(lengths) - lengths
    first_key = start_of(places, starts)
    half_cosine, half_sine = angle_tables(places - first_key)
    half_cosine, half_sine = half_cosine[:, 0], half_sine[:, 0]
    cosine = jnp.concatenate([half_cosine, half_cosine], axis=1)
    sine_part = jnp.concatenate([-half_sine, half_sine], axis=1)
    gains_all, qkv_columns, normed_one, qkv, attended, attended_b, log_total, gate_up, seed = attend(
        slab_qkv,
        slab_gate_up,
        gains,
        block_input[0],
        cot[0],
        cosine,
        sine_part,
        first_key.reshape(seq, 1),
        places,
    )
    gain_one = gains_all[:, 0].reshape(1, width)
    gain_two = gains_all[:, 1].reshape(1, width)
    qkv_columns = qkv_columns.reshape(width, qkv_lanes)
    gate_up = gate_up.reshape(width, 2 * lanes)
    block_out, dresid, dattended, terms_two, gate_up_sum, down_sum, dresid_b = mlp_and_back(
        attended_b.reshape(n, tok_rows, head_lanes),
        w_out,
        block_input[0],
        gain_two,
        gate_up,
        lanes,
        w_down,
        seed,
        cot[0],
    )
    dattended = dattended.reshape(seq, heads, HEAD)
    out_grad = dot_t(attended_b, dresid_b.reshape(seq, width)).astype(bf16)
    delta = jnp.sum(
        dattended.astype(jnp.float32) * attended.reshape(seq, heads, HEAD), axis=-1
    ).T
    queries, keys, values = qkv.reshape(seq, 3, heads, HEAD).transpose(1, 0, 2, 3)
    allowed = (places[None, :] >= first_key[:, None]) & (places[None, :] <= places[:, None])
    scores = (
        jnp.einsum("qhd,khd->hqk", queries, keys, preferred_element_type=jnp.float32) * score_scale
    )
    probs = jnp.where(allowed[None], jnp.exp(scores - log_total), 0.0)
    dprobs = jnp.einsum("qhd,khd->hqk", dattended, values, preferred_element_type=jnp.float32)
    dscores = (probs * (dprobs - delta[..., None])).astype(bf16)
    dquery = score_scale * jnp.einsum(
        "hqk,khd->qhd", dscores, keys, preferred_element_type=jnp.float32
    )
    dkey = score_scale * jnp.einsum(
        "hqk,qhd->khd", dscores, queries, preferred_element_type=jnp.float32
    )
    dvalue = jnp.einsum(
        "hqk,qhd->khd", probs.astype(bf16), dattended, preferred_element_type=jnp.float32
    )
    dqkv = (
        jnp.stack(
            [
                unrotate(dquery, half_cosine[:, None], half_sine[:, None]),
                unrotate(dkey, half_cosine[:, None], half_sine[:, None]),
                dvalue,
            ],
            axis=1,
        )
        .reshape(n, tok_rows, qkv_lanes)
        .astype(bf16)
    )
    x_grad, gain_grads, wide_gate_up, wide_qkv, tall_down, tall_out = finish(
        dqkv,
        block_input[0],
        gain_one,
        dresid,
        terms_two,
        out_grad,
        qkv_columns,
        normed_one,
        gate_up_sum,
        down_sum,
    )
    shard_rows = 4 * quarter
    grad_qkv, grad_out, grad_gate, grad_up, grad_down = assemble(
        wide_qkv.reshape(n, shard_rows, qkv_lanes),
        wide_gate_up.reshape(n, shard_rows, 2 * lanes),
        tall_down.reshape(lanes, width),
        tall_out.reshape(head_lanes, width),
        units,
    )
    return (
        block_out[None],
        x_grad[None],
        gain_grads[0],
        grad_qkv,
        grad_out,
        gain_grads[1],
        grad_gate,
        grad_up,
        grad_down,
    )


def body_for(mesh):
    return per_device if HEADS % mesh.shape["blk"] == 0 else per_device_gather


def solution(mesh):
    return jax.shard_map(
        body_for(mesh),
        mesh=mesh,
        in_specs=(
            P("grp", "blk", None),
            P("grp", None),
            P("blk"),
            P("blk", None),
            P("blk", None),
            P("blk"),
            P("blk", None),
            P("blk", None),
            P("blk", None),
            P("grp", "blk", None),
        ),
        out_specs=(
            P("grp", "blk", None),
            P("grp", "blk", None),
            P("blk"),
            P("blk", None),
            P("blk", None),
            P("blk"),
            P("blk", None),
            P("blk", None),
            P("blk", None),
        ),
        check_vma=False,
    )
```

```python
import functools
import math

import jax
import jax.numpy as jnp
from jax import lax
from jax.experimental import pallas as pl
from jax.experimental.pallas import tpu as pltpu
from jax.sharding import PartitionSpec as P

HEADS = 16
HEAD = 128


EPS = 1e-05
NEGATIVE = -1e30


def angle_tables(places):
    half_size = HEAD // 2
    freqs = jnp.exp(jnp.arange(half_size, dtype=jnp.float32) * (-2.0 * math.log(10000.0) / HEAD))
    angles = places.astype(jnp.float32)[:, None] * freqs
    return (jnp.cos(angles)[:, None, :], jnp.sin(angles)[:, None, :])


def rotate(tensor, cosine, sine_part):
    half_size = HEAD // 2
    first_half = tensor[..., :half_size]
    second_half = tensor[..., half_size:]
    return jnp.concatenate(
        [
            first_half * cosine - second_half * sine_part,
            second_half * cosine + first_half * sine_part,
        ],
        axis=-1,
    )


def unrotate(tensor, cosine, sine_part):
    half_size = HEAD // 2
    first_half = tensor[..., :half_size]
    second_half = tensor[..., half_size:]
    return jnp.concatenate(
        [
            first_half * cosine + second_half * sine_part,
            second_half * cosine - first_half * sine_part,
        ],
        axis=-1,
    )


def segment_of(places, starts):
    return jnp.sum((starts[None, :] <= places[:, None]).astype(jnp.int32), axis=1) - 1


def start_of(places, starts):
    return jnp.max(jnp.where(starts[None, :] <= places[:, None], starts[None, :], 0), axis=1)


def contract_rows(left, right):
    return lax.dot_general(
        left, right, (((1,), (1,)), ((), ())), preferred_element_type=jnp.float32
    )


def weight_term(left, right):

    def term(start, count):
        return lax.dot_general(
            left, right, (((0,), (0,)), ((), ())), preferred_element_type=jnp.float32
        )

    return term


def shard_grad(term_fn, shard_rows):
    shared = lax.psum_scatter(
        term_fn(jnp.int32(0), shard_rows * lax.axis_size("blk")).astype(jnp.bfloat16),
        "blk",
        scatter_dimension=0,
        tiled=True,
    )
    return lax.psum(shared, "grp").astype(jnp.float32)


def per_device_gather(block_input, doc_lens, norm_attn, w_qkv, w_out, norm_mlp, w_gate, w_up, w_down, cot):
    tok_rows = block_input.shape[1]
    width = block_input.shape[2]
    score_scale = HEAD ** (-0.5)
    shards = (norm_attn, w_qkv, w_out, norm_mlp, w_gate, w_up, w_down)
    gathered = (
        lax.all_gather(shards[0], "blk", axis=0, tiled=True),
        lax.all_gather(shards[1], "blk", axis=0, tiled=True),
        lax.all_gather(shards[2], "blk", axis=0, tiled=True),
        lax.all_gather(shards[3], "blk", axis=0, tiled=True),
        lax.all_gather(shards[4], "blk", axis=0, tiled=True),
        lax.all_gather(shards[5], "blk", axis=0, tiled=True),
        lax.all_gather(shards[6], "blk", axis=0, tiled=True),
    )
    gain_one, weight_qkv, weight_out, gain_two, weight_gate, weight_up, weight_down = gathered
    place_rows = lax.axis_index("blk") * tok_rows + jnp.arange(tok_rows, dtype=jnp.int32)
    lengths = doc_lens[0]
    starts = jnp.cumsum(lengths) - lengths
    query_seg = segment_of(place_rows, starts)
    cosine, sine_part = angle_tables(place_rows - start_of(place_rows, starts))
    x_float = block_input[0].astype(jnp.float32)
    inv_one = lax.rsqrt(jnp.mean(x_float * x_float, axis=-1, keepdims=True) + EPS)
    normed_one = (x_float * inv_one * gain_one.astype(jnp.float32)).astype(jnp.bfloat16)
    projected = jnp.dot(normed_one, weight_qkv, preferred_element_type=jnp.float32)
    heads_all = projected.reshape(tok_rows, 3, HEADS, HEAD)
    queries = rotate(heads_all[:, 0], cosine, sine_part).astype(jnp.bfloat16)
    keys_own = rotate(heads_all[:, 1], cosine, sine_part).astype(jnp.bfloat16)
    values_own = heads_all[:, 2].astype(jnp.bfloat16)

    def pair_mask(count):
        key_places = jnp.arange(count, dtype=jnp.int32)
        key_seg = segment_of(key_places, starts)
        return (query_seg[:, None] == key_seg[None, :]) & (
            key_places[None, :] <= place_rows[:, None]
        )

    piece = (
        lax.all_gather(keys_own, "blk", axis=0, tiled=True),
        lax.all_gather(values_own, "blk", axis=0, tiled=True),
    )
    count = piece[0].shape[0]
    row_peak = jnp.full((HEADS, tok_rows), NEGATIVE, jnp.float32)
    key_piece, value_piece = piece
    count = key_piece.shape[0]
    allowed = pair_mask(count)[None]
    scores = (
        jnp.einsum("qhd,khd->hqk", queries, key_piece, preferred_element_type=jnp.float32)
        * score_scale
    )
    scores = jnp.where(allowed, scores, NEGATIVE)
    new_peak = jnp.maximum(row_peak, jnp.max(scores, axis=-1))
    weights_now = jnp.where(allowed, jnp.exp(scores - new_peak[..., None]), 0.0)
    row_total = jnp.sum(weights_now, axis=-1)
    accum = jnp.einsum(
        "hqk,khd->hqd",
        weights_now.astype(jnp.bfloat16),
        value_piece,
        preferred_element_type=jnp.float32,
    )
    row_peak, row_total, accum = (new_peak, row_total, accum)
    log_total = row_peak + jnp.log(row_total)
    attended = (accum / row_total[..., None]).transpose(1, 0, 2)
    attended_b = attended.reshape(tok_rows, width).astype(jnp.bfloat16)
    resid = x_float + jnp.dot(attended_b, weight_out, preferred_element_type=jnp.float32)
    inv_two = lax.rsqrt(jnp.mean(resid * resid, axis=-1, keepdims=True) + EPS)
    normed_two = (resid * inv_two * gain_two.astype(jnp.float32)).astype(jnp.bfloat16)
    gate_proj = jnp.dot(normed_two, weight_gate, preferred_element_type=jnp.float32)
    up_proj = jnp.dot(normed_two, weight_up, preferred_element_type=jnp.float32)
    sigmoid_gate = jax.nn.sigmoid(gate_proj)
    swish = gate_proj * sigmoid_gate
    hidden = (swish * up_proj).astype(jnp.bfloat16)
    block_out = (resid + jnp.dot(hidden, weight_down, preferred_element_type=jnp.float32)).astype(
        jnp.bfloat16
    )
    again = (
        lax.all_gather(shards[0], "blk", axis=0, tiled=True),
        lax.all_gather(shards[1], "blk", axis=0, tiled=True),
        lax.all_gather(shards[2], "blk", axis=0, tiled=True),
        lax.all_gather(shards[3], "blk", axis=0, tiled=True),
        lax.all_gather(shards[4], "blk", axis=0, tiled=True),
        lax.all_gather(shards[5], "blk", axis=0, tiled=True),
        lax.all_gather(shards[6], "blk", axis=0, tiled=True),
    )
    back_gain_one, back_qkv, back_out, back_gain_two, back_gate, back_up, back_down = again
    seed = cot[0]
    seed_float = seed.astype(jnp.float32)
    dhidden = contract_rows(seed, back_down)
    dgate = (dhidden * up_proj * sigmoid_gate * (1.0 + gate_proj * (1.0 - sigmoid_gate))).astype(
        jnp.bfloat16
    )
    dup = (dhidden * swish).astype(jnp.bfloat16)
    dnormed_two = contract_rows(dgate, back_gate) + contract_rows(dup, back_up)
    a_two = dnormed_two * back_gain_two.astype(jnp.float32)
    dresid = (
        seed_float
        + inv_two * a_two
        - resid * inv_two**3 * jnp.mean(a_two * resid, axis=-1, keepdims=True)
    )
    dresid_b = dresid.astype(jnp.bfloat16)
    dattended = (
        contract_rows(dresid_b, back_out).astype(jnp.bfloat16).reshape(tok_rows, HEADS, HEAD)
    )
    delta = jnp.sum(dattended.astype(jnp.float32) * attended, axis=-1).T
    piece = (
        lax.all_gather(keys_own, "blk", axis=0, tiled=True),
        lax.all_gather(values_own, "blk", axis=0, tiled=True),
    )
    count = piece[0].shape[0]
    key_piece, value_piece = piece
    count = key_piece.shape[0]
    score_count = key_piece.shape[0]
    allowed = pair_mask(score_count)[None]
    scores = (
        jnp.einsum("qhd,khd->hqk", queries, key_piece, preferred_element_type=jnp.float32)
        * score_scale
    )
    probs = jnp.where(allowed, jnp.exp(scores - log_total[..., None]), 0.0)
    dprobs = jnp.einsum("qhd,khd->hqk", dattended, value_piece, preferred_element_type=jnp.float32)
    dscores = (probs * (dprobs - delta[..., None])).astype(jnp.bfloat16)
    probs, dscores = (probs, dscores)
    dquery_acc = score_scale * jnp.einsum(
        "hqk,khd->hqd", dscores, key_piece, preferred_element_type=jnp.float32
    )
    dkeys = score_scale * jnp.einsum(
        "hqk,qhd->khd", dscores, queries, preferred_element_type=jnp.float32
    )
    dvalues = jnp.einsum(
        "hqk,qhd->khd", probs.astype(jnp.bfloat16), dattended, preferred_element_type=jnp.float32
    )
    stacked = jnp.concatenate([dkeys.reshape(count, width), dvalues.reshape(count, width)], axis=1)
    grads_buffer = stacked
    dquery_acc, grads_buffer = (dquery_acc, grads_buffer)
    own_grads = lax.psum_scatter(
        grads_buffer.astype(jnp.bfloat16), "blk", scatter_dimension=0, tiled=True
    ).astype(jnp.float32)
    dkey = unrotate(own_grads[:, :width].reshape(tok_rows, HEADS, HEAD), cosine, sine_part)
    dvalue = own_grads[:, width:].reshape(tok_rows, HEADS, HEAD)
    dquery = unrotate(dquery_acc.transpose(1, 0, 2), cosine, sine_part)
    dqkv = (
        jnp.stack([dquery, dkey, dvalue], axis=1).reshape(tok_rows, 3 * width).astype(jnp.bfloat16)
    )
    dnormed_one = contract_rows(dqkv, back_qkv)
    a_one = dnormed_one * back_gain_one.astype(jnp.float32)
    x_grad = (
        dresid
        + inv_one * a_one
        - x_float * inv_one**3 * jnp.mean(a_one * x_float, axis=-1, keepdims=True)
    ).astype(jnp.bfloat16)
    width_rows = norm_attn.shape[0]
    gain_terms = jnp.stack(
        [
            jnp.sum(dnormed_one * x_float * inv_one, axis=0),
            jnp.sum(dnormed_two * resid * inv_two, axis=0),
        ],
        axis=1,
    )

    def gain_slice(start, count):
        return gain_terms

    grad_down = shard_grad(weight_term(hidden, seed), w_down.shape[0])
    grad_gate = shard_grad(weight_term(normed_two, dgate), width_rows)
    grad_up = shard_grad(weight_term(normed_two, dup), width_rows)
    grad_out = shard_grad(weight_term(attended_b, dresid_b), width_rows)
    grad_qkv = shard_grad(weight_term(normed_one, dqkv), width_rows)
    gain_grads = shard_grad(gain_slice, width_rows)
    return (
        block_out[None],
        x_grad[None],
        gain_grads[:, 0],
        grad_qkv,
        grad_out,
        gain_grads[:, 1],
        grad_gate,
        grad_up,
        grad_down,
    )


MESH = pl.DeviceIdType.MESH
VMEM_BYTES = 62 * 2**20


def ring_place(block, n):
    up, row = block // 2, block % 2
    return (1 - row) * up + row * (n - 1 - up)


def ring_block(place, n):
    back = place // (n // 2)
    return (1 - back) * 2 * place + back * (2 * (n - 1 - place) + 1)


def at_offset(place, offset, n):
    return ring_block((place + offset + n) % n, n)


def greet(devices):
    barrier = pltpu.get_barrier_semaphore()
    for device in devices:
        pl.semaphore_signal(barrier, inc=1, device_id=device, device_id_type=MESH)
    pl.semaphore_wait(barrier, len(devices))


def push(src, dst, send_sem, recv_sem, device):
    return pltpu.make_async_remote_copy(
        src_ref=src,
        dst_ref=dst,
        send_sem=send_sem,
        recv_sem=recv_sem,
        device_id=device,
        device_id_type=MESH,
    )


def kernel_params(collective_id):
    return pltpu.CompilerParams(
        collective_id=collective_id, has_side_effects=True, vmem_limit_bytes=VMEM_BYTES
    )


def dot_f32(left, right):
    return jnp.dot(left, right, preferred_element_type=jnp.float32)


def dot_t(left, right):
    return lax.dot_general(
        left, right, (((0,), (0,)), ((), ())), preferred_element_type=jnp.float32
    )


def nt_dot(left, right):
    return lax.dot_general(
        left, right, (((1,), (1,)), ((), ())), preferred_element_type=jnp.float32
    )


def ring_ends(n):
    grp, me = lax.axis_index("grp"), lax.axis_index("blk")
    place = ring_place(me, n)
    return place, ((grp, at_offset(place, 1, n)), (grp, at_offset(place, -1, n)))


class Gather:
    def __init__(self, n, buf, send, recv, ends, own=None):
        self.n, self.buf, self.send, self.recv, self.ends = n, buf, send, recv, ends
        self.own = buf.at[0] if own is None else own
        self.half = buf.shape[1] // 2

    def copy(self, step, chunk, way):
        part = pl.ds(chunk * self.half, self.half)
        if isinstance(step, int):
            target = min(2 * step + 1 + way, self.n - 1)
        else:
            target = jnp.minimum(2 * step + 1 + way, self.n - 1)
        first = isinstance(step, int) and step == 0
        return push(
            self.own.at[part] if first else self.buf.at[2 * step - 1 + way, part],
            self.buf.at[target, part],
            self.send.at[step, chunk, way],
            self.recv.at[step, chunk, way],
            self.ends[way],
        )

    def landed(self, step, chunk, way):
        target = jnp.minimum(2 * step + 1 + way, self.n - 1)
        place = self.buf.at[target, pl.ds(chunk * self.half, self.half)]
        sems = (self.send.at[step, chunk, way], self.recv.at[step, chunk, way])
        return push(place, place, *sems, self.ends[way])

    def used(self, step, chunk, way):
        return step < self.n // 2 - 1 or chunk == way

    def start(self):
        for chunk in range(2):
            for way in range(2):
                self.copy(0, chunk, way).start()

    def advance(self, step):
        for chunk in range(2):
            for way in range(2):
                if isinstance(step, int):
                    if self.used(step, chunk, way):
                        self.copy(step, chunk, way).wait_recv()
                        if step + 1 < self.n // 2 and self.used(step + 1, chunk, way):
                            self.copy(step + 1, chunk, way).start()
                elif chunk == way:
                    self.landed(step, chunk, way).wait_recv()
                    pl.when(step + 1 < self.n // 2)(self.copy(step + 1, chunk, way).start)
                else:
                    pl.when(step < self.n // 2 - 1)(self.landed(step, chunk, way).wait_recv)
                    pl.when(step + 1 < self.n // 2 - 1)(self.copy(step + 1, chunk, way).start)

    def finish(self):
        for step in range(self.n // 2):
            for chunk in range(2):
                for way in range(2):
                    if self.used(step, chunk, way):
                        self.copy(step, chunk, way).wait_send()


class Scatter:
    def __init__(self, n, held, terms, send, recv, ends, term):
        self.n, self.held, self.terms, self.send, self.recv = n, held, terms, send, recv
        self.ends, self.term = ends, term
        self.half = held.shape[2] // 2

    def copy(self, step, chunk, way):
        part = pl.ds(chunk * self.half, self.half)
        return push(
            self.held.at[way, step, part],
            self.held.at[way, step + 1, part],
            self.send.at[step, chunk, way],
            self.recv.at[step, chunk, way],
            self.ends[way],
        )

    def step(self, step):
        for way in range(2):
            self.terms[way] = self.term(step, way)
        for chunk in range(2):
            for way in range(2):
                part = pl.ds(chunk * self.half, self.half)

                def first(way=way, part=part):
                    self.held[way, step, part] = self.terms[way, part].astype(jnp.bfloat16)

                def later(chunk=chunk, way=way, part=part):
                    self.copy(step - 1, chunk, way).wait_recv()
                    self.held[way, step, part] = (
                        self.terms[way, part] + self.held[way, step, part].astype(jnp.float32)
                    ).astype(jnp.bfloat16)

                if isinstance(step, int):
                    (later if step else first)()
                else:
                    pl.when(step == 0)(first)
                    pl.when(step > 0)(later)
                self.copy(step, chunk, way).start()

    def result(self, way):
        for chunk in range(2):
            self.copy(self.n - 2, chunk, way).wait_recv()
        return self.term(self.n - 1, way) + self.held[way, self.n - 1].astype(jnp.float32)

    def finish(self):
        def body(step, _):
            for chunk in range(2):
                for way in range(2):
                    self.copy(step, chunk, way).wait_send()
            return 0

        lax.fori_loop(0, self.n - 1, body, 0)


def behind(step, way, n):
    near = 2 * step + 1 + way
    far = 2 * (n - 1 - step) - way
    if isinstance(step, int):
        return 0 if step == n - 1 else min(near, far, n - 1)
    return jnp.where(step == n - 1, 0, jnp.minimum(jnp.minimum(near, far), n - 1))


def team(grp):
    over, core = grp // 2, grp % 2
    return over, core, (1 - over) * 2 + core, over * 2 + 1 - core


def mlp_kernel(
    n,
    lanes,
    ob,
    w_out,
    x_ref,
    gain,
    weights,
    w_down,
    seed_hbm,
    seed_own,
    block_out,
    dresid_out,
    dattended,
    gain_terms,
    wide_sum,
    down_sum,
    out_grad,
    dresid,
    normed,
    seed,
    gate_up,
    down,
    hidden,
    dgate_up,
    held_one,
    held_two,
    terms,
    resid,
    wide,
    wide_c,
    tall,
    tall_c,
    load_sem,
    s_one,
    r_one,
    s_two,
    r_two,
    s_three,
    r_three,
    s_norm,
    r_norm,
    s_dres,
    r_dres,
    s_wc,
    r_wc,
    s_wx,
    r_wx,
    s_tall,
    r_tall,
):
    f32, bf16 = jnp.float32, jnp.bfloat16
    grp, me = lax.axis_index("grp"), lax.axis_index("blk")
    over, core, grp_x, grp_c = team(grp)
    _, ends = ring_ends(n)
    units = w_down.shape[0]
    loads = [
        pltpu.make_async_copy(weights, gate_up, load_sem.at[0]),
        pltpu.make_async_copy(w_down, down.at[pl.ds(0, units)], load_sem.at[1]),
        pltpu.make_async_copy(
            seed_hbm.at[pl.ds(1, n - 1)], seed.at[pl.ds(1, n - 1)], load_sem.at[2]
        ),
        pltpu.make_async_copy(seed_own, seed.at[0], load_sem.at[3]),
    ]
    for load in loads:
        load.start()
    if units < lanes:
        down[pl.ds(units, lanes - units)] = jnp.zeros((lanes - units, down.shape[1]), bf16)
    greet(list(ends) + [(grp_x, me), (grp_c, me)])
    columns = x_ref.shape[1]
    half = columns // 2

    def out_term(step, way):
        return dot_f32(ob[behind(step, way, n)], w_out[:, way * half : (way + 1) * half])

    one = Scatter(n, held_one, terms, s_one, r_one, ends, out_term)
    one.step(0)
    lax.fori_loop(1, n - 1, lambda step, _: (one.step(step), 0)[1], 0)
    for way in range(2):
        part = slice(way * half, (way + 1) * half)
        resid[:, part] = x_ref[:, part].astype(f32) + one.result(way)
    value = resid[...]
    inv = lax.rsqrt(jnp.mean(value * value, axis=-1, keepdims=True) + EPS)
    normed[0] = (value * inv * gain[...]).astype(bf16)
    gather = Gather(n, normed, s_norm, r_norm, ends)
    gather.start()
    one.finish()
    for load in loads:
        load.wait()

    def mlp(slot, _):
        both = dot_f32(normed[slot], gate_up[...])
        grad = nt_dot(seed[slot], down[...])
        gate, up = both[:, :lanes], both[:, lanes:]
        sig = jax.nn.sigmoid(gate)
        swish = gate * sig
        hidden[slot] = (swish * up).astype(bf16)
        dgate_up[slot, :, :lanes] = (grad * up * sig * (1.0 + gate * (1.0 - sig))).astype(bf16)
        dgate_up[slot, :, lanes:] = (grad * swish).astype(bf16)
        return 0

    def norm_term(step, way):
        return nt_dot(dgate_up[behind(step, way, n)], gate_up[way * half : (way + 1) * half, :])

    two = Scatter(n, held_two, terms, s_two, r_two, ends, norm_term)

    def turn(t, _):
        pl.when(t > 0)(lambda: gather.advance(t - 1))
        low = jnp.maximum(2 * t - 1, 0)
        lax.fori_loop(low, jnp.minimum(2 * t + 1, n), mlp, 0)
        pl.when(t > 0)(lambda: two.step(t - 1))
        return 0

    lax.fori_loop(0, n // 2 + 1, turn, 0)

    tall_rows = lanes // 4

    def tall_at(first, count):
        return pl.ds(pl.multiple_of(first * tall_rows, tall_rows), count * tall_rows)

    tall_tile = 256 if lanes % 256 == 0 else 128
    tiles = lanes // tall_tile

    def tall_grad(tile):
        at = pl.multiple_of(tile * tall_tile, tall_tile)
        left = hidden[:, :, pl.ds(at, tall_tile)].reshape(-1, tall_tile)
        grad_rows = dot_t(left, seed[...].reshape(-1, columns)).astype(bf16)
        tall[pl.ds(at, tall_tile)] = grad_rows

    def rest(step, _):
        two.step(step)
        pl.when(step - n // 2 < tiles)(lambda: tall_grad(step - n // 2))
        return 0

    lax.fori_loop(n // 2, n - 1, rest, 0)
    for tile in range(n // 2 - 1, tiles):
        tall_grad(tile)
    tall_one = push(tall.at[tall_at(2 - 2 * core, 2)], tall_c, s_tall.at[0], r_tall.at[0], (grp_c, me))
    tall_one.start()

    value = resid[...]
    inv = lax.rsqrt(jnp.mean(value * value, axis=-1, keepdims=True) + EPS)
    for way in range(2):
        part = slice(way * half, (way + 1) * half)
        dresid_out[:, part] = two.result(way)
    dnormed = dresid_out[...]
    gain_terms[...] = jnp.sum(dnormed * value * inv, axis=0, keepdims=True)
    a_two = dnormed * gain[...]
    total = (
        seed[0].astype(f32)
        + inv * a_two
        - value * inv**3 * jnp.mean(a_two * value, axis=-1, keepdims=True)
    )
    dresid_out[...] = total
    dresid[0] = total.astype(bf16)
    back = Gather(n, dresid, s_dres, r_dres, ends)
    back.start()
    two.finish()

    def down_term(step, way):
        return dot_f32(hidden[behind(step, way, n)], down[:, way * half : (way + 1) * half])

    three = Scatter(n, held_one, terms, s_three, r_three, ends, down_term)

    def dob(slot, _):
        dattended[slot] = nt_dot(dresid[slot], w_out[...]).astype(bf16)
        return 0

    def wide_copy_c(tile):
        return push(
            wide.at[tile, 1 - core], wide_c.at[tile], s_wc.at[tile], r_wc.at[tile], (grp_c, me)
        )

    def wide_copy_x(tile):
        return push(
            wide_c.at[tile, 1 - over], wide_sum.at[tile], s_wx.at[tile], r_wx.at[tile], (grp_x, me)
        )

    quarter = wide.shape[3]

    def wide_grad(tile):
        at = pl.multiple_of(tile * 4 * quarter, 4 * quarter)
        left = normed[:, :, pl.ds(at, 4 * quarter)].reshape(-1, 4 * quarter)
        grad = dot_t(left, dgate_up[...].reshape(-1, 2 * lanes)).astype(bf16)
        wide[tile] = grad.reshape(2, 2, quarter, 2 * lanes)
        wide_copy_c(tile).start()

    def wide_pass(tile):
        wide_copy_c(tile).wait_recv()
        wide_c[tile, 1 - over] = (
            wide[tile, core, 1 - over].astype(f32) + wide_c[tile, 1 - over].astype(f32)
        ).astype(bf16)
        wide_copy_x(tile).start()

    tall_two = push(tall_c.at[tall_at(1 - over, 1)], down_sum, s_tall.at[1], r_tall.at[1], (grp_x, me))

    def again(t, _):
        pl.when(t > 0)(lambda: back.advance(t - 1))
        low = jnp.maximum(2 * t - 1, 0)
        lax.fori_loop(low, jnp.minimum(2 * t + 1, n), dob, 0)

        def inner(step, _):
            pl.when(step < n - 1)(lambda: three.step(step))
            pl.when(step > 0)(lambda: wide_pass(step - 1))
            wide_grad(step)
            return 0

        lax.fori_loop(2 * t, jnp.minimum(2 * t + 2, n), inner, 0)
        return 0

    lax.fori_loop(0, n // 2 + 1, again, 0)
    wide_pass(n - 1)
    tall_one.wait_recv()
    tall_c[tall_at(1 - over, 1)] = (
        tall[tall_at(2 * core + 1 - over, 1)].astype(f32)
        + tall_c[tall_at(1 - over, 1)].astype(f32)
    ).astype(bf16)
    tall_two.start()
    out_grad[...] = dot_t(
        ob[...].reshape(-1, ob.shape[2]), dresid[...].reshape(-1, columns)
    ).astype(bf16)
    for way in range(2):
        part = slice(way * half, (way + 1) * half)
        block_out[:, part] = (resid[:, part] + three.result(way)).astype(bf16)

    def wide_take(tile, _):
        wide_copy_x(tile).wait_recv()
        wide_sum[tile] = (
            wide[tile, core, over].astype(f32)
            + wide_c[tile, over].astype(f32)
            + wide_sum[tile].astype(f32)
        ).astype(bf16)
        return 0

    lax.fori_loop(0, n, wide_take, 0)
    tall_two.wait_recv()
    down_sum[...] = (
        tall[tall_at(2 * core + over, 1)].astype(f32)
        + tall_c[tall_at(over, 1)].astype(f32)
        + down_sum[...].astype(f32)
    ).astype(bf16)
    gather.finish()
    back.finish()
    three.finish()
    tall_one.wait_send()
    tall_two.wait_send()

    def sent(tile, _):
        wide_copy_c(tile).wait_send()
        wide_copy_x(tile).wait_send()
        return 0

    lax.fori_loop(0, n, sent, 0)


def mlp_and_back(ob, w_out, x_own, gain, weights, lanes, w_down, seed, seed_own):
    n = lax.axis_size("blk")
    _, rows, columns = seed.shape
    head_lanes = ob.shape[2]
    quarter = columns // (4 * n)
    f32, bf16 = jnp.float32, jnp.bfloat16
    vmem, dma = pltpu.VMEM, pltpu.SemaphoreType.DMA
    in_vmem, anywhere = pl.BlockSpec(memory_space=vmem), pl.BlockSpec(memory_space=pl.ANY)
    ring = [dma((n - 1, 2, 2))] * 6 + [dma((n // 2, 2, 2))] * 4
    return pl.pallas_call(
        functools.partial(mlp_kernel, n, lanes),
        out_shape=(
            jax.ShapeDtypeStruct((rows, columns), bf16),
            jax.ShapeDtypeStruct((rows, columns), f32),
            jax.ShapeDtypeStruct((n, rows, head_lanes), bf16),
            jax.ShapeDtypeStruct((1, columns), f32),
            jax.ShapeDtypeStruct((n, quarter, 2 * lanes), bf16),
            jax.ShapeDtypeStruct((lanes // 4, columns), bf16),
            jax.ShapeDtypeStruct((head_lanes, columns), bf16),
        ),
        in_specs=[in_vmem] * 4 + [anywhere] * 4,
        out_specs=[in_vmem] * 7,
        scratch_shapes=[
            vmem((n, rows, columns), bf16),
            vmem((n, rows, columns), bf16),
            vmem((n, rows, columns), bf16),
            vmem((columns, 2 * lanes), bf16),
            vmem((lanes, columns), bf16),
            vmem((n, rows, lanes), bf16),
            vmem((n, rows, 2 * lanes), bf16),
            vmem((2, n, rows, columns // 2), bf16),
            vmem((2, n, rows, columns // 2), bf16),
            vmem((2, rows, columns // 2), f32),
            vmem((rows, columns), f32),
            vmem((n, 2, 2, quarter, 2 * lanes), bf16),
            vmem((n, 2, quarter, 2 * lanes), bf16),
            vmem((lanes, columns), bf16),
            vmem((lanes // 2, columns), bf16),
            dma((4,)),
        ]
        + ring
        + [dma((n,))] * 4
        + [dma((2,))] * 2,
        compiler_params=kernel_params(5),
        name="mlp_and_back",
    )(ob, w_out, x_own, gain, weights, w_down, seed, seed_own)


class Spread:
    def __init__(self, n, pieces, out, sems):
        self.n, self.pieces, self.out = n, pieces, out
        self.s_blk, self.r_blk, self.s_x, self.r_x, self.s_c, self.r_c = sems
        self.grp, self.me = lax.axis_index("grp"), lax.axis_index("blk")
        self.over, self.core, self.grp_x, self.grp_c = team(self.grp)

    def first(self, k):
        to = (self.me + k) % self.n
        place = self.out.at[self.me, 2 * self.core + self.over]
        return push(
            self.pieces.at[to], place, self.s_blk.at[k], self.r_blk.at[k], (self.grp, to)
        )

    def own(self, sem):
        place = self.out.at[self.me, 2 * self.core + self.over]
        return pltpu.make_async_copy(self.pieces.at[self.me], place, sem)

    def to_x(self, k):
        piece = self.out.at[(self.me - k + self.n) % self.n, 2 * self.core + self.over]
        return push(piece, piece, self.s_x.at[k], self.r_x.at[k], (self.grp_x, self.me))

    def to_core(self, k, far):
        over = 1 - self.over if far else self.over
        piece = self.out.at[(self.me - k + self.n) % self.n, 2 * self.core + over]
        sems = (self.s_c.at[int(far), k], self.r_c.at[int(far), k])
        return push(piece, piece, *sems, (self.grp_c, self.me))

    def pass_on(self, k):
        pl.when(k > 0)(self.first(k).wait_recv)
        self.to_x(k).start()
        self.to_core(k, False).start()

    def pass_far(self, k):
        self.to_x(k).wait_recv()
        self.to_core(k, True).start()

    def arrived(self, k):
        for far in (False, True):
            self.to_core(k, far).wait_recv()

    def finish(self):
        def body(k, _):
            pl.when(k > 0)(self.first(k).wait_send)
            self.to_x(k).wait_send()
            for far in (False, True):
                self.to_core(k, far).wait_send()
            return 0

        lax.fori_loop(0, self.n, body, 0)


def each(count, body, low=0):
    lax.fori_loop(low, count, lambda k, _: (body(k), 0)[1], 0)


def spread_sems(n):
    dma = pltpu.SemaphoreType.DMA
    return [dma((n,)), dma((n,)), dma((n,)), dma((n,)), dma((2, n)), dma((2, n))]


def team_and_ring(n):
    grp, me = lax.axis_index("grp"), lax.axis_index("blk")
    _, _, grp_x, grp_c = team(grp)
    return [(grp, (me + k) % n) for k in range(1, n)] + [(grp_x, me), (grp_c, me)]


def fill_row(row, gains_all, which, share):
    for block in range(gains_all.shape[0]):
        row[:, block * share : (block + 1) * share] = gains_all[block, which : which + 1, :]


def turned(value, cosine, sine_part):
    half_size = HEAD // 2
    swapped = jnp.concatenate([value[:, half_size:], value[:, :half_size]], axis=1)
    return value * cosine + swapped * sine_part


def attend_kernel(
    n,
    heads,
    x_own,
    cosine,
    sine_part,
    first_key,
    query_place,
    key_place,
    slab_qkv,
    slab_gate_up,
    gains,
    seed_own,
    gains_all,
    columns_qkv,
    normed,
    qkv,
    attended,
    attended_b,
    log_total,
    gate_up,
    seed,
    x_all,
    gain_row,
    local,
    s_gain,
    r_gain,
    s_x,
    r_x,
    s_seed,
    r_seed,
    *spread_all,
):
    f32, bf16 = jnp.float32, jnp.bfloat16
    grp, me = lax.axis_index("grp"), lax.axis_index("blk")
    _, ends = ring_ends(n)
    rows, columns = x_own.shape
    spread_qkv = Spread(n, slab_qkv, columns_qkv, spread_all[:6])
    spread_gu = Spread(n, slab_gate_up, gate_up, spread_all[6:])
    near_gain = pltpu.make_async_copy(gains, gains_all.at[me], local.at[0])
    near_gain.start()
    near_qkv = spread_qkv.own(local.at[1])
    near_qkv.start()
    x_all[0] = x_own[...]
    greet(team_and_ring(n))

    def gain(k):
        return push(gains, gains_all.at[me], s_gain.at[k], r_gain.at[k], (grp, (me + k) % n))

    each(n, lambda k: gain(k).start(), 1)
    x_ring = Gather(n, x_all, s_x, r_x, ends)
    x_ring.start()
    each(n, lambda k: spread_qkv.first(k).start(), 1)
    near_gu = spread_gu.own(local.at[2])
    near_gu.start()

    def norm(slot):
        value = x_all[slot].astype(f32)
        inv = lax.rsqrt(jnp.mean(value * value, axis=-1, keepdims=True) + EPS)
        normed[slot] = (value * inv * gain_row[...]).astype(bf16)

    near_gain.wait()
    each(n, lambda k: gain(k).wait_recv(), 1)
    fill_row(gain_row, gains_all, 0, columns // n)

    def arrive(t):
        pl.when(t > 0)(lambda: x_ring.advance(t - 1))
        low = jnp.maximum(2 * t - 1, 0)
        each(jnp.minimum(2 * t + 1, n), norm, low)
        pl.when(t == 1)(near_qkv.wait)
        pl.when(t == 2)(lambda: each(n, spread_qkv.pass_on))
        pl.when(t == 3)(lambda: each(n, spread_qkv.pass_far))

    each(n // 2 + 1, arrive)
    seed_ring = Gather(n, seed, s_seed, r_seed, ends, seed_own)
    seed_ring.start()
    each(n, lambda k: spread_gu.first(k).start(), 1)
    each(n, spread_qkv.arrived)

    head_lanes = heads * HEAD
    pair = 2 * rows

    def project(i):
        both = normed[pl.ds(2 * i, 2)].reshape(pair, columns)
        result = dot_f32(both, columns_qkv[...].reshape(columns, 3 * head_lanes))
        at = pl.ds(pl.multiple_of(i * pair, pair), pair)
        table_c, table_s = cosine[at, :], sine_part[at, :]
        for piece in range(3 * heads):
            lane = slice(piece * HEAD, (piece + 1) * HEAD)
            value = result[:, lane]
            if piece < 2 * heads:
                value = turned(value, table_c, table_s)
            qkv[at, lane] = value.astype(bf16)

    each(n // 2, project)
    near_gu.wait()

    def tile(i):
        for head in range(heads):
            lane = slice(head * HEAD, (head + 1) * HEAD)
            at = pl.ds(pl.multiple_of(i * pair, pair), pair)
            keys = qkv[:, head_lanes + head * HEAD : head_lanes + (head + 1) * HEAD]
            values = qkv[:, 2 * head_lanes + head * HEAD : 2 * head_lanes + (head + 1) * HEAD]
            scores = nt_dot(qkv[at, lane], keys) * HEAD ** (-0.5)
            allowed = (key_place[...] >= first_key[at, :]) & (key_place[...] <= query_place[at, :])
            scores = jnp.where(allowed, scores, NEGATIVE)
            peak = jnp.max(scores, axis=-1, keepdims=True)
            raw = jnp.exp(scores - peak)
            total = jnp.sum(raw, axis=-1, keepdims=True)
            out = dot_f32(raw.astype(bf16), values) / total
            attended[at, lane] = out
            attended_b[at, lane] = out.astype(bf16)
            log_total[head, at, :] = peak + jnp.log(total)
        seed_ring.advance(i)
        each(2 * i + 2, spread_gu.pass_on, 2 * i)

    each(n // 2, tile)
    each(n, spread_gu.pass_far)
    each(n, spread_gu.arrived)
    near_qkv_sent = [spread_qkv, spread_gu]
    for spread in near_qkv_sent:
        spread.finish()
    each(n, lambda k: gain(k).wait_send(), 1)
    x_ring.finish()
    seed_ring.finish()


def attend(slab_qkv, slab_gate_up, gains, x_own, seed_own, cosine, sine_part, first_key, places):
    n = lax.axis_size("blk")
    rows, columns = x_own.shape
    seq = n * rows
    lanes = slab_qkv.shape[2]
    head_lanes = lanes // 3
    heads = head_lanes // HEAD
    f32, bf16 = jnp.float32, jnp.bfloat16
    vmem, dma = pltpu.VMEM, pltpu.SemaphoreType.DMA
    in_vmem, anywhere = pl.BlockSpec(memory_space=vmem), pl.BlockSpec(memory_space=pl.ANY)
    return pl.pallas_call(
        functools.partial(attend_kernel, n, heads),
        out_shape=(
            jax.ShapeDtypeStruct((n,) + gains.shape, f32),
            jax.ShapeDtypeStruct((n, 4) + slab_qkv.shape[1:], bf16),
            jax.ShapeDtypeStruct((n, rows, columns), bf16),
            jax.ShapeDtypeStruct((seq, lanes), bf16),
            jax.ShapeDtypeStruct((seq, head_lanes), f32),
            jax.ShapeDtypeStruct((seq, head_lanes), bf16),
            jax.ShapeDtypeStruct((heads, seq, 1), f32),
            jax.ShapeDtypeStruct((n, 4) + slab_gate_up.shape[1:], bf16),
            jax.ShapeDtypeStruct((n, rows, columns), bf16),
        ),
        in_specs=[in_vmem] * 6 + [anywhere] * 4,
        out_specs=[in_vmem] * 7 + [anywhere] * 2,
        scratch_shapes=[
            vmem((n, rows, columns), bf16),
            vmem((1, columns), f32),
            dma((3,)),
            dma((n,)),
            dma((n,)),
        ]
        + [dma((n // 2, 2, 2))] * 4
        + spread_sems(n) * 2,
        compiler_params=kernel_params(0),
        name="attend",
    )(
        x_own,
        cosine,
        sine_part,
        first_key,
        places.reshape(seq, 1),
        places.reshape(1, seq),
        slab_qkv,
        slab_gate_up,
        gains,
        seed_own,
    )


def finish_kernel(
    n,
    heads,
    qkv,
    attended,
    dattended,
    log_total,
    cosine,
    sine_part,
    first_key,
    query_place,
    key_place,
    x_own,
    gain,
    dresid,
    terms_two,
    out_grad,
    weights,
    normed_hbm,
    gate_up_sum,
    down_sum,
    x_grad,
    gain_grads,
    wide_gate_up,
    wide_qkv,
    tall_down,
    tall_out,
    normed,
    columns_qkv,
    dqkv,
    dkeys,
    dvalues,
    held,
    terms,
    wide,
    wide_c,
    wide_x,
    out_c,
    out_x,
    gain_slabs,
    gain_heard,
    gain_team,
    load_sem,
    s_ring,
    r_ring,
    s_wc,
    r_wc,
    s_wx,
    r_wx,
    s_tall,
    r_tall,
    s_gain,
    r_gain,
    *spread_all,
):
    f32, bf16 = jnp.float32, jnp.bfloat16
    grp, me = lax.axis_index("grp"), lax.axis_index("blk")
    over, core, grp_x, grp_c = team(grp)
    _, ends = ring_ends(n)
    rows, columns = x_own.shape
    half = columns // 2
    lanes = wide.shape[4]
    quarter = wide.shape[3]
    load_normed = pltpu.make_async_copy(normed_hbm, normed, load_sem.at[0])
    load_qkv = pltpu.make_async_copy(weights, columns_qkv, load_sem.at[1])
    load_normed.start()
    load_qkv.start()
    spread_gu = Spread(n, gate_up_sum, wide_gate_up, spread_all[:6])
    spread_qkv = Spread(n, wide_x, wide_qkv, spread_all[6:])
    near_gu = spread_gu.own(load_sem.at[2])
    near_gu.start()
    greet(team_and_ring(n))

    down_own = pltpu.make_async_copy(down_sum, tall_down.at[2 * core + over], load_sem.at[3])
    down_own.start()
    down_place = tall_down.at[2 * core + over]
    down_x = push(down_sum, down_place, s_tall.at[0], r_tall.at[0], (grp_x, me))
    down_c = push(down_sum, down_place, s_tall.at[1], r_tall.at[1], (grp_c, me))
    far_place = tall_down.at[2 * core + 1 - over]
    down_far = push(far_place, far_place, s_tall.at[2], r_tall.at[2], (grp_c, me))
    out_one = push(out_grad.at[1 - core], out_c, s_tall.at[3], r_tall.at[3], (grp_c, me))
    out_two = push(out_c.at[1 - over], out_x, s_tall.at[4], r_tall.at[4], (grp_x, me))
    out_place = tall_out.at[2 * core + over]
    out_own = pltpu.make_async_copy(out_x, out_place, load_sem.at[4])
    out_to_x = push(out_x, out_place, s_tall.at[5], r_tall.at[5], (grp_x, me))
    out_to_c = push(out_x, out_place, s_tall.at[6], r_tall.at[6], (grp_c, me))
    out_far_place = tall_out.at[2 * core + 1 - over]
    out_far = push(out_far_place, out_far_place, s_tall.at[7], r_tall.at[7], (grp_c, me))
    out_one.start()
    each(n, lambda k: spread_gu.first(k).start(), 1)
    down_x.start()
    down_c.start()

    pair = 2 * rows
    head_lanes = heads * HEAD
    scale = HEAD ** (-0.5)

    def unturned(value, at):
        return turned(value, cosine[at, :], -sine_part[at, :]).astype(bf16)

    def tile(i, head):
        at = pl.ds(pl.multiple_of(i * pair, pair), pair)
        lane = slice(head * HEAD, (head + 1) * HEAD)
        query = qkv[at, lane]
        keys = qkv[:, head_lanes + head * HEAD : head_lanes + (head + 1) * HEAD]
        values = qkv[:, 2 * head_lanes + head * HEAD : 2 * head_lanes + (head + 1) * HEAD]
        grad = dattended[at, lane]
        delta = jnp.sum(grad.astype(f32) * attended[at, lane], axis=-1, keepdims=True)
        scores = nt_dot(query, keys) * scale
        allowed = (key_place[...] >= first_key[at, :]) & (key_place[...] <= query_place[at, :])
        probs = jnp.where(allowed, jnp.exp(scores - log_total[head, at, :]), 0.0)
        dscores = (probs * (nt_dot(grad, values) - delta)).astype(bf16)
        dqkv[2 * i : 2 * i + 2, :, lane] = unturned(dot_f32(dscores, keys) * scale, at).reshape(
            2, rows, HEAD
        )
        more_keys = dot_t(dscores, query)
        more_values = dot_t(probs.astype(bf16), grad)
        if i == 0:
            dkeys[...] = more_keys
            dvalues[...] = more_values
        else:
            dkeys[...] += more_keys
            dvalues[...] += more_values

    for head in range(heads):
        for i in range(n // 2):
            tile(i, head)
        everything = slice(0, n * rows)
        lane = slice(head_lanes + head * HEAD, head_lanes + (head + 1) * HEAD)
        dqkv[:, :, lane] = unturned(dkeys[...] * scale, everything).reshape(n, rows, HEAD)
        lane = slice(2 * head_lanes + head * HEAD, 2 * head_lanes + (head + 1) * HEAD)
        dqkv[:, :, lane] = dvalues[...].astype(bf16).reshape(n, rows, HEAD)
    load_qkv.wait()

    def term(step, way):
        return nt_dot(dqkv[behind(step, way, n)], columns_qkv[way * half : (way + 1) * half, :])

    ring = Scatter(n, held, terms, s_ring, r_ring, ends, term)

    def copy_c(k):
        tile = (me + k) % n
        return push(wide.at[tile, 1 - core], wide_c.at[tile], s_wc.at[k], r_wc.at[k], (grp_c, me))

    def copy_x(k):
        tile = (me + k) % n
        return push(
            wide_c.at[tile, 1 - over], wide_x.at[tile], s_wx.at[k], r_wx.at[k], (grp_x, me)
        )

    def grad(k):
        tile = (me + k) % n
        at = pl.multiple_of(tile * 4 * quarter, 4 * quarter)
        left = normed[:, :, pl.ds(at, 4 * quarter)].reshape(-1, 4 * quarter)
        grad_rows = dot_t(left, dqkv[...].reshape(-1, lanes)).astype(bf16)
        wide[tile] = grad_rows.reshape(2, 2, quarter, lanes)
        copy_c(k).start()

    def pass_x(k):
        tile = (me + k) % n
        copy_c(k).wait_recv()
        wide_c[tile, 1 - over] = (
            wide[tile, core, 1 - over].astype(f32) + wide_c[tile, 1 - over].astype(f32)
        ).astype(bf16)
        copy_x(k).start()

    ring.step(0)
    out_one.wait_recv()
    out_c[1 - over] = (
        out_grad[core, 1 - over].astype(f32) + out_c[1 - over].astype(f32)
    ).astype(bf16)
    out_two.start()
    load_normed.wait()
    near_gu.wait()

    def turn(k):
        grad(k)
        pl.when(k > 0)(lambda: pass_x(k - 1))
        pl.when(k < n - 2)(lambda: ring.step(k + 1))
        spread_gu.pass_on(k)

    each(n, turn)
    pass_x(n - 1)

    x_float = x_own[...].astype(f32)
    inv = lax.rsqrt(jnp.mean(x_float * x_float, axis=-1, keepdims=True) + EPS)
    for way in range(2):
        terms[way] = ring.result(way)
    dnormed = jnp.concatenate([terms[0], terms[1]], axis=1)
    terms_one = jnp.sum(dnormed * x_float * inv, axis=0, keepdims=True)
    share = columns // n
    for block in range(n):
        gain_slabs[block] = jnp.zeros_like(gain_slabs[block])
        lane = slice(block * share, (block + 1) * share)
        gain_slabs[block, 0:1, :] = terms_one[:, lane]
        gain_slabs[block, 1:2, :] = terms_two[:, lane]

    def gain_blk(k):
        to = (me + k) % n
        return push(gain_slabs.at[to], gain_heard.at[k], s_gain.at[k], r_gain.at[k], (grp, to))

    each(n, lambda k: gain_blk(k).start(), 1)
    a_one = dnormed * gain[...]
    x_grad[...] = (
        dresid[...]
        + inv * a_one
        - x_float * inv**3 * jnp.mean(a_one * x_float, axis=-1, keepdims=True)
    ).astype(bf16)
    def take(k):
        tile = (me + k) % n
        copy_x(k).wait_recv()
        wide_x[tile] = (
            wide[tile, core, over].astype(f32)
            + wide_c[tile, over].astype(f32)
            + wide_x[tile].astype(f32)
        ).astype(bf16)

    def take_and_push(k):
        take(k)
        spread_qkv.first(k).start()

    each(n, take_and_push, 1)
    take(0)
    near_qkv = spread_qkv.own(load_sem.at[5])
    near_qkv.start()
    gain_heard[0] = gain_slabs[me]
    each(n, lambda k: gain_blk(k).wait_recv(), 1)
    gain_team[0] = jnp.sum(gain_heard[...], axis=0)
    gain_c = push(gain_team.at[0], gain_team.at[1], s_gain.at[n], r_gain.at[n], (grp_c, me))
    gain_c.start()
    out_two.wait_recv()
    out_x[...] = (
        out_grad[core, over].astype(f32) + out_c[over].astype(f32) + out_x[...].astype(f32)
    ).astype(bf16)
    out_own.start()
    out_to_x.start()
    out_to_c.start()
    each(n, spread_gu.pass_far)
    down_x.wait_recv()
    down_far.start()
    gain_c.wait_recv()
    gain_team[2] = gain_team[0] + gain_team[1]
    gain_x = push(
        gain_team.at[2], gain_team.at[3], s_gain.at[n + 1], r_gain.at[n + 1], (grp_x, me)
    )
    gain_x.start()
    near_qkv.wait()
    each(n, spread_qkv.pass_on)
    out_to_x.wait_recv()
    out_far.start()
    each(n, spread_qkv.pass_far)
    gain_x.wait_recv()
    gain_grads[...] = gain_team[2] + gain_team[3]
    each(n, spread_gu.arrived)
    each(n, spread_qkv.arrived)
    spread_gu.finish()
    spread_qkv.finish()
    ring.finish()
    down_own.wait()
    out_own.wait()
    for copy in (down_c, down_far, out_to_c, out_far):
        copy.wait()
    for copy in (down_x, out_one, out_two, out_to_x, gain_c, gain_x):
        copy.wait_send()

    def sent(k):
        copy_c(k).wait_send()
        copy_x(k).wait_send()
        pl.when(k > 0)(gain_blk(k).wait_send)

    each(n, sent)


def finish(
    attention, x_own, gain, dresid, terms_two, out_grad, weights, normed, gate_up_sum, down_sum
):
    n, rows, columns = normed.shape
    seq, lanes = attention[0].shape
    heads = lanes // (3 * HEAD)
    quarter = columns // (4 * n)
    share = columns // n
    f32, bf16 = jnp.float32, jnp.bfloat16
    vmem, dma = pltpu.VMEM, pltpu.SemaphoreType.DMA
    in_vmem, anywhere = pl.BlockSpec(memory_space=vmem), pl.BlockSpec(memory_space=pl.ANY)
    out_rows = out_grad.shape[0] // 4
    return pl.pallas_call(
        functools.partial(finish_kernel, n, heads),
        out_shape=(
            jax.ShapeDtypeStruct((rows, columns), bf16),
            jax.ShapeDtypeStruct((8, share), f32),
            jax.ShapeDtypeStruct((n, 4) + gate_up_sum.shape[1:], bf16),
            jax.ShapeDtypeStruct((n, 4, quarter, lanes), bf16),
            jax.ShapeDtypeStruct((4,) + down_sum.shape, bf16),
            jax.ShapeDtypeStruct((4, out_rows, columns), bf16),
        ),
        in_specs=[in_vmem] * 14 + [anywhere] * 4,
        out_specs=[in_vmem] * 2 + [anywhere] * 4,
        scratch_shapes=[
            vmem((n, rows, columns), bf16),
            vmem((columns, lanes), bf16),
            vmem((n, rows, lanes), bf16),
            vmem((seq, HEAD), f32),
            vmem((seq, HEAD), f32),
            vmem((2, n, rows, columns // 2), bf16),
            vmem((2, rows, columns // 2), f32),
            vmem((n, 2, 2, quarter, lanes), bf16),
            vmem((n, 2, quarter, lanes), bf16),
            vmem((n, quarter, lanes), bf16),
            vmem((2, out_rows, columns), bf16),
            vmem((out_rows, columns), bf16),
            vmem((n, 8, share), f32),
            vmem((n, 8, share), f32),
            vmem((4, 8, share), f32),
            dma((6,)),
        ]
        + [dma((n - 1, 2, 2))] * 2
        + [dma((n,))] * 4
        + [dma((8,))] * 2
        + [dma((n + 2,))] * 2
        + spread_sems(n) * 2,
        compiler_params=kernel_params(6),
        name="finish",
    )(
        *attention,
        x_own,
        gain,
        dresid,
        terms_two,
        out_grad.reshape(2, 2, out_rows, columns),
        weights,
        normed,
        gate_up_sum,
        down_sum,
    )


def assemble_kernel(n, units, lanes, head_lanes, qkv, gate_up, down, out, *grads):
    grad_qkv, grad_out, grad_gate, grad_up, grad_down = grads
    f32 = jnp.float32
    for source in range(n):
        for part in range(3):
            first = (part * n + source) * head_lanes
            grad_qkv[:, first : first + head_lanes] = qkv[
                source, :, part * head_lanes : (part + 1) * head_lanes
            ].astype(f32)
        first = source * units
        grad_gate[:, first : first + units] = gate_up[source, :, :units].astype(f32)
        grad_up[:, first : first + units] = gate_up[source, :, lanes : lanes + units].astype(f32)
    grad_out[...] = out[...].astype(f32)
    grad_down[...] = down[...].astype(f32)


def assemble(qkv, gate_up, down, out, units, steps=4):
    n, rows, qkv_lanes = qkv.shape
    columns = down.shape[1]
    lanes = gate_up.shape[2] // 2
    head_lanes = qkv_lanes // 3
    step = rows // steps
    down_step = units // steps
    f32 = jnp.float32

    def wide(width):
        return pl.BlockSpec((n, step, width), lambda i: (0, i, 0))

    def flat(height, width):
        return pl.BlockSpec((height, width), lambda i: (i, 0))

    return pl.pallas_call(
        functools.partial(assemble_kernel, n, units, lanes, head_lanes),
        grid=(steps,),
        out_shape=(
            jax.ShapeDtypeStruct((rows, n * qkv_lanes), f32),
            jax.ShapeDtypeStruct((rows, columns), f32),
            jax.ShapeDtypeStruct((rows, n * units), f32),
            jax.ShapeDtypeStruct((rows, n * units), f32),
            jax.ShapeDtypeStruct((units, columns), f32),
        ),
        in_specs=[
            wide(qkv_lanes),
            wide(2 * lanes),
            flat(down_step, columns),
            flat(out.shape[0] // steps, columns),
        ],
        out_specs=[
            flat(step, n * qkv_lanes),
            flat(step, columns),
            flat(step, n * units),
            flat(step, n * units),
            flat(down_step, columns),
        ],
        compiler_params=pltpu.CompilerParams(vmem_limit_bytes=VMEM_BYTES),
        name="assemble",
    )(qkv, gate_up, down, out)


def pad_to(array, axis, size):
    widths = [(0, 0)] * array.ndim
    widths[axis] = (0, size - array.shape[axis])
    return jnp.pad(array, widths)


def per_device(block_input, doc_lens, norm_attn, w_qkv, w_out, norm_mlp, w_gate, w_up, w_down, cot):
    n = lax.axis_size("blk")
    tok_rows, width = block_input.shape[1:]
    seq = tok_rows * n
    heads = HEADS // n
    head_lanes = heads * HEAD
    qkv_lanes = 3 * head_lanes
    units = w_down.shape[0]
    lanes = -(-units // 128) * 128
    bf16 = jnp.bfloat16

    over, core, _, _ = team(lax.axis_index("grp"))
    quarter = w_qkv.shape[0] // 4
    first_row = (2 * core + over) * quarter

    def quarter_of(weight):
        return lax.dynamic_slice_in_dim(weight, first_row, quarter, 0)

    slab_qkv = (
        quarter_of(w_qkv)
        .reshape(quarter, 3, n, head_lanes)
        .transpose(2, 0, 1, 3)
        .reshape(n, quarter, qkv_lanes)
    )
    slab_gate_up = jnp.concatenate(
        [
            pad_to(quarter_of(w).reshape(quarter, n, units).transpose(1, 0, 2), 2, lanes)
            for w in (w_gate, w_up)
        ],
        axis=2,
    )
    gains = pad_to(jnp.stack([norm_attn, norm_mlp]).astype(jnp.float32), 0, 8)
    place = ring_place(lax.axis_index("blk"), n)
    offsets = [0] + [k * sign for k in range(1, n // 2) for sign in (-1, 1)] + [n // 2]
    blocks = jnp.stack([at_offset(place, offset, n) for offset in offsets])
    places = (blocks[:, None] * tok_rows + jnp.arange(tok_rows, dtype=jnp.int32)).reshape(seq)
    lengths = doc_lens[0]
    starts = jnp.cumsum(lengths) - lengths
    first_key = start_of(places, starts)
    half_cosine, half_sine = angle_tables(places - first_key)
    first_key = first_key.reshape(seq, 1)
    half_cosine, half_sine = half_cosine[:, 0], half_sine[:, 0]
    cosine = jnp.concatenate([half_cosine, half_cosine], axis=1)
    sine_part = jnp.concatenate([-half_sine, half_sine], axis=1)
    gains_all, qkv_columns, normed_one, qkv, attended, attended_b, log_total, gate_up, seed = attend(
        slab_qkv,
        slab_gate_up,
        gains,
        block_input[0],
        cot[0],
        cosine,
        sine_part,
        first_key,
        places,
    )
    gain_one = gains_all[:, 0].reshape(1, width)
    gain_two = gains_all[:, 1].reshape(1, width)
    qkv_columns = qkv_columns.reshape(width, qkv_lanes)
    gate_up = gate_up.reshape(width, 2 * lanes)
    block_out, dresid, dattended, terms_two, gate_up_sum, down_sum, out_grad = mlp_and_back(
        attended_b.reshape(n, tok_rows, head_lanes),
        w_out,
        block_input[0],
        gain_two,
        gate_up,
        lanes,
        w_down,
        seed,
        cot[0],
    )
    x_grad, gain_grads, wide_gate_up, wide_qkv, tall_down, tall_out = finish(
        (
            qkv,
            attended,
            dattended.reshape(seq, head_lanes),
            log_total,
            cosine,
            sine_part,
            first_key,
            places.reshape(seq, 1),
            places.reshape(1, seq),
        ),
        block_input[0],
        gain_one,
        dresid,
        terms_two,
        out_grad,
        qkv_columns,
        normed_one,
        gate_up_sum,
        down_sum,
    )
    shard_rows = 4 * quarter
    grad_qkv, grad_out, grad_gate, grad_up, grad_down = assemble(
        wide_qkv.reshape(n, shard_rows, qkv_lanes),
        wide_gate_up.reshape(n, shard_rows, 2 * lanes),
        tall_down.reshape(lanes, width),
        tall_out.reshape(head_lanes, width),
        units,
    )
    return (
        block_out[None],
        x_grad[None],
        gain_grads[0],
        grad_qkv,
        grad_out,
        gain_grads[1],
        grad_gate,
        grad_up,
        grad_down,
    )


def body_for(mesh):
    return per_device if HEADS % mesh.shape["blk"] == 0 else per_device_gather


def solution(mesh):
    return jax.shard_map(
        body_for(mesh),
        mesh=mesh,
        in_specs=(
            P("grp", "blk", None),
            P("grp", None),
            P("blk"),
            P("blk", None),
            P("blk", None),
            P("blk"),
            P("blk", None),
            P("blk", None),
            P("blk", None),
            P("grp", "blk", None),
        ),
        out_specs=(
            P("grp", "blk", None),
            P("grp", "blk", None),
            P("blk"),
            P("blk", None),
            P("blk", None),
            P("blk"),
            P("blk", None),
            P("blk", None),
            P("blk", None),
        ),
        check_vma=False,
    )
```

```python
import functools
import math

import jax
import jax.numpy as jnp
from jax import lax
from jax.experimental import pallas as pl
from jax.experimental.pallas import tpu as pltpu
from jax.sharding import PartitionSpec as P

HEADS = 16
HEAD = 128


EPS = 1e-05
NEGATIVE = -1e30


def angle_tables(places):
    half_size = HEAD // 2
    freqs = jnp.exp(jnp.arange(half_size, dtype=jnp.float32) * (-2.0 * math.log(10000.0) / HEAD))
    angles = places.astype(jnp.float32)[:, None] * freqs
    return (jnp.cos(angles)[:, None, :], jnp.sin(angles)[:, None, :])


def rotate(tensor, cosine, sine_part):
    half_size = HEAD // 2
    first_half = tensor[..., :half_size]
    second_half = tensor[..., half_size:]
    return jnp.concatenate(
        [
            first_half * cosine - second_half * sine_part,
            second_half * cosine + first_half * sine_part,
        ],
        axis=-1,
    )


def unrotate(tensor, cosine, sine_part):
    half_size = HEAD // 2
    first_half = tensor[..., :half_size]
    second_half = tensor[..., half_size:]
    return jnp.concatenate(
        [
            first_half * cosine + second_half * sine_part,
            second_half * cosine - first_half * sine_part,
        ],
        axis=-1,
    )


def segment_of(places, starts):
    return jnp.sum((starts[None, :] <= places[:, None]).astype(jnp.int32), axis=1) - 1


def start_of(places, starts):
    return jnp.max(jnp.where(starts[None, :] <= places[:, None], starts[None, :], 0), axis=1)


def contract_rows(left, right):
    return lax.dot_general(
        left, right, (((1,), (1,)), ((), ())), preferred_element_type=jnp.float32
    )


def weight_term(left, right):

    def term(start, count):
        return lax.dot_general(
            left, right, (((0,), (0,)), ((), ())), preferred_element_type=jnp.float32
        )

    return term


def shard_grad(term_fn, shard_rows):
    shared = lax.psum_scatter(
        term_fn(jnp.int32(0), shard_rows * lax.axis_size("blk")).astype(jnp.bfloat16),
        "blk",
        scatter_dimension=0,
        tiled=True,
    )
    return lax.psum(shared, "grp").astype(jnp.float32)


def per_device_gather(block_input, doc_lens, norm_attn, w_qkv, w_out, norm_mlp, w_gate, w_up, w_down, cot):
    tok_rows = block_input.shape[1]
    width = block_input.shape[2]
    score_scale = HEAD ** (-0.5)
    shards = (norm_attn, w_qkv, w_out, norm_mlp, w_gate, w_up, w_down)
    gathered = (
        lax.all_gather(shards[0], "blk", axis=0, tiled=True),
        lax.all_gather(shards[1], "blk", axis=0, tiled=True),
        lax.all_gather(shards[2], "blk", axis=0, tiled=True),
        lax.all_gather(shards[3], "blk", axis=0, tiled=True),
        lax.all_gather(shards[4], "blk", axis=0, tiled=True),
        lax.all_gather(shards[5], "blk", axis=0, tiled=True),
        lax.all_gather(shards[6], "blk", axis=0, tiled=True),
    )
    gain_one, weight_qkv, weight_out, gain_two, weight_gate, weight_up, weight_down = gathered
    place_rows = lax.axis_index("blk") * tok_rows + jnp.arange(tok_rows, dtype=jnp.int32)
    lengths = doc_lens[0]
    starts = jnp.cumsum(lengths) - lengths
    query_seg = segment_of(place_rows, starts)
    cosine, sine_part = angle_tables(place_rows - start_of(place_rows, starts))
    x_float = block_input[0].astype(jnp.float32)
    inv_one = lax.rsqrt(jnp.mean(x_float * x_float, axis=-1, keepdims=True) + EPS)
    normed_one = (x_float * inv_one * gain_one.astype(jnp.float32)).astype(jnp.bfloat16)
    projected = jnp.dot(normed_one, weight_qkv, preferred_element_type=jnp.float32)
    heads_all = projected.reshape(tok_rows, 3, HEADS, HEAD)
    queries = rotate(heads_all[:, 0], cosine, sine_part).astype(jnp.bfloat16)
    keys_own = rotate(heads_all[:, 1], cosine, sine_part).astype(jnp.bfloat16)
    values_own = heads_all[:, 2].astype(jnp.bfloat16)

    def pair_mask(count):
        key_places = jnp.arange(count, dtype=jnp.int32)
        key_seg = segment_of(key_places, starts)
        return (query_seg[:, None] == key_seg[None, :]) & (
            key_places[None, :] <= place_rows[:, None]
        )

    piece = (
        lax.all_gather(keys_own, "blk", axis=0, tiled=True),
        lax.all_gather(values_own, "blk", axis=0, tiled=True),
    )
    count = piece[0].shape[0]
    row_peak = jnp.full((HEADS, tok_rows), NEGATIVE, jnp.float32)
    key_piece, value_piece = piece
    count = key_piece.shape[0]
    allowed = pair_mask(count)[None]
    scores = (
        jnp.einsum("qhd,khd->hqk", queries, key_piece, preferred_element_type=jnp.float32)
        * score_scale
    )
    scores = jnp.where(allowed, scores, NEGATIVE)
    new_peak = jnp.maximum(row_peak, jnp.max(scores, axis=-1))
    weights_now = jnp.where(allowed, jnp.exp(scores - new_peak[..., None]), 0.0)
    row_total = jnp.sum(weights_now, axis=-1)
    accum = jnp.einsum(
        "hqk,khd->hqd",
        weights_now.astype(jnp.bfloat16),
        value_piece,
        preferred_element_type=jnp.float32,
    )
    row_peak, row_total, accum = (new_peak, row_total, accum)
    log_total = row_peak + jnp.log(row_total)
    attended = (accum / row_total[..., None]).transpose(1, 0, 2)
    attended_b = attended.reshape(tok_rows, width).astype(jnp.bfloat16)
    resid = x_float + jnp.dot(attended_b, weight_out, preferred_element_type=jnp.float32)
    inv_two = lax.rsqrt(jnp.mean(resid * resid, axis=-1, keepdims=True) + EPS)
    normed_two = (resid * inv_two * gain_two.astype(jnp.float32)).astype(jnp.bfloat16)
    gate_proj = jnp.dot(normed_two, weight_gate, preferred_element_type=jnp.float32)
    up_proj = jnp.dot(normed_two, weight_up, preferred_element_type=jnp.float32)
    sigmoid_gate = jax.nn.sigmoid(gate_proj)
    swish = gate_proj * sigmoid_gate
    hidden = (swish * up_proj).astype(jnp.bfloat16)
    block_out = (resid + jnp.dot(hidden, weight_down, preferred_element_type=jnp.float32)).astype(
        jnp.bfloat16
    )
    again = (
        lax.all_gather(shards[0], "blk", axis=0, tiled=True),
        lax.all_gather(shards[1], "blk", axis=0, tiled=True),
        lax.all_gather(shards[2], "blk", axis=0, tiled=True),
        lax.all_gather(shards[3], "blk", axis=0, tiled=True),
        lax.all_gather(shards[4], "blk", axis=0, tiled=True),
        lax.all_gather(shards[5], "blk", axis=0, tiled=True),
        lax.all_gather(shards[6], "blk", axis=0, tiled=True),
    )
    back_gain_one, back_qkv, back_out, back_gain_two, back_gate, back_up, back_down = again
    seed = cot[0]
    seed_float = seed.astype(jnp.float32)
    dhidden = contract_rows(seed, back_down)
    dgate = (dhidden * up_proj * sigmoid_gate * (1.0 + gate_proj * (1.0 - sigmoid_gate))).astype(
        jnp.bfloat16
    )
    dup = (dhidden * swish).astype(jnp.bfloat16)
    dnormed_two = contract_rows(dgate, back_gate) + contract_rows(dup, back_up)
    a_two = dnormed_two * back_gain_two.astype(jnp.float32)
    dresid = (
        seed_float
        + inv_two * a_two
        - resid * inv_two**3 * jnp.mean(a_two * resid, axis=-1, keepdims=True)
    )
    dresid_b = dresid.astype(jnp.bfloat16)
    dattended = (
        contract_rows(dresid_b, back_out).astype(jnp.bfloat16).reshape(tok_rows, HEADS, HEAD)
    )
    delta = jnp.sum(dattended.astype(jnp.float32) * attended, axis=-1).T
    piece = (
        lax.all_gather(keys_own, "blk", axis=0, tiled=True),
        lax.all_gather(values_own, "blk", axis=0, tiled=True),
    )
    count = piece[0].shape[0]
    key_piece, value_piece = piece
    count = key_piece.shape[0]
    score_count = key_piece.shape[0]
    allowed = pair_mask(score_count)[None]
    scores = (
        jnp.einsum("qhd,khd->hqk", queries, key_piece, preferred_element_type=jnp.float32)
        * score_scale
    )
    probs = jnp.where(allowed, jnp.exp(scores - log_total[..., None]), 0.0)
    dprobs = jnp.einsum("qhd,khd->hqk", dattended, value_piece, preferred_element_type=jnp.float32)
    dscores = (probs * (dprobs - delta[..., None])).astype(jnp.bfloat16)
    probs, dscores = (probs, dscores)
    dquery_acc = score_scale * jnp.einsum(
        "hqk,khd->hqd", dscores, key_piece, preferred_element_type=jnp.float32
    )
    dkeys = score_scale * jnp.einsum(
        "hqk,qhd->khd", dscores, queries, preferred_element_type=jnp.float32
    )
    dvalues = jnp.einsum(
        "hqk,qhd->khd", probs.astype(jnp.bfloat16), dattended, preferred_element_type=jnp.float32
    )
    stacked = jnp.concatenate([dkeys.reshape(count, width), dvalues.reshape(count, width)], axis=1)
    grads_buffer = stacked
    dquery_acc, grads_buffer = (dquery_acc, grads_buffer)
    own_grads = lax.psum_scatter(
        grads_buffer.astype(jnp.bfloat16), "blk", scatter_dimension=0, tiled=True
    ).astype(jnp.float32)
    dkey = unrotate(own_grads[:, :width].reshape(tok_rows, HEADS, HEAD), cosine, sine_part)
    dvalue = own_grads[:, width:].reshape(tok_rows, HEADS, HEAD)
    dquery = unrotate(dquery_acc.transpose(1, 0, 2), cosine, sine_part)
    dqkv = (
        jnp.stack([dquery, dkey, dvalue], axis=1).reshape(tok_rows, 3 * width).astype(jnp.bfloat16)
    )
    dnormed_one = contract_rows(dqkv, back_qkv)
    a_one = dnormed_one * back_gain_one.astype(jnp.float32)
    x_grad = (
        dresid
        + inv_one * a_one
        - x_float * inv_one**3 * jnp.mean(a_one * x_float, axis=-1, keepdims=True)
    ).astype(jnp.bfloat16)
    width_rows = norm_attn.shape[0]
    gain_terms = jnp.stack(
        [
            jnp.sum(dnormed_one * x_float * inv_one, axis=0),
            jnp.sum(dnormed_two * resid * inv_two, axis=0),
        ],
        axis=1,
    )

    def gain_slice(start, count):
        return gain_terms

    grad_down = shard_grad(weight_term(hidden, seed), w_down.shape[0])
    grad_gate = shard_grad(weight_term(normed_two, dgate), width_rows)
    grad_up = shard_grad(weight_term(normed_two, dup), width_rows)
    grad_out = shard_grad(weight_term(attended_b, dresid_b), width_rows)
    grad_qkv = shard_grad(weight_term(normed_one, dqkv), width_rows)
    gain_grads = shard_grad(gain_slice, width_rows)
    return (
        block_out[None],
        x_grad[None],
        gain_grads[:, 0],
        grad_qkv,
        grad_out,
        gain_grads[:, 1],
        grad_gate,
        grad_up,
        grad_down,
    )


MESH = pl.DeviceIdType.MESH
VMEM_BYTES = 60 * 2**20


def ring_place(block, n):
    up, row = block // 2, block % 2
    return (1 - row) * up + row * (n - 1 - up)


def ring_block(place, n):
    back = place // (n // 2)
    return (1 - back) * 2 * place + back * (2 * (n - 1 - place) + 1)


def at_offset(place, offset, n):
    return ring_block((place + offset + n) % n, n)


def greet(devices):
    barrier = pltpu.get_barrier_semaphore()
    for device in devices:
        pl.semaphore_signal(barrier, inc=1, device_id=device, device_id_type=MESH)
    pl.semaphore_wait(barrier, len(devices))


def push(src, dst, send_sem, recv_sem, device):
    return pltpu.make_async_remote_copy(
        src_ref=src,
        dst_ref=dst,
        send_sem=send_sem,
        recv_sem=recv_sem,
        device_id=device,
        device_id_type=MESH,
    )


def kernel_params(collective_id):
    return pltpu.CompilerParams(
        collective_id=collective_id, has_side_effects=True, vmem_limit_bytes=VMEM_BYTES
    )


def dot_f32(left, right):
    return jnp.dot(left, right, preferred_element_type=jnp.float32)


def dot_t(left, right):
    return lax.dot_general(
        left, right, (((0,), (0,)), ((), ())), preferred_element_type=jnp.float32
    )


def nt_dot(left, right):
    return lax.dot_general(
        left, right, (((1,), (1,)), ((), ())), preferred_element_type=jnp.float32
    )


def ring_ends(n):
    grp, me = lax.axis_index("grp"), lax.axis_index("blk")
    place = ring_place(me, n)
    return place, ((grp, at_offset(place, 1, n)), (grp, at_offset(place, -1, n)))


class Gather:
    def __init__(self, n, buf, send, recv, ends, own=None):
        self.n, self.buf, self.send, self.recv, self.ends = n, buf, send, recv, ends
        self.own = buf.at[0] if own is None else own
        self.half = buf.shape[1] // 2

    def copy(self, step, chunk, way):
        part = pl.ds(chunk * self.half, self.half)
        if isinstance(step, int):
            target = min(2 * step + 1 + way, self.n - 1)
        else:
            target = jnp.minimum(2 * step + 1 + way, self.n - 1)
        first = isinstance(step, int) and step == 0
        return push(
            self.own.at[part] if first else self.buf.at[2 * step - 1 + way, part],
            self.buf.at[target, part],
            self.send.at[step, chunk, way],
            self.recv.at[step, chunk, way],
            self.ends[way],
        )

    def landed(self, step, chunk, way):
        target = jnp.minimum(2 * step + 1 + way, self.n - 1)
        place = self.buf.at[target, pl.ds(chunk * self.half, self.half)]
        sems = (self.send.at[step, chunk, way], self.recv.at[step, chunk, way])
        return push(place, place, *sems, self.ends[way])

    def used(self, step, chunk, way):
        return step < self.n // 2 - 1 or chunk == way

    def start(self):
        for chunk in range(2):
            for way in range(2):
                self.copy(0, chunk, way).start()

    def advance(self, step):
        for chunk in range(2):
            for way in range(2):
                if isinstance(step, int):
                    if self.used(step, chunk, way):
                        self.copy(step, chunk, way).wait_recv()
                        if step + 1 < self.n // 2 and self.used(step + 1, chunk, way):
                            self.copy(step + 1, chunk, way).start()
                elif chunk == way:
                    self.landed(step, chunk, way).wait_recv()
                    pl.when(step + 1 < self.n // 2)(self.copy(step + 1, chunk, way).start)
                else:
                    pl.when(step < self.n // 2 - 1)(self.landed(step, chunk, way).wait_recv)
                    pl.when(step + 1 < self.n // 2 - 1)(self.copy(step + 1, chunk, way).start)

    def finish(self):
        for step in range(self.n // 2):
            for chunk in range(2):
                for way in range(2):
                    if self.used(step, chunk, way):
                        self.copy(step, chunk, way).wait_send()


class Scatter:
    def __init__(self, n, held, terms, send, recv, ends, term):
        self.n, self.held, self.terms, self.send, self.recv = n, held, terms, send, recv
        self.ends, self.term = ends, term
        self.half = held.shape[2] // 2

    def copy(self, step, chunk, way):
        part = pl.ds(chunk * self.half, self.half)
        return push(
            self.held.at[way, step, part],
            self.held.at[way, step + 1, part],
            self.send.at[step, chunk, way],
            self.recv.at[step, chunk, way],
            self.ends[way],
        )

    def step(self, step):
        for way in range(2):
            self.terms[way] = self.term(step, way)
        for chunk in range(2):
            for way in range(2):
                part = pl.ds(chunk * self.half, self.half)

                def first(way=way, part=part):
                    self.held[way, step, part] = self.terms[way, part].astype(jnp.bfloat16)

                def later(chunk=chunk, way=way, part=part):
                    self.copy(step - 1, chunk, way).wait_recv()
                    self.held[way, step, part] = (
                        self.terms[way, part] + self.held[way, step, part].astype(jnp.float32)
                    ).astype(jnp.bfloat16)

                if isinstance(step, int):
                    (later if step else first)()
                else:
                    pl.when(step == 0)(first)
                    pl.when(step > 0)(later)
                self.copy(step, chunk, way).start()

    def result(self, way):
        for chunk in range(2):
            self.copy(self.n - 2, chunk, way).wait_recv()
        return self.term(self.n - 1, way) + self.held[way, self.n - 1].astype(jnp.float32)

    def finish(self):
        def body(step, _):
            for chunk in range(2):
                for way in range(2):
                    self.copy(step, chunk, way).wait_send()
            return 0

        lax.fori_loop(0, self.n - 1, body, 0)


def behind(step, way, n):
    near = 2 * step + 1 + way
    far = 2 * (n - 1 - step) - way
    if isinstance(step, int):
        return 0 if step == n - 1 else min(near, far, n - 1)
    return jnp.where(step == n - 1, 0, jnp.minimum(jnp.minimum(near, far), n - 1))


def team(grp):
    over, core = grp // 2, grp % 2
    return over, core, (1 - over) * 2 + core, over * 2 + 1 - core


def mlp_kernel(
    n,
    lanes,
    ob,
    w_out,
    x_ref,
    gain,
    weights,
    w_down,
    seed_hbm,
    seed_own,
    block_out,
    dresid_out,
    dattended,
    gain_terms,
    wide_sum,
    down_sum,
    out_grad,
    normed,
    seed,
    gate_up,
    down,
    hidden,
    dgate_up,
    held_one,
    held_two,
    terms,
    resid,
    wide,
    wide_c,
    tall,
    tall_c,
    load_sem,
    s_one,
    r_one,
    s_two,
    r_two,
    s_three,
    r_three,
    s_norm,
    r_norm,
    s_dres,
    r_dres,
    s_wc,
    r_wc,
    s_wx,
    r_wx,
    s_tall,
    r_tall,
):
    f32, bf16 = jnp.float32, jnp.bfloat16
    grp, me = lax.axis_index("grp"), lax.axis_index("blk")
    over, core, grp_x, grp_c = team(grp)
    _, ends = ring_ends(n)
    loads = [
        pltpu.make_async_copy(weights, gate_up, load_sem.at[0]),
        pltpu.make_async_copy(w_down, down, load_sem.at[1]),
        pltpu.make_async_copy(
            seed_hbm.at[pl.ds(1, n - 1)], seed.at[pl.ds(1, n - 1)], load_sem.at[2]
        ),
        pltpu.make_async_copy(seed_own, seed.at[0], load_sem.at[3]),
    ]
    for load in loads:
        load.start()
    greet(list(ends) + [(grp_x, me), (grp_c, me)])
    columns = x_ref.shape[1]
    half = columns // 2

    def out_term(step, way):
        return dot_f32(ob[behind(step, way, n)], w_out[:, way * half : (way + 1) * half])

    one = Scatter(n, held_one, terms, s_one, r_one, ends, out_term)
    one.step(0)
    lax.fori_loop(1, n - 1, lambda step, _: (one.step(step), 0)[1], 0)
    for way in range(2):
        part = slice(way * half, (way + 1) * half)
        resid[:, part] = x_ref[:, part].astype(f32) + one.result(way)
    value = resid[...]
    inv = lax.rsqrt(jnp.mean(value * value, axis=-1, keepdims=True) + EPS)
    normed[0] = (value * inv * gain[...]).astype(bf16)
    gather = Gather(n, normed, s_norm, r_norm, ends)
    gather.start()
    one.finish()
    for load in loads:
        load.wait()

    def mlp(slot, _):
        both = dot_f32(normed[slot], gate_up[...])
        grad = nt_dot(seed[slot], down[...])
        gate, up = both[:, :lanes], both[:, lanes:]
        sig = jax.nn.sigmoid(gate)
        swish = gate * sig
        hidden[slot] = (swish * up).astype(bf16)
        dgate_up[slot, :, :lanes] = (grad * up * sig * (1.0 + gate * (1.0 - sig))).astype(bf16)
        dgate_up[slot, :, lanes:] = (grad * swish).astype(bf16)
        return 0

    def norm_term(step, way):
        return nt_dot(dgate_up[behind(step, way, n)], gate_up[way * half : (way + 1) * half, :])

    two = Scatter(n, held_two, terms, s_two, r_two, ends, norm_term)

    def turn(t, _):
        pl.when(t > 0)(lambda: gather.advance(t - 1))
        low = jnp.maximum(2 * t - 1, 0)
        lax.fori_loop(low, jnp.minimum(2 * t + 1, n), mlp, 0)
        pl.when(t > 0)(lambda: two.step(t - 1))
        return 0

    lax.fori_loop(0, n // 2 + 1, turn, 0)

    tall_rows = lanes // 4

    def tall_at(first, count):
        return pl.ds(pl.multiple_of(first * tall_rows, tall_rows), count * tall_rows)

    tiles = [slice(at, min(at + 256, lanes)) for at in range(0, lanes, 256)]

    def tall_grad(tile):
        left = hidden[:, :, tile].reshape(-1, tile.stop - tile.start)
        tall[tile] = dot_t(left, seed[...].reshape(-1, columns)).astype(bf16)

    for index, step in enumerate(range(n // 2, n - 1)):
        for tile in tiles[index :: n // 2 - 1]:
            tall_grad(tile)
        two.step(step)
    tall_one = push(tall.at[tall_at(2 - 2 * core, 2)], tall_c, s_tall.at[0], r_tall.at[0], (grp_c, me))
    tall_one.start()

    value = resid[...]
    inv = lax.rsqrt(jnp.mean(value * value, axis=-1, keepdims=True) + EPS)
    for way in range(2):
        part = slice(way * half, (way + 1) * half)
        dresid_out[:, part] = two.result(way)
    dnormed = dresid_out[...]
    gain_terms[...] = jnp.sum(dnormed * value * inv, axis=0, keepdims=True)
    a_two = dnormed * gain[...]
    total = (
        seed[0].astype(f32)
        + inv * a_two
        - value * inv**3 * jnp.mean(a_two * value, axis=-1, keepdims=True)
    )
    dresid_out[...] = total
    dresid = seed
    dresid[0] = total.astype(bf16)
    back = Gather(n, dresid, s_dres, r_dres, ends)
    back.start()
    two.finish()

    def down_term(step, way):
        return dot_f32(hidden[behind(step, way, n)], down[:, way * half : (way + 1) * half])

    three = Scatter(n, held_one, terms, s_three, r_three, ends, down_term)

    def dob(slot, _):
        dattended[slot] = nt_dot(dresid[slot], w_out[...]).astype(bf16)
        return 0

    def wide_copy_c(tile):
        return push(
            wide.at[tile, 1 - core], wide_c.at[tile], s_wc.at[tile], r_wc.at[tile], (grp_c, me)
        )

    def wide_copy_x(tile):
        return push(
            wide_c.at[tile, 1 - over], wide_sum.at[tile], s_wx.at[tile], r_wx.at[tile], (grp_x, me)
        )

    quarter = wide.shape[3]

    def wide_grad(tile):
        at = pl.multiple_of(tile * 4 * quarter, 4 * quarter)
        left = normed[:, :, pl.ds(at, 4 * quarter)].reshape(-1, 4 * quarter)
        grad = dot_t(left, dgate_up[...].reshape(-1, 2 * lanes)).astype(bf16)
        wide[tile] = grad.reshape(2, 2, quarter, 2 * lanes)
        wide_copy_c(tile).start()

    def wide_pass(tile):
        wide_copy_c(tile).wait_recv()
        wide_c[tile, 1 - over] = (
            wide[tile, core, 1 - over].astype(f32) + wide_c[tile, 1 - over].astype(f32)
        ).astype(bf16)
        wide_copy_x(tile).start()

    tall_two = push(tall_c.at[tall_at(1 - over, 1)], down_sum, s_tall.at[1], r_tall.at[1], (grp_x, me))

    def tall_pass():
        tall_one.wait_recv()
        tall_c[tall_at(1 - over, 1)] = (
            tall[tall_at(2 * core + 1 - over, 1)].astype(f32)
            + tall_c[tall_at(1 - over, 1)].astype(f32)
        ).astype(bf16)
        tall_two.start()

    def wide_take(tile):
        wide_copy_x(tile).wait_recv()
        wide_sum[tile] = (
            wide[tile, core, over].astype(f32)
            + wide_c[tile, over].astype(f32)
            + wide_sum[tile].astype(f32)
        ).astype(bf16)

    def again(t, _):
        pl.when(t > 0)(lambda: back.advance(t - 1))
        low = jnp.maximum(2 * t - 1, 0)
        lax.fori_loop(low, jnp.minimum(2 * t + 1, n), dob, 0)

        def inner(step, _):
            pl.when(step < n - 1)(lambda: three.step(step))

            @pl.when(step < n // 2)
            def _():
                wide_grad(2 * step)
                pl.when(step == 0)(tall_pass)
                pl.when(step > 0)(lambda: wide_pass(2 * step - 1))
                wide_grad(2 * step + 1)
                wide_pass(2 * step)

            pl.when(step == n // 2)(lambda: wide_pass(n - 1))

            @pl.when(step >= n // 2)
            def _():
                wide_take(2 * step - n)
                pl.when(step < n - 1)(lambda: wide_take(2 * step - n + 1))

            return 0

        lax.fori_loop(2 * t, jnp.minimum(2 * t + 2, n), inner, 0)
        return 0

    lax.fori_loop(0, n // 2 + 1, again, 0)
    wide_take(n - 1)
    out_grad[...] = dot_t(
        ob[...].reshape(-1, ob.shape[2]), dresid[...].reshape(-1, columns)
    ).astype(bf16)
    for way in range(2):
        part = slice(way * half, (way + 1) * half)
        block_out[:, part] = (resid[:, part] + three.result(way)).astype(bf16)

    tall_two.wait_recv()
    down_sum[...] = (
        tall[tall_at(2 * core + over, 1)].astype(f32)
        + tall_c[tall_at(over, 1)].astype(f32)
        + down_sum[...].astype(f32)
    ).astype(bf16)
    gather.finish()
    back.finish()
    three.finish()
    tall_one.wait_send()
    tall_two.wait_send()

    def sent(tile, _):
        wide_copy_c(tile).wait_send()
        wide_copy_x(tile).wait_send()
        return 0

    lax.fori_loop(0, n, sent, 0)


def mlp_and_back(ob, w_out, x_own, gain, weights, lanes, w_down, seed, seed_own):
    n = lax.axis_size("blk")
    _, rows, columns = seed.shape
    head_lanes = ob.shape[2]
    quarter = columns // (4 * n)
    f32, bf16 = jnp.float32, jnp.bfloat16
    vmem, dma = pltpu.VMEM, pltpu.SemaphoreType.DMA
    in_vmem, anywhere = pl.BlockSpec(memory_space=vmem), pl.BlockSpec(memory_space=pl.ANY)
    ring = [dma((n - 1, 2, 2))] * 6 + [dma((n // 2, 2, 2))] * 4
    return pl.pallas_call(
        functools.partial(mlp_kernel, n, lanes),
        out_shape=(
            jax.ShapeDtypeStruct((rows, columns), bf16),
            jax.ShapeDtypeStruct((rows, columns), f32),
            jax.ShapeDtypeStruct((n, rows, head_lanes), bf16),
            jax.ShapeDtypeStruct((1, columns), f32),
            jax.ShapeDtypeStruct((n, quarter, 2 * lanes), bf16),
            jax.ShapeDtypeStruct((lanes // 4, columns), bf16),
            jax.ShapeDtypeStruct((head_lanes, columns), bf16),
        ),
        in_specs=[in_vmem] * 4 + [anywhere] * 4,
        out_specs=[in_vmem] * 7,
        scratch_shapes=[
            vmem((n, rows, columns), bf16),
            vmem((n, rows, columns), bf16),
            vmem((columns, 2 * lanes), bf16),
            vmem((lanes, columns), bf16),
            vmem((n, rows, lanes), bf16),
            vmem((n, rows, 2 * lanes), bf16),
            vmem((2, n, rows, columns // 2), bf16),
            vmem((2, n, rows, columns // 2), bf16),
            vmem((2, rows, columns // 2), f32),
            vmem((rows, columns), f32),
            vmem((n, 2, 2, quarter, 2 * lanes), bf16),
            vmem((n, 2, quarter, 2 * lanes), bf16),
            vmem((lanes, columns), bf16),
            vmem((lanes // 2, columns), bf16),
            dma((4,)),
        ]
        + ring
        + [dma((n,))] * 4
        + [dma((2,))] * 2,
        compiler_params=kernel_params(5),
        name="mlp_and_back",
    )(ob, w_out, x_own, gain, weights, w_down, seed, seed_own)


class Spread:
    def __init__(self, n, pieces, out, sems):
        self.n, self.pieces, self.out = n, pieces, out
        self.s_blk, self.r_blk, self.s_x, self.r_x, self.s_c, self.r_c = sems
        self.grp, self.me = lax.axis_index("grp"), lax.axis_index("blk")
        self.over, self.core, self.grp_x, self.grp_c = team(self.grp)

    def first(self, k):
        to = (self.me + k) % self.n
        place = self.out.at[self.me, 2 * self.core + self.over]
        return push(
            self.pieces.at[to], place, self.s_blk.at[k], self.r_blk.at[k], (self.grp, to)
        )

    def own(self, sem):
        place = self.out.at[self.me, 2 * self.core + self.over]
        return pltpu.make_async_copy(self.pieces.at[self.me], place, sem)

    def to_x(self, k, own=False):
        piece = self.out.at[(self.me - k + self.n) % self.n, 2 * self.core + self.over]
        source = self.pieces.at[self.me] if own else piece
        return push(source, piece, self.s_x.at[k], self.r_x.at[k], (self.grp_x, self.me))

    def to_core(self, k, far, own=False):
        over = 1 - self.over if far else self.over
        piece = self.out.at[(self.me - k + self.n) % self.n, 2 * self.core + over]
        source = self.pieces.at[self.me] if own else piece
        sems = (self.s_c.at[int(far), k], self.r_c.at[int(far), k])
        return push(source, piece, *sems, (self.grp_c, self.me))

    def pass_own(self):
        self.to_x(0, True).start()
        self.to_core(0, False, True).start()

    def pass_on(self, k):
        self.first(k).wait_recv()
        self.to_x(k).start()
        self.to_core(k, False).start()

    def pass_far(self, k):
        self.to_x(k).wait_recv()
        self.to_core(k, True).start()

    def arrived(self, k):
        for far in (False, True):
            self.to_core(k, far).wait_recv()

    def finish(self):
        def body(k, _):
            pl.when(k > 0)(self.first(k).wait_send)
            self.to_x(k).wait_send()
            for far in (False, True):
                self.to_core(k, far).wait_send()
            return 0

        lax.fori_loop(0, self.n, body, 0)


def each(count, body, low=0):
    lax.fori_loop(low, count, lambda k, _: (body(k), 0)[1], 0)


def spread_sems(n):
    dma = pltpu.SemaphoreType.DMA
    return [dma((n,)), dma((n,)), dma((n,)), dma((n,)), dma((2, n)), dma((2, n))]


def team_and_ring(n):
    grp, me = lax.axis_index("grp"), lax.axis_index("blk")
    _, _, grp_x, grp_c = team(grp)
    return [(grp, (me + k) % n) for k in range(1, n)] + [(grp_x, me), (grp_c, me)]


def fill_row(row, gains_all, which, share):
    for block in range(gains_all.shape[0]):
        row[:, block * share : (block + 1) * share] = gains_all[block, which : which + 1, :]


def turned(value, cosine, sine_part):
    half_size = HEAD // 2
    swapped = jnp.concatenate([value[:, half_size:], value[:, :half_size]], axis=1)
    return value * cosine + swapped * sine_part


def attend_kernel(
    n,
    heads,
    x_own,
    cosine,
    sine_part,
    first_key,
    query_place,
    key_place,
    slab_qkv,
    slab_gate_up,
    gains,
    seed_own,
    gains_all,
    columns_qkv,
    normed,
    qkv,
    attended,
    attended_b,
    log_total,
    gate_up,
    seed,
    x_all,
    gain_row,
    local,
    s_gain,
    r_gain,
    s_x,
    r_x,
    s_seed,
    r_seed,
    *spread_all,
):
    f32, bf16 = jnp.float32, jnp.bfloat16
    grp, me = lax.axis_index("grp"), lax.axis_index("blk")
    _, ends = ring_ends(n)
    rows, columns = x_own.shape
    spread_qkv = Spread(n, slab_qkv, columns_qkv, spread_all[:6])
    spread_gu = Spread(n, slab_gate_up, gate_up, spread_all[6:])
    near_gain = pltpu.make_async_copy(gains, gains_all.at[me], local.at[0])
    near_gain.start()
    near_qkv = spread_qkv.own(local.at[1])
    near_qkv.start()
    x_all[0] = x_own[...]
    greet(team_and_ring(n))

    def gain(k):
        return push(gains, gains_all.at[me], s_gain.at[k], r_gain.at[k], (grp, (me + k) % n))

    each(n, lambda k: gain(k).start(), 1)
    x_ring = Gather(n, x_all, s_x, r_x, ends)
    x_ring.start()
    each(n, lambda k: spread_qkv.first(k).start(), 1)
    spread_qkv.pass_own()
    near_gu = spread_gu.own(local.at[2])
    near_gu.start()


    def norm(slot):
        value = x_all[slot].astype(f32)
        inv = lax.rsqrt(jnp.mean(value * value, axis=-1, keepdims=True) + EPS)
        normed[slot] = (value * inv * gain_row[...]).astype(bf16)

    near_gain.wait()
    each(n, lambda k: gain(k).wait_recv(), 1)
    fill_row(gain_row, gains_all, 0, columns // n)

    def arrive(t):
        pl.when(t > 0)(lambda: x_ring.advance(t - 1))
        low = jnp.maximum(2 * t - 1, 0)
        each(jnp.minimum(2 * t + 1, n), norm, low)
        pl.when(t == 2)(lambda: each(n, spread_qkv.pass_on, 1))
        pl.when(t == 3)(lambda: each(n, spread_qkv.pass_far))

        @pl.when(t == 2)
        def _():
            each(n, lambda k: spread_gu.first(k).start(), 1)
            spread_gu.pass_own()


    each(n // 2 + 1, arrive)
    seed_ring = Gather(n, seed, s_seed, r_seed, ends, seed_own)
    each(n, spread_gu.pass_on, 1)
    seed_ring.start()
    each(n, spread_qkv.arrived)
    near_qkv.wait()


    head_lanes = heads * HEAD
    pair = 2 * rows

    def project(i):
        both = normed[pl.ds(2 * i, 2)].reshape(pair, columns)
        result = dot_f32(both, columns_qkv[...].reshape(columns, 3 * head_lanes))
        at = pl.ds(pl.multiple_of(i * pair, pair), pair)
        table_c, table_s = cosine[at, :], sine_part[at, :]
        for piece in range(3 * heads):
            lane = slice(piece * HEAD, (piece + 1) * HEAD)
            value = result[:, lane]
            if piece < 2 * heads:
                value = turned(value, table_c, table_s)
            qkv[at, lane] = value.astype(bf16)

    each(n // 2, project)


    def tile(i):
        for head in range(heads):
            lane = slice(head * HEAD, (head + 1) * HEAD)
            at = pl.ds(pl.multiple_of(i * pair, pair), pair)
            keys = qkv[:, head_lanes + head * HEAD : head_lanes + (head + 1) * HEAD]
            values = qkv[:, 2 * head_lanes + head * HEAD : 2 * head_lanes + (head + 1) * HEAD]
            scores = nt_dot(qkv[at, lane], keys) * HEAD ** (-0.5)
            allowed = (key_place[...] >= first_key[at, :]) & (key_place[...] <= query_place[at, :])
            scores = jnp.where(allowed, scores, NEGATIVE)
            peak = jnp.max(scores, axis=-1, keepdims=True)
            raw = jnp.exp(scores - peak)
            total = jnp.sum(raw, axis=-1, keepdims=True)
            out = dot_f32(raw.astype(bf16), values) / total
            attended[at, lane] = out
            attended_b[at, lane] = out.astype(bf16)
            log_total[head, at, :] = peak + jnp.log(total)
        seed_ring.advance(i)

    each(n // 2, tile)
    each(n, spread_gu.pass_far)
    each(n, spread_gu.arrived)
    near_gu.wait()
    for spread in (spread_qkv, spread_gu):
        spread.finish()
    each(n, lambda k: gain(k).wait_send(), 1)
    x_ring.finish()
    seed_ring.finish()


def attend(slab_qkv, slab_gate_up, gains, x_own, seed_own, cosine, sine_part, first_key, places):
    n = lax.axis_size("blk")
    rows, columns = x_own.shape
    seq = n * rows
    lanes = slab_qkv.shape[2]
    head_lanes = lanes // 3
    heads = head_lanes // HEAD
    f32, bf16 = jnp.float32, jnp.bfloat16
    vmem, dma = pltpu.VMEM, pltpu.SemaphoreType.DMA
    in_vmem, anywhere = pl.BlockSpec(memory_space=vmem), pl.BlockSpec(memory_space=pl.ANY)
    return pl.pallas_call(
        functools.partial(attend_kernel, n, heads),
        out_shape=(
            jax.ShapeDtypeStruct((n,) + gains.shape, f32),
            jax.ShapeDtypeStruct((n, 4) + slab_qkv.shape[1:], bf16),
            jax.ShapeDtypeStruct((n, rows, columns), bf16),
            jax.ShapeDtypeStruct((seq, lanes), bf16),
            jax.ShapeDtypeStruct((seq, head_lanes), f32),
            jax.ShapeDtypeStruct((seq, head_lanes), bf16),
            jax.ShapeDtypeStruct((heads, seq, 1), f32),
            jax.ShapeDtypeStruct((n, 4) + slab_gate_up.shape[1:], bf16),
            jax.ShapeDtypeStruct((n, rows, columns), bf16),
        ),
        in_specs=[in_vmem] * 6 + [anywhere] * 4,
        out_specs=[in_vmem] * 7 + [anywhere] * 2,
        scratch_shapes=[
            vmem((n, rows, columns), bf16),
            vmem((1, columns), f32),
            dma((3,)),
            dma((n,)),
            dma((n,)),
        ]
        + [dma((n // 2, 2, 2))] * 4
        + spread_sems(n) * 2,
        compiler_params=kernel_params(0),
        name="attend",
    )(
        x_own,
        cosine,
        sine_part,
        first_key,
        places.reshape(seq, 1),
        places.reshape(1, seq),
        slab_qkv,
        slab_gate_up,
        gains,
        seed_own,
    )


def finish_kernel(
    n,
    heads,
    qkv,
    attended,
    dattended,
    log_total,
    cosine,
    sine_part,
    first_key,
    query_place,
    key_place,
    x_own,
    gain,
    dresid,
    terms_two,
    out_grad,
    weights,
    normed_hbm,
    gate_up_sum,
    down_sum,
    x_grad,
    gain_grads,
    wide_gate_up,
    wide_qkv,
    tall_down,
    tall_out,
    normed,
    columns_qkv,
    dqkv,
    dkeys,
    dvalues,
    held,
    terms,
    wide,
    wide_c,
    wide_x,
    out_c,
    out_x,
    gain_slabs,
    gain_heard,
    gain_team,
    load_sem,
    s_ring,
    r_ring,
    s_wc,
    r_wc,
    s_wx,
    r_wx,
    s_tall,
    r_tall,
    s_gain,
    r_gain,
    *spread_all,
):
    f32, bf16 = jnp.float32, jnp.bfloat16
    grp, me = lax.axis_index("grp"), lax.axis_index("blk")
    over, core, grp_x, grp_c = team(grp)
    _, ends = ring_ends(n)
    rows, columns = x_own.shape
    half = columns // 2
    lanes = wide.shape[4]
    quarter = wide.shape[3]
    load_normed = pltpu.make_async_copy(normed_hbm, normed, load_sem.at[0])
    load_qkv = pltpu.make_async_copy(weights, columns_qkv, load_sem.at[1])
    load_normed.start()
    load_qkv.start()
    spread_gu = Spread(n, gate_up_sum, wide_gate_up, spread_all[:6])
    spread_qkv = Spread(n, wide_x, wide_qkv, spread_all[6:])
    near_gu = spread_gu.own(load_sem.at[2])
    near_gu.start()
    greet(team_and_ring(n))

    down_own = pltpu.make_async_copy(down_sum, tall_down.at[2 * core + over], load_sem.at[3])
    down_own.start()
    down_place = tall_down.at[2 * core + over]
    down_x = push(down_sum, down_place, s_tall.at[0], r_tall.at[0], (grp_x, me))
    down_c = push(down_sum, down_place, s_tall.at[1], r_tall.at[1], (grp_c, me))
    far_place = tall_down.at[2 * core + 1 - over]
    down_far = push(far_place, far_place, s_tall.at[2], r_tall.at[2], (grp_c, me))
    out_one = push(out_grad.at[1 - core], out_c, s_tall.at[3], r_tall.at[3], (grp_c, me))
    out_two = push(out_c.at[1 - over], out_x, s_tall.at[4], r_tall.at[4], (grp_x, me))
    out_place = tall_out.at[2 * core + over]
    out_own = pltpu.make_async_copy(out_x, out_place, load_sem.at[4])
    out_to_x = push(out_x, out_place, s_tall.at[5], r_tall.at[5], (grp_x, me))
    out_to_c = push(out_x, out_place, s_tall.at[6], r_tall.at[6], (grp_c, me))
    out_far_place = tall_out.at[2 * core + 1 - over]
    out_far = push(out_far_place, out_far_place, s_tall.at[7], r_tall.at[7], (grp_c, me))
    out_one.start()
    each(n, lambda k: spread_gu.first(k).start(), 1)
    spread_gu.pass_own()
    down_x.start()
    down_c.start()

    pair = 2 * rows
    head_lanes = heads * HEAD
    scale = HEAD ** (-0.5)

    def unturned(value, at):
        return turned(value, cosine[at, :], -sine_part[at, :]).astype(bf16)

    def tile(i, head):
        at = pl.ds(pl.multiple_of(i * pair, pair), pair)
        lane = slice(head * HEAD, (head + 1) * HEAD)
        query = qkv[at, lane]
        keys = qkv[:, head_lanes + head * HEAD : head_lanes + (head + 1) * HEAD]
        values = qkv[:, 2 * head_lanes + head * HEAD : 2 * head_lanes + (head + 1) * HEAD]
        grad = dattended[at, lane]
        delta = jnp.sum(grad.astype(f32) * attended[at, lane], axis=-1, keepdims=True)
        scores = nt_dot(query, keys) * scale
        allowed = (key_place[...] >= first_key[at, :]) & (key_place[...] <= query_place[at, :])
        probs = jnp.where(allowed, jnp.exp(scores - log_total[head, at, :]), 0.0)
        dscores = (probs * (nt_dot(grad, values) - delta)).astype(bf16)
        dqkv[2 * i : 2 * i + 2, :, lane] = unturned(dot_f32(dscores, keys) * scale, at).reshape(
            2, rows, HEAD
        )
        more_keys = dot_t(dscores, query)
        more_values = dot_t(probs.astype(bf16), grad)
        if i == 0:
            dkeys[...] = more_keys
            dvalues[...] = more_values
        else:
            dkeys[...] += more_keys
            dvalues[...] += more_values

    for head in range(heads):
        for i in range(n // 2):
            tile(i, head)
        everything = slice(0, n * rows)
        lane = slice(head_lanes + head * HEAD, head_lanes + (head + 1) * HEAD)
        dqkv[:, :, lane] = unturned(dkeys[...] * scale, everything).reshape(n, rows, HEAD)
        lane = slice(2 * head_lanes + head * HEAD, 2 * head_lanes + (head + 1) * HEAD)
        dqkv[:, :, lane] = dvalues[...].astype(bf16).reshape(n, rows, HEAD)
    load_qkv.wait()

    def term(step, way):
        return nt_dot(dqkv[behind(step, way, n)], columns_qkv[way * half : (way + 1) * half, :])

    ring = Scatter(n, held, terms, s_ring, r_ring, ends, term)

    def copy_c(k):
        tile = (me + k) % n
        return push(wide.at[tile, 1 - core], wide_c.at[tile], s_wc.at[k], r_wc.at[k], (grp_c, me))

    def copy_x(k):
        tile = (me + k) % n
        return push(
            wide_c.at[tile, 1 - over], wide_x.at[tile], s_wx.at[k], r_wx.at[k], (grp_x, me)
        )

    def grad(k):
        tile = (me + k) % n
        at = pl.multiple_of(tile * 4 * quarter, 4 * quarter)
        left = normed[:, :, pl.ds(at, 4 * quarter)].reshape(-1, 4 * quarter)
        grad_rows = dot_t(left, dqkv[...].reshape(-1, lanes)).astype(bf16)
        wide[tile] = grad_rows.reshape(2, 2, quarter, lanes)
        copy_c(k).start()

    def pass_x(k):
        tile = (me + k) % n
        copy_c(k).wait_recv()
        wide_c[tile, 1 - over] = (
            wide[tile, core, 1 - over].astype(f32) + wide_c[tile, 1 - over].astype(f32)
        ).astype(bf16)
        copy_x(k).start()

    def take(k):
        tile = (me + k) % n
        copy_x(k).wait_recv()
        wide_x[tile] = (
            wide[tile, core, over].astype(f32)
            + wide_c[tile, over].astype(f32)
            + wide_x[tile].astype(f32)
        ).astype(bf16)

    def take_and_push(k):
        take(k)
        spread_qkv.first(k).start()

    ring.step(0)
    load_normed.wait()

    def grads(i):
        k = (i + 1) % n
        grad(k)
        pl.when(i > 0)(lambda: pass_x(i))

    each(n, grads)
    pass_x(0)
    out_one.wait_recv()
    out_c[1 - over] = (
        out_grad[core, 1 - over].astype(f32) + out_c[1 - over].astype(f32)
    ).astype(bf16)
    out_two.start()

    def turn(k):
        pl.when(k < n - 2)(lambda: ring.step(k + 1))
        each(jnp.minimum(2 * k + 3, n), spread_gu.pass_on, jnp.minimum(2 * k + 1, n))
        pl.when(k < n - 1)(lambda: take_and_push(k + 1))

        @pl.when(k == n - 2)
        def _():
            take(0)
            spread_qkv.pass_own()

    each(n - 1, turn)
    near_qkv = spread_qkv.own(load_sem.at[5])
    near_qkv.start()

    x_float = x_own[...].astype(f32)
    inv = lax.rsqrt(jnp.mean(x_float * x_float, axis=-1, keepdims=True) + EPS)
    for way in range(2):
        terms[way] = ring.result(way)
    dnormed = jnp.concatenate([terms[0], terms[1]], axis=1)
    terms_one = jnp.sum(dnormed * x_float * inv, axis=0, keepdims=True)
    share = columns // n
    for block in range(n):
        gain_slabs[block] = jnp.zeros_like(gain_slabs[block])
        lane = slice(block * share, (block + 1) * share)
        gain_slabs[block, 0:1, :] = terms_one[:, lane]
        gain_slabs[block, 1:2, :] = terms_two[:, lane]

    def gain_blk(k):
        to = (me + k) % n
        return push(gain_slabs.at[to], gain_heard.at[k], s_gain.at[k], r_gain.at[k], (grp, to))

    each(n, lambda k: gain_blk(k).start(), 1)
    a_one = dnormed * gain[...]
    x_grad[...] = (
        dresid[...]
        + inv * a_one
        - x_float * inv**3 * jnp.mean(a_one * x_float, axis=-1, keepdims=True)
    ).astype(bf16)
    gain_heard[0] = gain_slabs[me]
    each(n, lambda k: gain_blk(k).wait_recv(), 1)
    gain_team[0] = jnp.sum(gain_heard[...], axis=0)
    gain_c = push(gain_team.at[0], gain_team.at[1], s_gain.at[n], r_gain.at[n], (grp_c, me))
    gain_c.start()
    out_two.wait_recv()
    out_x[...] = (
        out_grad[core, over].astype(f32) + out_c[over].astype(f32) + out_x[...].astype(f32)
    ).astype(bf16)
    out_own.start()
    out_to_x.start()
    out_to_c.start()
    each(n, spread_qkv.pass_on, 1)
    each(n, spread_gu.pass_far)
    down_x.wait_recv()
    down_far.start()
    gain_c.wait_recv()
    gain_team[2] = gain_team[0] + gain_team[1]
    gain_x = push(
        gain_team.at[2], gain_team.at[3], s_gain.at[n + 1], r_gain.at[n + 1], (grp_x, me)
    )
    gain_x.start()
    out_to_x.wait_recv()
    out_far.start()
    each(n, spread_qkv.pass_far)
    gain_x.wait_recv()
    gain_grads[...] = gain_team[2] + gain_team[3]
    near_gu.wait()
    near_qkv.wait()
    each(n, spread_gu.arrived)
    each(n, spread_qkv.arrived)
    spread_gu.finish()
    spread_qkv.finish()
    ring.finish()
    down_own.wait()
    out_own.wait()
    for copy in (down_c, down_far, out_to_c, out_far):
        copy.wait()
    for copy in (down_x, out_one, out_two, out_to_x, gain_c, gain_x):
        copy.wait_send()

    def sent(k):
        copy_c(k).wait_send()
        copy_x(k).wait_send()
        pl.when(k > 0)(gain_blk(k).wait_send)

    each(n, sent)


def finish(
    attention, x_own, gain, dresid, terms_two, out_grad, weights, normed, gate_up_sum, down_sum
):
    n, rows, columns = normed.shape
    seq, lanes = attention[0].shape
    heads = lanes // (3 * HEAD)
    quarter = columns // (4 * n)
    share = columns // n
    f32, bf16 = jnp.float32, jnp.bfloat16
    vmem, dma = pltpu.VMEM, pltpu.SemaphoreType.DMA
    in_vmem, anywhere = pl.BlockSpec(memory_space=vmem), pl.BlockSpec(memory_space=pl.ANY)
    out_rows = out_grad.shape[0] // 4
    return pl.pallas_call(
        functools.partial(finish_kernel, n, heads),
        out_shape=(
            jax.ShapeDtypeStruct((rows, columns), bf16),
            jax.ShapeDtypeStruct((8, share), f32),
            jax.ShapeDtypeStruct((n, 4) + gate_up_sum.shape[1:], bf16),
            jax.ShapeDtypeStruct((n, 4, quarter, lanes), bf16),
            jax.ShapeDtypeStruct((4,) + down_sum.shape, bf16),
            jax.ShapeDtypeStruct((4, out_rows, columns), bf16),
        ),
        in_specs=[in_vmem] * 14 + [anywhere] * 4,
        out_specs=[in_vmem] * 2 + [anywhere] * 4,
        scratch_shapes=[
            vmem((n, rows, columns), bf16),
            vmem((columns, lanes), bf16),
            vmem((n, rows, lanes), bf16),
            vmem((seq, HEAD), f32),
            vmem((seq, HEAD), f32),
            vmem((2, n, rows, columns // 2), bf16),
            vmem((2, rows, columns // 2), f32),
            vmem((n, 2, 2, quarter, lanes), bf16),
            vmem((n, 2, quarter, lanes), bf16),
            vmem((n, quarter, lanes), bf16),
            vmem((2, out_rows, columns), bf16),
            vmem((out_rows, columns), bf16),
            vmem((n, 8, share), f32),
            vmem((n, 8, share), f32),
            vmem((4, 8, share), f32),
            dma((6,)),
        ]
        + [dma((n - 1, 2, 2))] * 2
        + [dma((n,))] * 4
        + [dma((8,))] * 2
        + [dma((n + 2,))] * 2
        + spread_sems(n) * 2,
        compiler_params=kernel_params(6),
        name="finish",
    )(
        *attention,
        x_own,
        gain,
        dresid,
        terms_two,
        out_grad.reshape(2, 2, out_rows, columns),
        weights,
        normed,
        gate_up_sum,
        down_sum,
    )


def assemble_kernel(n, units, lanes, head_lanes, qkv, gate_up, down, out, *grads):
    grad_qkv, grad_out, grad_gate, grad_up, grad_down = grads
    f32 = jnp.float32
    for source in range(n):
        for part in range(3):
            first = (part * n + source) * head_lanes
            grad_qkv[:, first : first + head_lanes] = qkv[
                source, :, part * head_lanes : (part + 1) * head_lanes
            ].astype(f32)
        first = source * units
        grad_gate[:, first : first + units] = gate_up[source, :, :units].astype(f32)
        grad_up[:, first : first + units] = gate_up[source, :, lanes : lanes + units].astype(f32)
    grad_out[...] = out[...].astype(f32)
    grad_down[...] = down[...].astype(f32)


def assemble(qkv, gate_up, down, out, units, steps=4):
    n, rows, qkv_lanes = qkv.shape
    columns = down.shape[1]
    lanes = gate_up.shape[2] // 2
    head_lanes = qkv_lanes // 3
    step = rows // steps
    down_step = units // steps
    f32 = jnp.float32

    def wide(width):
        return pl.BlockSpec((n, step, width), lambda i: (0, i, 0))

    def flat(height, width):
        return pl.BlockSpec((height, width), lambda i: (i, 0))

    return pl.pallas_call(
        functools.partial(assemble_kernel, n, units, lanes, head_lanes),
        grid=(steps,),
        out_shape=(
            jax.ShapeDtypeStruct((rows, n * qkv_lanes), f32),
            jax.ShapeDtypeStruct((rows, columns), f32),
            jax.ShapeDtypeStruct((rows, n * units), f32),
            jax.ShapeDtypeStruct((rows, n * units), f32),
            jax.ShapeDtypeStruct((units, columns), f32),
        ),
        in_specs=[
            wide(qkv_lanes),
            wide(2 * lanes),
            flat(down_step, columns),
            flat(out.shape[0] // steps, columns),
        ],
        out_specs=[
            flat(step, n * qkv_lanes),
            flat(step, columns),
            flat(step, n * units),
            flat(step, n * units),
            flat(down_step, columns),
        ],
        compiler_params=pltpu.CompilerParams(vmem_limit_bytes=VMEM_BYTES),
        name="assemble",
    )(qkv, gate_up, down, out)


def pad_to(array, axis, size):
    widths = [(0, 0)] * array.ndim
    widths[axis] = (0, size - array.shape[axis])
    return jnp.pad(array, widths)


def per_device(block_input, doc_lens, norm_attn, w_qkv, w_out, norm_mlp, w_gate, w_up, w_down, cot):
    n = lax.axis_size("blk")
    tok_rows, width = block_input.shape[1:]
    seq = tok_rows * n
    heads = HEADS // n
    head_lanes = heads * HEAD
    qkv_lanes = 3 * head_lanes
    units = w_down.shape[0]
    lanes = units
    bf16 = jnp.bfloat16

    over, core, _, _ = team(lax.axis_index("grp"))
    quarter = w_qkv.shape[0] // 4
    first_row = (2 * core + over) * quarter

    def quarter_of(weight):
        return lax.dynamic_slice_in_dim(weight, first_row, quarter, 0)

    slab_qkv = (
        quarter_of(w_qkv)
        .reshape(quarter, 3, n, head_lanes)
        .transpose(2, 0, 1, 3)
        .reshape(n, quarter, qkv_lanes)
    )
    slab_gate_up = jnp.concatenate(
        [
            quarter_of(w).reshape(quarter, n, units).transpose(1, 0, 2)
            for w in (w_gate, w_up)
        ],
        axis=2,
    )
    gains = pad_to(jnp.stack([norm_attn, norm_mlp]).astype(jnp.float32), 0, 8)
    place = ring_place(lax.axis_index("blk"), n)
    offsets = [0] + [k * sign for k in range(1, n // 2) for sign in (-1, 1)] + [n // 2]
    blocks = jnp.stack([at_offset(place, offset, n) for offset in offsets])
    places = (blocks[:, None] * tok_rows + jnp.arange(tok_rows, dtype=jnp.int32)).reshape(seq)
    lengths = doc_lens[0]
    starts = jnp.cumsum(lengths) - lengths
    first_key = start_of(places, starts)
    half_cosine, half_sine = angle_tables(places - first_key)
    first_key = first_key.reshape(seq, 1)
    half_cosine, half_sine = half_cosine[:, 0], half_sine[:, 0]
    cosine = jnp.concatenate([half_cosine, half_cosine], axis=1)
    sine_part = jnp.concatenate([-half_sine, half_sine], axis=1)
    gains_all, qkv_columns, normed_one, qkv, attended, attended_b, log_total, gate_up, seed = attend(
        slab_qkv,
        slab_gate_up,
        gains,
        block_input[0],
        cot[0],
        cosine,
        sine_part,
        first_key,
        places,
    )
    gain_one = gains_all[:, 0].reshape(1, width)
    gain_two = gains_all[:, 1].reshape(1, width)
    qkv_columns = qkv_columns.reshape(width, qkv_lanes)
    gate_up = gate_up.reshape(width, 2 * lanes)
    block_out, dresid, dattended, terms_two, gate_up_sum, down_sum, out_grad = mlp_and_back(
        attended_b.reshape(n, tok_rows, head_lanes),
        w_out,
        block_input[0],
        gain_two,
        gate_up,
        lanes,
        w_down,
        seed,
        cot[0],
    )
    x_grad, gain_grads, wide_gate_up, wide_qkv, tall_down, tall_out = finish(
        (
            qkv,
            attended,
            dattended.reshape(seq, head_lanes),
            log_total,
            cosine,
            sine_part,
            first_key,
            places.reshape(seq, 1),
            places.reshape(1, seq),
        ),
        block_input[0],
        gain_one,
        dresid,
        terms_two,
        out_grad,
        qkv_columns,
        normed_one,
        gate_up_sum,
        down_sum,
    )
    shard_rows = 4 * quarter
    grad_qkv, grad_out, grad_gate, grad_up, grad_down = assemble(
        wide_qkv.reshape(n, shard_rows, qkv_lanes),
        wide_gate_up.reshape(n, shard_rows, 2 * lanes),
        tall_down.reshape(lanes, width),
        tall_out.reshape(head_lanes, width),
        units,
    )
    return (
        block_out[None],
        x_grad[None],
        gain_grads[0],
        grad_qkv,
        grad_out,
        gain_grads[1],
        grad_gate,
        grad_up,
        grad_down,
    )


def body_for(mesh):
    return per_device if HEADS % mesh.shape["blk"] == 0 else per_device_gather


def solution(mesh):
    return jax.shard_map(
        body_for(mesh),
        mesh=mesh,
        in_specs=(
            P("grp", "blk", None),
            P("grp", None),
            P("blk"),
            P("blk", None),
            P("blk", None),
            P("blk"),
            P("blk", None),
            P("blk", None),
            P("blk", None),
            P("grp", "blk", None),
        ),
        out_specs=(
            P("grp", "blk", None),
            P("grp", "blk", None),
            P("blk"),
            P("blk", None),
            P("blk", None),
            P("blk"),
            P("blk", None),
            P("blk", None),
            P("blk", None),
        ),
        check_vma=False,
    )
```

```python
import functools
import math

import jax
import jax.numpy as jnp
import numpy as np
from jax import lax
from jax.experimental import pallas as pl
from jax.experimental.pallas import tpu as pltpu
from jax.sharding import PartitionSpec as P

HEADS = 16
HEAD = 128


EPS = 1e-05
NEGATIVE = -1e30


def angle_tables(places):
    half_size = HEAD // 2
    freqs = jnp.exp(jnp.arange(half_size, dtype=jnp.float32) * (-2.0 * math.log(10000.0) / HEAD))
    angles = places.astype(jnp.float32)[:, None] * freqs
    return (jnp.cos(angles)[:, None, :], jnp.sin(angles)[:, None, :])


def rotate(tensor, cosine, sine_part):
    half_size = HEAD // 2
    first_half = tensor[..., :half_size]
    second_half = tensor[..., half_size:]
    return jnp.concatenate(
        [
            first_half * cosine - second_half * sine_part,
            second_half * cosine + first_half * sine_part,
        ],
        axis=-1,
    )


def unrotate(tensor, cosine, sine_part):
    half_size = HEAD // 2
    first_half = tensor[..., :half_size]
    second_half = tensor[..., half_size:]
    return jnp.concatenate(
        [
            first_half * cosine + second_half * sine_part,
            second_half * cosine - first_half * sine_part,
        ],
        axis=-1,
    )


def segment_of(places, starts):
    return jnp.sum((starts[None, :] <= places[:, None]).astype(jnp.int32), axis=1) - 1


def start_of(places, starts):
    return jnp.max(jnp.where(starts[None, :] <= places[:, None], starts[None, :], 0), axis=1)


def contract_rows(left, right):
    return lax.dot_general(
        left, right, (((1,), (1,)), ((), ())), preferred_element_type=jnp.float32
    )


def weight_term(left, right):

    def term(start, count):
        return lax.dot_general(
            left, right, (((0,), (0,)), ((), ())), preferred_element_type=jnp.float32
        )

    return term


def shard_grad(term_fn, shard_rows):
    shared = lax.psum_scatter(
        term_fn(jnp.int32(0), shard_rows * lax.axis_size("blk")).astype(jnp.bfloat16),
        "blk",
        scatter_dimension=0,
        tiled=True,
    )
    return lax.psum(shared, "grp").astype(jnp.float32)


def per_device_gather(block_input, doc_lens, norm_attn, w_qkv, w_out, norm_mlp, w_gate, w_up, w_down, cot):
    tok_rows = block_input.shape[1]
    width = block_input.shape[2]
    score_scale = HEAD ** (-0.5)
    shards = (norm_attn, w_qkv, w_out, norm_mlp, w_gate, w_up, w_down)
    gathered = (
        lax.all_gather(shards[0], "blk", axis=0, tiled=True),
        lax.all_gather(shards[1], "blk", axis=0, tiled=True),
        lax.all_gather(shards[2], "blk", axis=0, tiled=True),
        lax.all_gather(shards[3], "blk", axis=0, tiled=True),
        lax.all_gather(shards[4], "blk", axis=0, tiled=True),
        lax.all_gather(shards[5], "blk", axis=0, tiled=True),
        lax.all_gather(shards[6], "blk", axis=0, tiled=True),
    )
    gain_one, weight_qkv, weight_out, gain_two, weight_gate, weight_up, weight_down = gathered
    place_rows = lax.axis_index("blk") * tok_rows + jnp.arange(tok_rows, dtype=jnp.int32)
    lengths = doc_lens[0]
    starts = jnp.cumsum(lengths) - lengths
    query_seg = segment_of(place_rows, starts)
    cosine, sine_part = angle_tables(place_rows - start_of(place_rows, starts))
    x_float = block_input[0].astype(jnp.float32)
    inv_one = lax.rsqrt(jnp.mean(x_float * x_float, axis=-1, keepdims=True) + EPS)
    normed_one = (x_float * inv_one * gain_one.astype(jnp.float32)).astype(jnp.bfloat16)
    projected = jnp.dot(normed_one, weight_qkv, preferred_element_type=jnp.float32)
    heads_all = projected.reshape(tok_rows, 3, HEADS, HEAD)
    queries = rotate(heads_all[:, 0], cosine, sine_part).astype(jnp.bfloat16)
    keys_own = rotate(heads_all[:, 1], cosine, sine_part).astype(jnp.bfloat16)
    values_own = heads_all[:, 2].astype(jnp.bfloat16)

    def pair_mask(count):
        key_places = jnp.arange(count, dtype=jnp.int32)
        key_seg = segment_of(key_places, starts)
        return (query_seg[:, None] == key_seg[None, :]) & (
            key_places[None, :] <= place_rows[:, None]
        )

    piece = (
        lax.all_gather(keys_own, "blk", axis=0, tiled=True),
        lax.all_gather(values_own, "blk", axis=0, tiled=True),
    )
    count = piece[0].shape[0]
    row_peak = jnp.full((HEADS, tok_rows), NEGATIVE, jnp.float32)
    key_piece, value_piece = piece
    count = key_piece.shape[0]
    allowed = pair_mask(count)[None]
    scores = (
        jnp.einsum("qhd,khd->hqk", queries, key_piece, preferred_element_type=jnp.float32)
        * score_scale
    )
    scores = jnp.where(allowed, scores, NEGATIVE)
    new_peak = jnp.maximum(row_peak, jnp.max(scores, axis=-1))
    weights_now = jnp.where(allowed, jnp.exp(scores - new_peak[..., None]), 0.0)
    row_total = jnp.sum(weights_now, axis=-1)
    accum = jnp.einsum(
        "hqk,khd->hqd",
        weights_now.astype(jnp.bfloat16),
        value_piece,
        preferred_element_type=jnp.float32,
    )
    row_peak, row_total, accum = (new_peak, row_total, accum)
    log_total = row_peak + jnp.log(row_total)
    attended = (accum / row_total[..., None]).transpose(1, 0, 2)
    attended_b = attended.reshape(tok_rows, width).astype(jnp.bfloat16)
    resid = x_float + jnp.dot(attended_b, weight_out, preferred_element_type=jnp.float32)
    inv_two = lax.rsqrt(jnp.mean(resid * resid, axis=-1, keepdims=True) + EPS)
    normed_two = (resid * inv_two * gain_two.astype(jnp.float32)).astype(jnp.bfloat16)
    gate_proj = jnp.dot(normed_two, weight_gate, preferred_element_type=jnp.float32)
    up_proj = jnp.dot(normed_two, weight_up, preferred_element_type=jnp.float32)
    sigmoid_gate = jax.nn.sigmoid(gate_proj)
    swish = gate_proj * sigmoid_gate
    hidden = (swish * up_proj).astype(jnp.bfloat16)
    block_out = (resid + jnp.dot(hidden, weight_down, preferred_element_type=jnp.float32)).astype(
        jnp.bfloat16
    )
    again = (
        lax.all_gather(shards[0], "blk", axis=0, tiled=True),
        lax.all_gather(shards[1], "blk", axis=0, tiled=True),
        lax.all_gather(shards[2], "blk", axis=0, tiled=True),
        lax.all_gather(shards[3], "blk", axis=0, tiled=True),
        lax.all_gather(shards[4], "blk", axis=0, tiled=True),
        lax.all_gather(shards[5], "blk", axis=0, tiled=True),
        lax.all_gather(shards[6], "blk", axis=0, tiled=True),
    )
    back_gain_one, back_qkv, back_out, back_gain_two, back_gate, back_up, back_down = again
    seed = cot[0]
    seed_float = seed.astype(jnp.float32)
    dhidden = contract_rows(seed, back_down)
    dgate = (dhidden * up_proj * sigmoid_gate * (1.0 + gate_proj * (1.0 - sigmoid_gate))).astype(
        jnp.bfloat16
    )
    dup = (dhidden * swish).astype(jnp.bfloat16)
    dnormed_two = contract_rows(dgate, back_gate) + contract_rows(dup, back_up)
    a_two = dnormed_two * back_gain_two.astype(jnp.float32)
    dresid = (
        seed_float
        + inv_two * a_two
        - resid * inv_two**3 * jnp.mean(a_two * resid, axis=-1, keepdims=True)
    )
    dresid_b = dresid.astype(jnp.bfloat16)
    dattended = (
        contract_rows(dresid_b, back_out).astype(jnp.bfloat16).reshape(tok_rows, HEADS, HEAD)
    )
    delta = jnp.sum(dattended.astype(jnp.float32) * attended, axis=-1).T
    piece = (
        lax.all_gather(keys_own, "blk", axis=0, tiled=True),
        lax.all_gather(values_own, "blk", axis=0, tiled=True),
    )
    count = piece[0].shape[0]
    key_piece, value_piece = piece
    count = key_piece.shape[0]
    score_count = key_piece.shape[0]
    allowed = pair_mask(score_count)[None]
    scores = (
        jnp.einsum("qhd,khd->hqk", queries, key_piece, preferred_element_type=jnp.float32)
        * score_scale
    )
    probs = jnp.where(allowed, jnp.exp(scores - log_total[..., None]), 0.0)
    dprobs = jnp.einsum("qhd,khd->hqk", dattended, value_piece, preferred_element_type=jnp.float32)
    dscores = (probs * (dprobs - delta[..., None])).astype(jnp.bfloat16)
    probs, dscores = (probs, dscores)
    dquery_acc = score_scale * jnp.einsum(
        "hqk,khd->hqd", dscores, key_piece, preferred_element_type=jnp.float32
    )
    dkeys = score_scale * jnp.einsum(
        "hqk,qhd->khd", dscores, queries, preferred_element_type=jnp.float32
    )
    dvalues = jnp.einsum(
        "hqk,qhd->khd", probs.astype(jnp.bfloat16), dattended, preferred_element_type=jnp.float32
    )
    stacked = jnp.concatenate([dkeys.reshape(count, width), dvalues.reshape(count, width)], axis=1)
    grads_buffer = stacked
    dquery_acc, grads_buffer = (dquery_acc, grads_buffer)
    own_grads = lax.psum_scatter(
        grads_buffer.astype(jnp.bfloat16), "blk", scatter_dimension=0, tiled=True
    ).astype(jnp.float32)
    dkey = unrotate(own_grads[:, :width].reshape(tok_rows, HEADS, HEAD), cosine, sine_part)
    dvalue = own_grads[:, width:].reshape(tok_rows, HEADS, HEAD)
    dquery = unrotate(dquery_acc.transpose(1, 0, 2), cosine, sine_part)
    dqkv = (
        jnp.stack([dquery, dkey, dvalue], axis=1).reshape(tok_rows, 3 * width).astype(jnp.bfloat16)
    )
    dnormed_one = contract_rows(dqkv, back_qkv)
    a_one = dnormed_one * back_gain_one.astype(jnp.float32)
    x_grad = (
        dresid
        + inv_one * a_one
        - x_float * inv_one**3 * jnp.mean(a_one * x_float, axis=-1, keepdims=True)
    ).astype(jnp.bfloat16)
    width_rows = norm_attn.shape[0]
    gain_terms = jnp.stack(
        [
            jnp.sum(dnormed_one * x_float * inv_one, axis=0),
            jnp.sum(dnormed_two * resid * inv_two, axis=0),
        ],
        axis=1,
    )

    def gain_slice(start, count):
        return gain_terms

    grad_down = shard_grad(weight_term(hidden, seed), w_down.shape[0])
    grad_gate = shard_grad(weight_term(normed_two, dgate), width_rows)
    grad_up = shard_grad(weight_term(normed_two, dup), width_rows)
    grad_out = shard_grad(weight_term(attended_b, dresid_b), width_rows)
    grad_qkv = shard_grad(weight_term(normed_one, dqkv), width_rows)
    gain_grads = shard_grad(gain_slice, width_rows)
    return (
        block_out[None],
        x_grad[None],
        gain_grads[:, 0],
        grad_qkv,
        grad_out,
        gain_grads[:, 1],
        grad_gate,
        grad_up,
        grad_down,
    )


MESH = pl.DeviceIdType.MESH
VMEM_BYTES = 60 * 2**20


def ring_place(block, n):
    up, row = block // 2, block % 2
    return (1 - row) * up + row * (n - 1 - up)


def ring_block(place, n):
    back = place // (n // 2)
    return (1 - back) * 2 * place + back * (2 * (n - 1 - place) + 1)


def at_offset(place, offset, n):
    return ring_block((place + offset + n) % n, n)


def greet(devices):
    barrier = pltpu.get_barrier_semaphore()
    for device in devices:
        pl.semaphore_signal(barrier, inc=1, device_id=device, device_id_type=MESH)
    pl.semaphore_wait(barrier, len(devices))


def push(src, dst, send_sem, recv_sem, device):
    return pltpu.make_async_remote_copy(
        src_ref=src,
        dst_ref=dst,
        send_sem=send_sem,
        recv_sem=recv_sem,
        device_id=device,
        device_id_type=MESH,
    )


def kernel_params(collective_id):
    return pltpu.CompilerParams(
        collective_id=collective_id, has_side_effects=True, vmem_limit_bytes=VMEM_BYTES
    )


def dot_f32(left, right):
    return jnp.dot(left, right, preferred_element_type=jnp.float32)


def dot_t(left, right):
    return lax.dot_general(
        left, right, (((0,), (0,)), ((), ())), preferred_element_type=jnp.float32
    )


def nt_dot(left, right):
    return lax.dot_general(
        left, right, (((1,), (1,)), ((), ())), preferred_element_type=jnp.float32
    )


def ring_ends(n):
    grp, me = lax.axis_index("grp"), lax.axis_index("blk")
    place = ring_place(me, n)
    return place, ((grp, at_offset(place, 1, n)), (grp, at_offset(place, -1, n)))


class Gather:
    def __init__(self, n, buf, send, recv, ends, own=None):
        self.n, self.buf, self.send, self.recv, self.ends = n, buf, send, recv, ends
        self.own = buf.at[0] if own is None else own
        self.half = buf.shape[1] // 2

    def copy(self, step, chunk, way):
        part = pl.ds(chunk * self.half, self.half)
        if isinstance(step, int):
            target = min(2 * step + 1 + way, self.n - 1)
        else:
            target = jnp.minimum(2 * step + 1 + way, self.n - 1)
        first = isinstance(step, int) and step == 0
        return push(
            self.own.at[part] if first else self.buf.at[2 * step - 1 + way, part],
            self.buf.at[target, part],
            self.send.at[step, chunk, way],
            self.recv.at[step, chunk, way],
            self.ends[way],
        )

    def landed(self, step, chunk, way):
        target = jnp.minimum(2 * step + 1 + way, self.n - 1)
        place = self.buf.at[target, pl.ds(chunk * self.half, self.half)]
        sems = (self.send.at[step, chunk, way], self.recv.at[step, chunk, way])
        return push(place, place, *sems, self.ends[way])

    def used(self, step, chunk, way):
        return step < self.n // 2 - 1 or chunk == way

    def start(self):
        for chunk in range(2):
            for way in range(2):
                self.copy(0, chunk, way).start()

    def advance(self, step):
        for chunk in range(2):
            for way in range(2):
                if isinstance(step, int):
                    if self.used(step, chunk, way):
                        self.copy(step, chunk, way).wait_recv()
                        if step + 1 < self.n // 2 and self.used(step + 1, chunk, way):
                            self.copy(step + 1, chunk, way).start()
                elif chunk == way:
                    self.landed(step, chunk, way).wait_recv()
                    pl.when(step + 1 < self.n // 2)(self.copy(step + 1, chunk, way).start)
                else:
                    pl.when(step < self.n // 2 - 1)(self.landed(step, chunk, way).wait_recv)
                    pl.when(step + 1 < self.n // 2 - 1)(self.copy(step + 1, chunk, way).start)

    def finish(self):
        for step in range(self.n // 2):
            for chunk in range(2):
                for way in range(2):
                    if self.used(step, chunk, way):
                        self.copy(step, chunk, way).wait_send()


class Scatter:
    def __init__(self, n, held, terms, send, recv, ends, term):
        self.n, self.held, self.terms, self.send, self.recv = n, held, terms, send, recv
        self.ends, self.term = ends, term
        self.half = held.shape[2] // 2

    def copy(self, step, chunk, way):
        part = pl.ds(chunk * self.half, self.half)
        return push(
            self.held.at[way, step, part],
            self.held.at[way, step + 1, part],
            self.send.at[step, chunk, way],
            self.recv.at[step, chunk, way],
            self.ends[way],
        )

    def step(self, step):
        for way in range(2):
            self.terms[way] = self.term(step, way)
        for chunk in range(2):
            for way in range(2):
                part = pl.ds(chunk * self.half, self.half)

                def first(way=way, part=part):
                    self.held[way, step, part] = self.terms[way, part].astype(jnp.bfloat16)

                def later(chunk=chunk, way=way, part=part):
                    self.copy(step - 1, chunk, way).wait_recv()
                    self.held[way, step, part] = (
                        self.terms[way, part] + self.held[way, step, part].astype(jnp.float32)
                    ).astype(jnp.bfloat16)

                if isinstance(step, int):
                    (later if step else first)()
                else:
                    pl.when(step == 0)(first)
                    pl.when(step > 0)(later)
                self.copy(step, chunk, way).start()

    def result(self, way):
        for chunk in range(2):
            self.copy(self.n - 2, chunk, way).wait_recv()
        return self.term(self.n - 1, way) + self.held[way, self.n - 1].astype(jnp.float32)

    def finish(self):
        def body(step, _):
            for chunk in range(2):
                for way in range(2):
                    self.copy(step, chunk, way).wait_send()
            return 0

        lax.fori_loop(0, self.n - 1, body, 0)


def behind(step, way, n):
    near = 2 * step + 1 + way
    far = 2 * (n - 1 - step) - way
    if isinstance(step, int):
        return 0 if step == n - 1 else min(near, far, n - 1)
    return jnp.where(step == n - 1, 0, jnp.minimum(jnp.minimum(near, far), n - 1))


def team(grp):
    over, core = grp // 2, grp % 2
    return over, core, (1 - over) * 2 + core, over * 2 + 1 - core


def mlp_kernel(
    n,
    lanes,
    ob,
    w_out,
    x_ref,
    gain,
    weights,
    w_down,
    seed_hbm,
    seed_own,
    block_out,
    dresid_out,
    dattended,
    gain_terms,
    wide_sum,
    down_sum,
    out_grad,
    normed,
    seed,
    gate_up,
    down,
    hidden,
    dgate_up,
    held_one,
    held_two,
    terms,
    resid,
    wide,
    wide_c,
    tall,
    tall_c,
    load_sem,
    s_one,
    r_one,
    s_two,
    r_two,
    s_three,
    r_three,
    s_norm,
    r_norm,
    s_dres,
    r_dres,
    s_wc,
    r_wc,
    s_wx,
    r_wx,
    s_tall,
    r_tall,
):
    f32, bf16 = jnp.float32, jnp.bfloat16
    grp, me = lax.axis_index("grp"), lax.axis_index("blk")
    over, core, grp_x, grp_c = team(grp)
    _, ends = ring_ends(n)
    loads = [
        pltpu.make_async_copy(weights, gate_up, load_sem.at[0]),
        pltpu.make_async_copy(w_down, down, load_sem.at[1]),
        pltpu.make_async_copy(
            seed_hbm.at[pl.ds(1, n - 1)], seed.at[pl.ds(1, n - 1)], load_sem.at[2]
        ),
        pltpu.make_async_copy(seed_own, seed.at[0], load_sem.at[3]),
    ]
    for load in loads:
        load.start()
    greet(list(ends) + [(grp_x, me), (grp_c, me)])
    columns = x_ref.shape[1]
    half = columns // 2

    def out_term(step, way):
        return dot_f32(ob[behind(step, way, n)], w_out[:, way * half : (way + 1) * half])

    one = Scatter(n, held_one, terms, s_one, r_one, ends, out_term)
    one.step(0)
    lax.fori_loop(1, n - 1, lambda step, _: (one.step(step), 0)[1], 0)
    for way in range(2):
        part = slice(way * half, (way + 1) * half)
        resid[:, part] = x_ref[:, part].astype(f32) + one.result(way)
    value = resid[...]
    inv = lax.rsqrt(jnp.mean(value * value, axis=-1, keepdims=True) + EPS)
    normed[0] = (value * inv * gain[...]).astype(bf16)
    gather = Gather(n, normed, s_norm, r_norm, ends)
    gather.start()
    one.finish()
    for load in loads:
        load.wait()

    def mlp(slot, _):
        both = dot_f32(normed[slot], gate_up[...])
        grad = nt_dot(seed[slot], down[...])
        gate, up = both[:, :lanes], both[:, lanes:]
        sig = jax.nn.sigmoid(gate)
        swish = gate * sig
        hidden[slot] = (swish * up).astype(bf16)
        dgate_up[slot, :, :lanes] = (grad * up * sig * (1.0 + gate * (1.0 - sig))).astype(bf16)
        dgate_up[slot, :, lanes:] = (grad * swish).astype(bf16)
        return 0

    def norm_term(step, way):
        return nt_dot(dgate_up[behind(step, way, n)], gate_up[way * half : (way + 1) * half, :])

    two = Scatter(n, held_two, terms, s_two, r_two, ends, norm_term)

    def turn(t, _):
        pl.when(t > 0)(lambda: gather.advance(t - 1))
        low = jnp.maximum(2 * t - 1, 0)
        lax.fori_loop(low, jnp.minimum(2 * t + 1, n), mlp, 0)
        pl.when(t > 0)(lambda: two.step(t - 1))
        return 0

    lax.fori_loop(0, n // 2 + 1, turn, 0)

    tall_rows = lanes // 4

    def tall_at(first, count):
        return pl.ds(pl.multiple_of(first * tall_rows, tall_rows), count * tall_rows)

    tiles = [slice(at, min(at + 256, lanes)) for at in range(0, lanes, 256)]

    def tall_grad(tile):
        left = hidden[:, :, tile].reshape(-1, tile.stop - tile.start)
        tall[tile] = dot_t(left, seed[...].reshape(-1, columns)).astype(bf16)

    for index, step in enumerate(range(n // 2, n - 1)):
        for tile in tiles[index :: n // 2 - 1]:
            tall_grad(tile)
        two.step(step)
    tall_one = push(tall.at[tall_at(2 - 2 * core, 2)], tall_c, s_tall.at[0], r_tall.at[0], (grp_c, me))
    tall_one.start()

    value = resid[...]
    inv = lax.rsqrt(jnp.mean(value * value, axis=-1, keepdims=True) + EPS)
    for way in range(2):
        part = slice(way * half, (way + 1) * half)
        dresid_out[:, part] = two.result(way)
    dnormed = dresid_out[...]
    gain_terms[...] = jnp.sum(dnormed * value * inv, axis=0, keepdims=True)
    a_two = dnormed * gain[...]
    total = (
        seed[0].astype(f32)
        + inv * a_two
        - value * inv**3 * jnp.mean(a_two * value, axis=-1, keepdims=True)
    )
    dresid_out[...] = total
    dresid = seed
    dresid[0] = total.astype(bf16)
    back = Gather(n, dresid, s_dres, r_dres, ends)
    back.start()
    two.finish()

    def down_term(step, way):
        return dot_f32(hidden[behind(step, way, n)], down[:, way * half : (way + 1) * half])

    three = Scatter(n, held_one, terms, s_three, r_three, ends, down_term)

    def dob(slot, _):
        dattended[slot] = nt_dot(dresid[slot], w_out[...]).astype(bf16)
        return 0

    def wide_copy_c(tile):
        return push(
            wide.at[tile, 1 - core], wide_c.at[tile], s_wc.at[tile], r_wc.at[tile], (grp_c, me)
        )

    def wide_copy_x(tile):
        return push(
            wide_c.at[tile, 1 - over], wide_sum.at[tile], s_wx.at[tile], r_wx.at[tile], (grp_x, me)
        )

    quarter = wide.shape[3]

    def wide_grad(tile):
        at = pl.multiple_of(tile * 4 * quarter, 4 * quarter)
        left = normed[:, :, pl.ds(at, 4 * quarter)].reshape(-1, 4 * quarter)
        grad = dot_t(left, dgate_up[...].reshape(-1, 2 * lanes)).astype(bf16)
        wide[tile] = grad.reshape(2, 2, quarter, 2 * lanes)
        wide_copy_c(tile).start()

    def wide_pass(tile):
        wide_copy_c(tile).wait_recv()
        wide_c[tile, 1 - over] = (
            wide[tile, core, 1 - over].astype(f32) + wide_c[tile, 1 - over].astype(f32)
        ).astype(bf16)
        wide_copy_x(tile).start()

    tall_two = push(tall_c.at[tall_at(1 - over, 1)], down_sum, s_tall.at[1], r_tall.at[1], (grp_x, me))

    def tall_pass():
        tall_one.wait_recv()
        tall_c[tall_at(1 - over, 1)] = (
            tall[tall_at(2 * core + 1 - over, 1)].astype(f32)
            + tall_c[tall_at(1 - over, 1)].astype(f32)
        ).astype(bf16)
        tall_two.start()

    def wide_take(tile):
        wide_copy_x(tile).wait_recv()
        wide_sum[tile] = (
            wide[tile, core, over].astype(f32)
            + wide_c[tile, over].astype(f32)
            + wide_sum[tile].astype(f32)
        ).astype(bf16)

    def again(t, _):
        pl.when(t > 0)(lambda: back.advance(t - 1))
        low = jnp.maximum(2 * t - 1, 0)
        lax.fori_loop(low, jnp.minimum(2 * t + 1, n), dob, 0)

        def inner(step, _):
            pl.when(step < n - 1)(lambda: three.step(step))

            @pl.when(step < n // 2)
            def _():
                wide_grad(2 * step)
                pl.when(step == 0)(tall_pass)
                pl.when(step > 0)(lambda: wide_pass(2 * step - 1))
                wide_grad(2 * step + 1)
                wide_pass(2 * step)

            pl.when(step == n // 2)(lambda: wide_pass(n - 1))

            @pl.when(step >= n // 2)
            def _():
                wide_take(2 * step - n)
                pl.when(step < n - 1)(lambda: wide_take(2 * step - n + 1))

            return 0

        lax.fori_loop(2 * t, jnp.minimum(2 * t + 2, n), inner, 0)
        return 0

    lax.fori_loop(0, n // 2 + 1, again, 0)
    wide_take(n - 1)
    out_grad[...] = dot_t(
        ob[...].reshape(-1, ob.shape[2]), dresid[...].reshape(-1, columns)
    ).astype(bf16)
    for way in range(2):
        part = slice(way * half, (way + 1) * half)
        block_out[:, part] = (resid[:, part] + three.result(way)).astype(bf16)

    tall_two.wait_recv()
    down_sum[...] = (
        tall[tall_at(2 * core + over, 1)].astype(f32)
        + tall_c[tall_at(over, 1)].astype(f32)
        + down_sum[...].astype(f32)
    ).astype(bf16)
    gather.finish()
    back.finish()
    three.finish()
    tall_one.wait_send()
    tall_two.wait_send()

    def sent(tile, _):
        wide_copy_c(tile).wait_send()
        wide_copy_x(tile).wait_send()
        return 0

    lax.fori_loop(0, n, sent, 0)


def mlp_and_back(ob, w_out, x_own, gain, weights, lanes, w_down, seed, seed_own):
    n = lax.axis_size("blk")
    _, rows, columns = seed.shape
    head_lanes = ob.shape[2]
    quarter = columns // (4 * n)
    f32, bf16 = jnp.float32, jnp.bfloat16
    vmem, dma = pltpu.VMEM, pltpu.SemaphoreType.DMA
    in_vmem, anywhere = pl.BlockSpec(memory_space=vmem), pl.BlockSpec(memory_space=pl.ANY)
    ring = [dma((n - 1, 2, 2))] * 6 + [dma((n // 2, 2, 2))] * 4
    return pl.pallas_call(
        functools.partial(mlp_kernel, n, lanes),
        out_shape=(
            jax.ShapeDtypeStruct((rows, columns), bf16),
            jax.ShapeDtypeStruct((rows, columns), f32),
            jax.ShapeDtypeStruct((n, rows, head_lanes), bf16),
            jax.ShapeDtypeStruct((1, columns), f32),
            jax.ShapeDtypeStruct((n, quarter, 2 * lanes), bf16),
            jax.ShapeDtypeStruct((lanes // 4, columns), bf16),
            jax.ShapeDtypeStruct((head_lanes, columns), bf16),
        ),
        in_specs=[in_vmem] * 4 + [anywhere] * 4,
        out_specs=[in_vmem] * 7,
        scratch_shapes=[
            vmem((n, rows, columns), bf16),
            vmem((n, rows, columns), bf16),
            vmem((columns, 2 * lanes), bf16),
            vmem((lanes, columns), bf16),
            vmem((n, rows, lanes), bf16),
            vmem((n, rows, 2 * lanes), bf16),
            vmem((2, n, rows, columns // 2), bf16),
            vmem((2, n, rows, columns // 2), bf16),
            vmem((2, rows, columns // 2), f32),
            vmem((rows, columns), f32),
            vmem((n, 2, 2, quarter, 2 * lanes), bf16),
            vmem((n, 2, quarter, 2 * lanes), bf16),
            vmem((lanes, columns), bf16),
            vmem((lanes // 2, columns), bf16),
            dma((4,)),
        ]
        + ring
        + [dma((n,))] * 4
        + [dma((2,))] * 2,
        compiler_params=kernel_params(5),
        name="mlp_and_back",
    )(ob, w_out, x_own, gain, weights, w_down, seed, seed_own)


class Spread:
    def __init__(self, n, pieces, out, sems):
        self.n, self.pieces, self.out = n, pieces, out
        self.s_blk, self.r_blk, self.s_x, self.r_x, self.s_c, self.r_c = sems
        self.grp, self.me = lax.axis_index("grp"), lax.axis_index("blk")
        self.over, self.core, self.grp_x, self.grp_c = team(self.grp)

    def first(self, k):
        to = (self.me + k) % self.n
        place = self.out.at[self.me, 2 * self.core + self.over]
        return push(
            self.pieces.at[to], place, self.s_blk.at[k], self.r_blk.at[k], (self.grp, to)
        )

    def own(self, sem):
        place = self.out.at[self.me, 2 * self.core + self.over]
        return pltpu.make_async_copy(self.pieces.at[self.me], place, sem)

    def to_x(self, k, own=False):
        piece = self.out.at[(self.me - k + self.n) % self.n, 2 * self.core + self.over]
        source = self.pieces.at[self.me] if own else piece
        return push(source, piece, self.s_x.at[k], self.r_x.at[k], (self.grp_x, self.me))

    def to_core(self, k, far, own=False):
        over = 1 - self.over if far else self.over
        piece = self.out.at[(self.me - k + self.n) % self.n, 2 * self.core + over]
        source = self.pieces.at[self.me] if own else piece
        sems = (self.s_c.at[int(far), k], self.r_c.at[int(far), k])
        return push(source, piece, *sems, (self.grp_c, self.me))

    def pass_own(self):
        self.to_x(0, True).start()
        self.to_core(0, False, True).start()

    def pass_on(self, k):
        self.first(k).wait_recv()
        self.to_x(k).start()
        self.to_core(k, False).start()

    def pass_far(self, k):
        self.to_x(k).wait_recv()
        self.to_core(k, True).start()

    def arrived(self, k):
        for far in (False, True):
            self.to_core(k, far).wait_recv()

    def finish(self):
        def body(k, _):
            pl.when(k > 0)(self.first(k).wait_send)
            self.to_x(k).wait_send()
            for far in (False, True):
                self.to_core(k, far).wait_send()
            return 0

        lax.fori_loop(0, self.n, body, 0)


def each(count, body, low=0):
    lax.fori_loop(low, count, lambda k, _: (body(k), 0)[1], 0)


def spread_sems(n):
    dma = pltpu.SemaphoreType.DMA
    return [dma((n,)), dma((n,)), dma((n,)), dma((n,)), dma((2, n)), dma((2, n))]


def team_and_ring(n):
    grp, me = lax.axis_index("grp"), lax.axis_index("blk")
    _, _, grp_x, grp_c = team(grp)
    return [(grp, (me + k) % n) for k in range(1, n)] + [(grp_x, me), (grp_c, me)]


def fill_row(row, gains_all, which, share):
    for block in range(gains_all.shape[0]):
        row[:, block * share : (block + 1) * share] = gains_all[block, which : which + 1, :]


def turned(value, cosine, sine_part):
    half_size = HEAD // 2
    swapped = jnp.concatenate([value[:, half_size:], value[:, :half_size]], axis=1)
    return value * cosine + swapped * sine_part


def mark_places(n, doc_lens, rows, first_key, query_place, key_place):
    place = ring_place(lax.axis_index("blk"), n)
    for slot in range(n):
        offset = (slot + 1) // 2 * (1 if slot % 2 == 0 else -1)
        first_row = at_offset(place, offset, n) * rows
        part = slice(slot * rows, (slot + 1) * rows)
        here = first_row + lax.broadcasted_iota(jnp.int32, (rows, 1), 0)
        query_place[part, :] = here
        key_place[:, part] = first_row + lax.broadcasted_iota(jnp.int32, (1, rows), 1)
        start = jnp.int32(0)
        found = jnp.zeros((rows, 1), jnp.int32)
        for index in range(doc_lens.shape[1]):
            found = jnp.maximum(found, jnp.where(here >= start, start, 0))
            start = start + doc_lens[0, index]
        first_key[part, :] = found


def attend_kernel(
    n,
    heads,
    doc_lens,
    x_own,
    freqs,
    norm_attn,
    norm_mlp,
    w_qkv,
    w_gate,
    w_up,
    seed_own,
    gains_all,
    columns_qkv,
    normed,
    qkv,
    attended,
    attended_b,
    log_total,
    cosine,
    sine_part,
    gate_up,
    seed,
    x_all,
    gain_row,
    gains,
    raw_qkv,
    raw_gate,
    raw_up,
    slab_qkv,
    slab_gate_up,
    first_key,
    query_place,
    key_place,
    local,
    s_gain,
    r_gain,
    s_x,
    r_x,
    s_seed,
    r_seed,
    *spread_all,
):
    f32, bf16 = jnp.float32, jnp.bfloat16
    grp, me = lax.axis_index("grp"), lax.axis_index("blk")
    _, ends = ring_ends(n)
    rows, columns = x_own.shape
    spread_qkv = Spread(n, slab_qkv, columns_qkv, spread_all[:6])
    spread_gu = Spread(n, slab_gate_up, gate_up, spread_all[6:])
    over, core, _, _ = team(grp)
    quarter = slab_qkv.shape[1]
    own_rows = pl.ds(pl.multiple_of((2 * core + over) * quarter, quarter), quarter)
    loads = [
        pltpu.make_async_copy(weight.at[own_rows], raw, local.at[index])
        for index, (weight, raw) in enumerate(
            ((w_qkv, raw_qkv), (w_gate, raw_gate), (w_up, raw_up))
        )
    ]
    for load in loads:
        load.start()
    x_all[0] = x_own[...]
    gains[...] = jnp.zeros_like(gains)
    gains[0:1, :] = norm_attn[...].astype(f32)
    gains[1:2, :] = norm_mlp[...].astype(f32)
    gains_all[me] = gains[...]
    greet(team_and_ring(n))

    def gain(k):
        return push(gains, gains_all.at[me], s_gain.at[k], r_gain.at[k], (grp, (me + k) % n))

    each(n, lambda k: gain(k).start(), 1)
    x_ring = Gather(n, x_all, s_x, r_x, ends)
    x_ring.start()
    share = heads * HEAD
    loads[0].wait()
    for to in range(n):
        for part in range(3):
            slab_qkv[to, :, part * share : (part + 1) * share] = raw_qkv[
                :, (part * n + to) * share : (part * n + to + 1) * share
            ]
    near_qkv = spread_qkv.own(local.at[3])
    near_qkv.start()
    each(n, lambda k: spread_qkv.first(k).start(), 1)
    spread_qkv.pass_own()
    units = raw_gate.shape[1] // n
    loads[1].wait()
    loads[2].wait()
    for to in range(n):
        lane = slice(to * units, (to + 1) * units)
        slab_gate_up[to] = jnp.concatenate(
            [raw_gate[:, lane].astype(f32), raw_up[:, lane].astype(f32)], axis=1
        ).astype(bf16)
    near_gu = spread_gu.own(local.at[4])
    near_gu.start()
    mark_places(n, doc_lens, rows, first_key, query_place, key_place)

    def norm(slot):
        value = x_all[slot].astype(f32)
        inv = lax.rsqrt(jnp.mean(value * value, axis=-1, keepdims=True) + EPS)
        normed[slot] = (value * inv * gain_row[...]).astype(bf16)

    each(n, lambda k: gain(k).wait_recv(), 1)
    fill_row(gain_row, gains_all, 0, columns // n)

    def table(slot):
        at = pl.ds(pl.multiple_of(slot * rows, rows), rows)
        angle = (query_place[at, :] - first_key[at, :]).astype(f32) * freqs[...]
        lane = lax.broadcasted_iota(jnp.int32, (rows, HEAD), 1)
        sine = jnp.sin(angle)
        cosine[at, :] = jnp.cos(angle)
        sine_part[at, :] = jnp.where(lane < HEAD // 2, -sine, sine)

    def arrive(t):
        pl.when(t > 0)(lambda: x_ring.advance(t - 1))
        low = jnp.maximum(2 * t - 1, 0)
        each(jnp.minimum(2 * t + 1, n), norm, low)
        each(jnp.minimum(2 * t + 1, n), table, low)
        pl.when(t == 2)(lambda: each(n, spread_qkv.pass_on, 1))
        pl.when(t == 3)(lambda: each(n, spread_qkv.pass_far))

        @pl.when(t == 2)
        def _():
            each(n, lambda k: spread_gu.first(k).start(), 1)
            spread_gu.pass_own()


    each(n // 2 + 1, arrive)
    seed_ring = Gather(n, seed, s_seed, r_seed, ends, seed_own)
    each(n, spread_gu.pass_on, 1)
    seed_ring.start()
    each(n, spread_qkv.arrived)
    near_qkv.wait()


    head_lanes = heads * HEAD
    pair = 2 * rows

    def project(i):
        both = normed[pl.ds(2 * i, 2)].reshape(pair, columns)
        result = dot_f32(both, columns_qkv[...].reshape(columns, 3 * head_lanes))
        at = pl.ds(pl.multiple_of(i * pair, pair), pair)
        table_c, table_s = cosine[at, :], sine_part[at, :]
        for piece in range(3 * heads):
            lane = slice(piece * HEAD, (piece + 1) * HEAD)
            value = result[:, lane]
            if piece < 2 * heads:
                value = turned(value, table_c, table_s)
            qkv[at, lane] = value.astype(bf16)

    each(n // 2, project)


    def tile(i):
        for head in range(heads):
            lane = slice(head * HEAD, (head + 1) * HEAD)
            at = pl.ds(pl.multiple_of(i * pair, pair), pair)
            keys = qkv[:, head_lanes + head * HEAD : head_lanes + (head + 1) * HEAD]
            values = qkv[:, 2 * head_lanes + head * HEAD : 2 * head_lanes + (head + 1) * HEAD]
            scores = nt_dot(qkv[at, lane], keys) * HEAD ** (-0.5)
            allowed = (key_place[...] >= first_key[at, :]) & (key_place[...] <= query_place[at, :])
            scores = jnp.where(allowed, scores, NEGATIVE)
            peak = jnp.max(scores, axis=-1, keepdims=True)
            raw = jnp.exp(scores - peak)
            total = jnp.sum(raw, axis=-1, keepdims=True)
            out = dot_f32(raw.astype(bf16), values) / total
            attended[at, lane] = out
            attended_b[at, lane] = out.astype(bf16)
            log_total[head, at, :] = peak + jnp.log(total)
        seed_ring.advance(i)

    each(n // 2, tile)
    each(n, spread_gu.pass_far)
    each(n, spread_gu.arrived)
    near_gu.wait()
    for spread in (spread_qkv, spread_gu):
        spread.finish()
    each(n, lambda k: gain(k).wait_send(), 1)
    x_ring.finish()
    seed_ring.finish()


def attend(doc_lens, x_own, norm_attn, norm_mlp, w_qkv, w_gate, w_up, seed_own):
    n = lax.axis_size("blk")
    rows, columns = x_own.shape
    seq = n * rows
    lanes = w_qkv.shape[1] // n
    quarter = w_qkv.shape[0] // 4
    both = 2 * w_gate.shape[1] // n
    head_lanes = lanes // 3
    heads = head_lanes // HEAD
    share = norm_attn.shape[0]
    f32, bf16, i32 = jnp.float32, jnp.bfloat16, jnp.int32
    vmem, dma = pltpu.VMEM, pltpu.SemaphoreType.DMA
    in_vmem, anywhere = pl.BlockSpec(memory_space=vmem), pl.BlockSpec(memory_space=pl.ANY)
    half_freqs = np.exp(
        np.arange(HEAD // 2, dtype=np.float32) * np.float32(-2.0 * math.log(10000.0) / HEAD)
    )
    freqs = jnp.asarray(np.concatenate([half_freqs, half_freqs])[None].astype(np.float32))
    return pl.pallas_call(
        functools.partial(attend_kernel, n, heads),
        out_shape=(
            jax.ShapeDtypeStruct((n, 8, share), f32),
            jax.ShapeDtypeStruct((n, 4, quarter, lanes), bf16),
            jax.ShapeDtypeStruct((n, rows, columns), bf16),
            jax.ShapeDtypeStruct((seq, lanes), bf16),
            jax.ShapeDtypeStruct((seq, head_lanes), f32),
            jax.ShapeDtypeStruct((seq, head_lanes), bf16),
            jax.ShapeDtypeStruct((heads, seq, 1), f32),
            jax.ShapeDtypeStruct((seq, HEAD), f32),
            jax.ShapeDtypeStruct((seq, HEAD), f32),
            jax.ShapeDtypeStruct((n, 4, quarter, both), bf16),
            jax.ShapeDtypeStruct((n, rows, columns), bf16),
        ),
        in_specs=[pl.BlockSpec(memory_space=pltpu.SMEM)] + [in_vmem] * 4 + [anywhere] * 4,
        out_specs=[in_vmem] * 9 + [anywhere] * 2,
        scratch_shapes=[
            vmem((n, rows, columns), bf16),
            vmem((1, columns), f32),
            vmem((8, share), f32),
            vmem((quarter, n * lanes), bf16),
            vmem((quarter, w_gate.shape[1]), bf16),
            vmem((quarter, w_gate.shape[1]), bf16),
            vmem((n, quarter, lanes), bf16),
            vmem((n, quarter, both), bf16),
            vmem((seq, 1), i32),
            vmem((seq, 1), i32),
            vmem((1, seq), i32),
            dma((5,)),
            dma((n,)),
            dma((n,)),
        ]
        + [dma((n // 2, 2, 2))] * 4
        + spread_sems(n) * 2,
        compiler_params=kernel_params(0),
        name="attend",
    )(
        doc_lens,
        x_own,
        freqs,
        norm_attn.reshape(1, share),
        norm_mlp.reshape(1, share),
        w_qkv,
        w_gate,
        w_up,
        seed_own,
    )


def finish_kernel(
    n,
    heads,
    qkv,
    attended,
    dattended,
    log_total,
    cosine,
    sine_part,
    doc_lens,
    x_own,
    gain,
    dresid,
    terms_two,
    out_grad,
    weights,
    normed_hbm,
    gate_up_sum,
    down_sum,
    x_grad,
    gain_grads,
    wide_gate_up,
    wide_qkv,
    tall_down,
    tall_out,
    normed,
    columns_qkv,
    dqkv,
    dkeys,
    dvalues,
    first_key,
    query_place,
    key_place,
    held,
    terms,
    wide,
    wide_c,
    wide_x,
    out_c,
    out_x,
    gain_slabs,
    gain_heard,
    gain_team,
    load_sem,
    s_ring,
    r_ring,
    s_wc,
    r_wc,
    s_wx,
    r_wx,
    s_tall,
    r_tall,
    s_gain,
    r_gain,
    *spread_all,
):
    f32, bf16 = jnp.float32, jnp.bfloat16
    grp, me = lax.axis_index("grp"), lax.axis_index("blk")
    over, core, grp_x, grp_c = team(grp)
    _, ends = ring_ends(n)
    rows, columns = x_own.shape
    half = columns // 2
    lanes = wide.shape[4]
    quarter = wide.shape[3]
    load_normed = pltpu.make_async_copy(normed_hbm, normed, load_sem.at[0])
    load_qkv = pltpu.make_async_copy(weights, columns_qkv, load_sem.at[1])
    load_normed.start()
    load_qkv.start()
    spread_gu = Spread(n, gate_up_sum, wide_gate_up, spread_all[:6])
    spread_qkv = Spread(n, wide_x, wide_qkv, spread_all[6:])
    near_gu = spread_gu.own(load_sem.at[2])
    near_gu.start()
    greet(team_and_ring(n))

    down_own = pltpu.make_async_copy(down_sum, tall_down.at[2 * core + over], load_sem.at[3])
    down_own.start()
    down_place = tall_down.at[2 * core + over]
    down_x = push(down_sum, down_place, s_tall.at[0], r_tall.at[0], (grp_x, me))
    down_c = push(down_sum, down_place, s_tall.at[1], r_tall.at[1], (grp_c, me))
    far_place = tall_down.at[2 * core + 1 - over]
    down_far = push(far_place, far_place, s_tall.at[2], r_tall.at[2], (grp_c, me))
    out_one = push(out_grad.at[1 - core], out_c, s_tall.at[3], r_tall.at[3], (grp_c, me))
    out_two = push(out_c.at[1 - over], out_x, s_tall.at[4], r_tall.at[4], (grp_x, me))
    out_place = tall_out.at[2 * core + over]
    out_own = pltpu.make_async_copy(out_x, out_place, load_sem.at[4])
    out_to_x = push(out_x, out_place, s_tall.at[5], r_tall.at[5], (grp_x, me))
    out_to_c = push(out_x, out_place, s_tall.at[6], r_tall.at[6], (grp_c, me))
    out_far_place = tall_out.at[2 * core + 1 - over]
    out_far = push(out_far_place, out_far_place, s_tall.at[7], r_tall.at[7], (grp_c, me))
    out_one.start()
    each(n, lambda k: spread_gu.first(k).start(), 1)
    spread_gu.pass_own()
    down_x.start()
    down_c.start()

    mark_places(n, doc_lens, rows, first_key, query_place, key_place)
    pair = 2 * rows
    head_lanes = heads * HEAD
    scale = HEAD ** (-0.5)

    def unturned(value, at):
        return turned(value, cosine[at, :], -sine_part[at, :]).astype(bf16)

    def tile(i, head):
        at = pl.ds(pl.multiple_of(i * pair, pair), pair)
        lane = slice(head * HEAD, (head + 1) * HEAD)
        query = qkv[at, lane]
        keys = qkv[:, head_lanes + head * HEAD : head_lanes + (head + 1) * HEAD]
        values = qkv[:, 2 * head_lanes + head * HEAD : 2 * head_lanes + (head + 1) * HEAD]
        grad = dattended[at, lane]
        delta = jnp.sum(grad.astype(f32) * attended[at, lane], axis=-1, keepdims=True)
        scores = nt_dot(query, keys) * scale
        allowed = (key_place[...] >= first_key[at, :]) & (key_place[...] <= query_place[at, :])
        probs = jnp.where(allowed, jnp.exp(scores - log_total[head, at, :]), 0.0)
        dscores = (probs * (nt_dot(grad, values) - delta)).astype(bf16)
        dqkv[2 * i : 2 * i + 2, :, lane] = unturned(dot_f32(dscores, keys) * scale, at).reshape(
            2, rows, HEAD
        )
        more_keys = dot_t(dscores, query)
        more_values = dot_t(probs.astype(bf16), grad)
        if i == 0:
            dkeys[...] = more_keys
            dvalues[...] = more_values
        else:
            dkeys[...] += more_keys
            dvalues[...] += more_values

    for head in range(heads):
        for i in range(n // 2):
            tile(i, head)
        everything = slice(0, n * rows)
        lane = slice(head_lanes + head * HEAD, head_lanes + (head + 1) * HEAD)
        dqkv[:, :, lane] = unturned(dkeys[...] * scale, everything).reshape(n, rows, HEAD)
        lane = slice(2 * head_lanes + head * HEAD, 2 * head_lanes + (head + 1) * HEAD)
        dqkv[:, :, lane] = dvalues[...].astype(bf16).reshape(n, rows, HEAD)
    load_qkv.wait()

    def term(step, way):
        return nt_dot(dqkv[behind(step, way, n)], columns_qkv[way * half : (way + 1) * half, :])

    ring = Scatter(n, held, terms, s_ring, r_ring, ends, term)

    def copy_c(k):
        tile = (me + k) % n
        return push(wide.at[tile, 1 - core], wide_c.at[tile], s_wc.at[k], r_wc.at[k], (grp_c, me))

    def copy_x(k):
        tile = (me + k) % n
        return push(
            wide_c.at[tile, 1 - over], wide_x.at[tile], s_wx.at[k], r_wx.at[k], (grp_x, me)
        )

    def grad(k):
        tile = (me + k) % n
        at = pl.multiple_of(tile * 4 * quarter, 4 * quarter)
        left = normed[:, :, pl.ds(at, 4 * quarter)].reshape(-1, 4 * quarter)
        grad_rows = dot_t(left, dqkv[...].reshape(-1, lanes)).astype(bf16)
        wide[tile] = grad_rows.reshape(2, 2, quarter, lanes)
        copy_c(k).start()

    def pass_x(k):
        tile = (me + k) % n
        copy_c(k).wait_recv()
        wide_c[tile, 1 - over] = (
            wide[tile, core, 1 - over].astype(f32) + wide_c[tile, 1 - over].astype(f32)
        ).astype(bf16)
        copy_x(k).start()

    def take(k):
        tile = (me + k) % n
        copy_x(k).wait_recv()
        wide_x[tile] = (
            wide[tile, core, over].astype(f32)
            + wide_c[tile, over].astype(f32)
            + wide_x[tile].astype(f32)
        ).astype(bf16)

    def take_and_push(k):
        take(k)
        spread_qkv.first(k).start()

    ring.step(0)
    load_normed.wait()

    def grads(i):
        k = (i + 1) % n
        grad(k)
        pl.when(i > 0)(lambda: pass_x(i))

    each(n, grads)
    pass_x(0)
    out_one.wait_recv()
    out_c[1 - over] = (
        out_grad[core, 1 - over].astype(f32) + out_c[1 - over].astype(f32)
    ).astype(bf16)
    out_two.start()

    def turn(k):
        pl.when(k < n - 2)(lambda: ring.step(k + 1))
        each(jnp.minimum(2 * k + 3, n), spread_gu.pass_on, jnp.minimum(2 * k + 1, n))
        pl.when(k < n - 1)(lambda: take_and_push(k + 1))

        @pl.when(k == n - 2)
        def _():
            take(0)
            spread_qkv.pass_own()

    each(n - 1, turn)
    near_qkv = spread_qkv.own(load_sem.at[5])
    near_qkv.start()

    x_float = x_own[...].astype(f32)
    inv = lax.rsqrt(jnp.mean(x_float * x_float, axis=-1, keepdims=True) + EPS)
    for way in range(2):
        terms[way] = ring.result(way)
    dnormed = jnp.concatenate([terms[0], terms[1]], axis=1)
    terms_one = jnp.sum(dnormed * x_float * inv, axis=0, keepdims=True)
    share = columns // n
    for block in range(n):
        gain_slabs[block] = jnp.zeros_like(gain_slabs[block])
        lane = slice(block * share, (block + 1) * share)
        gain_slabs[block, 0:1, :] = terms_one[:, lane]
        gain_slabs[block, 1:2, :] = terms_two[:, lane]

    def gain_blk(k):
        to = (me + k) % n
        return push(gain_slabs.at[to], gain_heard.at[k], s_gain.at[k], r_gain.at[k], (grp, to))

    each(n, lambda k: gain_blk(k).start(), 1)
    a_one = dnormed * gain[...]
    x_grad[...] = (
        dresid[...]
        + inv * a_one
        - x_float * inv**3 * jnp.mean(a_one * x_float, axis=-1, keepdims=True)
    ).astype(bf16)
    gain_heard[0] = gain_slabs[me]
    each(n, lambda k: gain_blk(k).wait_recv(), 1)
    gain_team[0] = jnp.sum(gain_heard[...], axis=0)
    gain_c = push(gain_team.at[0], gain_team.at[1], s_gain.at[n], r_gain.at[n], (grp_c, me))
    gain_c.start()
    out_two.wait_recv()
    out_x[...] = (
        out_grad[core, over].astype(f32) + out_c[over].astype(f32) + out_x[...].astype(f32)
    ).astype(bf16)
    out_own.start()
    out_to_x.start()
    out_to_c.start()
    each(n, spread_qkv.pass_on, 1)
    each(n, spread_gu.pass_far)
    down_x.wait_recv()
    down_far.start()
    gain_c.wait_recv()
    gain_team[2] = gain_team[0] + gain_team[1]
    gain_x = push(
        gain_team.at[2], gain_team.at[3], s_gain.at[n + 1], r_gain.at[n + 1], (grp_x, me)
    )
    gain_x.start()
    out_to_x.wait_recv()
    out_far.start()
    each(n, spread_qkv.pass_far)
    gain_x.wait_recv()
    gain_grads[...] = gain_team[2] + gain_team[3]
    near_gu.wait()
    near_qkv.wait()
    each(n, spread_gu.arrived)
    each(n, spread_qkv.arrived)
    spread_gu.finish()
    spread_qkv.finish()
    ring.finish()
    down_own.wait()
    out_own.wait()
    for copy in (down_c, down_far, out_to_c, out_far):
        copy.wait()
    for copy in (down_x, out_one, out_two, out_to_x, gain_c, gain_x):
        copy.wait_send()

    def sent(k):
        copy_c(k).wait_send()
        copy_x(k).wait_send()
        pl.when(k > 0)(gain_blk(k).wait_send)

    each(n, sent)


def finish(
    attention, x_own, gain, dresid, terms_two, out_grad, weights, normed, gate_up_sum, down_sum
):
    n, rows, columns = normed.shape
    seq, lanes = attention[0].shape
    heads = lanes // (3 * HEAD)
    quarter = columns // (4 * n)
    share = columns // n
    f32, bf16 = jnp.float32, jnp.bfloat16
    vmem, dma = pltpu.VMEM, pltpu.SemaphoreType.DMA
    in_vmem, anywhere = pl.BlockSpec(memory_space=vmem), pl.BlockSpec(memory_space=pl.ANY)
    out_rows = out_grad.shape[0] // 4
    return pl.pallas_call(
        functools.partial(finish_kernel, n, heads),
        out_shape=(
            jax.ShapeDtypeStruct((rows, columns), bf16),
            jax.ShapeDtypeStruct((8, share), f32),
            jax.ShapeDtypeStruct((n, 4) + gate_up_sum.shape[1:], bf16),
            jax.ShapeDtypeStruct((n, 4, quarter, lanes), bf16),
            jax.ShapeDtypeStruct((4,) + down_sum.shape, bf16),
            jax.ShapeDtypeStruct((4, out_rows, columns), bf16),
        ),
        in_specs=[in_vmem] * 6
        + [pl.BlockSpec(memory_space=pltpu.SMEM)]
        + [in_vmem] * 5
        + [anywhere] * 4,
        out_specs=[in_vmem] * 2 + [anywhere] * 4,
        scratch_shapes=[
            vmem((n, rows, columns), bf16),
            vmem((columns, lanes), bf16),
            vmem((n, rows, lanes), bf16),
            vmem((seq, HEAD), f32),
            vmem((seq, HEAD), f32),
            vmem((seq, 1), jnp.int32),
            vmem((seq, 1), jnp.int32),
            vmem((1, seq), jnp.int32),
            vmem((2, n, rows, columns // 2), bf16),
            vmem((2, rows, columns // 2), f32),
            vmem((n, 2, 2, quarter, lanes), bf16),
            vmem((n, 2, quarter, lanes), bf16),
            vmem((n, quarter, lanes), bf16),
            vmem((2, out_rows, columns), bf16),
            vmem((out_rows, columns), bf16),
            vmem((n, 8, share), f32),
            vmem((n, 8, share), f32),
            vmem((4, 8, share), f32),
            dma((6,)),
        ]
        + [dma((n - 1, 2, 2))] * 2
        + [dma((n,))] * 4
        + [dma((8,))] * 2
        + [dma((n + 2,))] * 2
        + spread_sems(n) * 2,
        compiler_params=kernel_params(6),
        name="finish",
    )(
        *attention,
        x_own,
        gain,
        dresid,
        terms_two,
        out_grad.reshape(2, 2, out_rows, columns),
        weights,
        normed,
        gate_up_sum,
        down_sum,
    )


def assemble_kernel(n, units, lanes, head_lanes, qkv, gate_up, down, out, *grads):
    grad_qkv, grad_out, grad_gate, grad_up, grad_down = grads
    f32 = jnp.float32
    for source in range(n):
        for part in range(3):
            first = (part * n + source) * head_lanes
            grad_qkv[:, first : first + head_lanes] = qkv[
                source, :, part * head_lanes : (part + 1) * head_lanes
            ].astype(f32)
        first = source * units
        grad_gate[:, first : first + units] = gate_up[source, :, :units].astype(f32)
        grad_up[:, first : first + units] = gate_up[source, :, lanes : lanes + units].astype(f32)
    grad_out[...] = out[...].astype(f32)
    grad_down[...] = down[...].astype(f32)


def assemble(qkv, gate_up, down, out, units, steps=4):
    n, rows, qkv_lanes = qkv.shape
    columns = down.shape[1]
    lanes = gate_up.shape[2] // 2
    head_lanes = qkv_lanes // 3
    step = rows // steps
    down_step = units // steps
    f32 = jnp.float32

    def wide(width):
        return pl.BlockSpec((n, step, width), lambda i: (0, i, 0))

    def flat(height, width):
        return pl.BlockSpec((height, width), lambda i: (i, 0))

    return pl.pallas_call(
        functools.partial(assemble_kernel, n, units, lanes, head_lanes),
        grid=(steps,),
        out_shape=(
            jax.ShapeDtypeStruct((rows, n * qkv_lanes), f32),
            jax.ShapeDtypeStruct((rows, columns), f32),
            jax.ShapeDtypeStruct((rows, n * units), f32),
            jax.ShapeDtypeStruct((rows, n * units), f32),
            jax.ShapeDtypeStruct((units, columns), f32),
        ),
        in_specs=[
            wide(qkv_lanes),
            wide(2 * lanes),
            flat(down_step, columns),
            flat(out.shape[0] // steps, columns),
        ],
        out_specs=[
            flat(step, n * qkv_lanes),
            flat(step, columns),
            flat(step, n * units),
            flat(step, n * units),
            flat(down_step, columns),
        ],
        compiler_params=pltpu.CompilerParams(vmem_limit_bytes=VMEM_BYTES),
        name="assemble",
    )(qkv, gate_up, down, out)


def per_device(block_input, doc_lens, norm_attn, w_qkv, w_out, norm_mlp, w_gate, w_up, w_down, cot):
    n = lax.axis_size("blk")
    tok_rows, width = block_input.shape[1:]
    seq = tok_rows * n
    heads = HEADS // n
    head_lanes = heads * HEAD
    qkv_lanes = 3 * head_lanes
    units = w_down.shape[0]
    lanes = units
    quarter = w_qkv.shape[0] // 4
    (
        gains_all,
        qkv_columns,
        normed_one,
        qkv,
        attended,
        attended_b,
        log_total,
        cosine,
        sine_part,
        gate_up,
        seed,
    ) = attend(doc_lens, block_input[0], norm_attn, norm_mlp, w_qkv, w_gate, w_up, cot[0])
    gain_one = gains_all[:, 0].reshape(1, width)
    gain_two = gains_all[:, 1].reshape(1, width)
    qkv_columns = qkv_columns.reshape(width, qkv_lanes)
    gate_up = gate_up.reshape(width, 2 * lanes)
    block_out, dresid, dattended, terms_two, gate_up_sum, down_sum, out_grad = mlp_and_back(
        attended_b.reshape(n, tok_rows, head_lanes),
        w_out,
        block_input[0],
        gain_two,
        gate_up,
        lanes,
        w_down,
        seed,
        cot[0],
    )
    x_grad, gain_grads, wide_gate_up, wide_qkv, tall_down, tall_out = finish(
        (
            qkv,
            attended,
            dattended.reshape(seq, head_lanes),
            log_total,
            cosine,
            sine_part,
            doc_lens,
        ),
        block_input[0],
        gain_one,
        dresid,
        terms_two,
        out_grad,
        qkv_columns,
        normed_one,
        gate_up_sum,
        down_sum,
    )
    shard_rows = 4 * quarter
    grad_qkv, grad_out, grad_gate, grad_up, grad_down = assemble(
        wide_qkv.reshape(n, shard_rows, qkv_lanes),
        wide_gate_up.reshape(n, shard_rows, 2 * lanes),
        tall_down.reshape(lanes, width),
        tall_out.reshape(head_lanes, width),
        units,
    )
    return (
        block_out[None],
        x_grad[None],
        gain_grads[0],
        grad_qkv,
        grad_out,
        gain_grads[1],
        grad_gate,
        grad_up,
        grad_down,
    )


def body_for(mesh):
    return per_device if HEADS % mesh.shape["blk"] == 0 else per_device_gather


def solution(mesh):
    return jax.shard_map(
        body_for(mesh),
        mesh=mesh,
        in_specs=(
            P("grp", "blk", None),
            P("grp", None),
            P("blk"),
            P("blk", None),
            P("blk", None),
            P("blk"),
            P("blk", None),
            P("blk", None),
            P("blk", None),
            P("grp", "blk", None),
        ),
        out_specs=(
            P("grp", "blk", None),
            P("grp", "blk", None),
            P("blk"),
            P("blk", None),
            P("blk", None),
            P("blk"),
            P("blk", None),
            P("blk", None),
            P("blk", None),
        ),
        check_vma=False,
    )
```

```python
import functools
import math

import jax
import jax.numpy as jnp
import numpy as np
from jax import lax
from jax.experimental import pallas as pl
from jax.experimental.pallas import tpu as pltpu
from jax.sharding import PartitionSpec as P

HEADS = 16
HEAD = 128


EPS = 1e-05
NEGATIVE = -1e30


def angle_tables(places):
    half_size = HEAD // 2
    freqs = jnp.exp(jnp.arange(half_size, dtype=jnp.float32) * (-2.0 * math.log(10000.0) / HEAD))
    angles = places.astype(jnp.float32)[:, None] * freqs
    return (jnp.cos(angles)[:, None, :], jnp.sin(angles)[:, None, :])


def rotate(tensor, cosine, sine_part):
    half_size = HEAD // 2
    first_half = tensor[..., :half_size]
    second_half = tensor[..., half_size:]
    return jnp.concatenate(
        [
            first_half * cosine - second_half * sine_part,
            second_half * cosine + first_half * sine_part,
        ],
        axis=-1,
    )


def unrotate(tensor, cosine, sine_part):
    half_size = HEAD // 2
    first_half = tensor[..., :half_size]
    second_half = tensor[..., half_size:]
    return jnp.concatenate(
        [
            first_half * cosine + second_half * sine_part,
            second_half * cosine - first_half * sine_part,
        ],
        axis=-1,
    )


def segment_of(places, starts):
    return jnp.sum((starts[None, :] <= places[:, None]).astype(jnp.int32), axis=1) - 1


def start_of(places, starts):
    return jnp.max(jnp.where(starts[None, :] <= places[:, None], starts[None, :], 0), axis=1)


def contract_rows(left, right):
    return lax.dot_general(
        left, right, (((1,), (1,)), ((), ())), preferred_element_type=jnp.float32
    )


def weight_term(left, right):

    def term(start, count):
        return lax.dot_general(
            left, right, (((0,), (0,)), ((), ())), preferred_element_type=jnp.float32
        )

    return term


def shard_grad(term_fn, shard_rows):
    shared = lax.psum_scatter(
        term_fn(jnp.int32(0), shard_rows * lax.axis_size("blk")).astype(jnp.bfloat16),
        "blk",
        scatter_dimension=0,
        tiled=True,
    )
    return lax.psum(shared, "grp").astype(jnp.float32)


def per_device_gather(block_input, doc_lens, norm_attn, w_qkv, w_out, norm_mlp, w_gate, w_up, w_down, cot):
    tok_rows = block_input.shape[1]
    width = block_input.shape[2]
    score_scale = HEAD ** (-0.5)
    shards = (norm_attn, w_qkv, w_out, norm_mlp, w_gate, w_up, w_down)
    gathered = (
        lax.all_gather(shards[0], "blk", axis=0, tiled=True),
        lax.all_gather(shards[1], "blk", axis=0, tiled=True),
        lax.all_gather(shards[2], "blk", axis=0, tiled=True),
        lax.all_gather(shards[3], "blk", axis=0, tiled=True),
        lax.all_gather(shards[4], "blk", axis=0, tiled=True),
        lax.all_gather(shards[5], "blk", axis=0, tiled=True),
        lax.all_gather(shards[6], "blk", axis=0, tiled=True),
    )
    gain_one, weight_qkv, weight_out, gain_two, weight_gate, weight_up, weight_down = gathered
    place_rows = lax.axis_index("blk") * tok_rows + jnp.arange(tok_rows, dtype=jnp.int32)
    lengths = doc_lens[0]
    starts = jnp.cumsum(lengths) - lengths
    query_seg = segment_of(place_rows, starts)
    cosine, sine_part = angle_tables(place_rows - start_of(place_rows, starts))
    x_float = block_input[0].astype(jnp.float32)
    inv_one = lax.rsqrt(jnp.mean(x_float * x_float, axis=-1, keepdims=True) + EPS)
    normed_one = (x_float * inv_one * gain_one.astype(jnp.float32)).astype(jnp.bfloat16)
    projected = jnp.dot(normed_one, weight_qkv, preferred_element_type=jnp.float32)
    heads_all = projected.reshape(tok_rows, 3, HEADS, HEAD)
    queries = rotate(heads_all[:, 0], cosine, sine_part).astype(jnp.bfloat16)
    keys_own = rotate(heads_all[:, 1], cosine, sine_part).astype(jnp.bfloat16)
    values_own = heads_all[:, 2].astype(jnp.bfloat16)

    def pair_mask(count):
        key_places = jnp.arange(count, dtype=jnp.int32)
        key_seg = segment_of(key_places, starts)
        return (query_seg[:, None] == key_seg[None, :]) & (
            key_places[None, :] <= place_rows[:, None]
        )

    piece = (
        lax.all_gather(keys_own, "blk", axis=0, tiled=True),
        lax.all_gather(values_own, "blk", axis=0, tiled=True),
    )
    count = piece[0].shape[0]
    row_peak = jnp.full((HEADS, tok_rows), NEGATIVE, jnp.float32)
    key_piece, value_piece = piece
    count = key_piece.shape[0]
    allowed = pair_mask(count)[None]
    scores = (
        jnp.einsum("qhd,khd->hqk", queries, key_piece, preferred_element_type=jnp.float32)
        * score_scale
    )
    scores = jnp.where(allowed, scores, NEGATIVE)
    new_peak = jnp.maximum(row_peak, jnp.max(scores, axis=-1))
    weights_now = jnp.where(allowed, jnp.exp(scores - new_peak[..., None]), 0.0)
    row_total = jnp.sum(weights_now, axis=-1)
    accum = jnp.einsum(
        "hqk,khd->hqd",
        weights_now.astype(jnp.bfloat16),
        value_piece,
        preferred_element_type=jnp.float32,
    )
    row_peak, row_total, accum = (new_peak, row_total, accum)
    log_total = row_peak + jnp.log(row_total)
    attended = (accum / row_total[..., None]).transpose(1, 0, 2)
    attended_b = attended.reshape(tok_rows, width).astype(jnp.bfloat16)
    resid = x_float + jnp.dot(attended_b, weight_out, preferred_element_type=jnp.float32)
    inv_two = lax.rsqrt(jnp.mean(resid * resid, axis=-1, keepdims=True) + EPS)
    normed_two = (resid * inv_two * gain_two.astype(jnp.float32)).astype(jnp.bfloat16)
    gate_proj = jnp.dot(normed_two, weight_gate, preferred_element_type=jnp.float32)
    up_proj = jnp.dot(normed_two, weight_up, preferred_element_type=jnp.float32)
    sigmoid_gate = jax.nn.sigmoid(gate_proj)
    swish = gate_proj * sigmoid_gate
    hidden = (swish * up_proj).astype(jnp.bfloat16)
    block_out = (resid + jnp.dot(hidden, weight_down, preferred_element_type=jnp.float32)).astype(
        jnp.bfloat16
    )
    again = (
        lax.all_gather(shards[0], "blk", axis=0, tiled=True),
        lax.all_gather(shards[1], "blk", axis=0, tiled=True),
        lax.all_gather(shards[2], "blk", axis=0, tiled=True),
        lax.all_gather(shards[3], "blk", axis=0, tiled=True),
        lax.all_gather(shards[4], "blk", axis=0, tiled=True),
        lax.all_gather(shards[5], "blk", axis=0, tiled=True),
        lax.all_gather(shards[6], "blk", axis=0, tiled=True),
    )
    back_gain_one, back_qkv, back_out, back_gain_two, back_gate, back_up, back_down = again
    seed = cot[0]
    seed_float = seed.astype(jnp.float32)
    dhidden = contract_rows(seed, back_down)
    dgate = (dhidden * up_proj * sigmoid_gate * (1.0 + gate_proj * (1.0 - sigmoid_gate))).astype(
        jnp.bfloat16
    )
    dup = (dhidden * swish).astype(jnp.bfloat16)
    dnormed_two = contract_rows(dgate, back_gate) + contract_rows(dup, back_up)
    a_two = dnormed_two * back_gain_two.astype(jnp.float32)
    dresid = (
        seed_float
        + inv_two * a_two
        - resid * inv_two**3 * jnp.mean(a_two * resid, axis=-1, keepdims=True)
    )
    dresid_b = dresid.astype(jnp.bfloat16)
    dattended = (
        contract_rows(dresid_b, back_out).astype(jnp.bfloat16).reshape(tok_rows, HEADS, HEAD)
    )
    delta = jnp.sum(dattended.astype(jnp.float32) * attended, axis=-1).T
    piece = (
        lax.all_gather(keys_own, "blk", axis=0, tiled=True),
        lax.all_gather(values_own, "blk", axis=0, tiled=True),
    )
    count = piece[0].shape[0]
    key_piece, value_piece = piece
    count = key_piece.shape[0]
    score_count = key_piece.shape[0]
    allowed = pair_mask(score_count)[None]
    scores = (
        jnp.einsum("qhd,khd->hqk", queries, key_piece, preferred_element_type=jnp.float32)
        * score_scale
    )
    probs = jnp.where(allowed, jnp.exp(scores - log_total[..., None]), 0.0)
    dprobs = jnp.einsum("qhd,khd->hqk", dattended, value_piece, preferred_element_type=jnp.float32)
    dscores = (probs * (dprobs - delta[..., None])).astype(jnp.bfloat16)
    probs, dscores = (probs, dscores)
    dquery_acc = score_scale * jnp.einsum(
        "hqk,khd->hqd", dscores, key_piece, preferred_element_type=jnp.float32
    )
    dkeys = score_scale * jnp.einsum(
        "hqk,qhd->khd", dscores, queries, preferred_element_type=jnp.float32
    )
    dvalues = jnp.einsum(
        "hqk,qhd->khd", probs.astype(jnp.bfloat16), dattended, preferred_element_type=jnp.float32
    )
    stacked = jnp.concatenate([dkeys.reshape(count, width), dvalues.reshape(count, width)], axis=1)
    grads_buffer = stacked
    dquery_acc, grads_buffer = (dquery_acc, grads_buffer)
    own_grads = lax.psum_scatter(
        grads_buffer.astype(jnp.bfloat16), "blk", scatter_dimension=0, tiled=True
    ).astype(jnp.float32)
    dkey = unrotate(own_grads[:, :width].reshape(tok_rows, HEADS, HEAD), cosine, sine_part)
    dvalue = own_grads[:, width:].reshape(tok_rows, HEADS, HEAD)
    dquery = unrotate(dquery_acc.transpose(1, 0, 2), cosine, sine_part)
    dqkv = (
        jnp.stack([dquery, dkey, dvalue], axis=1).reshape(tok_rows, 3 * width).astype(jnp.bfloat16)
    )
    dnormed_one = contract_rows(dqkv, back_qkv)
    a_one = dnormed_one * back_gain_one.astype(jnp.float32)
    x_grad = (
        dresid
        + inv_one * a_one
        - x_float * inv_one**3 * jnp.mean(a_one * x_float, axis=-1, keepdims=True)
    ).astype(jnp.bfloat16)
    width_rows = norm_attn.shape[0]
    gain_terms = jnp.stack(
        [
            jnp.sum(dnormed_one * x_float * inv_one, axis=0),
            jnp.sum(dnormed_two * resid * inv_two, axis=0),
        ],
        axis=1,
    )

    def gain_slice(start, count):
        return gain_terms

    grad_down = shard_grad(weight_term(hidden, seed), w_down.shape[0])
    grad_gate = shard_grad(weight_term(normed_two, dgate), width_rows)
    grad_up = shard_grad(weight_term(normed_two, dup), width_rows)
    grad_out = shard_grad(weight_term(attended_b, dresid_b), width_rows)
    grad_qkv = shard_grad(weight_term(normed_one, dqkv), width_rows)
    gain_grads = shard_grad(gain_slice, width_rows)
    return (
        block_out[None],
        x_grad[None],
        gain_grads[:, 0],
        grad_qkv,
        grad_out,
        gain_grads[:, 1],
        grad_gate,
        grad_up,
        grad_down,
    )


MESH = pl.DeviceIdType.MESH
VMEM_BYTES = 60 * 2**20


def ring_place(block, n):
    up, row = block // 2, block % 2
    return (1 - row) * up + row * (n - 1 - up)


def ring_block(place, n):
    back = place // (n // 2)
    return (1 - back) * 2 * place + back * (2 * (n - 1 - place) + 1)


def at_offset(place, offset, n):
    return ring_block((place + offset + n) % n, n)


def greet(devices):
    barrier = pltpu.get_barrier_semaphore()
    for device in devices:
        pl.semaphore_signal(barrier, inc=1, device_id=device, device_id_type=MESH)
    pl.semaphore_wait(barrier, len(devices))


def push(src, dst, send_sem, recv_sem, device):
    return pltpu.make_async_remote_copy(
        src_ref=src,
        dst_ref=dst,
        send_sem=send_sem,
        recv_sem=recv_sem,
        device_id=device,
        device_id_type=MESH,
    )


def kernel_params(collective_id):
    return pltpu.CompilerParams(
        collective_id=collective_id, has_side_effects=True, vmem_limit_bytes=VMEM_BYTES
    )


def dot_f32(left, right):
    return jnp.dot(left, right, preferred_element_type=jnp.float32)


def dot_t(left, right):
    return lax.dot_general(
        left, right, (((0,), (0,)), ((), ())), preferred_element_type=jnp.float32
    )


def nt_dot(left, right):
    return lax.dot_general(
        left, right, (((1,), (1,)), ((), ())), preferred_element_type=jnp.float32
    )


def ring_ends(n):
    grp, me = lax.axis_index("grp"), lax.axis_index("blk")
    place = ring_place(me, n)
    return place, ((grp, at_offset(place, 1, n)), (grp, at_offset(place, -1, n)))


class Gather:
    def __init__(self, n, buf, send, recv, ends, own=None):
        self.n, self.buf, self.send, self.recv, self.ends = n, buf, send, recv, ends
        self.own = buf.at[0] if own is None else own
        self.half = buf.shape[1] // 2

    def copy(self, step, chunk, way):
        part = pl.ds(chunk * self.half, self.half)
        if isinstance(step, int):
            target = min(2 * step + 1 + way, self.n - 1)
        else:
            target = jnp.minimum(2 * step + 1 + way, self.n - 1)
        first = isinstance(step, int) and step == 0
        return push(
            self.own.at[part] if first else self.buf.at[2 * step - 1 + way, part],
            self.buf.at[target, part],
            self.send.at[step, chunk, way],
            self.recv.at[step, chunk, way],
            self.ends[way],
        )

    def landed(self, step, chunk, way):
        target = jnp.minimum(2 * step + 1 + way, self.n - 1)
        place = self.buf.at[target, pl.ds(chunk * self.half, self.half)]
        sems = (self.send.at[step, chunk, way], self.recv.at[step, chunk, way])
        return push(place, place, *sems, self.ends[way])

    def used(self, step, chunk, way):
        return step < self.n // 2 - 1 or chunk == way

    def start(self):
        for chunk in range(2):
            for way in range(2):
                self.copy(0, chunk, way).start()

    def advance(self, step):
        for chunk in range(2):
            for way in range(2):
                if isinstance(step, int):
                    if self.used(step, chunk, way):
                        self.copy(step, chunk, way).wait_recv()
                        if step + 1 < self.n // 2 and self.used(step + 1, chunk, way):
                            self.copy(step + 1, chunk, way).start()
                elif chunk == way:
                    self.landed(step, chunk, way).wait_recv()
                    pl.when(step + 1 < self.n // 2)(self.copy(step + 1, chunk, way).start)
                else:
                    pl.when(step < self.n // 2 - 1)(self.landed(step, chunk, way).wait_recv)
                    pl.when(step + 1 < self.n // 2 - 1)(self.copy(step + 1, chunk, way).start)

    def finish(self):
        for step in range(self.n // 2):
            for chunk in range(2):
                for way in range(2):
                    if self.used(step, chunk, way):
                        self.copy(step, chunk, way).wait_send()


class Scatter:
    def __init__(self, n, held, terms, send, recv, ends, term):
        self.n, self.held, self.terms, self.send, self.recv = n, held, terms, send, recv
        self.ends, self.term = ends, term
        self.half = held.shape[2] // 2

    def copy(self, step, chunk, way):
        part = pl.ds(chunk * self.half, self.half)
        return push(
            self.held.at[way, step, part],
            self.held.at[way, step + 1, part],
            self.send.at[step, chunk, way],
            self.recv.at[step, chunk, way],
            self.ends[way],
        )

    def step(self, step):
        for way in range(2):
            self.terms[way] = self.term(step, way)
        for chunk in range(2):
            for way in range(2):
                part = pl.ds(chunk * self.half, self.half)

                def first(way=way, part=part):
                    self.held[way, step, part] = self.terms[way, part].astype(jnp.bfloat16)

                def later(chunk=chunk, way=way, part=part):
                    self.copy(step - 1, chunk, way).wait_recv()
                    self.held[way, step, part] = (
                        self.terms[way, part] + self.held[way, step, part].astype(jnp.float32)
                    ).astype(jnp.bfloat16)

                if isinstance(step, int):
                    (later if step else first)()
                else:
                    pl.when(step == 0)(first)
                    pl.when(step > 0)(later)
                self.copy(step, chunk, way).start()

    def result(self, way):
        for chunk in range(2):
            self.copy(self.n - 2, chunk, way).wait_recv()
        return self.term(self.n - 1, way) + self.held[way, self.n - 1].astype(jnp.float32)

    def finish(self):
        def body(step, _):
            for chunk in range(2):
                for way in range(2):
                    self.copy(step, chunk, way).wait_send()
            return 0

        lax.fori_loop(0, self.n - 1, body, 0)


def behind(step, way, n):
    near = 2 * step + 1 + way
    far = 2 * (n - 1 - step) - way
    if isinstance(step, int):
        return 0 if step == n - 1 else min(near, far, n - 1)
    return jnp.where(step == n - 1, 0, jnp.minimum(jnp.minimum(near, far), n - 1))


def team(grp):
    over, core = grp // 2, grp % 2
    return over, core, (1 - over) * 2 + core, over * 2 + 1 - core


def mlp_kernel(
    n,
    lanes,
    ob,
    w_out,
    x_ref,
    gain,
    weights,
    w_down,
    seed_hbm,
    seed_own,
    block_out,
    dresid_out,
    dattended,
    gain_terms,
    wide_sum,
    down_sum,
    out_grad,
    normed,
    seed,
    gate_up,
    down,
    hidden,
    dgate_up,
    held_one,
    held_two,
    terms,
    resid,
    wide,
    wide_c,
    tall,
    tall_c,
    load_sem,
    s_one,
    r_one,
    s_two,
    r_two,
    s_three,
    r_three,
    s_norm,
    r_norm,
    s_dres,
    r_dres,
    s_wc,
    r_wc,
    s_wx,
    r_wx,
    s_tall,
    r_tall,
):
    f32, bf16 = jnp.float32, jnp.bfloat16
    grp, me = lax.axis_index("grp"), lax.axis_index("blk")
    over, core, grp_x, grp_c = team(grp)
    _, ends = ring_ends(n)
    loads = [
        pltpu.make_async_copy(weights, gate_up, load_sem.at[0]),
        pltpu.make_async_copy(w_down, down, load_sem.at[1]),
        pltpu.make_async_copy(
            seed_hbm.at[pl.ds(1, n - 1)], seed.at[pl.ds(1, n - 1)], load_sem.at[2]
        ),
        pltpu.make_async_copy(seed_own, seed.at[0], load_sem.at[3]),
    ]
    for load in loads:
        load.start()
    greet(list(ends) + [(grp_x, me), (grp_c, me)])
    columns = x_ref.shape[1]
    half = columns // 2

    def out_term(step, way):
        return dot_f32(ob[behind(step, way, n)], w_out[:, way * half : (way + 1) * half])

    one = Scatter(n, held_one, terms, s_one, r_one, ends, out_term)
    one.step(0)
    lax.fori_loop(1, n - 1, lambda step, _: (one.step(step), 0)[1], 0)
    for way in range(2):
        part = slice(way * half, (way + 1) * half)
        resid[:, part] = x_ref[:, part].astype(f32) + one.result(way)
    value = resid[...]
    inv = lax.rsqrt(jnp.mean(value * value, axis=-1, keepdims=True) + EPS)
    normed[0] = (value * inv * gain[...]).astype(bf16)
    gather = Gather(n, normed, s_norm, r_norm, ends)
    gather.start()
    one.finish()
    for load in loads:
        load.wait()

    def mlp(slot, _):
        both = dot_f32(normed[slot], gate_up[...])
        grad = nt_dot(seed[slot], down[...])
        gate, up = both[:, :lanes], both[:, lanes:]
        sig = jax.nn.sigmoid(gate)
        swish = gate * sig
        hidden[slot] = (swish * up).astype(bf16)
        dgate_up[slot, :, :lanes] = (grad * up * sig * (1.0 + gate * (1.0 - sig))).astype(bf16)
        dgate_up[slot, :, lanes:] = (grad * swish).astype(bf16)
        return 0

    def norm_term(step, way):
        return nt_dot(dgate_up[behind(step, way, n)], gate_up[way * half : (way + 1) * half, :])

    two = Scatter(n, held_two, terms, s_two, r_two, ends, norm_term)

    def turn(t, _):
        pl.when(t > 0)(lambda: gather.advance(t - 1))
        low = jnp.maximum(2 * t - 1, 0)
        lax.fori_loop(low, jnp.minimum(2 * t + 1, n), mlp, 0)
        pl.when(t > 0)(lambda: two.step(t - 1))
        return 0

    lax.fori_loop(0, n // 2 + 1, turn, 0)

    tall_rows = lanes // 4

    def tall_at(first, count):
        return pl.ds(pl.multiple_of(first * tall_rows, tall_rows), count * tall_rows)

    tiles = [slice(at, min(at + 256, lanes)) for at in range(0, lanes, 256)]

    def tall_grad(tile):
        left = hidden[:, :, tile].reshape(-1, tile.stop - tile.start)
        tall[tile] = dot_t(left, seed[...].reshape(-1, columns)).astype(bf16)

    for index, step in enumerate(range(n // 2, n - 1)):
        for tile in tiles[index :: n // 2 - 1]:
            tall_grad(tile)
        two.step(step)
    tall_one = push(tall.at[tall_at(2 - 2 * core, 2)], tall_c, s_tall.at[0], r_tall.at[0], (grp_c, me))
    tall_one.start()

    value = resid[...]
    inv = lax.rsqrt(jnp.mean(value * value, axis=-1, keepdims=True) + EPS)
    for way in range(2):
        part = slice(way * half, (way + 1) * half)
        dresid_out[:, part] = two.result(way)
    dnormed = dresid_out[...]
    gain_terms[...] = jnp.sum(dnormed * value * inv, axis=0, keepdims=True)
    a_two = dnormed * gain[...]
    total = (
        seed[0].astype(f32)
        + inv * a_two
        - value * inv**3 * jnp.mean(a_two * value, axis=-1, keepdims=True)
    )
    dresid_out[...] = total
    dresid = seed
    dresid[0] = total.astype(bf16)
    back = Gather(n, dresid, s_dres, r_dres, ends)
    back.start()
    two.finish()

    def down_term(step, way):
        return dot_f32(hidden[behind(step, way, n)], down[:, way * half : (way + 1) * half])

    three = Scatter(n, held_one, terms, s_three, r_three, ends, down_term)

    def dob(slot, _):
        dattended[slot] = nt_dot(dresid[slot], w_out[...]).astype(bf16)
        return 0

    def wide_copy_c(tile):
        return push(
            wide.at[tile, 1 - core], wide_c.at[tile], s_wc.at[tile], r_wc.at[tile], (grp_c, me)
        )

    def wide_copy_x(tile):
        return push(
            wide_c.at[tile, 1 - over], wide_sum.at[tile], s_wx.at[tile], r_wx.at[tile], (grp_x, me)
        )

    quarter = wide.shape[3]

    def wide_grad(tile):
        at = pl.multiple_of(tile * 4 * quarter, 4 * quarter)
        left = normed[:, :, pl.ds(at, 4 * quarter)].reshape(-1, 4 * quarter)
        grad = dot_t(left, dgate_up[...].reshape(-1, 2 * lanes)).astype(bf16)
        wide[tile] = grad.reshape(2, 2, quarter, 2 * lanes)
        wide_copy_c(tile).start()

    def wide_pass(tile):
        wide_copy_c(tile).wait_recv()
        wide_c[tile, 1 - over] = (
            wide[tile, core, 1 - over].astype(f32) + wide_c[tile, 1 - over].astype(f32)
        ).astype(bf16)
        wide_copy_x(tile).start()

    tall_two = push(tall_c.at[tall_at(1 - over, 1)], down_sum, s_tall.at[1], r_tall.at[1], (grp_x, me))

    def tall_pass():
        tall_one.wait_recv()
        tall_c[tall_at(1 - over, 1)] = (
            tall[tall_at(2 * core + 1 - over, 1)].astype(f32)
            + tall_c[tall_at(1 - over, 1)].astype(f32)
        ).astype(bf16)
        tall_two.start()

    def wide_take(tile):
        wide_copy_x(tile).wait_recv()
        wide_sum[tile] = (
            wide[tile, core, over].astype(f32)
            + wide_c[tile, over].astype(f32)
            + wide_sum[tile].astype(f32)
        ).astype(bf16)

    def again(t, _):
        pl.when(t > 0)(lambda: back.advance(t - 1))
        low = jnp.maximum(2 * t - 1, 0)
        lax.fori_loop(low, jnp.minimum(2 * t + 1, n), dob, 0)

        def inner(step, _):
            pl.when(step < n - 1)(lambda: three.step(step))

            @pl.when(step < n // 2)
            def _():
                wide_grad(2 * step)
                pl.when(step == 0)(tall_pass)
                pl.when(step > 0)(lambda: wide_pass(2 * step - 1))
                wide_grad(2 * step + 1)
                wide_pass(2 * step)

            pl.when(step == n // 2)(lambda: wide_pass(n - 1))

            @pl.when(step >= n // 2)
            def _():
                wide_take(2 * step - n)
                pl.when(step < n - 1)(lambda: wide_take(2 * step - n + 1))

            return 0

        lax.fori_loop(2 * t, jnp.minimum(2 * t + 2, n), inner, 0)
        return 0

    lax.fori_loop(0, n // 2 + 1, again, 0)
    wide_take(n - 1)
    out_grad[...] = dot_t(
        ob[...].reshape(-1, ob.shape[2]), dresid[...].reshape(-1, columns)
    ).astype(bf16)
    for way in range(2):
        part = slice(way * half, (way + 1) * half)
        block_out[:, part] = (resid[:, part] + three.result(way)).astype(bf16)

    tall_two.wait_recv()
    down_sum[...] = (
        tall[tall_at(2 * core + over, 1)].astype(f32)
        + tall_c[tall_at(over, 1)].astype(f32)
        + down_sum[...].astype(f32)
    ).astype(bf16)
    gather.finish()
    back.finish()
    three.finish()
    tall_one.wait_send()
    tall_two.wait_send()

    def sent(tile, _):
        wide_copy_c(tile).wait_send()
        wide_copy_x(tile).wait_send()
        return 0

    lax.fori_loop(0, n, sent, 0)


def mlp_and_back(ob, w_out, x_own, gain, weights, lanes, w_down, seed, seed_own):
    n = lax.axis_size("blk")
    _, rows, columns = seed.shape
    head_lanes = ob.shape[2]
    quarter = columns // (4 * n)
    f32, bf16 = jnp.float32, jnp.bfloat16
    vmem, dma = pltpu.VMEM, pltpu.SemaphoreType.DMA
    in_vmem, anywhere = pl.BlockSpec(memory_space=vmem), pl.BlockSpec(memory_space=pl.ANY)
    ring = [dma((n - 1, 2, 2))] * 6 + [dma((n // 2, 2, 2))] * 4
    return pl.pallas_call(
        functools.partial(mlp_kernel, n, lanes),
        out_shape=(
            jax.ShapeDtypeStruct((rows, columns), bf16),
            jax.ShapeDtypeStruct((rows, columns), f32),
            jax.ShapeDtypeStruct((n, rows, head_lanes), bf16),
            jax.ShapeDtypeStruct((1, columns), f32),
            jax.ShapeDtypeStruct((n, quarter, 2 * lanes), bf16),
            jax.ShapeDtypeStruct((lanes // 4, columns), bf16),
            jax.ShapeDtypeStruct((head_lanes, columns), bf16),
        ),
        in_specs=[in_vmem] * 4 + [anywhere] * 4,
        out_specs=[in_vmem] * 7,
        scratch_shapes=[
            vmem((n, rows, columns), bf16),
            vmem((n, rows, columns), bf16),
            vmem((columns, 2 * lanes), bf16),
            vmem((lanes, columns), bf16),
            vmem((n, rows, lanes), bf16),
            vmem((n, rows, 2 * lanes), bf16),
            vmem((2, n, rows, columns // 2), bf16),
            vmem((2, n, rows, columns // 2), bf16),
            vmem((2, rows, columns // 2), f32),
            vmem((rows, columns), f32),
            vmem((n, 2, 2, quarter, 2 * lanes), bf16),
            vmem((n, 2, quarter, 2 * lanes), bf16),
            vmem((lanes, columns), bf16),
            vmem((lanes // 2, columns), bf16),
            dma((4,)),
        ]
        + ring
        + [dma((n,))] * 4
        + [dma((2,))] * 2,
        compiler_params=kernel_params(5),
        name="mlp_and_back",
    )(ob, w_out, x_own, gain, weights, w_down, seed, seed_own)


class Spread:
    def __init__(self, n, pieces, out, sems):
        self.n, self.pieces, self.out = n, pieces, out
        self.s_blk, self.r_blk, self.s_x, self.r_x, self.s_c, self.r_c = sems
        self.grp, self.me = lax.axis_index("grp"), lax.axis_index("blk")
        self.over, self.core, self.grp_x, self.grp_c = team(self.grp)

    def first(self, k):
        to = (self.me + k) % self.n
        place = self.out.at[self.me, 2 * self.core + self.over]
        return push(
            self.pieces.at[to], place, self.s_blk.at[k], self.r_blk.at[k], (self.grp, to)
        )

    def own(self, sem):
        place = self.out.at[self.me, 2 * self.core + self.over]
        return pltpu.make_async_copy(self.pieces.at[self.me], place, sem)

    def to_x(self, k, own=False):
        piece = self.out.at[(self.me - k + self.n) % self.n, 2 * self.core + self.over]
        source = self.pieces.at[self.me] if own else piece
        return push(source, piece, self.s_x.at[k], self.r_x.at[k], (self.grp_x, self.me))

    def to_core(self, k, far, own=False):
        over = 1 - self.over if far else self.over
        piece = self.out.at[(self.me - k + self.n) % self.n, 2 * self.core + over]
        source = self.pieces.at[self.me] if own else piece
        sems = (self.s_c.at[int(far), k], self.r_c.at[int(far), k])
        return push(source, piece, *sems, (self.grp_c, self.me))

    def pass_own(self):
        self.to_x(0, True).start()
        self.to_core(0, False, True).start()

    def pass_on(self, k):
        self.first(k).wait_recv()
        self.to_x(k).start()
        self.to_core(k, False).start()

    def pass_far(self, k):
        self.to_x(k).wait_recv()
        self.to_core(k, True).start()

    def arrived(self, k):
        for far in (False, True):
            self.to_core(k, far).wait_recv()

    def finish(self):
        def body(k, _):
            pl.when(k > 0)(self.first(k).wait_send)
            self.to_x(k).wait_send()
            for far in (False, True):
                self.to_core(k, far).wait_send()
            return 0

        lax.fori_loop(0, self.n, body, 0)


def each(count, body, low=0):
    lax.fori_loop(low, count, lambda k, _: (body(k), 0)[1], 0)


def spread_sems(n):
    dma = pltpu.SemaphoreType.DMA
    return [dma((n,)), dma((n,)), dma((n,)), dma((n,)), dma((2, n)), dma((2, n))]


def team_and_ring(n):
    grp, me = lax.axis_index("grp"), lax.axis_index("blk")
    _, _, grp_x, grp_c = team(grp)
    return [(grp, (me + k) % n) for k in range(1, n)] + [(grp_x, me), (grp_c, me)]


def fill_row(row, gains_all, which, share):
    for block in range(gains_all.shape[0]):
        row[:, block * share : (block + 1) * share] = gains_all[block, which : which + 1, :]


def turned(value, cosine, sine_part):
    half_size = HEAD // 2
    swapped = jnp.concatenate([value[:, half_size:], value[:, :half_size]], axis=1)
    return value * cosine + swapped * sine_part


def mark_places(n, doc_lens, rows, first_key, query_place, key_place):
    place = ring_place(lax.axis_index("blk"), n)
    for slot in range(n):
        offset = (slot + 1) // 2 * (1 if slot % 2 == 0 else -1)
        first_row = at_offset(place, offset, n) * rows
        part = slice(slot * rows, (slot + 1) * rows)
        here = first_row + lax.broadcasted_iota(jnp.int32, (rows, 1), 0)
        query_place[part, :] = here
        key_place[:, part] = first_row + lax.broadcasted_iota(jnp.int32, (1, rows), 1)
        start = jnp.int32(0)
        found = jnp.zeros((rows, 1), jnp.int32)
        for index in range(doc_lens.shape[1]):
            found = jnp.maximum(found, jnp.where(here >= start, start, 0))
            start = start + doc_lens[0, index]
        first_key[part, :] = found


def attend_kernel(
    n,
    heads,
    doc_lens,
    x_own,
    freqs,
    norm_attn,
    norm_mlp,
    w_qkv,
    w_gate,
    w_up,
    seed_own,
    gain_row,
    gain_two,
    columns_qkv,
    normed,
    qkv,
    attended,
    attended_b,
    log_total,
    cosine,
    sine_part,
    gate_up,
    seed,
    x_all,
    gains_all,
    gains,
    raw_qkv,
    raw_gate,
    raw_up,
    slab_qkv,
    slab_gate_up,
    first_key,
    query_place,
    key_place,
    local,
    s_gain,
    r_gain,
    s_x,
    r_x,
    s_seed,
    r_seed,
    *spread_all,
):
    f32, bf16 = jnp.float32, jnp.bfloat16
    grp, me = lax.axis_index("grp"), lax.axis_index("blk")
    _, ends = ring_ends(n)
    rows, columns = x_own.shape
    spread_qkv = Spread(n, slab_qkv, columns_qkv, spread_all[:6])
    spread_gu = Spread(n, slab_gate_up, gate_up, spread_all[6:])
    over, core, _, _ = team(grp)
    quarter = slab_qkv.shape[1]
    own_rows = pl.ds(pl.multiple_of((2 * core + over) * quarter, quarter), quarter)
    loads = [
        pltpu.make_async_copy(weight.at[own_rows], raw, local.at[index])
        for index, (weight, raw) in enumerate(
            ((w_qkv, raw_qkv), (w_gate, raw_gate), (w_up, raw_up))
        )
    ]
    for load in loads:
        load.start()
    x_all[0] = x_own[...]
    gains[...] = jnp.zeros_like(gains)
    gains[0:1, :] = norm_attn[...].astype(f32)
    gains[1:2, :] = norm_mlp[...].astype(f32)
    gains_all[me] = gains[...]
    greet(team_and_ring(n))

    def gain(k):
        return push(gains, gains_all.at[me], s_gain.at[k], r_gain.at[k], (grp, (me + k) % n))

    each(n, lambda k: gain(k).start(), 1)
    x_ring = Gather(n, x_all, s_x, r_x, ends)
    x_ring.start()
    share = heads * HEAD
    loads[0].wait()
    for to in range(n):
        for part in range(3):
            slab_qkv[to, :, part * share : (part + 1) * share] = raw_qkv[
                :, (part * n + to) * share : (part * n + to + 1) * share
            ]
    near_qkv = spread_qkv.own(local.at[3])
    near_qkv.start()
    each(n, lambda k: spread_qkv.first(k).start(), 1)
    spread_qkv.pass_own()
    units = raw_gate.shape[1] // n
    loads[1].wait()
    loads[2].wait()
    for to in range(n):
        lane = slice(to * units, (to + 1) * units)
        slab_gate_up[to] = jnp.concatenate(
            [raw_gate[:, lane].astype(f32), raw_up[:, lane].astype(f32)], axis=1
        ).astype(bf16)
    near_gu = spread_gu.own(local.at[4])
    near_gu.start()
    mark_places(n, doc_lens, rows, first_key, query_place, key_place)

    def norm(slot):
        value = x_all[slot].astype(f32)
        inv = lax.rsqrt(jnp.mean(value * value, axis=-1, keepdims=True) + EPS)
        normed[slot] = (value * inv * gain_row[...]).astype(bf16)

    each(n, lambda k: gain(k).wait_recv(), 1)
    fill_row(gain_row, gains_all, 0, columns // n)
    fill_row(gain_two, gains_all, 1, columns // n)

    def table(slot):
        at = pl.ds(pl.multiple_of(slot * rows, rows), rows)
        angle = (query_place[at, :] - first_key[at, :]).astype(f32) * freqs[...]
        lane = lax.broadcasted_iota(jnp.int32, (rows, HEAD), 1)
        sine = jnp.sin(angle)
        cosine[at, :] = jnp.cos(angle)
        sine_part[at, :] = jnp.where(lane < HEAD // 2, -sine, sine)

    def arrive(t):
        pl.when(t > 0)(lambda: x_ring.advance(t - 1))
        low = jnp.maximum(2 * t - 1, 0)
        each(jnp.minimum(2 * t + 1, n), norm, low)
        each(jnp.minimum(2 * t + 1, n), table, low)
        pl.when(t == 2)(lambda: each(n, spread_qkv.pass_on, 1))
        pl.when(t == 3)(lambda: each(n, spread_qkv.pass_far))

        @pl.when(t == 2)
        def _():
            each(n, lambda k: spread_gu.first(k).start(), 1)
            spread_gu.pass_own()


    each(n // 2 + 1, arrive)
    seed_ring = Gather(n, seed, s_seed, r_seed, ends, seed_own)
    each(n, spread_gu.pass_on, 1)
    seed_ring.start()
    each(n, spread_qkv.arrived)
    near_qkv.wait()


    head_lanes = heads * HEAD
    pair = 2 * rows

    def project(i):
        both = normed[pl.ds(2 * i, 2)].reshape(pair, columns)
        result = dot_f32(both, columns_qkv[...].reshape(columns, 3 * head_lanes))
        at = pl.ds(pl.multiple_of(i * pair, pair), pair)
        table_c, table_s = cosine[at, :], sine_part[at, :]
        for piece in range(3 * heads):
            lane = slice(piece * HEAD, (piece + 1) * HEAD)
            value = result[:, lane]
            if piece < 2 * heads:
                value = turned(value, table_c, table_s)
            qkv[at, lane] = value.astype(bf16)

    each(n // 2, project)


    def tile(i):
        for head in range(heads):
            lane = slice(head * HEAD, (head + 1) * HEAD)
            at = pl.ds(pl.multiple_of(i * pair, pair), pair)
            keys = qkv[:, head_lanes + head * HEAD : head_lanes + (head + 1) * HEAD]
            values = qkv[:, 2 * head_lanes + head * HEAD : 2 * head_lanes + (head + 1) * HEAD]
            scores = nt_dot(qkv[at, lane], keys) * HEAD ** (-0.5)
            allowed = (key_place[...] >= first_key[at, :]) & (key_place[...] <= query_place[at, :])
            scores = jnp.where(allowed, scores, NEGATIVE)
            peak = jnp.max(scores, axis=-1, keepdims=True)
            raw = jnp.exp(scores - peak)
            total = jnp.sum(raw, axis=-1, keepdims=True)
            out = dot_f32(raw.astype(bf16), values) / total
            attended[at, lane] = out
            attended_b[at, lane] = out.astype(bf16)
            log_total[head, at, :] = peak + jnp.log(total)
        seed_ring.advance(i)
        pl.when(i == 1)(lambda: each(n, spread_gu.pass_far))

    each(n // 2, tile)
    each(n, spread_gu.arrived)
    near_gu.wait()
    for spread in (spread_qkv, spread_gu):
        spread.finish()
    each(n, lambda k: gain(k).wait_send(), 1)
    x_ring.finish()
    seed_ring.finish()


def attend(doc_lens, x_own, norm_attn, norm_mlp, w_qkv, w_gate, w_up, seed_own):
    n = lax.axis_size("blk")
    rows, columns = x_own.shape
    seq = n * rows
    lanes = w_qkv.shape[1] // n
    quarter = w_qkv.shape[0] // 4
    both = 2 * w_gate.shape[1] // n
    head_lanes = lanes // 3
    heads = head_lanes // HEAD
    share = norm_attn.shape[0]
    f32, bf16, i32 = jnp.float32, jnp.bfloat16, jnp.int32
    vmem, dma = pltpu.VMEM, pltpu.SemaphoreType.DMA
    in_vmem, anywhere = pl.BlockSpec(memory_space=vmem), pl.BlockSpec(memory_space=pl.ANY)
    half_freqs = np.exp(
        np.arange(HEAD // 2, dtype=np.float32) * np.float32(-2.0 * math.log(10000.0) / HEAD)
    )
    freqs = jnp.asarray(np.concatenate([half_freqs, half_freqs])[None].astype(np.float32))
    return pl.pallas_call(
        functools.partial(attend_kernel, n, heads),
        out_shape=(
            jax.ShapeDtypeStruct((1, columns), f32),
            jax.ShapeDtypeStruct((1, columns), f32),
            jax.ShapeDtypeStruct((n, 4, quarter, lanes), bf16),
            jax.ShapeDtypeStruct((n, rows, columns), bf16),
            jax.ShapeDtypeStruct((seq, lanes), bf16),
            jax.ShapeDtypeStruct((seq, head_lanes), f32),
            jax.ShapeDtypeStruct((seq, head_lanes), bf16),
            jax.ShapeDtypeStruct((heads, seq, 1), f32),
            jax.ShapeDtypeStruct((seq, HEAD), f32),
            jax.ShapeDtypeStruct((seq, HEAD), f32),
            jax.ShapeDtypeStruct((n, 4, quarter, both), bf16),
            jax.ShapeDtypeStruct((n, rows, columns), bf16),
        ),
        in_specs=[pl.BlockSpec(memory_space=pltpu.SMEM)] + [in_vmem] * 4 + [anywhere] * 4,
        out_specs=[in_vmem] * 10 + [anywhere] * 2,
        scratch_shapes=[
            vmem((n, rows, columns), bf16),
            vmem((n, 8, share), f32),
            vmem((8, share), f32),
            vmem((quarter, n * lanes), bf16),
            vmem((quarter, w_gate.shape[1]), bf16),
            vmem((quarter, w_gate.shape[1]), bf16),
            vmem((n, quarter, lanes), bf16),
            vmem((n, quarter, both), bf16),
            vmem((seq, 1), i32),
            vmem((seq, 1), i32),
            vmem((1, seq), i32),
            dma((5,)),
            dma((n,)),
            dma((n,)),
        ]
        + [dma((n // 2, 2, 2))] * 4
        + spread_sems(n) * 2,
        compiler_params=kernel_params(0),
        name="attend",
    )(
        doc_lens,
        x_own,
        freqs,
        norm_attn.reshape(1, share),
        norm_mlp.reshape(1, share),
        w_qkv,
        w_gate,
        w_up,
        seed_own,
    )


def finish_kernel(
    n,
    heads,
    qkv,
    attended,
    dattended,
    log_total,
    cosine,
    sine_part,
    doc_lens,
    x_own,
    gain,
    dresid,
    terms_two,
    out_grad,
    weights,
    normed_hbm,
    gate_up_sum,
    down_sum,
    x_grad,
    gain_grads,
    wide_gate_up,
    wide_qkv,
    tall_down,
    tall_out,
    normed,
    columns_qkv,
    dqkv,
    dkeys,
    dvalues,
    first_key,
    query_place,
    key_place,
    held,
    terms,
    wide,
    wide_c,
    wide_x,
    out_c,
    out_x,
    gain_slabs,
    gain_heard,
    gain_team,
    load_sem,
    s_ring,
    r_ring,
    s_wc,
    r_wc,
    s_wx,
    r_wx,
    s_tall,
    r_tall,
    s_gain,
    r_gain,
    *spread_all,
):
    f32, bf16 = jnp.float32, jnp.bfloat16
    grp, me = lax.axis_index("grp"), lax.axis_index("blk")
    over, core, grp_x, grp_c = team(grp)
    _, ends = ring_ends(n)
    rows, columns = x_own.shape
    half = columns // 2
    lanes = wide.shape[4]
    quarter = wide.shape[3]
    load_normed = pltpu.make_async_copy(normed_hbm, normed, load_sem.at[0])
    load_qkv = pltpu.make_async_copy(weights, columns_qkv, load_sem.at[1])
    load_normed.start()
    load_qkv.start()
    spread_gu = Spread(n, gate_up_sum, wide_gate_up, spread_all[:6])
    spread_qkv = Spread(n, wide_x, wide_qkv, spread_all[6:])
    near_gu = spread_gu.own(load_sem.at[2])
    near_gu.start()
    greet(team_and_ring(n))

    down_own = pltpu.make_async_copy(down_sum, tall_down.at[2 * core + over], load_sem.at[3])
    down_own.start()
    down_place = tall_down.at[2 * core + over]
    down_x = push(down_sum, down_place, s_tall.at[0], r_tall.at[0], (grp_x, me))
    down_c = push(down_sum, down_place, s_tall.at[1], r_tall.at[1], (grp_c, me))
    far_place = tall_down.at[2 * core + 1 - over]
    down_far = push(far_place, far_place, s_tall.at[2], r_tall.at[2], (grp_c, me))
    out_one = push(out_grad.at[1 - core], out_c, s_tall.at[3], r_tall.at[3], (grp_c, me))
    out_two = push(out_c.at[1 - over], out_x, s_tall.at[4], r_tall.at[4], (grp_x, me))
    out_place = tall_out.at[2 * core + over]
    out_own = pltpu.make_async_copy(out_x, out_place, load_sem.at[4])
    out_to_x = push(out_x, out_place, s_tall.at[5], r_tall.at[5], (grp_x, me))
    out_to_c = push(out_x, out_place, s_tall.at[6], r_tall.at[6], (grp_c, me))
    out_far_place = tall_out.at[2 * core + 1 - over]
    out_far = push(out_far_place, out_far_place, s_tall.at[7], r_tall.at[7], (grp_c, me))
    out_one.start()
    each(n, lambda k: spread_gu.first(k).start(), 1)
    spread_gu.pass_own()
    down_x.start()
    down_c.start()

    mark_places(n, doc_lens, rows, first_key, query_place, key_place)
    pair = 2 * rows
    head_lanes = heads * HEAD
    scale = HEAD ** (-0.5)

    def unturned(value, at):
        return turned(value, cosine[at, :], -sine_part[at, :]).astype(bf16)

    def tile(i, head):
        at = pl.ds(pl.multiple_of(i * pair, pair), pair)
        lane = slice(head * HEAD, (head + 1) * HEAD)
        query = qkv[at, lane]
        keys = qkv[:, head_lanes + head * HEAD : head_lanes + (head + 1) * HEAD]
        values = qkv[:, 2 * head_lanes + head * HEAD : 2 * head_lanes + (head + 1) * HEAD]
        grad = dattended[at, lane]
        delta = jnp.sum(grad.astype(f32) * attended[at, lane], axis=-1, keepdims=True)
        scores = nt_dot(query, keys) * scale
        allowed = (key_place[...] >= first_key[at, :]) & (key_place[...] <= query_place[at, :])
        probs = jnp.where(allowed, jnp.exp(scores - log_total[head, at, :]), 0.0)
        dscores = (probs * (nt_dot(grad, values) - delta)).astype(bf16)
        dqkv[2 * i : 2 * i + 2, :, lane] = unturned(dot_f32(dscores, keys) * scale, at).reshape(
            2, rows, HEAD
        )
        more_keys = dot_t(dscores, query)
        more_values = dot_t(probs.astype(bf16), grad)
        if i == 0:
            dkeys[...] = more_keys
            dvalues[...] = more_values
        else:
            dkeys[...] += more_keys
            dvalues[...] += more_values

    for head in range(heads):
        for i in range(n // 2):
            tile(i, head)
        everything = slice(0, n * rows)
        lane = slice(head_lanes + head * HEAD, head_lanes + (head + 1) * HEAD)
        dqkv[:, :, lane] = unturned(dkeys[...] * scale, everything).reshape(n, rows, HEAD)
        lane = slice(2 * head_lanes + head * HEAD, 2 * head_lanes + (head + 1) * HEAD)
        dqkv[:, :, lane] = dvalues[...].astype(bf16).reshape(n, rows, HEAD)
    load_qkv.wait()

    def term(step, way):
        return nt_dot(dqkv[behind(step, way, n)], columns_qkv[way * half : (way + 1) * half, :])

    ring = Scatter(n, held, terms, s_ring, r_ring, ends, term)

    def copy_c(k):
        tile = (me + k) % n
        return push(wide.at[tile, 1 - core], wide_c.at[tile], s_wc.at[k], r_wc.at[k], (grp_c, me))

    def copy_x(k):
        tile = (me + k) % n
        return push(
            wide_c.at[tile, 1 - over], wide_x.at[tile], s_wx.at[k], r_wx.at[k], (grp_x, me)
        )

    def grad(k):
        tile = (me + k) % n
        at = pl.multiple_of(tile * 4 * quarter, 4 * quarter)
        left = normed[:, :, pl.ds(at, 4 * quarter)].reshape(-1, 4 * quarter)
        grad_rows = dot_t(left, dqkv[...].reshape(-1, lanes)).astype(bf16)
        wide[tile] = grad_rows.reshape(2, 2, quarter, lanes)
        copy_c(k).start()

    def pass_x(k):
        tile = (me + k) % n
        copy_c(k).wait_recv()
        wide_c[tile, 1 - over] = (
            wide[tile, core, 1 - over].astype(f32) + wide_c[tile, 1 - over].astype(f32)
        ).astype(bf16)
        copy_x(k).start()

    def take(k):
        tile = (me + k) % n
        copy_x(k).wait_recv()
        wide_x[tile] = (
            wide[tile, core, over].astype(f32)
            + wide_c[tile, over].astype(f32)
            + wide_x[tile].astype(f32)
        ).astype(bf16)

    def take_and_push(k):
        take(k)
        spread_qkv.first(k).start()

    ring.step(0)
    load_normed.wait()

    def grads(i):
        k = (i + 1) % n
        grad(k)
        pl.when(i > 0)(lambda: pass_x(i))

    each(n, grads)
    pass_x(0)
    out_one.wait_recv()
    out_c[1 - over] = (
        out_grad[core, 1 - over].astype(f32) + out_c[1 - over].astype(f32)
    ).astype(bf16)
    out_two.start()

    def turn(k):
        pl.when(k < n - 2)(lambda: ring.step(k + 1))
        each(jnp.minimum(2 * k + 3, n), spread_gu.pass_on, jnp.minimum(2 * k + 1, n))
        pl.when(k < n - 1)(lambda: take_and_push(k + 1))
        pl.when(k >= 2)(lambda: spread_qkv.pass_on(k - 1))

        @pl.when(k == n - 2)
        def _():
            take(0)
            spread_qkv.pass_own()

    each(n - 1, turn)
    near_qkv = spread_qkv.own(load_sem.at[5])
    near_qkv.start()
    each(n, spread_qkv.pass_on, n - 2)

    x_float = x_own[...].astype(f32)
    inv = lax.rsqrt(jnp.mean(x_float * x_float, axis=-1, keepdims=True) + EPS)
    for way in range(2):
        terms[way] = ring.result(way)
    dnormed = jnp.concatenate([terms[0], terms[1]], axis=1)
    terms_one = jnp.sum(dnormed * x_float * inv, axis=0, keepdims=True)
    share = columns // n
    for block in range(n):
        gain_slabs[block] = jnp.zeros_like(gain_slabs[block])
        lane = slice(block * share, (block + 1) * share)
        gain_slabs[block, 0:1, :] = terms_one[:, lane]
        gain_slabs[block, 1:2, :] = terms_two[:, lane]

    def gain_blk(k):
        to = (me + k) % n
        return push(gain_slabs.at[to], gain_heard.at[k], s_gain.at[k], r_gain.at[k], (grp, to))

    each(n, lambda k: gain_blk(k).start(), 1)
    a_one = dnormed * gain[...]
    x_grad[...] = (
        dresid[...]
        + inv * a_one
        - x_float * inv**3 * jnp.mean(a_one * x_float, axis=-1, keepdims=True)
    ).astype(bf16)
    gain_heard[0] = gain_slabs[me]
    each(n, lambda k: gain_blk(k).wait_recv(), 1)
    gain_team[0] = jnp.sum(gain_heard[...], axis=0)
    gain_c = push(gain_team.at[0], gain_team.at[1], s_gain.at[n], r_gain.at[n], (grp_c, me))
    gain_c.start()
    out_two.wait_recv()
    out_x[...] = (
        out_grad[core, over].astype(f32) + out_c[over].astype(f32) + out_x[...].astype(f32)
    ).astype(bf16)
    out_own.start()
    out_to_x.start()
    out_to_c.start()
    each(n, spread_gu.pass_far)
    down_x.wait_recv()
    down_far.start()
    gain_c.wait_recv()
    gain_team[2] = gain_team[0] + gain_team[1]
    gain_x = push(
        gain_team.at[2], gain_team.at[3], s_gain.at[n + 1], r_gain.at[n + 1], (grp_x, me)
    )
    gain_x.start()
    out_to_x.wait_recv()
    out_far.start()
    each(n, spread_qkv.pass_far)
    gain_x.wait_recv()
    gain_grads[...] = gain_team[2] + gain_team[3]
    near_gu.wait()
    near_qkv.wait()
    each(n, spread_gu.arrived)
    each(n, spread_qkv.arrived)
    spread_gu.finish()
    spread_qkv.finish()
    ring.finish()
    down_own.wait()
    out_own.wait()
    for copy in (down_c, down_far, out_to_c, out_far):
        copy.wait()
    for copy in (down_x, out_one, out_two, out_to_x, gain_c, gain_x):
        copy.wait_send()

    def sent(k):
        copy_c(k).wait_send()
        copy_x(k).wait_send()
        pl.when(k > 0)(gain_blk(k).wait_send)

    each(n, sent)


def finish(
    attention, x_own, gain, dresid, terms_two, out_grad, weights, normed, gate_up_sum, down_sum
):
    n, rows, columns = normed.shape
    seq, lanes = attention[0].shape
    heads = lanes // (3 * HEAD)
    quarter = columns // (4 * n)
    share = columns // n
    f32, bf16 = jnp.float32, jnp.bfloat16
    vmem, dma = pltpu.VMEM, pltpu.SemaphoreType.DMA
    in_vmem, anywhere = pl.BlockSpec(memory_space=vmem), pl.BlockSpec(memory_space=pl.ANY)
    out_rows = out_grad.shape[0] // 4
    return pl.pallas_call(
        functools.partial(finish_kernel, n, heads),
        out_shape=(
            jax.ShapeDtypeStruct((rows, columns), bf16),
            jax.ShapeDtypeStruct((8, share), f32),
            jax.ShapeDtypeStruct((n, 4) + gate_up_sum.shape[1:], bf16),
            jax.ShapeDtypeStruct((n, 4, quarter, lanes), bf16),
            jax.ShapeDtypeStruct((4,) + down_sum.shape, bf16),
            jax.ShapeDtypeStruct((4, out_rows, columns), bf16),
        ),
        in_specs=[in_vmem] * 6
        + [pl.BlockSpec(memory_space=pltpu.SMEM)]
        + [in_vmem] * 5
        + [anywhere] * 4,
        out_specs=[in_vmem] * 2 + [anywhere] * 4,
        scratch_shapes=[
            vmem((n, rows, columns), bf16),
            vmem((columns, lanes), bf16),
            vmem((n, rows, lanes), bf16),
            vmem((seq, HEAD), f32),
            vmem((seq, HEAD), f32),
            vmem((seq, 1), jnp.int32),
            vmem((seq, 1), jnp.int32),
            vmem((1, seq), jnp.int32),
            vmem((2, n, rows, columns // 2), bf16),
            vmem((2, rows, columns // 2), f32),
            vmem((n, 2, 2, quarter, lanes), bf16),
            vmem((n, 2, quarter, lanes), bf16),
            vmem((n, quarter, lanes), bf16),
            vmem((2, out_rows, columns), bf16),
            vmem((out_rows, columns), bf16),
            vmem((n, 8, share), f32),
            vmem((n, 8, share), f32),
            vmem((4, 8, share), f32),
            dma((6,)),
        ]
        + [dma((n - 1, 2, 2))] * 2
        + [dma((n,))] * 4
        + [dma((8,))] * 2
        + [dma((n + 2,))] * 2
        + spread_sems(n) * 2,
        compiler_params=kernel_params(6),
        name="finish",
    )(
        *attention,
        x_own,
        gain,
        dresid,
        terms_two,
        out_grad.reshape(2, 2, out_rows, columns),
        weights,
        normed,
        gate_up_sum,
        down_sum,
    )


def assemble_kernel(n, units, lanes, head_lanes, qkv, gate_up, down, out, *grads):
    grad_qkv, grad_out, grad_gate, grad_up, grad_down = grads
    f32 = jnp.float32
    for source in range(n):
        for part in range(3):
            first = (part * n + source) * head_lanes
            grad_qkv[:, first : first + head_lanes] = qkv[
                source, :, part * head_lanes : (part + 1) * head_lanes
            ].astype(f32)
        first = source * units
        grad_gate[:, first : first + units] = gate_up[source, :, :units].astype(f32)
        grad_up[:, first : first + units] = gate_up[source, :, lanes : lanes + units].astype(f32)
    grad_out[...] = out[...].astype(f32)
    grad_down[...] = down[...].astype(f32)


def assemble(qkv, gate_up, down, out, units, steps=4):
    n, rows, qkv_lanes = qkv.shape
    columns = down.shape[1]
    lanes = gate_up.shape[2] // 2
    head_lanes = qkv_lanes // 3
    step = rows // steps
    down_step = units // steps
    f32 = jnp.float32

    def wide(width):
        return pl.BlockSpec((n, step, width), lambda i: (0, i, 0))

    def flat(height, width):
        return pl.BlockSpec((height, width), lambda i: (i, 0))

    return pl.pallas_call(
        functools.partial(assemble_kernel, n, units, lanes, head_lanes),
        grid=(steps,),
        out_shape=(
            jax.ShapeDtypeStruct((rows, n * qkv_lanes), f32),
            jax.ShapeDtypeStruct((rows, columns), f32),
            jax.ShapeDtypeStruct((rows, n * units), f32),
            jax.ShapeDtypeStruct((rows, n * units), f32),
            jax.ShapeDtypeStruct((units, columns), f32),
        ),
        in_specs=[
            wide(qkv_lanes),
            wide(2 * lanes),
            flat(down_step, columns),
            flat(out.shape[0] // steps, columns),
        ],
        out_specs=[
            flat(step, n * qkv_lanes),
            flat(step, columns),
            flat(step, n * units),
            flat(step, n * units),
            flat(down_step, columns),
        ],
        compiler_params=pltpu.CompilerParams(vmem_limit_bytes=VMEM_BYTES),
        name="assemble",
    )(qkv, gate_up, down, out)


def per_device(block_input, doc_lens, norm_attn, w_qkv, w_out, norm_mlp, w_gate, w_up, w_down, cot):
    n = lax.axis_size("blk")
    tok_rows, width = block_input.shape[1:]
    seq = tok_rows * n
    heads = HEADS // n
    head_lanes = heads * HEAD
    qkv_lanes = 3 * head_lanes
    units = w_down.shape[0]
    lanes = units
    quarter = w_qkv.shape[0] // 4
    (
        gain_one,
        gain_two,
        qkv_columns,
        normed_one,
        qkv,
        attended,
        attended_b,
        log_total,
        cosine,
        sine_part,
        gate_up,
        seed,
    ) = attend(doc_lens, block_input[0], norm_attn, norm_mlp, w_qkv, w_gate, w_up, cot[0])
    qkv_columns = qkv_columns.reshape(width, qkv_lanes)
    gate_up = gate_up.reshape(width, 2 * lanes)
    block_out, dresid, dattended, terms_two, gate_up_sum, down_sum, out_grad = mlp_and_back(
        attended_b.reshape(n, tok_rows, head_lanes),
        w_out,
        block_input[0],
        gain_two,
        gate_up,
        lanes,
        w_down,
        seed,
        cot[0],
    )
    x_grad, gain_grads, wide_gate_up, wide_qkv, tall_down, tall_out = finish(
        (
            qkv,
            attended,
            dattended.reshape(seq, head_lanes),
            log_total,
            cosine,
            sine_part,
            doc_lens,
        ),
        block_input[0],
        gain_one,
        dresid,
        terms_two,
        out_grad,
        qkv_columns,
        normed_one,
        gate_up_sum,
        down_sum,
    )
    shard_rows = 4 * quarter
    grad_qkv, grad_out, grad_gate, grad_up, grad_down = assemble(
        wide_qkv.reshape(n, shard_rows, qkv_lanes),
        wide_gate_up.reshape(n, shard_rows, 2 * lanes),
        tall_down.reshape(lanes, width),
        tall_out.reshape(head_lanes, width),
        units,
    )
    return (
        block_out[None],
        x_grad[None],
        gain_grads[0],
        grad_qkv,
        grad_out,
        gain_grads[1],
        grad_gate,
        grad_up,
        grad_down,
    )


def body_for(mesh):
    return per_device if HEADS % mesh.shape["blk"] == 0 else per_device_gather


def solution(mesh):
    return jax.shard_map(
        body_for(mesh),
        mesh=mesh,
        in_specs=(
            P("grp", "blk", None),
            P("grp", None),
            P("blk"),
            P("blk", None),
            P("blk", None),
            P("blk"),
            P("blk", None),
            P("blk", None),
            P("blk", None),
            P("grp", "blk", None),
        ),
        out_specs=(
            P("grp", "blk", None),
            P("grp", "blk", None),
            P("blk"),
            P("blk", None),
            P("blk", None),
            P("blk"),
            P("blk", None),
            P("blk", None),
            P("blk", None),
        ),
        check_vma=False,
    )
```

```python
import functools
import math

import jax
import jax.numpy as jnp
import numpy as np
from jax import lax
from jax.experimental import pallas as pl
from jax.experimental.pallas import tpu as pltpu
from jax.sharding import PartitionSpec as P

HEADS = 16
HEAD = 128


EPS = 1e-05
NEGATIVE = -1e30


def angle_tables(places):
    half_size = HEAD // 2
    freqs = jnp.exp(jnp.arange(half_size, dtype=jnp.float32) * (-2.0 * math.log(10000.0) / HEAD))
    angles = places.astype(jnp.float32)[:, None] * freqs
    return (jnp.cos(angles)[:, None, :], jnp.sin(angles)[:, None, :])


def rotate(tensor, cosine, sine_part):
    half_size = HEAD // 2
    first_half = tensor[..., :half_size]
    second_half = tensor[..., half_size:]
    return jnp.concatenate(
        [
            first_half * cosine - second_half * sine_part,
            second_half * cosine + first_half * sine_part,
        ],
        axis=-1,
    )


def unrotate(tensor, cosine, sine_part):
    half_size = HEAD // 2
    first_half = tensor[..., :half_size]
    second_half = tensor[..., half_size:]
    return jnp.concatenate(
        [
            first_half * cosine + second_half * sine_part,
            second_half * cosine - first_half * sine_part,
        ],
        axis=-1,
    )


def segment_of(places, starts):
    return jnp.sum((starts[None, :] <= places[:, None]).astype(jnp.int32), axis=1) - 1


def start_of(places, starts):
    return jnp.max(jnp.where(starts[None, :] <= places[:, None], starts[None, :], 0), axis=1)


def contract_rows(left, right):
    return lax.dot_general(
        left, right, (((1,), (1,)), ((), ())), preferred_element_type=jnp.float32
    )


def weight_term(left, right):

    def term(start, count):
        return lax.dot_general(
            left, right, (((0,), (0,)), ((), ())), preferred_element_type=jnp.float32
        )

    return term


def shard_grad(term_fn, shard_rows):
    shared = lax.psum_scatter(
        term_fn(jnp.int32(0), shard_rows * lax.axis_size("blk")).astype(jnp.bfloat16),
        "blk",
        scatter_dimension=0,
        tiled=True,
    )
    return lax.psum(shared, "grp").astype(jnp.float32)


def per_device_gather(block_input, doc_lens, norm_attn, w_qkv, w_out, norm_mlp, w_gate, w_up, w_down, cot):
    tok_rows = block_input.shape[1]
    width = block_input.shape[2]
    score_scale = HEAD ** (-0.5)
    shards = (norm_attn, w_qkv, w_out, norm_mlp, w_gate, w_up, w_down)
    gathered = (
        lax.all_gather(shards[0], "blk", axis=0, tiled=True),
        lax.all_gather(shards[1], "blk", axis=0, tiled=True),
        lax.all_gather(shards[2], "blk", axis=0, tiled=True),
        lax.all_gather(shards[3], "blk", axis=0, tiled=True),
        lax.all_gather(shards[4], "blk", axis=0, tiled=True),
        lax.all_gather(shards[5], "blk", axis=0, tiled=True),
        lax.all_gather(shards[6], "blk", axis=0, tiled=True),
    )
    gain_one, weight_qkv, weight_out, gain_two, weight_gate, weight_up, weight_down = gathered
    place_rows = lax.axis_index("blk") * tok_rows + jnp.arange(tok_rows, dtype=jnp.int32)
    lengths = doc_lens[0]
    starts = jnp.cumsum(lengths) - lengths
    query_seg = segment_of(place_rows, starts)
    cosine, sine_part = angle_tables(place_rows - start_of(place_rows, starts))
    x_float = block_input[0].astype(jnp.float32)
    inv_one = lax.rsqrt(jnp.mean(x_float * x_float, axis=-1, keepdims=True) + EPS)
    normed_one = (x_float * inv_one * gain_one.astype(jnp.float32)).astype(jnp.bfloat16)
    projected = jnp.dot(normed_one, weight_qkv, preferred_element_type=jnp.float32)
    heads_all = projected.reshape(tok_rows, 3, HEADS, HEAD)
    queries = rotate(heads_all[:, 0], cosine, sine_part).astype(jnp.bfloat16)
    keys_own = rotate(heads_all[:, 1], cosine, sine_part).astype(jnp.bfloat16)
    values_own = heads_all[:, 2].astype(jnp.bfloat16)

    def pair_mask(count):
        key_places = jnp.arange(count, dtype=jnp.int32)
        key_seg = segment_of(key_places, starts)
        return (query_seg[:, None] == key_seg[None, :]) & (
            key_places[None, :] <= place_rows[:, None]
        )

    piece = (
        lax.all_gather(keys_own, "blk", axis=0, tiled=True),
        lax.all_gather(values_own, "blk", axis=0, tiled=True),
    )
    count = piece[0].shape[0]
    row_peak = jnp.full((HEADS, tok_rows), NEGATIVE, jnp.float32)
    key_piece, value_piece = piece
    count = key_piece.shape[0]
    allowed = pair_mask(count)[None]
    scores = (
        jnp.einsum("qhd,khd->hqk", queries, key_piece, preferred_element_type=jnp.float32)
        * score_scale
    )
    scores = jnp.where(allowed, scores, NEGATIVE)
    new_peak = jnp.maximum(row_peak, jnp.max(scores, axis=-1))
    weights_now = jnp.where(allowed, jnp.exp(scores - new_peak[..., None]), 0.0)
    row_total = jnp.sum(weights_now, axis=-1)
    accum = jnp.einsum(
        "hqk,khd->hqd",
        weights_now.astype(jnp.bfloat16),
        value_piece,
        preferred_element_type=jnp.float32,
    )
    row_peak, row_total, accum = (new_peak, row_total, accum)
    log_total = row_peak + jnp.log(row_total)
    attended = (accum / row_total[..., None]).transpose(1, 0, 2)
    attended_b = attended.reshape(tok_rows, width).astype(jnp.bfloat16)
    resid = x_float + jnp.dot(attended_b, weight_out, preferred_element_type=jnp.float32)
    inv_two = lax.rsqrt(jnp.mean(resid * resid, axis=-1, keepdims=True) + EPS)
    normed_two = (resid * inv_two * gain_two.astype(jnp.float32)).astype(jnp.bfloat16)
    gate_proj = jnp.dot(normed_two, weight_gate, preferred_element_type=jnp.float32)
    up_proj = jnp.dot(normed_two, weight_up, preferred_element_type=jnp.float32)
    sigmoid_gate = jax.nn.sigmoid(gate_proj)
    swish = gate_proj * sigmoid_gate
    hidden = (swish * up_proj).astype(jnp.bfloat16)
    block_out = (resid + jnp.dot(hidden, weight_down, preferred_element_type=jnp.float32)).astype(
        jnp.bfloat16
    )
    again = (
        lax.all_gather(shards[0], "blk", axis=0, tiled=True),
        lax.all_gather(shards[1], "blk", axis=0, tiled=True),
        lax.all_gather(shards[2], "blk", axis=0, tiled=True),
        lax.all_gather(shards[3], "blk", axis=0, tiled=True),
        lax.all_gather(shards[4], "blk", axis=0, tiled=True),
        lax.all_gather(shards[5], "blk", axis=0, tiled=True),
        lax.all_gather(shards[6], "blk", axis=0, tiled=True),
    )
    back_gain_one, back_qkv, back_out, back_gain_two, back_gate, back_up, back_down = again
    seed = cot[0]
    seed_float = seed.astype(jnp.float32)
    dhidden = contract_rows(seed, back_down)
    dgate = (dhidden * up_proj * sigmoid_gate * (1.0 + gate_proj * (1.0 - sigmoid_gate))).astype(
        jnp.bfloat16
    )
    dup = (dhidden * swish).astype(jnp.bfloat16)
    dnormed_two = contract_rows(dgate, back_gate) + contract_rows(dup, back_up)
    a_two = dnormed_two * back_gain_two.astype(jnp.float32)
    dresid = (
        seed_float
        + inv_two * a_two
        - resid * inv_two**3 * jnp.mean(a_two * resid, axis=-1, keepdims=True)
    )
    dresid_b = dresid.astype(jnp.bfloat16)
    dattended = (
        contract_rows(dresid_b, back_out).astype(jnp.bfloat16).reshape(tok_rows, HEADS, HEAD)
    )
    delta = jnp.sum(dattended.astype(jnp.float32) * attended, axis=-1).T
    piece = (
        lax.all_gather(keys_own, "blk", axis=0, tiled=True),
        lax.all_gather(values_own, "blk", axis=0, tiled=True),
    )
    count = piece[0].shape[0]
    key_piece, value_piece = piece
    count = key_piece.shape[0]
    score_count = key_piece.shape[0]
    allowed = pair_mask(score_count)[None]
    scores = (
        jnp.einsum("qhd,khd->hqk", queries, key_piece, preferred_element_type=jnp.float32)
        * score_scale
    )
    probs = jnp.where(allowed, jnp.exp(scores - log_total[..., None]), 0.0)
    dprobs = jnp.einsum("qhd,khd->hqk", dattended, value_piece, preferred_element_type=jnp.float32)
    dscores = (probs * (dprobs - delta[..., None])).astype(jnp.bfloat16)
    probs, dscores = (probs, dscores)
    dquery_acc = score_scale * jnp.einsum(
        "hqk,khd->hqd", dscores, key_piece, preferred_element_type=jnp.float32
    )
    dkeys = score_scale * jnp.einsum(
        "hqk,qhd->khd", dscores, queries, preferred_element_type=jnp.float32
    )
    dvalues = jnp.einsum(
        "hqk,qhd->khd", probs.astype(jnp.bfloat16), dattended, preferred_element_type=jnp.float32
    )
    stacked = jnp.concatenate([dkeys.reshape(count, width), dvalues.reshape(count, width)], axis=1)
    grads_buffer = stacked
    dquery_acc, grads_buffer = (dquery_acc, grads_buffer)
    own_grads = lax.psum_scatter(
        grads_buffer.astype(jnp.bfloat16), "blk", scatter_dimension=0, tiled=True
    ).astype(jnp.float32)
    dkey = unrotate(own_grads[:, :width].reshape(tok_rows, HEADS, HEAD), cosine, sine_part)
    dvalue = own_grads[:, width:].reshape(tok_rows, HEADS, HEAD)
    dquery = unrotate(dquery_acc.transpose(1, 0, 2), cosine, sine_part)
    dqkv = (
        jnp.stack([dquery, dkey, dvalue], axis=1).reshape(tok_rows, 3 * width).astype(jnp.bfloat16)
    )
    dnormed_one = contract_rows(dqkv, back_qkv)
    a_one = dnormed_one * back_gain_one.astype(jnp.float32)
    x_grad = (
        dresid
        + inv_one * a_one
        - x_float * inv_one**3 * jnp.mean(a_one * x_float, axis=-1, keepdims=True)
    ).astype(jnp.bfloat16)
    width_rows = norm_attn.shape[0]
    gain_terms = jnp.stack(
        [
            jnp.sum(dnormed_one * x_float * inv_one, axis=0),
            jnp.sum(dnormed_two * resid * inv_two, axis=0),
        ],
        axis=1,
    )

    def gain_slice(start, count):
        return gain_terms

    grad_down = shard_grad(weight_term(hidden, seed), w_down.shape[0])
    grad_gate = shard_grad(weight_term(normed_two, dgate), width_rows)
    grad_up = shard_grad(weight_term(normed_two, dup), width_rows)
    grad_out = shard_grad(weight_term(attended_b, dresid_b), width_rows)
    grad_qkv = shard_grad(weight_term(normed_one, dqkv), width_rows)
    gain_grads = shard_grad(gain_slice, width_rows)
    return (
        block_out[None],
        x_grad[None],
        gain_grads[:, 0],
        grad_qkv,
        grad_out,
        gain_grads[:, 1],
        grad_gate,
        grad_up,
        grad_down,
    )


MESH = pl.DeviceIdType.MESH
VMEM_BYTES = 60 * 2**20


def ring_place(block, n):
    up, row = block // 2, block % 2
    return (1 - row) * up + row * (n - 1 - up)


def ring_block(place, n):
    back = place // (n // 2)
    return (1 - back) * 2 * place + back * (2 * (n - 1 - place) + 1)


def at_offset(place, offset, n):
    return ring_block((place + offset + n) % n, n)


def greet(devices):
    barrier = pltpu.get_barrier_semaphore()
    for device in devices:
        pl.semaphore_signal(barrier, inc=1, device_id=device, device_id_type=MESH)
    pl.semaphore_wait(barrier, len(devices))


def push(src, dst, send_sem, recv_sem, device):
    return pltpu.make_async_remote_copy(
        src_ref=src,
        dst_ref=dst,
        send_sem=send_sem,
        recv_sem=recv_sem,
        device_id=device,
        device_id_type=MESH,
    )


def kernel_params(collective_id):
    return pltpu.CompilerParams(
        collective_id=collective_id, has_side_effects=True, vmem_limit_bytes=VMEM_BYTES
    )


def dot_f32(left, right):
    return jnp.dot(left, right, preferred_element_type=jnp.float32)


def dot_t(left, right):
    return lax.dot_general(
        left, right, (((0,), (0,)), ((), ())), preferred_element_type=jnp.float32
    )


def nt_dot(left, right):
    return lax.dot_general(
        left, right, (((1,), (1,)), ((), ())), preferred_element_type=jnp.float32
    )


def ring_ends(n):
    grp, me = lax.axis_index("grp"), lax.axis_index("blk")
    place = ring_place(me, n)
    return place, ((grp, at_offset(place, 1, n)), (grp, at_offset(place, -1, n)))


class Gather:
    def __init__(self, n, buf, send, recv, ends, own=None):
        self.n, self.buf, self.send, self.recv, self.ends = n, buf, send, recv, ends
        self.own = buf.at[0] if own is None else own
        self.half = buf.shape[1] // 2

    def copy(self, step, chunk, way):
        part = pl.ds(chunk * self.half, self.half)
        if isinstance(step, int):
            target = min(2 * step + 1 + way, self.n - 1)
        else:
            target = jnp.minimum(2 * step + 1 + way, self.n - 1)
        first = isinstance(step, int) and step == 0
        return push(
            self.own.at[part] if first else self.buf.at[2 * step - 1 + way, part],
            self.buf.at[target, part],
            self.send.at[step, chunk, way],
            self.recv.at[step, chunk, way],
            self.ends[way],
        )

    def landed(self, step, chunk, way):
        target = jnp.minimum(2 * step + 1 + way, self.n - 1)
        place = self.buf.at[target, pl.ds(chunk * self.half, self.half)]
        sems = (self.send.at[step, chunk, way], self.recv.at[step, chunk, way])
        return push(place, place, *sems, self.ends[way])

    def used(self, step, chunk, way):
        return step < self.n // 2 - 1 or chunk == way

    def start(self):
        for chunk in range(2):
            for way in range(2):
                self.copy(0, chunk, way).start()

    def advance(self, step):
        for chunk in range(2):
            for way in range(2):
                if isinstance(step, int):
                    if self.used(step, chunk, way):
                        self.copy(step, chunk, way).wait_recv()
                        if step + 1 < self.n // 2 and self.used(step + 1, chunk, way):
                            self.copy(step + 1, chunk, way).start()
                elif chunk == way:
                    self.landed(step, chunk, way).wait_recv()
                    pl.when(step + 1 < self.n // 2)(self.copy(step + 1, chunk, way).start)
                else:
                    pl.when(step < self.n // 2 - 1)(self.landed(step, chunk, way).wait_recv)
                    pl.when(step + 1 < self.n // 2 - 1)(self.copy(step + 1, chunk, way).start)

    def finish(self):
        for step in range(self.n // 2):
            for chunk in range(2):
                for way in range(2):
                    if self.used(step, chunk, way):
                        self.copy(step, chunk, way).wait_send()


class Scatter:
    def __init__(self, n, held, terms, send, recv, ends, term):
        self.n, self.held, self.terms, self.send, self.recv = n, held, terms, send, recv
        self.ends, self.term = ends, term
        self.half = held.shape[2] // 2

    def copy(self, step, chunk, way):
        part = pl.ds(chunk * self.half, self.half)
        return push(
            self.held.at[way, step, part],
            self.held.at[way, step + 1, part],
            self.send.at[step, chunk, way],
            self.recv.at[step, chunk, way],
            self.ends[way],
        )

    def step(self, step):
        for way in range(2):
            self.terms[way] = self.term(step, way)
        for chunk in range(2):
            for way in range(2):
                part = pl.ds(chunk * self.half, self.half)

                def first(way=way, part=part):
                    self.held[way, step, part] = self.terms[way, part].astype(jnp.bfloat16)

                def later(chunk=chunk, way=way, part=part):
                    self.copy(step - 1, chunk, way).wait_recv()
                    self.held[way, step, part] = (
                        self.terms[way, part] + self.held[way, step, part].astype(jnp.float32)
                    ).astype(jnp.bfloat16)

                if isinstance(step, int):
                    (later if step else first)()
                else:
                    pl.when(step == 0)(first)
                    pl.when(step > 0)(later)
                self.copy(step, chunk, way).start()

    def result(self, way):
        for chunk in range(2):
            self.copy(self.n - 2, chunk, way).wait_recv()
        return self.term(self.n - 1, way) + self.held[way, self.n - 1].astype(jnp.float32)

    def finish(self):
        def body(step, _):
            for chunk in range(2):
                for way in range(2):
                    self.copy(step, chunk, way).wait_send()
            return 0

        lax.fori_loop(0, self.n - 1, body, 0)


def behind(step, way, n):
    near = 2 * step + 1 + way
    far = 2 * (n - 1 - step) - way
    if isinstance(step, int):
        return 0 if step == n - 1 else min(near, far, n - 1)
    return jnp.where(step == n - 1, 0, jnp.minimum(jnp.minimum(near, far), n - 1))


def team(grp):
    over, core = grp // 2, grp % 2
    return over, core, (1 - over) * 2 + core, over * 2 + 1 - core


def mlp_kernel(
    n,
    lanes,
    ob,
    w_out,
    x_ref,
    gain,
    weights,
    w_down,
    seed_hbm,
    seed_own,
    block_out,
    dresid_out,
    dattended,
    gain_terms,
    wide_sum,
    down_sum,
    out_grad,
    normed,
    seed,
    gate_up,
    down,
    hidden,
    dgate_up,
    held_one,
    held_two,
    terms,
    resid,
    wide,
    wide_c,
    tall,
    tall_c,
    load_sem,
    s_one,
    r_one,
    s_two,
    r_two,
    s_three,
    r_three,
    s_norm,
    r_norm,
    s_dres,
    r_dres,
    s_wc,
    r_wc,
    s_wx,
    r_wx,
    s_tall,
    r_tall,
):
    f32, bf16 = jnp.float32, jnp.bfloat16
    grp, me = lax.axis_index("grp"), lax.axis_index("blk")
    over, core, grp_x, grp_c = team(grp)
    _, ends = ring_ends(n)
    loads = [
        pltpu.make_async_copy(weights, gate_up, load_sem.at[0]),
        pltpu.make_async_copy(w_down, down, load_sem.at[1]),
        pltpu.make_async_copy(
            seed_hbm.at[pl.ds(1, n - 1)], seed.at[pl.ds(1, n - 1)], load_sem.at[2]
        ),
        pltpu.make_async_copy(seed_own, seed.at[0], load_sem.at[3]),
    ]
    for load in loads:
        load.start()
    greet(list(ends) + [(grp_x, me), (grp_c, me)])
    columns = x_ref.shape[1]
    half = columns // 2

    def out_term(step, way):
        return dot_f32(ob[behind(step, way, n)], w_out[:, way * half : (way + 1) * half])

    one = Scatter(n, held_one, terms, s_one, r_one, ends, out_term)
    one.step(0)
    lax.fori_loop(1, n - 1, lambda step, _: (one.step(step), 0)[1], 0)
    for way in range(2):
        part = slice(way * half, (way + 1) * half)
        resid[:, part] = x_ref[:, part].astype(f32) + one.result(way)
    value = resid[...]
    inv = lax.rsqrt(jnp.mean(value * value, axis=-1, keepdims=True) + EPS)
    normed[0] = (value * inv * gain[...]).astype(bf16)
    gather = Gather(n, normed, s_norm, r_norm, ends)
    gather.start()
    one.finish()
    for load in loads:
        load.wait()

    def mlp(slot, _):
        both = dot_f32(normed[slot], gate_up[...])
        grad = nt_dot(seed[slot], down[...])
        gate, up = both[:, :lanes], both[:, lanes:]
        sig = jax.nn.sigmoid(gate)
        swish = gate * sig
        hidden[slot] = (swish * up).astype(bf16)
        dgate_up[slot, :, :lanes] = (grad * up * sig * (1.0 + gate * (1.0 - sig))).astype(bf16)
        dgate_up[slot, :, lanes:] = (grad * swish).astype(bf16)
        return 0

    def norm_term(step, way):
        return nt_dot(dgate_up[behind(step, way, n)], gate_up[way * half : (way + 1) * half, :])

    two = Scatter(n, held_two, terms, s_two, r_two, ends, norm_term)

    def turn(t, _):
        pl.when(t > 0)(lambda: gather.advance(t - 1))
        low = jnp.maximum(2 * t - 1, 0)
        lax.fori_loop(low, jnp.minimum(2 * t + 1, n), mlp, 0)
        pl.when(t > 0)(lambda: two.step(t - 1))
        return 0

    lax.fori_loop(0, n // 2 + 1, turn, 0)

    tall_rows = lanes // 4

    def tall_at(first, count):
        return pl.ds(pl.multiple_of(first * tall_rows, tall_rows), count * tall_rows)

    tiles = [slice(at, min(at + 256, lanes)) for at in range(0, lanes, 256)]

    def tall_grad(tile):
        left = hidden[:, :, tile].reshape(-1, tile.stop - tile.start)
        tall[tile] = dot_t(left, seed[...].reshape(-1, columns)).astype(bf16)

    for index, step in enumerate(range(n // 2, n - 1)):
        for tile in tiles[index :: n // 2 - 1]:
            tall_grad(tile)
        two.step(step)
    tall_one = push(tall.at[tall_at(2 - 2 * core, 2)], tall_c, s_tall.at[0], r_tall.at[0], (grp_c, me))
    tall_one.start()

    value = resid[...]
    inv = lax.rsqrt(jnp.mean(value * value, axis=-1, keepdims=True) + EPS)
    for way in range(2):
        part = slice(way * half, (way + 1) * half)
        dresid_out[:, part] = two.result(way)
    dnormed = dresid_out[...]
    gain_terms[...] = jnp.sum(dnormed * value * inv, axis=0, keepdims=True)
    a_two = dnormed * gain[...]
    total = (
        seed[0].astype(f32)
        + inv * a_two
        - value * inv**3 * jnp.mean(a_two * value, axis=-1, keepdims=True)
    )
    dresid_out[...] = total
    dresid = seed
    dresid[0] = total.astype(bf16)
    back = Gather(n, dresid, s_dres, r_dres, ends)
    back.start()
    two.finish()

    def down_term(step, way):
        return dot_f32(hidden[behind(step, way, n)], down[:, way * half : (way + 1) * half])

    three = Scatter(n, held_one, terms, s_three, r_three, ends, down_term)

    def dob(slot, _):
        dattended[slot] = nt_dot(dresid[slot], w_out[...]).astype(bf16)
        return 0

    def wide_copy_c(tile):
        return push(
            wide.at[tile, 1 - core], wide_c.at[tile], s_wc.at[tile], r_wc.at[tile], (grp_c, me)
        )

    def wide_copy_x(tile):
        return push(
            wide_c.at[tile, 1 - over], wide_sum.at[tile], s_wx.at[tile], r_wx.at[tile], (grp_x, me)
        )

    quarter = wide.shape[3]

    def wide_grad(tile):
        at = pl.multiple_of(tile * 4 * quarter, 4 * quarter)
        left = normed[:, :, pl.ds(at, 4 * quarter)].reshape(-1, 4 * quarter)
        grad = dot_t(left, dgate_up[...].reshape(-1, 2 * lanes)).astype(bf16)
        wide[tile] = grad.reshape(2, 2, quarter, 2 * lanes)
        wide_copy_c(tile).start()

    def wide_pass(tile):
        wide_copy_c(tile).wait_recv()
        wide_c[tile, 1 - over] = (
            wide[tile, core, 1 - over].astype(f32) + wide_c[tile, 1 - over].astype(f32)
        ).astype(bf16)
        wide_copy_x(tile).start()

    tall_two = push(tall_c.at[tall_at(1 - over, 1)], down_sum, s_tall.at[1], r_tall.at[1], (grp_x, me))

    def tall_pass():
        tall_one.wait_recv()
        tall_c[tall_at(1 - over, 1)] = (
            tall[tall_at(2 * core + 1 - over, 1)].astype(f32)
            + tall_c[tall_at(1 - over, 1)].astype(f32)
        ).astype(bf16)
        tall_two.start()

    def wide_take(tile):
        wide_copy_x(tile).wait_recv()
        wide_sum[tile] = (
            wide[tile, core, over].astype(f32)
            + wide_c[tile, over].astype(f32)
            + wide_sum[tile].astype(f32)
        ).astype(bf16)

    def again(t, _):
        pl.when(t > 0)(lambda: back.advance(t - 1))
        low = jnp.maximum(2 * t - 1, 0)
        lax.fori_loop(low, jnp.minimum(2 * t + 1, n), dob, 0)

        def inner(step, _):
            pl.when(step < n - 1)(lambda: three.step(step))

            @pl.when(step < n // 2)
            def _():
                wide_grad(2 * step)
                pl.when(step == 0)(tall_pass)
                pl.when(step > 0)(lambda: wide_pass(2 * step - 1))
                wide_grad(2 * step + 1)
                wide_pass(2 * step)

            pl.when(step == n // 2)(lambda: wide_pass(n - 1))

            @pl.when(step >= n // 2)
            def _():
                wide_take(2 * step - n)
                pl.when(step < n - 1)(lambda: wide_take(2 * step - n + 1))

            return 0

        lax.fori_loop(2 * t, jnp.minimum(2 * t + 2, n), inner, 0)
        return 0

    lax.fori_loop(0, n // 2 + 1, again, 0)
    wide_take(n - 1)
    out_grad[...] = dot_t(
        ob[...].reshape(-1, ob.shape[2]), dresid[...].reshape(-1, columns)
    ).astype(bf16)
    for way in range(2):
        part = slice(way * half, (way + 1) * half)
        block_out[:, part] = (resid[:, part] + three.result(way)).astype(bf16)

    tall_two.wait_recv()
    down_sum[...] = (
        tall[tall_at(2 * core + over, 1)].astype(f32)
        + tall_c[tall_at(over, 1)].astype(f32)
        + down_sum[...].astype(f32)
    ).astype(bf16)
    gather.finish()
    back.finish()
    three.finish()
    tall_one.wait_send()
    tall_two.wait_send()

    def sent(tile, _):
        wide_copy_c(tile).wait_send()
        wide_copy_x(tile).wait_send()
        return 0

    lax.fori_loop(0, n, sent, 0)


def mlp_and_back(ob, w_out, x_own, gain, weights, lanes, w_down, seed, seed_own):
    n = lax.axis_size("blk")
    _, rows, columns = seed.shape
    head_lanes = ob.shape[2]
    quarter = columns // (4 * n)
    f32, bf16 = jnp.float32, jnp.bfloat16
    vmem, dma = pltpu.VMEM, pltpu.SemaphoreType.DMA
    in_vmem, anywhere = pl.BlockSpec(memory_space=vmem), pl.BlockSpec(memory_space=pl.ANY)
    ring = [dma((n - 1, 2, 2))] * 6 + [dma((n // 2, 2, 2))] * 4
    return pl.pallas_call(
        functools.partial(mlp_kernel, n, lanes),
        out_shape=(
            jax.ShapeDtypeStruct((rows, columns), bf16),
            jax.ShapeDtypeStruct((rows, columns), f32),
            jax.ShapeDtypeStruct((n, rows, head_lanes), bf16),
            jax.ShapeDtypeStruct((1, columns), f32),
            jax.ShapeDtypeStruct((n, quarter, 2 * lanes), bf16),
            jax.ShapeDtypeStruct((lanes // 4, columns), bf16),
            jax.ShapeDtypeStruct((head_lanes, columns), bf16),
        ),
        in_specs=[in_vmem] * 4 + [anywhere] * 4,
        out_specs=[in_vmem] * 7,
        scratch_shapes=[
            vmem((n, rows, columns), bf16),
            vmem((n, rows, columns), bf16),
            vmem((columns, 2 * lanes), bf16),
            vmem((lanes, columns), bf16),
            vmem((n, rows, lanes), bf16),
            vmem((n, rows, 2 * lanes), bf16),
            vmem((2, n, rows, columns // 2), bf16),
            vmem((2, n, rows, columns // 2), bf16),
            vmem((2, rows, columns // 2), f32),
            vmem((rows, columns), f32),
            vmem((n, 2, 2, quarter, 2 * lanes), bf16),
            vmem((n, 2, quarter, 2 * lanes), bf16),
            vmem((lanes, columns), bf16),
            vmem((lanes // 2, columns), bf16),
            dma((4,)),
        ]
        + ring
        + [dma((n,))] * 4
        + [dma((2,))] * 2,
        compiler_params=kernel_params(5),
        name="mlp_and_back",
    )(ob, w_out, x_own, gain, weights, w_down, seed, seed_own)


class Spread:
    def __init__(self, n, pieces, out, sems):
        self.n, self.pieces, self.out = n, pieces, out
        self.s_blk, self.r_blk, self.s_x, self.r_x, self.s_c, self.r_c = sems
        self.grp, self.me = lax.axis_index("grp"), lax.axis_index("blk")
        self.over, self.core, self.grp_x, self.grp_c = team(self.grp)

    def first(self, k):
        to = (self.me + k) % self.n
        place = self.out.at[self.me, 2 * self.core + self.over]
        return push(
            self.pieces.at[to], place, self.s_blk.at[k], self.r_blk.at[k], (self.grp, to)
        )

    def own(self, sem):
        place = self.out.at[self.me, 2 * self.core + self.over]
        return pltpu.make_async_copy(self.pieces.at[self.me], place, sem)

    def to_x(self, k, own=False):
        piece = self.out.at[(self.me - k + self.n) % self.n, 2 * self.core + self.over]
        source = self.pieces.at[self.me] if own else piece
        return push(source, piece, self.s_x.at[k], self.r_x.at[k], (self.grp_x, self.me))

    def to_core(self, k, far, own=False):
        over = 1 - self.over if far else self.over
        piece = self.out.at[(self.me - k + self.n) % self.n, 2 * self.core + over]
        source = self.pieces.at[self.me] if own else piece
        sems = (self.s_c.at[int(far), k], self.r_c.at[int(far), k])
        return push(source, piece, *sems, (self.grp_c, self.me))

    def pass_own(self):
        self.to_x(0, True).start()
        self.to_core(0, False, True).start()

    def pass_on(self, k):
        self.first(k).wait_recv()
        self.to_x(k).start()
        self.to_core(k, False).start()

    def pass_far(self, k):
        self.to_x(k).wait_recv()
        self.to_core(k, True).start()

    def arrived(self, k):
        for far in (False, True):
            self.to_core(k, far).wait_recv()

    def finish(self):
        def body(k, _):
            pl.when(k > 0)(self.first(k).wait_send)
            self.to_x(k).wait_send()
            for far in (False, True):
                self.to_core(k, far).wait_send()
            return 0

        lax.fori_loop(0, self.n, body, 0)


def each(count, body, low=0):
    lax.fori_loop(low, count, lambda k, _: (body(k), 0)[1], 0)


def spread_sems(n):
    dma = pltpu.SemaphoreType.DMA
    return [dma((n,)), dma((n,)), dma((n,)), dma((n,)), dma((2, n)), dma((2, n))]


def team_and_ring(n):
    grp, me = lax.axis_index("grp"), lax.axis_index("blk")
    _, _, grp_x, grp_c = team(grp)
    return [(grp, (me + k) % n) for k in range(1, n)] + [(grp_x, me), (grp_c, me)]


def fill_row(row, gains_all, which, share):
    for block in range(gains_all.shape[0]):
        row[:, block * share : (block + 1) * share] = gains_all[block, which : which + 1, :]


def turned(value, cosine, sine_part):
    half_size = HEAD // 2
    swapped = jnp.concatenate([value[:, half_size:], value[:, :half_size]], axis=1)
    return value * cosine + swapped * sine_part


def mark_places(n, doc_lens, rows, first_key, query_place, key_place):
    place = ring_place(lax.axis_index("blk"), n)
    for slot in range(n):
        offset = (slot + 1) // 2 * (1 if slot % 2 == 0 else -1)
        first_row = at_offset(place, offset, n) * rows
        part = slice(slot * rows, (slot + 1) * rows)
        here = first_row + lax.broadcasted_iota(jnp.int32, (rows, 1), 0)
        query_place[part, :] = here
        key_place[:, part] = first_row + lax.broadcasted_iota(jnp.int32, (1, rows), 1)
        start = jnp.int32(0)
        found = jnp.zeros((rows, 1), jnp.int32)
        for index in range(doc_lens.shape[1]):
            found = jnp.maximum(found, jnp.where(here >= start, start, 0))
            start = start + doc_lens[0, index]
        first_key[part, :] = found


def attend_kernel(
    n,
    heads,
    doc_lens,
    x_own,
    freqs,
    norm_attn,
    norm_mlp,
    w_qkv,
    w_gate,
    w_up,
    seed_own,
    gain_row,
    gain_two,
    columns_qkv,
    normed,
    qkv,
    attended,
    attended_b,
    log_total,
    cosine,
    sine_part,
    gate_up,
    seed,
    x_all,
    gains_all,
    gains,
    raw_qkv,
    raw_gate,
    raw_up,
    slab_qkv,
    slab_gate_up,
    first_key,
    query_place,
    key_place,
    local,
    s_gain,
    r_gain,
    s_x,
    r_x,
    s_seed,
    r_seed,
    *spread_all,
):
    f32, bf16 = jnp.float32, jnp.bfloat16
    grp, me = lax.axis_index("grp"), lax.axis_index("blk")
    _, ends = ring_ends(n)
    rows, columns = x_own.shape
    spread_qkv = Spread(n, slab_qkv, columns_qkv, spread_all[:6])
    spread_gu = Spread(n, slab_gate_up, gate_up, spread_all[6:])
    over, core, _, _ = team(grp)
    quarter = slab_qkv.shape[1]
    own_rows = pl.ds(pl.multiple_of((2 * core + over) * quarter, quarter), quarter)
    loads = [
        pltpu.make_async_copy(weight.at[own_rows], raw, local.at[index])
        for index, (weight, raw) in enumerate(
            ((w_qkv, raw_qkv), (w_gate, raw_gate), (w_up, raw_up))
        )
    ]
    for load in loads:
        load.start()
    x_all[0] = x_own[...]
    gains[...] = jnp.zeros_like(gains)
    gains[0:1, :] = norm_attn[...].astype(f32).reshape(1, -1)
    gains[1:2, :] = norm_mlp[...].astype(f32).reshape(1, -1)
    gains_all[me] = gains[...]
    greet(team_and_ring(n))

    def gain(k):
        return push(gains, gains_all.at[me], s_gain.at[k], r_gain.at[k], (grp, (me + k) % n))

    each(n, lambda k: gain(k).start(), 1)
    x_ring = Gather(n, x_all, s_x, r_x, ends)
    x_ring.start()
    share = heads * HEAD
    loads[0].wait()
    for to in range(n):
        for part in range(3):
            slab_qkv[to, :, part * share : (part + 1) * share] = raw_qkv[
                :, (part * n + to) * share : (part * n + to + 1) * share
            ]
    near_qkv = spread_qkv.own(local.at[3])
    near_qkv.start()
    each(n, lambda k: spread_qkv.first(k).start(), 1)
    spread_qkv.pass_own()
    units = raw_gate.shape[1] // n
    loads[1].wait()
    loads[2].wait()
    for to in range(n):
        lane = slice(to * units, (to + 1) * units)
        slab_gate_up[to] = jnp.concatenate(
            [raw_gate[:, lane].astype(f32), raw_up[:, lane].astype(f32)], axis=1
        ).astype(bf16)
    near_gu = spread_gu.own(local.at[4])
    near_gu.start()
    mark_places(n, doc_lens, rows, first_key, query_place, key_place)

    def norm(slot):
        value = x_all[slot].astype(f32)
        inv = lax.rsqrt(jnp.mean(value * value, axis=-1, keepdims=True) + EPS)
        normed[slot] = (value * inv * gain_row[...]).astype(bf16)

    each(n, lambda k: gain(k).wait_recv(), 1)
    fill_row(gain_row, gains_all, 0, columns // n)
    fill_row(gain_two, gains_all, 1, columns // n)

    def table(slot):
        at = pl.ds(pl.multiple_of(slot * rows, rows), rows)
        angle = (query_place[at, :] - first_key[at, :]).astype(f32) * freqs[...]
        lane = lax.broadcasted_iota(jnp.int32, (rows, HEAD), 1)
        sine = jnp.sin(angle)
        cosine[at, :] = jnp.cos(angle)
        sine_part[at, :] = jnp.where(lane < HEAD // 2, -sine, sine)

    def arrive(t):
        pl.when(t > 0)(lambda: x_ring.advance(t - 1))
        low = jnp.maximum(2 * t - 1, 0)
        each(jnp.minimum(2 * t + 1, n), norm, low)
        each(jnp.minimum(2 * t + 1, n), table, low)
        pl.when(t == 2)(lambda: each(n, spread_qkv.pass_on, 1))
        pl.when(t == 3)(lambda: each(n, spread_qkv.pass_far))

        @pl.when(t == 2)
        def _():
            each(n, lambda k: spread_gu.first(k).start(), 1)
            spread_gu.pass_own()


    each(n // 2 + 1, arrive)
    seed_ring = Gather(n, seed, s_seed, r_seed, ends, seed_own)
    each(n, spread_gu.pass_on, 1)
    seed_ring.start()
    each(n, spread_qkv.arrived)
    near_qkv.wait()


    head_lanes = heads * HEAD
    pair = 2 * rows

    def project(i):
        both = normed[pl.ds(2 * i, 2)].reshape(pair, columns)
        result = dot_f32(both, columns_qkv[...].reshape(columns, 3 * head_lanes))
        at = pl.ds(pl.multiple_of(i * pair, pair), pair)
        table_c, table_s = cosine[at, :], sine_part[at, :]
        for piece in range(3 * heads):
            lane = slice(piece * HEAD, (piece + 1) * HEAD)
            value = result[:, lane]
            if piece < 2 * heads:
                value = turned(value, table_c, table_s)
            qkv[at, lane] = value.astype(bf16)

    each(n // 2, project)


    def tile(i):
        for head in range(heads):
            lane = slice(head * HEAD, (head + 1) * HEAD)
            at = pl.ds(pl.multiple_of(i * pair, pair), pair)
            keys = qkv[:, head_lanes + head * HEAD : head_lanes + (head + 1) * HEAD]
            values = qkv[:, 2 * head_lanes + head * HEAD : 2 * head_lanes + (head + 1) * HEAD]
            scores = nt_dot(qkv[at, lane], keys) * HEAD ** (-0.5)
            allowed = (key_place[...] >= first_key[at, :]) & (key_place[...] <= query_place[at, :])
            scores = jnp.where(allowed, scores, NEGATIVE)
            peak = jnp.max(scores, axis=-1, keepdims=True)
            raw = jnp.exp(scores - peak)
            total = jnp.sum(raw, axis=-1, keepdims=True)
            out = dot_f32(raw.astype(bf16), values) / total
            attended[at, lane] = out
            attended_b[at, lane] = out.astype(bf16)
            log_total[head, at, :] = peak + jnp.log(total)
        seed_ring.advance(i)
        pl.when(i == 1)(lambda: each(n, spread_gu.pass_far))

    each(n // 2, tile)
    each(n, spread_gu.arrived)
    near_gu.wait()
    for spread in (spread_qkv, spread_gu):
        spread.finish()
    each(n, lambda k: gain(k).wait_send(), 1)
    x_ring.finish()
    seed_ring.finish()


def attend(doc_lens, x_own, norm_attn, norm_mlp, w_qkv, w_gate, w_up, seed_own):
    n = lax.axis_size("blk")
    rows, columns = x_own.shape
    seq = n * rows
    lanes = w_qkv.shape[1] // n
    quarter = w_qkv.shape[0] // 4
    both = 2 * w_gate.shape[1] // n
    head_lanes = lanes // 3
    heads = head_lanes // HEAD
    share = norm_attn.shape[0]
    f32, bf16, i32 = jnp.float32, jnp.bfloat16, jnp.int32
    vmem, dma = pltpu.VMEM, pltpu.SemaphoreType.DMA
    in_vmem, anywhere = pl.BlockSpec(memory_space=vmem), pl.BlockSpec(memory_space=pl.ANY)
    half_freqs = np.exp(
        np.arange(HEAD // 2, dtype=np.float32) * np.float32(-2.0 * math.log(10000.0) / HEAD)
    )
    freqs = jnp.asarray(np.concatenate([half_freqs, half_freqs])[None].astype(np.float32))
    return pl.pallas_call(
        functools.partial(attend_kernel, n, heads),
        out_shape=(
            jax.ShapeDtypeStruct((1, columns), f32),
            jax.ShapeDtypeStruct((1, columns), f32),
            jax.ShapeDtypeStruct((n, 4, quarter, lanes), bf16),
            jax.ShapeDtypeStruct((n, rows, columns), bf16),
            jax.ShapeDtypeStruct((seq, lanes), bf16),
            jax.ShapeDtypeStruct((seq, head_lanes), f32),
            jax.ShapeDtypeStruct((seq, head_lanes), bf16),
            jax.ShapeDtypeStruct((heads, seq, 1), f32),
            jax.ShapeDtypeStruct((seq, HEAD), f32),
            jax.ShapeDtypeStruct((seq, HEAD), f32),
            jax.ShapeDtypeStruct((n, 4, quarter, both), bf16),
            jax.ShapeDtypeStruct((n, rows, columns), bf16),
        ),
        in_specs=[pl.BlockSpec(memory_space=pltpu.SMEM)] + [in_vmem] * 4 + [anywhere] * 4,
        out_specs=[in_vmem] * 10 + [anywhere] * 2,
        scratch_shapes=[
            vmem((n, rows, columns), bf16),
            vmem((n, 8, share), f32),
            vmem((8, share), f32),
            vmem((quarter, n * lanes), bf16),
            vmem((quarter, w_gate.shape[1]), bf16),
            vmem((quarter, w_gate.shape[1]), bf16),
            vmem((n, quarter, lanes), bf16),
            vmem((n, quarter, both), bf16),
            vmem((seq, 1), i32),
            vmem((seq, 1), i32),
            vmem((1, seq), i32),
            dma((5,)),
            dma((n,)),
            dma((n,)),
        ]
        + [dma((n // 2, 2, 2))] * 4
        + spread_sems(n) * 2,
        compiler_params=kernel_params(0),
        name="attend",
    )(
        doc_lens,
        x_own,
        freqs,
        norm_attn,
        norm_mlp,
        w_qkv,
        w_gate,
        w_up,
        seed_own,
    )


def finish_kernel(
    n,
    heads,
    qkv,
    attended,
    dattended,
    log_total,
    cosine,
    sine_part,
    doc_lens,
    x_own,
    gain,
    dresid,
    terms_two,
    out_grad,
    weights,
    normed_hbm,
    gate_up_sum,
    down_sum,
    x_grad,
    gain_grads,
    wide_gate_up,
    wide_qkv,
    tall_down,
    tall_out,
    normed,
    columns_qkv,
    dqkv,
    dkeys,
    dvalues,
    first_key,
    query_place,
    key_place,
    held,
    terms,
    wide,
    wide_c,
    wide_x,
    out_c,
    out_x,
    gain_slabs,
    gain_heard,
    gain_team,
    load_sem,
    s_ring,
    r_ring,
    s_wc,
    r_wc,
    s_wx,
    r_wx,
    s_tall,
    r_tall,
    s_gain,
    r_gain,
    *spread_all,
):
    f32, bf16 = jnp.float32, jnp.bfloat16
    grp, me = lax.axis_index("grp"), lax.axis_index("blk")
    over, core, grp_x, grp_c = team(grp)
    _, ends = ring_ends(n)
    rows, columns = x_own.shape
    half = columns // 2
    lanes = wide.shape[4]
    quarter = wide.shape[3]
    load_normed = pltpu.make_async_copy(normed_hbm, normed, load_sem.at[0])
    load_qkv = pltpu.make_async_copy(weights, columns_qkv, load_sem.at[1])
    load_normed.start()
    load_qkv.start()
    spread_gu = Spread(n, gate_up_sum, wide_gate_up, spread_all[:6])
    spread_qkv = Spread(n, wide_x, wide_qkv, spread_all[6:])
    near_gu = spread_gu.own(load_sem.at[2])
    near_gu.start()
    greet(team_and_ring(n))

    down_own = pltpu.make_async_copy(down_sum, tall_down.at[2 * core + over], load_sem.at[3])
    down_own.start()
    down_place = tall_down.at[2 * core + over]
    down_x = push(down_sum, down_place, s_tall.at[0], r_tall.at[0], (grp_x, me))
    down_c = push(down_sum, down_place, s_tall.at[1], r_tall.at[1], (grp_c, me))
    far_place = tall_down.at[2 * core + 1 - over]
    down_far = push(far_place, far_place, s_tall.at[2], r_tall.at[2], (grp_c, me))
    out_one = push(out_grad.at[1 - core], out_c, s_tall.at[3], r_tall.at[3], (grp_c, me))
    out_two = push(out_c.at[1 - over], out_x, s_tall.at[4], r_tall.at[4], (grp_x, me))
    out_place = tall_out.at[2 * core + over]
    out_own = pltpu.make_async_copy(out_x, out_place, load_sem.at[4])
    out_to_x = push(out_x, out_place, s_tall.at[5], r_tall.at[5], (grp_x, me))
    out_to_c = push(out_x, out_place, s_tall.at[6], r_tall.at[6], (grp_c, me))
    out_far_place = tall_out.at[2 * core + 1 - over]
    out_far = push(out_far_place, out_far_place, s_tall.at[7], r_tall.at[7], (grp_c, me))
    out_one.start()
    each(n, lambda k: spread_gu.first(k).start(), 1)
    spread_gu.pass_own()
    down_x.start()
    down_c.start()

    mark_places(n, doc_lens, rows, first_key, query_place, key_place)
    pair = 2 * rows
    head_lanes = heads * HEAD
    scale = HEAD ** (-0.5)

    def unturned(value, at):
        return turned(value, cosine[at, :], -sine_part[at, :]).astype(bf16)

    def tile(i, head):
        at = pl.ds(pl.multiple_of(i * pair, pair), pair)
        lane = slice(head * HEAD, (head + 1) * HEAD)
        query = qkv[at, lane]
        keys = qkv[:, head_lanes + head * HEAD : head_lanes + (head + 1) * HEAD]
        values = qkv[:, 2 * head_lanes + head * HEAD : 2 * head_lanes + (head + 1) * HEAD]
        grad = dattended[at, lane]
        delta = jnp.sum(grad.astype(f32) * attended[at, lane], axis=-1, keepdims=True)
        scores = nt_dot(query, keys) * scale
        allowed = (key_place[...] >= first_key[at, :]) & (key_place[...] <= query_place[at, :])
        probs = jnp.where(allowed, jnp.exp(scores - log_total[head, at, :]), 0.0)
        dscores = (probs * (nt_dot(grad, values) - delta)).astype(bf16)
        dqkv[2 * i : 2 * i + 2, :, lane] = unturned(dot_f32(dscores, keys) * scale, at).reshape(
            2, rows, HEAD
        )
        more_keys = dot_t(dscores, query)
        more_values = dot_t(probs.astype(bf16), grad)
        if i == 0:
            dkeys[...] = more_keys
            dvalues[...] = more_values
        else:
            dkeys[...] += more_keys
            dvalues[...] += more_values

    for head in range(heads):
        for i in range(n // 2):
            tile(i, head)
        everything = slice(0, n * rows)
        lane = slice(head_lanes + head * HEAD, head_lanes + (head + 1) * HEAD)
        dqkv[:, :, lane] = unturned(dkeys[...] * scale, everything).reshape(n, rows, HEAD)
        lane = slice(2 * head_lanes + head * HEAD, 2 * head_lanes + (head + 1) * HEAD)
        dqkv[:, :, lane] = dvalues[...].astype(bf16).reshape(n, rows, HEAD)
    load_qkv.wait()

    def term(step, way):
        return nt_dot(dqkv[behind(step, way, n)], columns_qkv[way * half : (way + 1) * half, :])

    ring = Scatter(n, held, terms, s_ring, r_ring, ends, term)

    def copy_c(k):
        tile = (me + k) % n
        return push(wide.at[tile, 1 - core], wide_c.at[tile], s_wc.at[k], r_wc.at[k], (grp_c, me))

    def copy_x(k):
        tile = (me + k) % n
        return push(
            wide_c.at[tile, 1 - over], wide_x.at[tile], s_wx.at[k], r_wx.at[k], (grp_x, me)
        )

    def grad(k):
        tile = (me + k) % n
        at = pl.multiple_of(tile * 4 * quarter, 4 * quarter)
        left = normed[:, :, pl.ds(at, 4 * quarter)].reshape(-1, 4 * quarter)
        grad_rows = dot_t(left, dqkv[...].reshape(-1, lanes)).astype(bf16)
        wide[tile] = grad_rows.reshape(2, 2, quarter, lanes)
        copy_c(k).start()

    def pass_x(k):
        tile = (me + k) % n
        copy_c(k).wait_recv()
        wide_c[tile, 1 - over] = (
            wide[tile, core, 1 - over].astype(f32) + wide_c[tile, 1 - over].astype(f32)
        ).astype(bf16)
        copy_x(k).start()

    def take(k):
        tile = (me + k) % n
        copy_x(k).wait_recv()
        wide_x[tile] = (
            wide[tile, core, over].astype(f32)
            + wide_c[tile, over].astype(f32)
            + wide_x[tile].astype(f32)
        ).astype(bf16)

    def take_and_push(k):
        take(k)
        spread_qkv.first(k).start()

    ring.step(0)
    load_normed.wait()

    def grads(i):
        k = (i + 1) % n
        grad(k)
        pl.when(i > 0)(lambda: pass_x(i))

    each(n, grads)
    pass_x(0)
    out_one.wait_recv()
    out_c[1 - over] = (
        out_grad[core, 1 - over].astype(f32) + out_c[1 - over].astype(f32)
    ).astype(bf16)
    out_two.start()

    def turn(k):
        pl.when(k < n - 2)(lambda: ring.step(k + 1))
        each(jnp.minimum(2 * k + 3, n), spread_gu.pass_on, jnp.minimum(2 * k + 1, n))
        pl.when(k < n - 1)(lambda: take_and_push(k + 1))
        pl.when(k >= 2)(lambda: spread_qkv.pass_on(k - 1))

        @pl.when(k == n - 2)
        def _():
            take(0)
            spread_qkv.pass_own()

    each(n - 1, turn)
    near_qkv = spread_qkv.own(load_sem.at[5])
    near_qkv.start()
    each(n, spread_qkv.pass_on, n - 2)

    x_float = x_own[...].astype(f32)
    inv = lax.rsqrt(jnp.mean(x_float * x_float, axis=-1, keepdims=True) + EPS)
    for way in range(2):
        terms[way] = ring.result(way)
    dnormed = jnp.concatenate([terms[0], terms[1]], axis=1)
    terms_one = jnp.sum(dnormed * x_float * inv, axis=0, keepdims=True)
    share = columns // n
    for block in range(n):
        gain_slabs[block] = jnp.zeros_like(gain_slabs[block])
        lane = slice(block * share, (block + 1) * share)
        gain_slabs[block, 0:1, :] = terms_one[:, lane]
        gain_slabs[block, 1:2, :] = terms_two[:, lane]

    def gain_blk(k):
        to = (me + k) % n
        return push(gain_slabs.at[to], gain_heard.at[k], s_gain.at[k], r_gain.at[k], (grp, to))

    each(n, lambda k: gain_blk(k).start(), 1)
    a_one = dnormed * gain[...]
    x_grad[...] = (
        dresid[...]
        + inv * a_one
        - x_float * inv**3 * jnp.mean(a_one * x_float, axis=-1, keepdims=True)
    ).astype(bf16)
    gain_heard[0] = gain_slabs[me]
    each(n, lambda k: gain_blk(k).wait_recv(), 1)
    gain_team[0] = jnp.sum(gain_heard[...], axis=0)
    gain_c = push(gain_team.at[0], gain_team.at[1], s_gain.at[n], r_gain.at[n], (grp_c, me))
    gain_c.start()
    out_two.wait_recv()
    out_x[...] = (
        out_grad[core, over].astype(f32) + out_c[over].astype(f32) + out_x[...].astype(f32)
    ).astype(bf16)
    out_own.start()
    out_to_x.start()
    out_to_c.start()
    each(n, spread_gu.pass_far)
    down_x.wait_recv()
    down_far.start()
    gain_c.wait_recv()
    gain_team[2] = gain_team[0] + gain_team[1]
    gain_x = push(
        gain_team.at[2], gain_team.at[3], s_gain.at[n + 1], r_gain.at[n + 1], (grp_x, me)
    )
    gain_x.start()
    out_to_x.wait_recv()
    out_far.start()
    each(n, spread_qkv.pass_far)
    gain_x.wait_recv()
    gain_grads[...] = gain_team[2] + gain_team[3]
    near_gu.wait()
    near_qkv.wait()
    each(n, spread_gu.arrived)
    each(n, spread_qkv.arrived)
    spread_gu.finish()
    spread_qkv.finish()
    ring.finish()
    down_own.wait()
    out_own.wait()
    for copy in (down_c, down_far, out_to_c, out_far):
        copy.wait()
    for copy in (down_x, out_one, out_two, out_to_x, gain_c, gain_x):
        copy.wait_send()

    def sent(k):
        copy_c(k).wait_send()
        copy_x(k).wait_send()
        pl.when(k > 0)(gain_blk(k).wait_send)

    each(n, sent)


def finish(
    attention, x_own, gain, dresid, terms_two, out_grad, weights, normed, gate_up_sum, down_sum
):
    n, rows, columns = normed.shape
    seq, lanes = attention[0].shape
    heads = lanes // (3 * HEAD)
    quarter = columns // (4 * n)
    share = columns // n
    f32, bf16 = jnp.float32, jnp.bfloat16
    vmem, dma = pltpu.VMEM, pltpu.SemaphoreType.DMA
    in_vmem, anywhere = pl.BlockSpec(memory_space=vmem), pl.BlockSpec(memory_space=pl.ANY)
    out_rows = out_grad.shape[0] // 4
    return pl.pallas_call(
        functools.partial(finish_kernel, n, heads),
        out_shape=(
            jax.ShapeDtypeStruct((rows, columns), bf16),
            jax.ShapeDtypeStruct((8, share), f32),
            jax.ShapeDtypeStruct((n, 4) + gate_up_sum.shape[1:], bf16),
            jax.ShapeDtypeStruct((n, 4, quarter, lanes), bf16),
            jax.ShapeDtypeStruct((4,) + down_sum.shape, bf16),
            jax.ShapeDtypeStruct((4, out_rows, columns), bf16),
        ),
        in_specs=[in_vmem] * 6
        + [pl.BlockSpec(memory_space=pltpu.SMEM)]
        + [in_vmem] * 5
        + [anywhere] * 4,
        out_specs=[in_vmem] * 2 + [anywhere] * 4,
        scratch_shapes=[
            vmem((n, rows, columns), bf16),
            vmem((columns, lanes), bf16),
            vmem((n, rows, lanes), bf16),
            vmem((seq, HEAD), f32),
            vmem((seq, HEAD), f32),
            vmem((seq, 1), jnp.int32),
            vmem((seq, 1), jnp.int32),
            vmem((1, seq), jnp.int32),
            vmem((2, n, rows, columns // 2), bf16),
            vmem((2, rows, columns // 2), f32),
            vmem((n, 2, 2, quarter, lanes), bf16),
            vmem((n, 2, quarter, lanes), bf16),
            vmem((n, quarter, lanes), bf16),
            vmem((2, out_rows, columns), bf16),
            vmem((out_rows, columns), bf16),
            vmem((n, 8, share), f32),
            vmem((n, 8, share), f32),
            vmem((4, 8, share), f32),
            dma((6,)),
        ]
        + [dma((n - 1, 2, 2))] * 2
        + [dma((n,))] * 4
        + [dma((8,))] * 2
        + [dma((n + 2,))] * 2
        + spread_sems(n) * 2,
        compiler_params=kernel_params(6),
        name="finish",
    )(
        *attention,
        x_own,
        gain,
        dresid,
        terms_two,
        out_grad.reshape(2, 2, out_rows, columns),
        weights,
        normed,
        gate_up_sum,
        down_sum,
    )


def assemble_kernel(n, units, lanes, head_lanes, qkv, gate_up, down, out, blocks, shift, *grads):
    grad_qkv, grad_out, grad_gate, grad_up, grad_down, block_out, x_grad = grads
    block_out[...] = blocks[...]
    x_grad[...] = shift[...]
    f32 = jnp.float32
    for source in range(n):
        for part in range(3):
            first = (part * n + source) * head_lanes
            grad_qkv[:, first : first + head_lanes] = qkv[
                source, :, part * head_lanes : (part + 1) * head_lanes
            ].astype(f32)
        first = source * units
        grad_gate[:, first : first + units] = gate_up[source, :, :units].astype(f32)
        grad_up[:, first : first + units] = gate_up[source, :, lanes : lanes + units].astype(f32)
    grad_out[...] = out[...].astype(f32)
    grad_down[...] = down[...].astype(f32)


def assemble(qkv, gate_up, down, out, block_out, x_grad, units, steps=4):
    n, rows, qkv_lanes = qkv.shape
    columns = down.shape[1]
    lanes = gate_up.shape[2] // 2
    head_lanes = qkv_lanes // 3
    step = rows // steps
    down_step = units // steps
    tokens = x_grad.shape[0] // steps
    f32 = jnp.float32

    def wide(width):
        return pl.BlockSpec((n, step, width), lambda i: (0, i, 0))

    def flat(height, width):
        return pl.BlockSpec((height, width), lambda i: (i, 0))

    return pl.pallas_call(
        functools.partial(assemble_kernel, n, units, lanes, head_lanes),
        grid=(steps,),
        out_shape=(
            jax.ShapeDtypeStruct((rows, n * qkv_lanes), f32),
            jax.ShapeDtypeStruct((rows, columns), f32),
            jax.ShapeDtypeStruct((rows, n * units), f32),
            jax.ShapeDtypeStruct((rows, n * units), f32),
            jax.ShapeDtypeStruct((units, columns), f32),
            jax.ShapeDtypeStruct(block_out.shape, block_out.dtype),
            jax.ShapeDtypeStruct(x_grad.shape, x_grad.dtype),
        ),
        in_specs=[
            wide(qkv_lanes),
            wide(2 * lanes),
            flat(down_step, columns),
            flat(out.shape[0] // steps, columns),
            flat(tokens, columns),
            flat(tokens, columns),
        ],
        out_specs=[
            flat(step, n * qkv_lanes),
            flat(step, columns),
            flat(step, n * units),
            flat(step, n * units),
            flat(down_step, columns),
            flat(tokens, columns),
            flat(tokens, columns),
        ],
        compiler_params=pltpu.CompilerParams(vmem_limit_bytes=VMEM_BYTES),
        name="assemble",
    )(qkv, gate_up, down, out, block_out, x_grad)


def per_device(block_input, doc_lens, norm_attn, w_qkv, w_out, norm_mlp, w_gate, w_up, w_down, cot):
    n = lax.axis_size("blk")
    tok_rows, width = block_input.shape[1:]
    seq = tok_rows * n
    heads = HEADS // n
    head_lanes = heads * HEAD
    qkv_lanes = 3 * head_lanes
    units = w_down.shape[0]
    lanes = units
    quarter = w_qkv.shape[0] // 4
    (
        gain_one,
        gain_two,
        qkv_columns,
        normed_one,
        qkv,
        attended,
        attended_b,
        log_total,
        cosine,
        sine_part,
        gate_up,
        seed,
    ) = attend(doc_lens, block_input[0], norm_attn, norm_mlp, w_qkv, w_gate, w_up, cot[0])
    qkv_columns = qkv_columns.reshape(width, qkv_lanes)
    gate_up = gate_up.reshape(width, 2 * lanes)
    block_out, dresid, dattended, terms_two, gate_up_sum, down_sum, out_grad = mlp_and_back(
        attended_b.reshape(n, tok_rows, head_lanes),
        w_out,
        block_input[0],
        gain_two,
        gate_up,
        lanes,
        w_down,
        seed,
        cot[0],
    )
    x_grad, gain_grads, wide_gate_up, wide_qkv, tall_down, tall_out = finish(
        (
            qkv,
            attended,
            dattended.reshape(seq, head_lanes),
            log_total,
            cosine,
            sine_part,
            doc_lens,
        ),
        block_input[0],
        gain_one,
        dresid,
        terms_two,
        out_grad,
        qkv_columns,
        normed_one,
        gate_up_sum,
        down_sum,
    )
    shard_rows = 4 * quarter
    grad_qkv, grad_out, grad_gate, grad_up, grad_down, block_out, x_grad = assemble(
        wide_qkv.reshape(n, shard_rows, qkv_lanes),
        wide_gate_up.reshape(n, shard_rows, 2 * lanes),
        tall_down.reshape(lanes, width),
        tall_out.reshape(head_lanes, width),
        block_out,
        x_grad,
        units,
    )
    return (
        block_out[None],
        x_grad[None],
        gain_grads[0],
        grad_qkv,
        grad_out,
        gain_grads[1],
        grad_gate,
        grad_up,
        grad_down,
    )


def body_for(mesh):
    return per_device if HEADS % mesh.shape["blk"] == 0 else per_device_gather


def solution(mesh):
    return jax.shard_map(
        body_for(mesh),
        mesh=mesh,
        in_specs=(
            P("grp", "blk", None),
            P("grp", None),
            P("blk"),
            P("blk", None),
            P("blk", None),
            P("blk"),
            P("blk", None),
            P("blk", None),
            P("blk", None),
            P("grp", "blk", None),
        ),
        out_specs=(
            P("grp", "blk", None),
            P("grp", "blk", None),
            P("blk"),
            P("blk", None),
            P("blk", None),
            P("blk"),
            P("blk", None),
            P("blk", None),
            P("blk", None),
        ),
        check_vma=False,
    )
```

```python
import functools
import math

import jax
import jax.numpy as jnp
import numpy as np
from jax import lax
from jax.experimental import pallas as pl
from jax.experimental.pallas import tpu as pltpu
from jax.sharding import PartitionSpec as P

HEADS = 16
HEAD = 128


EPS = 1e-05
NEGATIVE = -1e30


def angle_tables(places):
    half_size = HEAD // 2
    freqs = jnp.exp(jnp.arange(half_size, dtype=jnp.float32) * (-2.0 * math.log(10000.0) / HEAD))
    angles = places.astype(jnp.float32)[:, None] * freqs
    return (jnp.cos(angles)[:, None, :], jnp.sin(angles)[:, None, :])


def rotate(tensor, cosine, sine_part):
    half_size = HEAD // 2
    first_half = tensor[..., :half_size]
    second_half = tensor[..., half_size:]
    return jnp.concatenate(
        [
            first_half * cosine - second_half * sine_part,
            second_half * cosine + first_half * sine_part,
        ],
        axis=-1,
    )


def unrotate(tensor, cosine, sine_part):
    half_size = HEAD // 2
    first_half = tensor[..., :half_size]
    second_half = tensor[..., half_size:]
    return jnp.concatenate(
        [
            first_half * cosine + second_half * sine_part,
            second_half * cosine - first_half * sine_part,
        ],
        axis=-1,
    )


def segment_of(places, starts):
    return jnp.sum((starts[None, :] <= places[:, None]).astype(jnp.int32), axis=1) - 1


def start_of(places, starts):
    return jnp.max(jnp.where(starts[None, :] <= places[:, None], starts[None, :], 0), axis=1)


def contract_rows(left, right):
    return lax.dot_general(
        left, right, (((1,), (1,)), ((), ())), preferred_element_type=jnp.float32
    )


def weight_term(left, right):

    def term(start, count):
        return lax.dot_general(
            left, right, (((0,), (0,)), ((), ())), preferred_element_type=jnp.float32
        )

    return term


def shard_grad(term_fn, shard_rows):
    shared = lax.psum_scatter(
        term_fn(jnp.int32(0), shard_rows * lax.axis_size("blk")).astype(jnp.bfloat16),
        "blk",
        scatter_dimension=0,
        tiled=True,
    )
    return lax.psum(shared, "grp").astype(jnp.float32)


def per_device_gather(block_input, doc_lens, norm_attn, w_qkv, w_out, norm_mlp, w_gate, w_up, w_down, cot):
    tok_rows = block_input.shape[1]
    width = block_input.shape[2]
    score_scale = HEAD ** (-0.5)
    shards = (norm_attn, w_qkv, w_out, norm_mlp, w_gate, w_up, w_down)
    gathered = (
        lax.all_gather(shards[0], "blk", axis=0, tiled=True),
        lax.all_gather(shards[1], "blk", axis=0, tiled=True),
        lax.all_gather(shards[2], "blk", axis=0, tiled=True),
        lax.all_gather(shards[3], "blk", axis=0, tiled=True),
        lax.all_gather(shards[4], "blk", axis=0, tiled=True),
        lax.all_gather(shards[5], "blk", axis=0, tiled=True),
        lax.all_gather(shards[6], "blk", axis=0, tiled=True),
    )
    gain_one, weight_qkv, weight_out, gain_two, weight_gate, weight_up, weight_down = gathered
    place_rows = lax.axis_index("blk") * tok_rows + jnp.arange(tok_rows, dtype=jnp.int32)
    lengths = doc_lens[0]
    starts = jnp.cumsum(lengths) - lengths
    query_seg = segment_of(place_rows, starts)
    cosine, sine_part = angle_tables(place_rows - start_of(place_rows, starts))
    x_float = block_input[0].astype(jnp.float32)
    inv_one = lax.rsqrt(jnp.mean(x_float * x_float, axis=-1, keepdims=True) + EPS)
    normed_one = (x_float * inv_one * gain_one.astype(jnp.float32)).astype(jnp.bfloat16)
    projected = jnp.dot(normed_one, weight_qkv, preferred_element_type=jnp.float32)
    heads_all = projected.reshape(tok_rows, 3, HEADS, HEAD)
    queries = rotate(heads_all[:, 0], cosine, sine_part).astype(jnp.bfloat16)
    keys_own = rotate(heads_all[:, 1], cosine, sine_part).astype(jnp.bfloat16)
    values_own = heads_all[:, 2].astype(jnp.bfloat16)

    def pair_mask(count):
        key_places = jnp.arange(count, dtype=jnp.int32)
        key_seg = segment_of(key_places, starts)
        return (query_seg[:, None] == key_seg[None, :]) & (
            key_places[None, :] <= place_rows[:, None]
        )

    piece = (
        lax.all_gather(keys_own, "blk", axis=0, tiled=True),
        lax.all_gather(values_own, "blk", axis=0, tiled=True),
    )
    count = piece[0].shape[0]
    row_peak = jnp.full((HEADS, tok_rows), NEGATIVE, jnp.float32)
    key_piece, value_piece = piece
    count = key_piece.shape[0]
    allowed = pair_mask(count)[None]
    scores = (
        jnp.einsum("qhd,khd->hqk", queries, key_piece, preferred_element_type=jnp.float32)
        * score_scale
    )
    scores = jnp.where(allowed, scores, NEGATIVE)
    new_peak = jnp.maximum(row_peak, jnp.max(scores, axis=-1))
    weights_now = jnp.where(allowed, jnp.exp(scores - new_peak[..., None]), 0.0)
    row_total = jnp.sum(weights_now, axis=-1)
    accum = jnp.einsum(
        "hqk,khd->hqd",
        weights_now.astype(jnp.bfloat16),
        value_piece,
        preferred_element_type=jnp.float32,
    )
    row_peak, row_total, accum = (new_peak, row_total, accum)
    log_total = row_peak + jnp.log(row_total)
    attended = (accum / row_total[..., None]).transpose(1, 0, 2)
    attended_b = attended.reshape(tok_rows, width).astype(jnp.bfloat16)
    resid = x_float + jnp.dot(attended_b, weight_out, preferred_element_type=jnp.float32)
    inv_two = lax.rsqrt(jnp.mean(resid * resid, axis=-1, keepdims=True) + EPS)
    normed_two = (resid * inv_two * gain_two.astype(jnp.float32)).astype(jnp.bfloat16)
    gate_proj = jnp.dot(normed_two, weight_gate, preferred_element_type=jnp.float32)
    up_proj = jnp.dot(normed_two, weight_up, preferred_element_type=jnp.float32)
    sigmoid_gate = jax.nn.sigmoid(gate_proj)
    swish = gate_proj * sigmoid_gate
    hidden = (swish * up_proj).astype(jnp.bfloat16)
    block_out = (resid + jnp.dot(hidden, weight_down, preferred_element_type=jnp.float32)).astype(
        jnp.bfloat16
    )
    again = (
        lax.all_gather(shards[0], "blk", axis=0, tiled=True),
        lax.all_gather(shards[1], "blk", axis=0, tiled=True),
        lax.all_gather(shards[2], "blk", axis=0, tiled=True),
        lax.all_gather(shards[3], "blk", axis=0, tiled=True),
        lax.all_gather(shards[4], "blk", axis=0, tiled=True),
        lax.all_gather(shards[5], "blk", axis=0, tiled=True),
        lax.all_gather(shards[6], "blk", axis=0, tiled=True),
    )
    back_gain_one, back_qkv, back_out, back_gain_two, back_gate, back_up, back_down = again
    seed = cot[0]
    seed_float = seed.astype(jnp.float32)
    dhidden = contract_rows(seed, back_down)
    dgate = (dhidden * up_proj * sigmoid_gate * (1.0 + gate_proj * (1.0 - sigmoid_gate))).astype(
        jnp.bfloat16
    )
    dup = (dhidden * swish).astype(jnp.bfloat16)
    dnormed_two = contract_rows(dgate, back_gate) + contract_rows(dup, back_up)
    a_two = dnormed_two * back_gain_two.astype(jnp.float32)
    dresid = (
        seed_float
        + inv_two * a_two
        - resid * inv_two**3 * jnp.mean(a_two * resid, axis=-1, keepdims=True)
    )
    dresid_b = dresid.astype(jnp.bfloat16)
    dattended = (
        contract_rows(dresid_b, back_out).astype(jnp.bfloat16).reshape(tok_rows, HEADS, HEAD)
    )
    delta = jnp.sum(dattended.astype(jnp.float32) * attended, axis=-1).T
    piece = (
        lax.all_gather(keys_own, "blk", axis=0, tiled=True),
        lax.all_gather(values_own, "blk", axis=0, tiled=True),
    )
    count = piece[0].shape[0]
    key_piece, value_piece = piece
    count = key_piece.shape[0]
    score_count = key_piece.shape[0]
    allowed = pair_mask(score_count)[None]
    scores = (
        jnp.einsum("qhd,khd->hqk", queries, key_piece, preferred_element_type=jnp.float32)
        * score_scale
    )
    probs = jnp.where(allowed, jnp.exp(scores - log_total[..., None]), 0.0)
    dprobs = jnp.einsum("qhd,khd->hqk", dattended, value_piece, preferred_element_type=jnp.float32)
    dscores = (probs * (dprobs - delta[..., None])).astype(jnp.bfloat16)
    probs, dscores = (probs, dscores)
    dquery_acc = score_scale * jnp.einsum(
        "hqk,khd->hqd", dscores, key_piece, preferred_element_type=jnp.float32
    )
    dkeys = score_scale * jnp.einsum(
        "hqk,qhd->khd", dscores, queries, preferred_element_type=jnp.float32
    )
    dvalues = jnp.einsum(
        "hqk,qhd->khd", probs.astype(jnp.bfloat16), dattended, preferred_element_type=jnp.float32
    )
    stacked = jnp.concatenate([dkeys.reshape(count, width), dvalues.reshape(count, width)], axis=1)
    grads_buffer = stacked
    dquery_acc, grads_buffer = (dquery_acc, grads_buffer)
    own_grads = lax.psum_scatter(
        grads_buffer.astype(jnp.bfloat16), "blk", scatter_dimension=0, tiled=True
    ).astype(jnp.float32)
    dkey = unrotate(own_grads[:, :width].reshape(tok_rows, HEADS, HEAD), cosine, sine_part)
    dvalue = own_grads[:, width:].reshape(tok_rows, HEADS, HEAD)
    dquery = unrotate(dquery_acc.transpose(1, 0, 2), cosine, sine_part)
    dqkv = (
        jnp.stack([dquery, dkey, dvalue], axis=1).reshape(tok_rows, 3 * width).astype(jnp.bfloat16)
    )
    dnormed_one = contract_rows(dqkv, back_qkv)
    a_one = dnormed_one * back_gain_one.astype(jnp.float32)
    x_grad = (
        dresid
        + inv_one * a_one
        - x_float * inv_one**3 * jnp.mean(a_one * x_float, axis=-1, keepdims=True)
    ).astype(jnp.bfloat16)
    width_rows = norm_attn.shape[0]
    gain_terms = jnp.stack(
        [
            jnp.sum(dnormed_one * x_float * inv_one, axis=0),
            jnp.sum(dnormed_two * resid * inv_two, axis=0),
        ],
        axis=1,
    )

    def gain_slice(start, count):
        return gain_terms

    grad_down = shard_grad(weight_term(hidden, seed), w_down.shape[0])
    grad_gate = shard_grad(weight_term(normed_two, dgate), width_rows)
    grad_up = shard_grad(weight_term(normed_two, dup), width_rows)
    grad_out = shard_grad(weight_term(attended_b, dresid_b), width_rows)
    grad_qkv = shard_grad(weight_term(normed_one, dqkv), width_rows)
    gain_grads = shard_grad(gain_slice, width_rows)
    return (
        block_out[None],
        x_grad[None],
        gain_grads[:, 0],
        grad_qkv,
        grad_out,
        gain_grads[:, 1],
        grad_gate,
        grad_up,
        grad_down,
    )


MESH = pl.DeviceIdType.MESH
VMEM_BYTES = 60 * 2**20


def ring_place(block, n):
    up, row = block // 2, block % 2
    return (1 - row) * up + row * (n - 1 - up)


def ring_block(place, n):
    back = place // (n // 2)
    return (1 - back) * 2 * place + back * (2 * (n - 1 - place) + 1)


def at_offset(place, offset, n):
    return ring_block((place + offset + n) % n, n)


def greet(devices):
    barrier = pltpu.get_barrier_semaphore()
    for device in devices:
        pl.semaphore_signal(barrier, inc=1, device_id=device, device_id_type=MESH)
    pl.semaphore_wait(barrier, len(devices))


def push(src, dst, send_sem, recv_sem, device):
    return pltpu.make_async_remote_copy(
        src_ref=src,
        dst_ref=dst,
        send_sem=send_sem,
        recv_sem=recv_sem,
        device_id=device,
        device_id_type=MESH,
    )


def kernel_params(collective_id):
    return pltpu.CompilerParams(
        collective_id=collective_id, has_side_effects=True, vmem_limit_bytes=VMEM_BYTES
    )


def dot_f32(left, right):
    return jnp.dot(left, right, preferred_element_type=jnp.float32)


def dot_t(left, right):
    return lax.dot_general(
        left, right, (((0,), (0,)), ((), ())), preferred_element_type=jnp.float32
    )


def nt_dot(left, right):
    return lax.dot_general(
        left, right, (((1,), (1,)), ((), ())), preferred_element_type=jnp.float32
    )


def ring_ends(n):
    grp, me = lax.axis_index("grp"), lax.axis_index("blk")
    place = ring_place(me, n)
    return place, ((grp, at_offset(place, 1, n)), (grp, at_offset(place, -1, n)))


class Gather:
    def __init__(self, n, buf, send, recv, ends, own=None):
        self.n, self.buf, self.send, self.recv, self.ends = n, buf, send, recv, ends
        self.own = buf.at[0] if own is None else own
        self.half = buf.shape[1] // 2

    def copy(self, step, chunk, way):
        part = pl.ds(chunk * self.half, self.half)
        if isinstance(step, int):
            target = min(2 * step + 1 + way, self.n - 1)
        else:
            target = jnp.minimum(2 * step + 1 + way, self.n - 1)
        first = isinstance(step, int) and step == 0
        return push(
            self.own.at[part] if first else self.buf.at[2 * step - 1 + way, part],
            self.buf.at[target, part],
            self.send.at[step, chunk, way],
            self.recv.at[step, chunk, way],
            self.ends[way],
        )

    def landed(self, step, chunk, way):
        target = jnp.minimum(2 * step + 1 + way, self.n - 1)
        place = self.buf.at[target, pl.ds(chunk * self.half, self.half)]
        sems = (self.send.at[step, chunk, way], self.recv.at[step, chunk, way])
        return push(place, place, *sems, self.ends[way])

    def used(self, step, chunk, way):
        return step < self.n // 2 - 1 or chunk == way

    def start(self):
        for chunk in range(2):
            for way in range(2):
                self.copy(0, chunk, way).start()

    def advance(self, step):
        for chunk in range(2):
            for way in range(2):
                if isinstance(step, int):
                    if self.used(step, chunk, way):
                        self.copy(step, chunk, way).wait_recv()
                        if step + 1 < self.n // 2 and self.used(step + 1, chunk, way):
                            self.copy(step + 1, chunk, way).start()
                elif chunk == way:
                    self.landed(step, chunk, way).wait_recv()
                    pl.when(step + 1 < self.n // 2)(self.copy(step + 1, chunk, way).start)
                else:
                    pl.when(step < self.n // 2 - 1)(self.landed(step, chunk, way).wait_recv)
                    pl.when(step + 1 < self.n // 2 - 1)(self.copy(step + 1, chunk, way).start)

    def finish(self):
        for step in range(self.n // 2):
            for chunk in range(2):
                for way in range(2):
                    if self.used(step, chunk, way):
                        self.copy(step, chunk, way).wait_send()


class Scatter:
    def __init__(self, n, held, terms, send, recv, ends, term):
        self.n, self.held, self.terms, self.send, self.recv = n, held, terms, send, recv
        self.ends, self.term = ends, term
        self.half = held.shape[2] // 2

    def copy(self, step, chunk, way):
        part = pl.ds(chunk * self.half, self.half)
        return push(
            self.held.at[way, step, part],
            self.held.at[way, step + 1, part],
            self.send.at[step, chunk, way],
            self.recv.at[step, chunk, way],
            self.ends[way],
        )

    def step(self, step):
        for way in range(2):
            self.terms[way] = self.term(step, way)
        for chunk in range(2):
            for way in range(2):
                part = pl.ds(chunk * self.half, self.half)

                def first(way=way, part=part):
                    self.held[way, step, part] = self.terms[way, part].astype(jnp.bfloat16)

                def later(chunk=chunk, way=way, part=part):
                    self.copy(step - 1, chunk, way).wait_recv()
                    self.held[way, step, part] = (
                        self.terms[way, part] + self.held[way, step, part].astype(jnp.float32)
                    ).astype(jnp.bfloat16)

                if isinstance(step, int):
                    (later if step else first)()
                else:
                    pl.when(step == 0)(first)
                    pl.when(step > 0)(later)
                self.copy(step, chunk, way).start()

    def result(self, way):
        for chunk in range(2):
            self.copy(self.n - 2, chunk, way).wait_recv()
        return self.term(self.n - 1, way) + self.held[way, self.n - 1].astype(jnp.float32)

    def finish(self):
        def body(step, _):
            for chunk in range(2):
                for way in range(2):
                    self.copy(step, chunk, way).wait_send()
            return 0

        lax.fori_loop(0, self.n - 1, body, 0)


def behind(step, way, n):
    near = 2 * step + 1 + way
    far = 2 * (n - 1 - step) - way
    if isinstance(step, int):
        return 0 if step == n - 1 else min(near, far, n - 1)
    return jnp.where(step == n - 1, 0, jnp.minimum(jnp.minimum(near, far), n - 1))


def team(grp):
    over, core = grp // 2, grp % 2
    return over, core, (1 - over) * 2 + core, over * 2 + 1 - core


def mlp_kernel(
    n,
    lanes,
    ob,
    w_out,
    x_ref,
    gain,
    weights,
    w_down,
    seed_hbm,
    seed_own,
    block_out,
    dresid_out,
    dattended,
    gain_terms,
    wide_sum,
    down_sum,
    out_grad,
    normed,
    seed,
    gate_up,
    down,
    hidden,
    dgate_up,
    held_one,
    held_two,
    terms,
    resid,
    wide,
    wide_c,
    tall,
    tall_c,
    load_sem,
    s_one,
    r_one,
    s_two,
    r_two,
    s_three,
    r_three,
    s_norm,
    r_norm,
    s_dres,
    r_dres,
    s_wc,
    r_wc,
    s_wx,
    r_wx,
    s_tall,
    r_tall,
):
    f32, bf16 = jnp.float32, jnp.bfloat16
    grp, me = lax.axis_index("grp"), lax.axis_index("blk")
    over, core, grp_x, grp_c = team(grp)
    _, ends = ring_ends(n)
    loads = [
        pltpu.make_async_copy(weights, gate_up, load_sem.at[0]),
        pltpu.make_async_copy(w_down, down, load_sem.at[1]),
        pltpu.make_async_copy(
            seed_hbm.at[pl.ds(1, n - 1)], seed.at[pl.ds(1, n - 1)], load_sem.at[2]
        ),
        pltpu.make_async_copy(seed_own, seed.at[0], load_sem.at[3]),
    ]
    for load in loads:
        load.start()
    greet(list(ends) + [(grp_x, me), (grp_c, me)])
    columns = x_ref.shape[1]
    half = columns // 2

    def out_term(step, way):
        return dot_f32(ob[behind(step, way, n)], w_out[:, way * half : (way + 1) * half])

    one = Scatter(n, held_one, terms, s_one, r_one, ends, out_term)
    one.step(0)
    lax.fori_loop(1, n - 1, lambda step, _: (one.step(step), 0)[1], 0)
    for way in range(2):
        part = slice(way * half, (way + 1) * half)
        resid[:, part] = x_ref[:, part].astype(f32) + one.result(way)
    value = resid[...]
    inv = lax.rsqrt(jnp.mean(value * value, axis=-1, keepdims=True) + EPS)
    normed[0] = (value * inv * gain[...]).astype(bf16)
    gather = Gather(n, normed, s_norm, r_norm, ends)
    gather.start()
    one.finish()
    for load in loads:
        load.wait()

    def mlp(slot, _):
        both = dot_f32(normed[slot], gate_up[...])
        grad = nt_dot(seed[slot], down[...])
        gate, up = both[:, :lanes], both[:, lanes:]
        sig = jax.nn.sigmoid(gate)
        swish = gate * sig
        hidden[slot] = (swish * up).astype(bf16)
        dgate_up[slot, :, :lanes] = (grad * up * sig * (1.0 + gate * (1.0 - sig))).astype(bf16)
        dgate_up[slot, :, lanes:] = (grad * swish).astype(bf16)
        return 0

    def norm_term(step, way):
        return nt_dot(dgate_up[behind(step, way, n)], gate_up[way * half : (way + 1) * half, :])

    two = Scatter(n, held_two, terms, s_two, r_two, ends, norm_term)

    def turn(t, _):
        pl.when(t > 0)(lambda: gather.advance(t - 1))
        low = jnp.maximum(2 * t - 1, 0)
        lax.fori_loop(low, jnp.minimum(2 * t + 1, n), mlp, 0)
        pl.when(t > 0)(lambda: two.step(t - 1))
        return 0

    lax.fori_loop(0, n // 2 + 1, turn, 0)

    tall_rows = lanes // 4

    def tall_at(first, count):
        return pl.ds(pl.multiple_of(first * tall_rows, tall_rows), count * tall_rows)

    tiles = [slice(at, min(at + 256, lanes)) for at in range(0, lanes, 256)]

    def tall_grad(tile):
        left = hidden[:, :, tile].reshape(-1, tile.stop - tile.start)
        tall[tile] = dot_t(left, seed[...].reshape(-1, columns)).astype(bf16)

    for index, step in enumerate(range(n // 2, n - 1)):
        for tile in tiles[index :: n // 2 - 1]:
            tall_grad(tile)
        two.step(step)
    def down_term(step, way):
        return dot_f32(hidden[behind(step, way, n)], down[:, way * half : (way + 1) * half])

    three = Scatter(n, held_one, terms, s_three, r_three, ends, down_term)

    three.step(0)
    tall_one = push(tall.at[tall_at(2 - 2 * core, 2)], tall_c, s_tall.at[0], r_tall.at[0], (grp_c, me))
    tall_one.start()

    value = resid[...]
    inv = lax.rsqrt(jnp.mean(value * value, axis=-1, keepdims=True) + EPS)
    for way in range(2):
        part = slice(way * half, (way + 1) * half)
        dresid_out[:, part] = two.result(way)
    dnormed = dresid_out[...]
    gain_terms[...] = jnp.sum(dnormed * value * inv, axis=0, keepdims=True)
    a_two = dnormed * gain[...]
    total = (
        seed[0].astype(f32)
        + inv * a_two
        - value * inv**3 * jnp.mean(a_two * value, axis=-1, keepdims=True)
    )
    dresid_out[...] = total
    dresid = seed
    dresid[0] = total.astype(bf16)
    back = Gather(n, dresid, s_dres, r_dres, ends)
    back.start()
    two.finish()

    def dob(slot, _):
        dattended[slot] = nt_dot(dresid[slot], w_out[...]).astype(bf16)
        return 0

    def wide_copy_c(tile):
        return push(
            wide.at[tile, 1 - core], wide_c.at[tile], s_wc.at[tile], r_wc.at[tile], (grp_c, me)
        )

    def wide_copy_x(tile):
        return push(
            wide_c.at[tile, 1 - over], wide_sum.at[tile], s_wx.at[tile], r_wx.at[tile], (grp_x, me)
        )

    quarter = wide.shape[3]

    def wide_grad(tile):
        at = pl.multiple_of(tile * 4 * quarter, 4 * quarter)
        left = normed[:, :, pl.ds(at, 4 * quarter)].reshape(-1, 4 * quarter)
        grad = dot_t(left, dgate_up[...].reshape(-1, 2 * lanes)).astype(bf16)
        wide[tile] = grad.reshape(2, 2, quarter, 2 * lanes)
        wide_copy_c(tile).start()

    def wide_pass(tile):
        wide_copy_c(tile).wait_recv()
        wide_c[tile, 1 - over] = (
            wide[tile, core, 1 - over].astype(f32) + wide_c[tile, 1 - over].astype(f32)
        ).astype(bf16)
        wide_copy_x(tile).start()

    tall_two = push(tall_c.at[tall_at(1 - over, 1)], down_sum, s_tall.at[1], r_tall.at[1], (grp_x, me))

    def tall_pass():
        tall_one.wait_recv()
        tall_c[tall_at(1 - over, 1)] = (
            tall[tall_at(2 * core + 1 - over, 1)].astype(f32)
            + tall_c[tall_at(1 - over, 1)].astype(f32)
        ).astype(bf16)
        tall_two.start()

    def wide_take(tile):
        wide_copy_x(tile).wait_recv()
        wide_sum[tile] = (
            wide[tile, core, over].astype(f32)
            + wide_c[tile, over].astype(f32)
            + wide_sum[tile].astype(f32)
        ).astype(bf16)

    def again(t, _):
        pl.when(t > 0)(lambda: back.advance(t - 1))
        low = jnp.maximum(2 * t - 1, 0)
        lax.fori_loop(low, jnp.minimum(2 * t + 1, n), dob, 0)

        def inner(step, _):
            pl.when(step < n - 2)(lambda: three.step(step + 1))

            @pl.when(step < n // 2)
            def _():
                wide_grad(2 * step)
                pl.when(step == 0)(tall_pass)
                pl.when(step > 0)(lambda: wide_pass(2 * step - 1))
                wide_grad(2 * step + 1)
                wide_pass(2 * step)

            pl.when(step == n // 2)(lambda: wide_pass(n - 1))

            @pl.when(step >= n // 2)
            def _():
                wide_take(2 * step - n)
                pl.when(step < n - 1)(lambda: wide_take(2 * step - n + 1))

            return 0

        lax.fori_loop(2 * t, jnp.minimum(2 * t + 2, n), inner, 0)
        return 0

    lax.fori_loop(0, n // 2 + 1, again, 0)
    wide_take(n - 1)
    out_grad[...] = dot_t(
        ob[...].reshape(-1, ob.shape[2]), dresid[...].reshape(-1, columns)
    ).astype(bf16)
    for way in range(2):
        part = slice(way * half, (way + 1) * half)
        block_out[:, part] = (resid[:, part] + three.result(way)).astype(bf16)

    tall_two.wait_recv()
    down_sum[...] = (
        tall[tall_at(2 * core + over, 1)].astype(f32)
        + tall_c[tall_at(over, 1)].astype(f32)
        + down_sum[...].astype(f32)
    ).astype(bf16)
    gather.finish()
    back.finish()
    three.finish()
    tall_one.wait_send()
    tall_two.wait_send()

    def sent(tile, _):
        wide_copy_c(tile).wait_send()
        wide_copy_x(tile).wait_send()
        return 0

    lax.fori_loop(0, n, sent, 0)


def mlp_and_back(ob, w_out, x_own, gain, weights, lanes, w_down, seed, seed_own):
    n = lax.axis_size("blk")
    _, rows, columns = seed.shape
    head_lanes = ob.shape[2]
    quarter = columns // (4 * n)
    f32, bf16 = jnp.float32, jnp.bfloat16
    vmem, dma = pltpu.VMEM, pltpu.SemaphoreType.DMA
    in_vmem, anywhere = pl.BlockSpec(memory_space=vmem), pl.BlockSpec(memory_space=pl.ANY)
    ring = [dma((n - 1, 2, 2))] * 6 + [dma((n // 2, 2, 2))] * 4
    return pl.pallas_call(
        functools.partial(mlp_kernel, n, lanes),
        out_shape=(
            jax.ShapeDtypeStruct((rows, columns), bf16),
            jax.ShapeDtypeStruct((rows, columns), f32),
            jax.ShapeDtypeStruct((n, rows, head_lanes), bf16),
            jax.ShapeDtypeStruct((1, columns), f32),
            jax.ShapeDtypeStruct((n, quarter, 2 * lanes), bf16),
            jax.ShapeDtypeStruct((lanes // 4, columns), bf16),
            jax.ShapeDtypeStruct((head_lanes, columns), bf16),
        ),
        in_specs=[in_vmem] * 4 + [anywhere] * 4,
        out_specs=[in_vmem] * 7,
        scratch_shapes=[
            vmem((n, rows, columns), bf16),
            vmem((n, rows, columns), bf16),
            vmem((columns, 2 * lanes), bf16),
            vmem((lanes, columns), bf16),
            vmem((n, rows, lanes), bf16),
            vmem((n, rows, 2 * lanes), bf16),
            vmem((2, n, rows, columns // 2), bf16),
            vmem((2, n, rows, columns // 2), bf16),
            vmem((2, rows, columns // 2), f32),
            vmem((rows, columns), f32),
            vmem((n, 2, 2, quarter, 2 * lanes), bf16),
            vmem((n, 2, quarter, 2 * lanes), bf16),
            vmem((lanes, columns), bf16),
            vmem((lanes // 2, columns), bf16),
            dma((4,)),
        ]
        + ring
        + [dma((n,))] * 4
        + [dma((2,))] * 2,
        compiler_params=kernel_params(5),
        name="mlp_and_back",
    )(ob, w_out, x_own, gain, weights, w_down, seed, seed_own)


class Spread:
    def __init__(self, n, pieces, out, sems):
        self.n, self.pieces, self.out = n, pieces, out
        self.s_blk, self.r_blk, self.s_x, self.r_x, self.s_c, self.r_c = sems
        self.grp, self.me = lax.axis_index("grp"), lax.axis_index("blk")
        self.over, self.core, self.grp_x, self.grp_c = team(self.grp)

    def first(self, k):
        to = (self.me + k) % self.n
        place = self.out.at[self.me, 2 * self.core + self.over]
        return push(
            self.pieces.at[to], place, self.s_blk.at[k], self.r_blk.at[k], (self.grp, to)
        )

    def own(self, sem):
        place = self.out.at[self.me, 2 * self.core + self.over]
        return pltpu.make_async_copy(self.pieces.at[self.me], place, sem)

    def to_x(self, k, own=False):
        piece = self.out.at[(self.me - k + self.n) % self.n, 2 * self.core + self.over]
        source = self.pieces.at[self.me] if own else piece
        return push(source, piece, self.s_x.at[k], self.r_x.at[k], (self.grp_x, self.me))

    def to_core(self, k, far, own=False):
        over = 1 - self.over if far else self.over
        piece = self.out.at[(self.me - k + self.n) % self.n, 2 * self.core + over]
        source = self.pieces.at[self.me] if own else piece
        sems = (self.s_c.at[int(far), k], self.r_c.at[int(far), k])
        return push(source, piece, *sems, (self.grp_c, self.me))

    def pass_own(self):
        self.to_x(0, True).start()
        self.to_core(0, False, True).start()

    def pass_on(self, k):
        self.first(k).wait_recv()
        self.to_x(k).start()
        self.to_core(k, False).start()

    def pass_far(self, k):
        self.to_x(k).wait_recv()
        self.to_core(k, True).start()

    def arrived(self, k):
        for far in (False, True):
            self.to_core(k, far).wait_recv()

    def finish(self):
        def body(k, _):
            pl.when(k > 0)(self.first(k).wait_send)
            self.to_x(k).wait_send()
            for far in (False, True):
                self.to_core(k, far).wait_send()
            return 0

        lax.fori_loop(0, self.n, body, 0)


def each(count, body, low=0):
    lax.fori_loop(low, count, lambda k, _: (body(k), 0)[1], 0)


def spread_sems(n):
    dma = pltpu.SemaphoreType.DMA
    return [dma((n,)), dma((n,)), dma((n,)), dma((n,)), dma((2, n)), dma((2, n))]


def team_and_ring(n):
    grp, me = lax.axis_index("grp"), lax.axis_index("blk")
    _, _, grp_x, grp_c = team(grp)
    return [(grp, (me + k) % n) for k in range(1, n)] + [(grp_x, me), (grp_c, me)]


def fill_row(row, gains_all, which, share):
    for block in range(gains_all.shape[0]):
        row[:, block * share : (block + 1) * share] = gains_all[block, which : which + 1, :]


def turned(value, cosine, sine_part):
    half_size = HEAD // 2
    swapped = jnp.concatenate([value[:, half_size:], value[:, :half_size]], axis=1)
    return value * cosine + swapped * sine_part


def mark_places(n, doc_lens, rows, first_key, query_place, key_place):
    place = ring_place(lax.axis_index("blk"), n)
    for slot in range(n):
        offset = (slot + 1) // 2 * (1 if slot % 2 == 0 else -1)
        first_row = at_offset(place, offset, n) * rows
        part = slice(slot * rows, (slot + 1) * rows)
        here = first_row + lax.broadcasted_iota(jnp.int32, (rows, 1), 0)
        query_place[part, :] = here
        key_place[:, part] = first_row + lax.broadcasted_iota(jnp.int32, (1, rows), 1)
        start = jnp.int32(0)
        found = jnp.zeros((rows, 1), jnp.int32)
        for index in range(doc_lens.shape[1]):
            found = jnp.maximum(found, jnp.where(here >= start, start, 0))
            start = start + doc_lens[0, index]
        first_key[part, :] = found


def attend_kernel(
    n,
    heads,
    doc_lens,
    x_own,
    freqs,
    norm_attn,
    norm_mlp,
    w_qkv,
    w_gate,
    w_up,
    seed_own,
    gain_row,
    gain_two,
    columns_qkv,
    normed,
    qkv,
    attended,
    attended_b,
    log_total,
    cosine,
    sine_part,
    gate_up,
    seed,
    x_all,
    gains_all,
    gains,
    raw_qkv,
    raw_gate,
    raw_up,
    slab_qkv,
    slab_gate_up,
    first_key,
    query_place,
    key_place,
    local,
    s_gain,
    r_gain,
    s_x,
    r_x,
    s_seed,
    r_seed,
    *spread_all,
):
    f32, bf16 = jnp.float32, jnp.bfloat16
    grp, me = lax.axis_index("grp"), lax.axis_index("blk")
    _, ends = ring_ends(n)
    rows, columns = x_own.shape
    spread_qkv = Spread(n, slab_qkv, columns_qkv, spread_all[:6])
    spread_gu = Spread(n, slab_gate_up, gate_up, spread_all[6:])
    over, core, _, _ = team(grp)
    quarter = slab_qkv.shape[1]
    own_rows = pl.ds(pl.multiple_of((2 * core + over) * quarter, quarter), quarter)
    loads = [
        pltpu.make_async_copy(weight.at[own_rows], raw, local.at[index])
        for index, (weight, raw) in enumerate(
            ((w_qkv, raw_qkv), (w_gate, raw_gate), (w_up, raw_up))
        )
    ]
    for load in loads:
        load.start()
    x_all[0] = x_own[...]
    gains[...] = jnp.zeros_like(gains)
    gains[0:1, :] = norm_attn[...].astype(f32).reshape(1, -1)
    gains[1:2, :] = norm_mlp[...].astype(f32).reshape(1, -1)
    gains_all[me] = gains[...]
    greet(team_and_ring(n))

    def gain(k):
        return push(gains, gains_all.at[me], s_gain.at[k], r_gain.at[k], (grp, (me + k) % n))

    each(n, lambda k: gain(k).start(), 1)
    x_ring = Gather(n, x_all, s_x, r_x, ends)
    x_ring.start()
    share = heads * HEAD
    loads[0].wait()
    for to in range(n):
        for part in range(3):
            slab_qkv[to, :, part * share : (part + 1) * share] = raw_qkv[
                :, (part * n + to) * share : (part * n + to + 1) * share
            ]
    near_qkv = spread_qkv.own(local.at[3])
    near_qkv.start()
    each(n, lambda k: spread_qkv.first(k).start(), 1)
    spread_qkv.pass_own()
    units = raw_gate.shape[1] // n
    loads[1].wait()
    loads[2].wait()
    for to in range(n):
        lane = slice(to * units, (to + 1) * units)
        slab_gate_up[to] = jnp.concatenate(
            [raw_gate[:, lane].astype(f32), raw_up[:, lane].astype(f32)], axis=1
        ).astype(bf16)
    near_gu = spread_gu.own(local.at[4])
    near_gu.start()
    mark_places(n, doc_lens, rows, first_key, query_place, key_place)

    def norm(slot):
        value = x_all[slot].astype(f32)
        inv = lax.rsqrt(jnp.mean(value * value, axis=-1, keepdims=True) + EPS)
        normed[slot] = (value * inv * gain_row[...]).astype(bf16)

    each(n, lambda k: gain(k).wait_recv(), 1)
    fill_row(gain_row, gains_all, 0, columns // n)
    fill_row(gain_two, gains_all, 1, columns // n)

    def table(slot):
        at = pl.ds(pl.multiple_of(slot * rows, rows), rows)
        angle = (query_place[at, :] - first_key[at, :]).astype(f32) * freqs[...]
        lane = lax.broadcasted_iota(jnp.int32, (rows, HEAD), 1)
        sine = jnp.sin(angle)
        cosine[at, :] = jnp.cos(angle)
        sine_part[at, :] = jnp.where(lane < HEAD // 2, -sine, sine)

    def arrive(t):
        pl.when(t > 0)(lambda: x_ring.advance(t - 1))
        low = jnp.maximum(2 * t - 1, 0)
        each(jnp.minimum(2 * t + 1, n), norm, low)
        each(jnp.minimum(2 * t + 1, n), table, low)
        pl.when(t == 2)(lambda: each(n, spread_qkv.pass_on, 1))
        pl.when(t == 3)(lambda: each(n, spread_qkv.pass_far))

        @pl.when(t == 2)
        def _():
            each(n, lambda k: spread_gu.first(k).start(), 1)
            spread_gu.pass_own()


    each(n // 2 + 1, arrive)
    seed_ring = Gather(n, seed, s_seed, r_seed, ends, seed_own)
    each(n, spread_gu.pass_on, 1)
    seed_ring.start()
    each(n, spread_qkv.arrived)
    near_qkv.wait()


    head_lanes = heads * HEAD
    pair = 2 * rows

    def project(i):
        both = normed[pl.ds(2 * i, 2)].reshape(pair, columns)
        result = dot_f32(both, columns_qkv[...].reshape(columns, 3 * head_lanes))
        at = pl.ds(pl.multiple_of(i * pair, pair), pair)
        table_c, table_s = cosine[at, :], sine_part[at, :]
        for piece in range(3 * heads):
            lane = slice(piece * HEAD, (piece + 1) * HEAD)
            value = result[:, lane]
            if piece < 2 * heads:
                value = turned(value, table_c, table_s)
            qkv[at, lane] = value.astype(bf16)

    each(n // 2, project)


    def tile(i):
        for head in range(heads):
            lane = slice(head * HEAD, (head + 1) * HEAD)
            at = pl.ds(pl.multiple_of(i * pair, pair), pair)
            keys = qkv[:, head_lanes + head * HEAD : head_lanes + (head + 1) * HEAD]
            values = qkv[:, 2 * head_lanes + head * HEAD : 2 * head_lanes + (head + 1) * HEAD]
            scores = nt_dot(qkv[at, lane], keys) * HEAD ** (-0.5)
            allowed = (key_place[...] >= first_key[at, :]) & (key_place[...] <= query_place[at, :])
            scores = jnp.where(allowed, scores, NEGATIVE)
            peak = jnp.max(scores, axis=-1, keepdims=True)
            raw = jnp.exp(scores - peak)
            total = jnp.sum(raw, axis=-1, keepdims=True)
            out = dot_f32(raw.astype(bf16), values) / total
            attended[at, lane] = out
            attended_b[at, lane] = out.astype(bf16)
            log_total[head, at, :] = peak + jnp.log(total)
        seed_ring.advance(i)
        pl.when(i == 1)(lambda: each(n, spread_gu.pass_far))

    each(n // 2, tile)
    each(n, spread_gu.arrived)
    near_gu.wait()
    for spread in (spread_qkv, spread_gu):
        spread.finish()
    each(n, lambda k: gain(k).wait_send(), 1)
    x_ring.finish()
    seed_ring.finish()


def attend(doc_lens, x_own, norm_attn, norm_mlp, w_qkv, w_gate, w_up, seed_own):
    n = lax.axis_size("blk")
    rows, columns = x_own.shape
    seq = n * rows
    lanes = w_qkv.shape[1] // n
    quarter = w_qkv.shape[0] // 4
    both = 2 * w_gate.shape[1] // n
    head_lanes = lanes // 3
    heads = head_lanes // HEAD
    share = norm_attn.shape[0]
    f32, bf16, i32 = jnp.float32, jnp.bfloat16, jnp.int32
    vmem, dma = pltpu.VMEM, pltpu.SemaphoreType.DMA
    in_vmem, anywhere = pl.BlockSpec(memory_space=vmem), pl.BlockSpec(memory_space=pl.ANY)
    half_freqs = np.exp(
        np.arange(HEAD // 2, dtype=np.float32) * np.float32(-2.0 * math.log(10000.0) / HEAD)
    )
    freqs = jnp.asarray(np.concatenate([half_freqs, half_freqs])[None].astype(np.float32))
    return pl.pallas_call(
        functools.partial(attend_kernel, n, heads),
        out_shape=(
            jax.ShapeDtypeStruct((1, columns), f32),
            jax.ShapeDtypeStruct((1, columns), f32),
            jax.ShapeDtypeStruct((n, 4, quarter, lanes), bf16),
            jax.ShapeDtypeStruct((n, rows, columns), bf16),
            jax.ShapeDtypeStruct((seq, lanes), bf16),
            jax.ShapeDtypeStruct((seq, head_lanes), f32),
            jax.ShapeDtypeStruct((seq, head_lanes), bf16),
            jax.ShapeDtypeStruct((heads, seq, 1), f32),
            jax.ShapeDtypeStruct((seq, HEAD), f32),
            jax.ShapeDtypeStruct((seq, HEAD), f32),
            jax.ShapeDtypeStruct((n, 4, quarter, both), bf16),
            jax.ShapeDtypeStruct((n, rows, columns), bf16),
        ),
        in_specs=[pl.BlockSpec(memory_space=pltpu.SMEM)] + [in_vmem] * 4 + [anywhere] * 4,
        out_specs=[in_vmem] * 10 + [anywhere] * 2,
        scratch_shapes=[
            vmem((n, rows, columns), bf16),
            vmem((n, 8, share), f32),
            vmem((8, share), f32),
            vmem((quarter, n * lanes), bf16),
            vmem((quarter, w_gate.shape[1]), bf16),
            vmem((quarter, w_gate.shape[1]), bf16),
            vmem((n, quarter, lanes), bf16),
            vmem((n, quarter, both), bf16),
            vmem((seq, 1), i32),
            vmem((seq, 1), i32),
            vmem((1, seq), i32),
            dma((5,)),
            dma((n,)),
            dma((n,)),
        ]
        + [dma((n // 2, 2, 2))] * 4
        + spread_sems(n) * 2,
        compiler_params=kernel_params(0),
        name="attend",
    )(
        doc_lens,
        x_own,
        freqs,
        norm_attn,
        norm_mlp,
        w_qkv,
        w_gate,
        w_up,
        seed_own,
    )


def finish_kernel(
    n,
    heads,
    qkv,
    attended,
    dattended,
    log_total,
    cosine,
    sine_part,
    doc_lens,
    x_own,
    gain,
    dresid,
    terms_two,
    out_grad,
    weights,
    normed_hbm,
    gate_up_sum,
    down_sum,
    x_grad,
    gain_grads,
    wide_gate_up,
    wide_qkv,
    tall_down,
    tall_out,
    normed,
    columns_qkv,
    dqkv,
    dkeys,
    dvalues,
    first_key,
    query_place,
    key_place,
    held,
    terms,
    wide,
    wide_c,
    wide_x,
    out_c,
    out_x,
    gain_slabs,
    gain_heard,
    gain_team,
    load_sem,
    s_ring,
    r_ring,
    s_wc,
    r_wc,
    s_wx,
    r_wx,
    s_tall,
    r_tall,
    s_gain,
    r_gain,
    *spread_all,
):
    f32, bf16 = jnp.float32, jnp.bfloat16
    grp, me = lax.axis_index("grp"), lax.axis_index("blk")
    over, core, grp_x, grp_c = team(grp)
    _, ends = ring_ends(n)
    rows, columns = x_own.shape
    half = columns // 2
    lanes = wide.shape[4]
    quarter = wide.shape[3]
    load_normed = pltpu.make_async_copy(normed_hbm, normed, load_sem.at[0])
    load_qkv = pltpu.make_async_copy(weights, columns_qkv, load_sem.at[1])
    load_normed.start()
    load_qkv.start()
    spread_gu = Spread(n, gate_up_sum, wide_gate_up, spread_all[:6])
    spread_qkv = Spread(n, wide_x, wide_qkv, spread_all[6:])
    near_gu = spread_gu.own(load_sem.at[2])
    near_gu.start()
    greet(team_and_ring(n))

    down_own = pltpu.make_async_copy(down_sum, tall_down.at[2 * core + over], load_sem.at[3])
    down_own.start()
    down_place = tall_down.at[2 * core + over]
    down_x = push(down_sum, down_place, s_tall.at[0], r_tall.at[0], (grp_x, me))
    down_c = push(down_sum, down_place, s_tall.at[1], r_tall.at[1], (grp_c, me))
    far_place = tall_down.at[2 * core + 1 - over]
    down_far = push(far_place, far_place, s_tall.at[2], r_tall.at[2], (grp_c, me))
    out_one = push(out_grad.at[1 - core], out_c, s_tall.at[3], r_tall.at[3], (grp_c, me))
    out_two = push(out_c.at[1 - over], out_x, s_tall.at[4], r_tall.at[4], (grp_x, me))
    out_place = tall_out.at[2 * core + over]
    out_own = pltpu.make_async_copy(out_x, out_place, load_sem.at[4])
    out_to_x = push(out_x, out_place, s_tall.at[5], r_tall.at[5], (grp_x, me))
    out_to_c = push(out_x, out_place, s_tall.at[6], r_tall.at[6], (grp_c, me))
    out_far_place = tall_out.at[2 * core + 1 - over]
    out_far = push(out_far_place, out_far_place, s_tall.at[7], r_tall.at[7], (grp_c, me))
    out_one.start()
    each(n, lambda k: spread_gu.first(k).start(), 1)
    spread_gu.pass_own()
    down_x.start()
    down_c.start()

    mark_places(n, doc_lens, rows, first_key, query_place, key_place)
    pair = 2 * rows
    head_lanes = heads * HEAD
    scale = HEAD ** (-0.5)

    def unturned(value, at):
        return turned(value, cosine[at, :], -sine_part[at, :]).astype(bf16)

    def tile(i, head):
        at = pl.ds(pl.multiple_of(i * pair, pair), pair)
        lane = slice(head * HEAD, (head + 1) * HEAD)
        query = qkv[at, lane]
        keys = qkv[:, head_lanes + head * HEAD : head_lanes + (head + 1) * HEAD]
        values = qkv[:, 2 * head_lanes + head * HEAD : 2 * head_lanes + (head + 1) * HEAD]
        grad = dattended[at, lane]
        delta = jnp.sum(grad.astype(f32) * attended[at, lane], axis=-1, keepdims=True)
        scores = nt_dot(query, keys) * scale
        allowed = (key_place[...] >= first_key[at, :]) & (key_place[...] <= query_place[at, :])
        probs = jnp.where(allowed, jnp.exp(scores - log_total[head, at, :]), 0.0)
        dscores = (probs * (nt_dot(grad, values) - delta)).astype(bf16)
        dqkv[2 * i : 2 * i + 2, :, lane] = unturned(dot_f32(dscores, keys) * scale, at).reshape(
            2, rows, HEAD
        )
        more_keys = dot_t(dscores, query)
        more_values = dot_t(probs.astype(bf16), grad)
        if i == 0:
            dkeys[...] = more_keys
            dvalues[...] = more_values
        else:
            dkeys[...] += more_keys
            dvalues[...] += more_values

    for head in range(heads):
        for i in range(n // 2):
            tile(i, head)
        everything = slice(0, n * rows)
        lane = slice(head_lanes + head * HEAD, head_lanes + (head + 1) * HEAD)
        dqkv[:, :, lane] = unturned(dkeys[...] * scale, everything).reshape(n, rows, HEAD)
        lane = slice(2 * head_lanes + head * HEAD, 2 * head_lanes + (head + 1) * HEAD)
        dqkv[:, :, lane] = dvalues[...].astype(bf16).reshape(n, rows, HEAD)
    load_qkv.wait()

    def term(step, way):
        return nt_dot(dqkv[behind(step, way, n)], columns_qkv[way * half : (way + 1) * half, :])

    ring = Scatter(n, held, terms, s_ring, r_ring, ends, term)

    def copy_c(k):
        tile = (me + k) % n
        return push(wide.at[tile, 1 - core], wide_c.at[tile], s_wc.at[k], r_wc.at[k], (grp_c, me))

    def copy_x(k):
        tile = (me + k) % n
        return push(
            wide_c.at[tile, 1 - over], wide_x.at[tile], s_wx.at[k], r_wx.at[k], (grp_x, me)
        )

    def grad(k):
        tile = (me + k) % n
        at = pl.multiple_of(tile * 4 * quarter, 4 * quarter)
        left = normed[:, :, pl.ds(at, 4 * quarter)].reshape(-1, 4 * quarter)
        grad_rows = dot_t(left, dqkv[...].reshape(-1, lanes)).astype(bf16)
        wide[tile] = grad_rows.reshape(2, 2, quarter, lanes)
        copy_c(k).start()

    def pass_x(k):
        tile = (me + k) % n
        copy_c(k).wait_recv()
        wide_c[tile, 1 - over] = (
            wide[tile, core, 1 - over].astype(f32) + wide_c[tile, 1 - over].astype(f32)
        ).astype(bf16)
        copy_x(k).start()

    def take(k):
        tile = (me + k) % n
        copy_x(k).wait_recv()
        wide_x[tile] = (
            wide[tile, core, over].astype(f32)
            + wide_c[tile, over].astype(f32)
            + wide_x[tile].astype(f32)
        ).astype(bf16)

    def take_and_push(k):
        take(k)
        spread_qkv.first(k).start()

    ring.step(0)
    load_normed.wait()

    def grads(i):
        k = (i + 1) % n
        grad(k)
        pl.when(i > 0)(lambda: pass_x(i))

    each(n, grads)
    pass_x(0)
    out_one.wait_recv()
    out_c[1 - over] = (
        out_grad[core, 1 - over].astype(f32) + out_c[1 - over].astype(f32)
    ).astype(bf16)
    out_two.start()

    def turn(k):
        pl.when(k < n - 2)(lambda: ring.step(k + 1))
        each(jnp.minimum(2 * k + 3, n), spread_gu.pass_on, jnp.minimum(2 * k + 1, n))
        pl.when(k < n - 1)(lambda: take_and_push(k + 1))
        pl.when(k >= 2)(lambda: spread_qkv.pass_on(k - 1))

        @pl.when(k == n - 2)
        def _():
            take(0)
            spread_qkv.pass_own()

    each(n - 1, turn)
    near_qkv = spread_qkv.own(load_sem.at[5])
    near_qkv.start()
    each(n, spread_qkv.pass_on, n - 2)

    x_float = x_own[...].astype(f32)
    inv = lax.rsqrt(jnp.mean(x_float * x_float, axis=-1, keepdims=True) + EPS)
    for way in range(2):
        terms[way] = ring.result(way)
    dnormed = jnp.concatenate([terms[0], terms[1]], axis=1)
    terms_one = jnp.sum(dnormed * x_float * inv, axis=0, keepdims=True)
    share = columns // n
    for block in range(n):
        gain_slabs[block] = jnp.zeros_like(gain_slabs[block])
        lane = slice(block * share, (block + 1) * share)
        gain_slabs[block, 0:1, :] = terms_one[:, lane]
        gain_slabs[block, 1:2, :] = terms_two[:, lane]

    def gain_blk(k):
        to = (me + k) % n
        return push(gain_slabs.at[to], gain_heard.at[k], s_gain.at[k], r_gain.at[k], (grp, to))

    each(n, lambda k: gain_blk(k).start(), 1)
    a_one = dnormed * gain[...]
    x_grad[...] = (
        dresid[...]
        + inv * a_one
        - x_float * inv**3 * jnp.mean(a_one * x_float, axis=-1, keepdims=True)
    ).astype(bf16)
    gain_heard[0] = gain_slabs[me]
    each(n, lambda k: gain_blk(k).wait_recv(), 1)
    gain_team[0] = jnp.sum(gain_heard[...], axis=0)
    gain_c = push(gain_team.at[0], gain_team.at[1], s_gain.at[n], r_gain.at[n], (grp_c, me))
    gain_c.start()
    out_two.wait_recv()
    out_x[...] = (
        out_grad[core, over].astype(f32) + out_c[over].astype(f32) + out_x[...].astype(f32)
    ).astype(bf16)
    out_own.start()
    out_to_x.start()
    out_to_c.start()
    each(n, spread_gu.pass_far)
    down_x.wait_recv()
    down_far.start()
    gain_c.wait_recv()
    gain_team[2] = gain_team[0] + gain_team[1]
    gain_x = push(
        gain_team.at[2], gain_team.at[3], s_gain.at[n + 1], r_gain.at[n + 1], (grp_x, me)
    )
    gain_x.start()
    out_to_x.wait_recv()
    out_far.start()
    each(n, spread_qkv.pass_far)
    gain_x.wait_recv()
    gain_grads[...] = gain_team[2] + gain_team[3]
    near_gu.wait()
    near_qkv.wait()
    each(n, spread_gu.arrived)
    each(n, spread_qkv.arrived)
    spread_gu.finish()
    spread_qkv.finish()
    ring.finish()
    down_own.wait()
    out_own.wait()
    for copy in (down_c, down_far, out_to_c, out_far):
        copy.wait()
    for copy in (down_x, out_one, out_two, out_to_x, gain_c, gain_x):
        copy.wait_send()

    def sent(k):
        copy_c(k).wait_send()
        copy_x(k).wait_send()
        pl.when(k > 0)(gain_blk(k).wait_send)

    each(n, sent)


def finish(
    attention, x_own, gain, dresid, terms_two, out_grad, weights, normed, gate_up_sum, down_sum
):
    n, rows, columns = normed.shape
    seq, lanes = attention[0].shape
    heads = lanes // (3 * HEAD)
    quarter = columns // (4 * n)
    share = columns // n
    f32, bf16 = jnp.float32, jnp.bfloat16
    vmem, dma = pltpu.VMEM, pltpu.SemaphoreType.DMA
    in_vmem, anywhere = pl.BlockSpec(memory_space=vmem), pl.BlockSpec(memory_space=pl.ANY)
    out_rows = out_grad.shape[0] // 4
    return pl.pallas_call(
        functools.partial(finish_kernel, n, heads),
        out_shape=(
            jax.ShapeDtypeStruct((rows, columns), bf16),
            jax.ShapeDtypeStruct((8, share), f32),
            jax.ShapeDtypeStruct((n, 4) + gate_up_sum.shape[1:], bf16),
            jax.ShapeDtypeStruct((n, 4, quarter, lanes), bf16),
            jax.ShapeDtypeStruct((4,) + down_sum.shape, bf16),
            jax.ShapeDtypeStruct((4, out_rows, columns), bf16),
        ),
        in_specs=[in_vmem] * 6
        + [pl.BlockSpec(memory_space=pltpu.SMEM)]
        + [in_vmem] * 5
        + [anywhere] * 4,
        out_specs=[in_vmem] * 2 + [anywhere] * 4,
        scratch_shapes=[
            vmem((n, rows, columns), bf16),
            vmem((columns, lanes), bf16),
            vmem((n, rows, lanes), bf16),
            vmem((seq, HEAD), f32),
            vmem((seq, HEAD), f32),
            vmem((seq, 1), jnp.int32),
            vmem((seq, 1), jnp.int32),
            vmem((1, seq), jnp.int32),
            vmem((2, n, rows, columns // 2), bf16),
            vmem((2, rows, columns // 2), f32),
            vmem((n, 2, 2, quarter, lanes), bf16),
            vmem((n, 2, quarter, lanes), bf16),
            vmem((n, quarter, lanes), bf16),
            vmem((2, out_rows, columns), bf16),
            vmem((out_rows, columns), bf16),
            vmem((n, 8, share), f32),
            vmem((n, 8, share), f32),
            vmem((4, 8, share), f32),
            dma((6,)),
        ]
        + [dma((n - 1, 2, 2))] * 2
        + [dma((n,))] * 4
        + [dma((8,))] * 2
        + [dma((n + 2,))] * 2
        + spread_sems(n) * 2,
        compiler_params=kernel_params(6),
        name="finish",
    )(
        *attention,
        x_own,
        gain,
        dresid,
        terms_two,
        out_grad.reshape(2, 2, out_rows, columns),
        weights,
        normed,
        gate_up_sum,
        down_sum,
    )


def assemble_kernel(n, units, lanes, head_lanes, qkv, gate_up, down, out, blocks, shift, gains, *grads):
    grad_qkv, grad_out, grad_gate, grad_up, grad_down, block_out, x_grad, gain_one, gain_two = grads
    gain_one[...] = gains[0]
    gain_two[...] = gains[1]
    block_out[...] = blocks[...]
    x_grad[...] = shift[...]
    f32 = jnp.float32
    for source in range(n):
        for part in range(3):
            first = (part * n + source) * head_lanes
            grad_qkv[:, first : first + head_lanes] = qkv[
                source, :, part * head_lanes : (part + 1) * head_lanes
            ].astype(f32)
        first = source * units
        grad_gate[:, first : first + units] = gate_up[source, :, :units].astype(f32)
        grad_up[:, first : first + units] = gate_up[source, :, lanes : lanes + units].astype(f32)
    grad_out[...] = out[...].astype(f32)
    grad_down[...] = down[...].astype(f32)


def assemble(qkv, gate_up, down, out, block_out, x_grad, gains, units, steps=4):
    n, rows, qkv_lanes = qkv.shape
    columns = down.shape[1]
    lanes = gate_up.shape[2] // 2
    head_lanes = qkv_lanes // 3
    step = rows // steps
    down_step = units // steps
    tokens = x_grad.shape[0] // steps
    f32 = jnp.float32

    def wide(width):
        return pl.BlockSpec((n, step, width), lambda i: (0, i, 0))

    def flat(height, width):
        return pl.BlockSpec((height, width), lambda i: (i, 0))

    return pl.pallas_call(
        functools.partial(assemble_kernel, n, units, lanes, head_lanes),
        grid=(steps,),
        out_shape=(
            jax.ShapeDtypeStruct((rows, n * qkv_lanes), f32),
            jax.ShapeDtypeStruct((rows, columns), f32),
            jax.ShapeDtypeStruct((rows, n * units), f32),
            jax.ShapeDtypeStruct((rows, n * units), f32),
            jax.ShapeDtypeStruct((units, columns), f32),
            jax.ShapeDtypeStruct(block_out.shape, block_out.dtype),
            jax.ShapeDtypeStruct(x_grad.shape, x_grad.dtype),
            jax.ShapeDtypeStruct(gains.shape[1:], f32),
            jax.ShapeDtypeStruct(gains.shape[1:], f32),
        ),
        in_specs=[
            wide(qkv_lanes),
            wide(2 * lanes),
            flat(down_step, columns),
            flat(out.shape[0] // steps, columns),
            flat(tokens, columns),
            flat(tokens, columns),
            pl.BlockSpec(gains.shape, lambda i: (0, 0)),
        ],
        out_specs=[
            flat(step, n * qkv_lanes),
            flat(step, columns),
            flat(step, n * units),
            flat(step, n * units),
            flat(down_step, columns),
            flat(tokens, columns),
            flat(tokens, columns),
            pl.BlockSpec(gains.shape[1:], lambda i: (0,)),
            pl.BlockSpec(gains.shape[1:], lambda i: (0,)),
        ],
        compiler_params=pltpu.CompilerParams(vmem_limit_bytes=VMEM_BYTES),
        name="assemble",
    )(qkv, gate_up, down, out, block_out, x_grad, gains)


def per_device(block_input, doc_lens, norm_attn, w_qkv, w_out, norm_mlp, w_gate, w_up, w_down, cot):
    n = lax.axis_size("blk")
    tok_rows, width = block_input.shape[1:]
    seq = tok_rows * n
    heads = HEADS // n
    head_lanes = heads * HEAD
    qkv_lanes = 3 * head_lanes
    units = w_down.shape[0]
    lanes = units
    quarter = w_qkv.shape[0] // 4
    (
        gain_one,
        gain_two,
        qkv_columns,
        normed_one,
        qkv,
        attended,
        attended_b,
        log_total,
        cosine,
        sine_part,
        gate_up,
        seed,
    ) = attend(doc_lens, block_input[0], norm_attn, norm_mlp, w_qkv, w_gate, w_up, cot[0])
    qkv_columns = qkv_columns.reshape(width, qkv_lanes)
    gate_up = gate_up.reshape(width, 2 * lanes)
    block_out, dresid, dattended, terms_two, gate_up_sum, down_sum, out_grad = mlp_and_back(
        attended_b.reshape(n, tok_rows, head_lanes),
        w_out,
        block_input[0],
        gain_two,
        gate_up,
        lanes,
        w_down,
        seed,
        cot[0],
    )
    x_grad, gain_grads, wide_gate_up, wide_qkv, tall_down, tall_out = finish(
        (
            qkv,
            attended,
            dattended.reshape(seq, head_lanes),
            log_total,
            cosine,
            sine_part,
            doc_lens,
        ),
        block_input[0],
        gain_one,
        dresid,
        terms_two,
        out_grad,
        qkv_columns,
        normed_one,
        gate_up_sum,
        down_sum,
    )
    shard_rows = 4 * quarter
    (
        grad_qkv,
        grad_out,
        grad_gate,
        grad_up,
        grad_down,
        block_out,
        x_grad,
        grad_norm_attn,
        grad_norm_mlp,
    ) = assemble(
        wide_qkv.reshape(n, shard_rows, qkv_lanes),
        wide_gate_up.reshape(n, shard_rows, 2 * lanes),
        tall_down.reshape(lanes, width),
        tall_out.reshape(head_lanes, width),
        block_out,
        x_grad,
        gain_grads,
        units,
    )
    return (
        block_out[None],
        x_grad[None],
        grad_norm_attn,
        grad_qkv,
        grad_out,
        grad_norm_mlp,
        grad_gate,
        grad_up,
        grad_down,
    )


def body_for(mesh):
    return per_device if HEADS % mesh.shape["blk"] == 0 else per_device_gather


def solution(mesh):
    return jax.shard_map(
        body_for(mesh),
        mesh=mesh,
        in_specs=(
            P("grp", "blk", None),
            P("grp", None),
            P("blk"),
            P("blk", None),
            P("blk", None),
            P("blk"),
            P("blk", None),
            P("blk", None),
            P("blk", None),
            P("grp", "blk", None),
        ),
        out_specs=(
            P("grp", "blk", None),
            P("grp", "blk", None),
            P("blk"),
            P("blk", None),
            P("blk", None),
            P("blk"),
            P("blk", None),
            P("blk", None),
            P("blk", None),
        ),
        check_vma=False,
    )
```
